32 devices in a mesh: batch: 4 (over x, core), blk: 8 (over z, y).
Axes of the slice: x: 2, y: 2, z: 4, core: 2. Of those that a mesh axis runs over, the one named last changes fastest.
Arguments:
- frames: bfloat16 [4096, 1024], P(('batch', 'blk')), may hold values from -6 to 6
- step_table: float32 [32, 1024], replicated, may hold values from -6 to 6
- clip_lengths: int32 [4, 4], P('batch'), may hold values from 1 to 866, as said below
- clip_steps: int32 [4, 4], P('batch'), may hold values from 0 to 31
- w_mod: bfloat16 [1024, 6144], replicated, may hold values from -0.1875 to 0.1875
- b_mod: float32 [6144], replicated, may hold values from -3 to 3
- w_qkv: bfloat16 [1024, 3072], replicated, may hold values from -0.1875 to 0.1875
- b_qkv: float32 [3072], replicated, may hold values from -3 to 3
- w_out: bfloat16 [1024, 1024], replicated, may hold values from -0.75 to 0.75
- b_out: float32 [1024], replicated, may hold values from -2 to 2
- w_up: bfloat16 [1024, 2048], replicated, may hold values from -0.1875 to 0.1875
- b_up: float32 [2048], replicated, may hold values from -3 to 3
- w_down: bfloat16 [2048, 1024], replicated, may hold values from -0.125 to 0.125
- b_down: float32 [1024], replicated, may hold values from -2 to 2
- cotangent: bfloat16 [4096, 1024], P(('batch', 'blk')), may hold values from -6 to 6
Outputs:
- frames_out: bfloat16 [4096, 1024], P(('batch', 'blk'))
- d_frames: bfloat16 [4096, 1024], P(('batch', 'blk'))
- d_table: float32 [32, 1024], replicated
- d_w_mod: float32 [1024, 6144], P('blk')
- d_b_mod: float32 [6144], replicated
- d_w_qkv: float32 [1024, 3072], P('blk')
- d_b_qkv: float32 [3072], replicated
- d_w_out: float32 [1024, 1024], P('blk')
- d_b_out: float32 [1024], replicated
- d_w_up: float32 [1024, 2048], P('blk')
- d_b_up: float32 [2048], replicated
- d_w_down: float32 [2048, 1024], P('blk')
- d_b_down: float32 [1024], replicated
The draws below stay inside these ranges and needn't reach their ends.
Inputs may be any that keep to these rules, and one draw needn't show every extreme that they name: `clip_lengths`: each length is at least one frame, and each row's lengths sum to 1024. In each row one clip has exactly the largest length; it begins within the first 128 frames and ends within the last 128 frames.
All inputs are finite; a program needn't handle non-finite values.
Results may differ from the reference program's by a relative error of at most 0.018.
The reference program's roundings to bfloat16 on the way count: a program that leaves them out, or rounds other values in their place, can miss the bound.
Values may be sent and summed in bfloat16 or wider, within the bound.
No kernel may reach another device: no remote copies, remote signals or barrier semaphores. Data moves between devices by JAX's collectives and lax.ppermute only.
A program may use at most 256 MiB of HBM per device.

```python
import jax
import jax.numpy as jnp
from jax import lax

D = 1024
HEADS = 16
HDIM = 64
FF = 2048
TOK_DEV = 128
CLIPS = 4
TSTEPS = 32
GROUPS = 4
SEQ = 1024
ROWS = 4096


def split_total(key, total, count):
    powers = jax.random.randint(key, (GROUPS, count), 0, 4, dtype=jnp.int32)
    weights = jnp.left_shift(jnp.ones_like(powers), powers)
    running = jnp.cumsum(weights, axis=1)
    spare = total - count
    bounds = spare * running // running[:, -1:]
    earlier = jnp.concatenate([jnp.zeros((GROUPS, 1), jnp.int32), bounds[:, :-1]], axis=1)
    return (1 + bounds - earlier).astype(jnp.int32)


def draw_clip_lengths(key, part):
    key = jax.random.fold_in(key, 11)
    moved_key = jax.random.fold_in(key, 1)
    before_key = jax.random.fold_in(key, 2)
    after_key = jax.random.fold_in(key, 3)
    before_count = (CLIPS - 1) // 2
    after_count = CLIPS - 1 - before_count
    moved = jax.random.randint(moved_key, (GROUPS, 1), 0, TOK_DEV // 2 + 1, dtype=jnp.int32)
    before_total = TOK_DEV // 4 + moved
    after_total = TOK_DEV - 2 - moved
    before = split_total(before_key, before_total, before_count)
    after = split_total(after_key, after_total, after_count)
    longest = jnp.full((GROUPS, 1), SEQ - TOK_DEV - TOK_DEV // 4 + 2, jnp.int32)
    return jnp.concatenate([before, longest, after], axis=1).astype(jnp.int32)


def plant(drawn, own_key, low, largest):
    extent = drawn.shape
    spot = [jax.random.randint(jax.random.fold_in(own_key, axis), (), 0, extent[axis]) for axis in range(len(extent))]
    drawn = drawn.at[tuple(spot)].set(low)
    longest = extent.index(max(extent))
    spot[longest] = (spot[longest] + 1) % extent[longest]
    return drawn.at[tuple(spot)].set(largest)


def steps_of(own_key, extent, cuts, smallest, top_value):
    factor_of, own = 1.0, jax.random.fold_in(own_key, 6)
    for axis_at, blocks in cuts:
        draws = jnp.exp(jax.random.uniform(jax.random.fold_in(own, axis_at), (blocks,), jnp.float32, smallest / len(cuts), top_value / len(cuts)))
        factor_of = factor_of * jnp.repeat(draws, extent[axis_at] // blocks).reshape([-1 if axis == axis_at else 1 for axis in range(len(extent))])
    return factor_of


def normal_values(rng, dims, deviation, reach, shards=(), kind=jnp.bfloat16):
    drawn = jax.random.normal(rng, dims, jnp.float32) * deviation
    if len(shards) > 0:
        drawn = steps_of(rng, dims, shards, -0.22, 0.18) * drawn
    return jnp.clip(drawn, min=-reach, max=reach).astype(kind)


def setup_inputs(seed: int = 0) -> dict:
    seeds = jax.random.split(jax.random.key(seed), 16)
    return {
        "frames": normal_values(seeds[0], (ROWS, D), 1.0, 6.0, ((0, 32),)),
        "step_table": normal_values(seeds[1], (TSTEPS, D), 1.0, 6.0, (), jnp.float32),
        "clip_lengths": draw_clip_lengths(jax.random.fold_in(seeds[15], 71), 0),
        "clip_steps": plant(jax.random.randint(seeds[3], (GROUPS, CLIPS), 0, TSTEPS), jax.random.fold_in(seeds[3], 1), 0, TSTEPS - 1).astype(jnp.int32),
        "w_mod": normal_values(seeds[4], (D, 6 * D), D ** -0.5, 0.1875),
        "b_mod": normal_values(seeds[5], (6 * D,), 0.5, 3.0, (), jnp.float32),
        "w_qkv": normal_values(seeds[6], (D, 3 * D), D ** -0.5, 0.1875),
        "b_qkv": normal_values(seeds[7], (3 * D,), 0.5, 3.0, (), jnp.float32),
        "w_out": normal_values(seeds[8], (D, D), HDIM ** -0.5, 0.75),
        "b_out": normal_values(seeds[9], (D,), 0.3, 2.0, (), jnp.float32),
        "w_up": normal_values(seeds[10], (D, FF), D ** -0.5, 0.1875),
        "b_up": normal_values(seeds[11], (FF,), 0.5, 3.0, (), jnp.float32),
        "w_down": normal_values(seeds[12], (FF, D), FF ** -0.5, 0.125),
        "b_down": normal_values(seeds[13], (D,), 0.3, 2.0, (), jnp.float32),
        "cotangent": normal_values(seeds[14], (ROWS, D), 1.0, 6.0, ((0, 32),)),
    }


@jax.custom_vjp
def low(v):
    return lax.optimization_barrier(v.astype(jnp.bfloat16)).astype(jnp.float32)

@jax.custom_vjp
def low_back(v):
    return v

def low_keep(v):
    return (low(v), None)

def low_pass(kept, grad):
    return (grad,)

def back_keep(v):
    return (v, None)

def back_low(kept, grad):
    return (low(grad),)
low.defvjp(low_keep, low_pass)
low_back.defvjp(back_keep, back_low)
HIGH_PRECISION = lax.Precision.HIGHEST

def exact_dot(left_side, right_side):
    return jnp.dot(left_side, right_side, precision=HIGH_PRECISION)

def norm_rows(inputs):
    average = lax.optimization_barrier(jnp.mean(inputs, axis=-1, keepdims=True))
    centred = inputs - average
    variance = lax.optimization_barrier(jnp.mean(centred * centred, axis=-1, keepdims=True))
    return centred * lax.rsqrt(variance + 1e-06)

def rotate(vectors, angles):
    half_size = vectors.shape[-1] // 2
    cosine = jnp.cos(angles)[:, None, :]
    sine_part = jnp.sin(angles)[:, None, :]
    first_half = vectors[..., :half_size]
    second_half = vectors[..., half_size:]
    return jnp.concatenate([first_half * cosine - second_half * sine_part, second_half * cosine + first_half * sine_part], axis=-1)

def layer_group(group_rows, lengths, steps, table, w_mod, b_mod, w_qkv, b_qkv, w_out, b_out, w_up, b_up, w_down, b_down):
    seq_len = group_rows.shape[0]
    clip_ends = jnp.cumsum(lengths)
    clip_starts = clip_ends - lengths
    places = jnp.arange(seq_len, dtype=jnp.int32)
    clip_ids = lax.optimization_barrier(jnp.sum((clip_ends[None, :] <= places[:, None]).astype(jnp.int32), axis=1))
    member = (clip_ids[:, None] == jnp.arange(CLIPS, dtype=jnp.int32)[None, :]).astype(jnp.float32)
    offsets = lax.optimization_barrier(jnp.sum(member * clip_starts[None, :].astype(jnp.float32), axis=1))
    freqs = 10000.0 ** (-2.0 * jnp.arange(HDIM // 2, dtype=jnp.float32) / HDIM)
    angles = (places.astype(jnp.float32) - offsets)[:, None] * freqs[None, :]
    step_pick = (steps[:, None] == jnp.arange(TSTEPS, dtype=jnp.int32)[None, :]).astype(jnp.float32)
    condition = exact_dot(step_pick, table)
    silu_low = low(jax.nn.silu(condition))
    modulation = exact_dot(silu_low, w_mod) + b_mod
    frame_mod = exact_dot(member, modulation)
    shift_one, scale_one, gate_one, shift_two, scale_two, gate_two = jnp.split(frame_mod, 6, axis=1)
    first = low(norm_rows(group_rows) * (1.0 + scale_one) + shift_one)
    projected = low_back(exact_dot(first, w_qkv) + b_qkv)
    query_part, key_part, value_part = jnp.split(projected, 3, axis=1)
    queries = low(rotate(query_part.reshape(seq_len, HEADS, HDIM), angles))
    key_rows = low(rotate(key_part.reshape(seq_len, HEADS, HDIM), angles))
    value_rows = low(value_part.reshape(seq_len, HEADS, HDIM))
    block_size = min(256, seq_len)
    blocks = seq_len // block_size

    def attend(block):
        query_block, clip_block = block
        scores = jnp.einsum('qhd,khd->hqk', query_block, key_rows, precision=HIGH_PRECISION) * HDIM ** (-0.5)
        scores = low_back(scores)
        visible = clip_block[:, None] == clip_ids[None, :]
        scores = jnp.where(visible[None], scores, -1e+30)
        highest = lax.optimization_barrier(jnp.max(scores, axis=-1, keepdims=True))
        expo = jnp.exp(scores - highest)
        probabilities = expo / lax.optimization_barrier(jnp.sum(expo, axis=-1, keepdims=True))
        return jnp.einsum('hqk,khd->qhd', low(probabilities), value_rows, precision=HIGH_PRECISION)
    attended = lax.map(jax.checkpoint(attend), (queries.reshape(blocks, block_size, HEADS, HDIM), clip_ids.reshape(blocks, block_size)))
    attended = attended.reshape(seq_len, HEADS * HDIM)
    attended = low(low_back(attended))
    attn_out = low_back(exact_dot(attended, w_out) + b_out)
    middle = group_rows + gate_one * attn_out
    second = low(norm_rows(middle) * (1.0 + scale_two) + shift_two)
    hidden = low_back(exact_dot(second, w_up) + b_up)
    activated = low(jax.nn.gelu(hidden, approximate=True))
    ffn_out = low_back(exact_dot(activated, w_down) + b_down)
    return middle + gate_two * ffn_out

def reference(frames, step_table, clip_lengths, clip_steps, w_mod, b_mod, w_qkv, b_qkv, w_out, b_out, w_up, b_up, w_down, b_down, cotangent):

    def forward(inputs, table, wm, bm, wq, bq, wo, bo, wu, bu, wd, bd):
        pieces = []
        for group_index in range(GROUPS):
            group_rows = inputs[group_index * SEQ:(group_index + 1) * SEQ]
            pieces.append(layer_group(group_rows, clip_lengths[group_index], clip_steps[group_index], table, wm, bm, wq, bq, wo, bo, wu, bu, wd, bd))
        return jnp.concatenate(pieces, axis=0)
    result, pull = jax.vjp(forward, frames.astype(jnp.float32), step_table, w_mod.astype(jnp.float32), b_mod, w_qkv.astype(jnp.float32), b_qkv, w_out.astype(jnp.float32), b_out, w_up.astype(jnp.float32), b_up, w_down.astype(jnp.float32), b_down)
    grads = pull(cotangent.astype(jnp.float32))
    return (result.astype(jnp.bfloat16), grads[0].astype(jnp.bfloat16), grads[1], grads[2], grads[3], grads[4], grads[5], grads[6], grads[7], grads[8], grads[9], grads[10], grads[11])
```

```python
import jax
import jax.numpy as jnp
import numpy as np
from jax import lax
from jax.experimental import pallas as pl
from jax.experimental.pallas import tpu as pltpu
from jax.sharding import PartitionSpec as P

HEADS = 16


HIGH_PRECISION = lax.Precision.HIGHEST
NEGATIVE = -1e30


def passed_along(value, axis, by):
    size = lax.axis_size(axis)
    return lax.ppermute(value, axis, [(i, (i + by) % size) for i in range(size)])


def norm_rows(inputs):
    average = jnp.mean(inputs, axis=-1, keepdims=True)
    centred = inputs - average
    variance = jnp.mean(centred * centred, axis=-1, keepdims=True)
    return centred * lax.rsqrt(variance + 1e-06)


def modulated(inputs, shift_part, scale_part):
    return norm_rows(inputs) * (1.0 + scale_part) + shift_part


def rotate(vectors, cosine, sine_part):
    half_size = vectors.shape[-1] // 2
    first_half = vectors[..., :half_size]
    second_half = vectors[..., half_size:]
    return jnp.concatenate(
        [
            first_half * cosine - second_half * sine_part,
            second_half * cosine + first_half * sine_part,
        ],
        axis=-1,
    )


def exact_dot(left_side, right_side):
    return jnp.dot(left_side, right_side, precision=HIGH_PRECISION)


def clip_index(positions, clip_ends):
    return jnp.sum((clip_ends[None, :] <= positions[:, None]).astype(jnp.int32), axis=1)


def attend_block(queries, key_rows, value_rows, visible, carry_state, scale):
    running_max, denominator, numerator = carry_state
    scores = (
        jnp.einsum("qhd,khd->hqk", queries, key_rows, preferred_element_type=jnp.float32) * scale
    )
    scores = jnp.where(visible[None], scores, NEGATIVE)
    new_max = jnp.maximum(running_max, jnp.max(scores, axis=-1))
    factor = jnp.exp(running_max - new_max)
    probabilities = jnp.where(visible[None], jnp.exp(scores - new_max[..., None]), 0.0)
    denominator = factor * denominator + jnp.sum(probabilities, axis=-1)
    numerator = numerator * jnp.transpose(factor)[:, :, None] + jnp.einsum(
        "hqk,khd->qhd",
        probabilities.astype(jnp.bfloat16),
        value_rows,
        preferred_element_type=jnp.float32,
    )
    return (new_max, denominator, numerator)


def grad_block(queries, upstream, log_total, row_delta, key_rows, value_rows, visible, scale):
    scores = (
        jnp.einsum("qhd,khd->hqk", queries, key_rows, preferred_element_type=jnp.float32) * scale
    )
    probabilities = jnp.where(
        visible[None],
        jnp.exp(jnp.where(visible[None], scores, NEGATIVE) - log_total[..., None]),
        0.0,
    )
    d_probs = jnp.einsum("qhd,khd->hqk", upstream, value_rows, preferred_element_type=jnp.float32)
    d_scores = (probabilities * (d_probs - row_delta[..., None])).astype(jnp.bfloat16)
    d_query = scale * jnp.einsum(
        "hqk,khd->qhd", d_scores, key_rows, preferred_element_type=jnp.float32
    )
    d_key = scale * jnp.einsum(
        "hqk,qhd->khd", d_scores, queries, preferred_element_type=jnp.float32
    )
    d_value = jnp.einsum(
        "hqk,qhd->khd",
        probabilities.astype(jnp.bfloat16),
        upstream,
        preferred_element_type=jnp.float32,
    )
    return (d_query, d_key, d_value)


def pass_key_grads(gradients):
    return (
        passed_along(gradients[0].astype(jnp.bfloat16), "blk", 1).astype(jnp.float32),
        passed_along(gradients[1].astype(jnp.bfloat16), "blk", 1).astype(jnp.float32),
    )


def ring_body(
    frames,
    step_table,
    clip_lengths,
    clip_steps,
    w_mod,
    b_mod,
    w_qkv,
    b_qkv,
    w_out,
    b_out,
    w_up,
    b_up,
    w_down,
    b_down,
    cotangent,
):
    frame_count, model_width = frames.shape
    ffn_width = w_up.shape[1]
    cycle_size = lax.axis_size("blk")
    cycle_place = lax.axis_index("blk")
    head_count = HEADS
    head_size = model_width // head_count
    scale = head_size ** (-0.5)
    lengths = clip_lengths[0]
    steps = clip_steps[0]
    clip_count = lengths.shape[0]
    clip_ends = jnp.cumsum(lengths)
    clip_starts = clip_ends - lengths
    local_rows = jnp.arange(frame_count, dtype=jnp.int32)
    places = cycle_place * frame_count + local_rows
    clip_own = clip_index(places, clip_ends)
    member = (clip_own[:, None] == jnp.arange(clip_count, dtype=jnp.int32)[None, :]).astype(
        jnp.float32
    )
    offsets = jnp.sum(member * clip_starts[None, :].astype(jnp.float32), axis=1)
    freqs = 10000.0 ** (-2.0 * jnp.arange(head_size // 2, dtype=jnp.float32) / head_size)
    angles = (places.astype(jnp.float32) - offsets)[:, None] * freqs[None, :]
    cosine = jnp.cos(angles)[:, None, :]
    sine_part = jnp.sin(angles)[:, None, :]

    def clip_of(turn_index):
        source = (cycle_place - turn_index) % cycle_size
        return clip_index(source * frame_count + local_rows, clip_ends)

    step_pick = (
        steps[:, None] == jnp.arange(step_table.shape[0], dtype=jnp.int32)[None, :]
    ).astype(jnp.float32)
    condition = exact_dot(step_pick, step_table)
    silu_low = jax.nn.silu(condition).astype(jnp.bfloat16)
    modulation = jnp.dot(silu_low, w_mod, preferred_element_type=jnp.float32) + b_mod
    frame_mod = exact_dot(member, modulation)
    shift_one, scale_one, gate_one, shift_two, scale_two, gate_two = jnp.split(frame_mod, 6, axis=1)
    inputs = frames.astype(jnp.float32)
    first, first_back = jax.vjp(modulated, inputs, shift_one, scale_one)
    first_low = first.astype(jnp.bfloat16)
    projected = jnp.dot(first_low, w_qkv, preferred_element_type=jnp.float32) + b_qkv
    query_part, key_part, value_part = jnp.split(projected, 3, axis=1)

    def spin(query_lin, key_lin):
        return (
            rotate(query_lin.reshape(frame_count, head_count, head_size), cosine, sine_part),
            rotate(key_lin.reshape(frame_count, head_count, head_size), cosine, sine_part),
        )

    (query_rot, key_rot), spin_back = jax.vjp(spin, query_part, key_part)
    queries = query_rot.astype(jnp.bfloat16)
    key_rows = key_rot.astype(jnp.bfloat16)
    value_rows = value_part.reshape(frame_count, head_count, head_size).astype(jnp.bfloat16)

    def forward_step(turn_index, key_value, carry_state):
        visible = clip_own[:, None] == clip_of(turn_index)[None, :]
        return attend_block(queries, key_value[0], key_value[1], visible, carry_state, scale)

    def forward_turn(turn_index, carry):
        key_value, carry_state = carry
        carry_state = forward_step(turn_index, key_value, carry_state)
        key_value = passed_along((key_value[0], key_value[1]), "blk", 1)
        return (key_value, carry_state)

    initial = (
        jnp.full((head_count, frame_count), NEGATIVE, jnp.float32),
        jnp.zeros((head_count, frame_count), jnp.float32),
        jnp.zeros((frame_count, head_count, head_size), jnp.float32),
    )
    key_value, carry_state = lax.fori_loop(
        0, cycle_size - 1, forward_turn, ((key_rows, value_rows), initial)
    )
    running_max, denominator, numerator = forward_step(cycle_size - 1, key_value, carry_state)
    attended = numerator / jnp.transpose(denominator)[:, :, None]
    log_total = running_max + jnp.log(denominator)
    attended_low = attended.reshape(frame_count, model_width).astype(jnp.bfloat16)
    attn_out = jnp.dot(attended_low, w_out, preferred_element_type=jnp.float32) + b_out
    middle = inputs + gate_one * attn_out
    second, second_back = jax.vjp(modulated, middle, shift_two, scale_two)
    second_low = second.astype(jnp.bfloat16)
    hidden = jnp.dot(second_low, w_up, preferred_element_type=jnp.float32) + b_up
    activated, gelu_back = jax.vjp(
        lambda values_in: jax.nn.gelu(values_in, approximate=True), hidden
    )
    activated_low = activated.astype(jnp.bfloat16)
    ffn_out = jnp.dot(activated_low, w_down, preferred_element_type=jnp.float32) + b_down
    result = middle + gate_two * ffn_out
    upstream_y = cotangent.astype(jnp.float32)
    d_ffn = (gate_two * upstream_y).astype(jnp.bfloat16)
    d_gate_two = upstream_y * ffn_out
    d_act = jnp.dot(d_ffn, w_down.T, preferred_element_type=jnp.float32)
    d_hidden = gelu_back(d_act)[0].astype(jnp.bfloat16)
    d_second = jnp.dot(d_hidden, w_up.T, preferred_element_type=jnp.float32)
    d_middle_norm, d_shift_two, d_scale_two = second_back(d_second)
    d_middle = upstream_y + d_middle_norm
    d_attn = (gate_one * d_middle).astype(jnp.bfloat16)
    d_gate_one = d_middle * attn_out
    d_attended = jnp.dot(d_attn, w_out.T, preferred_element_type=jnp.float32).astype(jnp.bfloat16)
    d_attended = d_attended.reshape(frame_count, head_count, head_size)
    row_delta = jnp.transpose(jnp.sum(d_attended.astype(jnp.float32) * attended, axis=-1))
    zeros_three = jnp.zeros((frame_count, head_count, head_size), jnp.float32)

    def key_step(turn_index, key_value, owed):
        visible = clip_own[:, None] == clip_of(turn_index)[None, :]
        d_query, d_key, d_value = grad_block(
            queries, d_attended, log_total, row_delta, key_value[0], key_value[1], visible, scale
        )
        return (owed[0] + d_query, (owed[1][0] + d_key, owed[1][1] + d_value))

    def key_turn(turn_index, carry):
        key_value, owed = carry
        d_query_sum, gradients = key_step(turn_index, key_value, owed)
        key_value = passed_along((key_value[0], key_value[1]), "blk", 1)
        gradients = pass_key_grads(gradients)
        return (key_value, (d_query_sum, gradients))

    key_value, owed = lax.fori_loop(
        0,
        cycle_size - 1,
        key_turn,
        ((key_rows, value_rows), (zeros_three, (zeros_three, zeros_three))),
    )
    d_query_rot, gradients = key_step(cycle_size - 1, key_value, owed)
    d_key_rot, d_value_all = pass_key_grads(gradients)
    d_query_lin, d_key_lin = spin_back((d_query_rot, d_key_rot))
    d_projected = jnp.concatenate(
        [d_query_lin, d_key_lin, d_value_all.reshape(frame_count, model_width)], axis=1
    ).astype(jnp.bfloat16)
    d_first = jnp.dot(d_projected, w_qkv.T, preferred_element_type=jnp.float32)
    d_input_norm, d_shift_one, d_scale_one = first_back(d_first)
    d_inputs = d_middle + d_input_norm
    d_frame_mod = jnp.concatenate(
        [d_shift_one, d_scale_one, d_gate_one, d_shift_two, d_scale_two, d_gate_two], axis=1
    )
    d_modulation = exact_dot(member.T, d_frame_mod)
    d_silu = jnp.dot(d_modulation, w_mod.T, precision=HIGH_PRECISION)
    d_condition = jax.vjp(jax.nn.silu, condition)[1](d_silu)[0]
    d_table_local = exact_dot(step_pick.T, d_condition)
    small = lax.psum(
        (
            jnp.sum(d_modulation, axis=0),
            jnp.sum(d_projected.astype(jnp.float32), axis=0),
            jnp.sum(d_attn.astype(jnp.float32), axis=0),
            jnp.sum(d_hidden.astype(jnp.float32), axis=0),
            jnp.sum(d_ffn.astype(jnp.float32), axis=0),
            d_table_local,
        ),
        ("batch", "blk"),
    )
    d_b_mod, d_b_qkv, d_b_out, d_b_up, d_b_down, d_table = small
    blocks_list = [
        jnp.dot(first_low.T, d_projected, preferred_element_type=jnp.float32),
        jnp.dot(attended_low.T, d_attn, preferred_element_type=jnp.float32),
        jnp.dot(second_low.T, d_hidden, preferred_element_type=jnp.float32),
    ]
    blocks_list.append(exact_dot(silu_low.T.astype(jnp.float32), d_modulation))
    wide_rows = lax.psum_scatter(
        jnp.concatenate(blocks_list, axis=1), "blk", scatter_dimension=0, tiled=True
    )
    down_part = lax.psum_scatter(
        jnp.dot(activated_low.T, d_ffn, preferred_element_type=jnp.float32),
        "blk",
        scatter_dimension=0,
        tiled=True,
    )
    wide_rows, down_part = (
        lax.psum(wide_rows.astype(jnp.bfloat16), "batch").astype(jnp.float32),
        lax.psum(down_part.astype(jnp.bfloat16), "batch").astype(jnp.float32),
    )
    qkv_end = 3 * model_width
    out_end = qkv_end + model_width
    up_end = out_end + ffn_width
    return (
        result.astype(jnp.bfloat16),
        d_inputs.astype(jnp.bfloat16),
        d_table,
        wide_rows[:, up_end:],
        d_b_mod,
        wide_rows[:, :qkv_end],
        d_b_qkv,
        wide_rows[:, qkv_end:out_end],
        d_b_out,
        wide_rows[:, out_end:up_end],
        d_b_up,
        down_part,
        d_b_down,
    )


BF = jnp.bfloat16
F32 = jnp.float32
LANES = 128
MIB = 1024 * 1024


def swapped_with(value, axis, offset):
    size = lax.axis_size(axis)
    return lax.ppermute(value, axis, [(i, i ^ offset) for i in range(size)])


def gathered_blocks(value, count):
    evens = [value] + [swapped_with(value, "blk", k) for k in range(2, count, 2)]
    odds = [swapped_with(e, "blk", 1) for e in evens]
    return [b for pair in zip(evens, odds) for b in pair]


def half_swap(value, lane):
    return jnp.where((lane % 64) < 32, pltpu.roll(value, 96, 1), pltpu.roll(value, 32, 1))


def by_clip(clip, table, first, count):
    chosen = table[first : first + 1, :]
    for c in range(1, count):
        chosen = jnp.where(clip == c, table[first + c : first + c + 1, :], chosen)
    return chosen


def project_kernel(clips, clip_ref, x_ref, mod_ref, w_ref, b_ref, cos_ref, sin_ref, h_ref, qkv_ref):
    width = x_ref.shape[1]
    x = x_ref[...].astype(F32)
    centred = x - jnp.mean(x, axis=-1, keepdims=True)
    rstd = lax.rsqrt(jnp.mean(centred * centred, axis=-1, keepdims=True) + 1e-06)
    clip = clip_ref[...]
    scale = by_clip(clip, mod_ref[...], clips, clips)
    shift = by_clip(clip, mod_ref[...], 0, clips)
    h = (centred * rstd * (1.0 + scale) + shift).astype(BF)
    h_ref[...] = h
    cosine, sine = cos_ref[...], sin_ref[...]
    lane = lax.broadcasted_iota(jnp.int32, cosine.shape, 1)
    step = 2 * LANES
    for start in range(0, 3 * width, step):
        part = jnp.dot(h, w_ref[:, start : start + step], preferred_element_type=F32)
        part = part + b_ref[:, start : start + step]
        for inner in range(0, step, LANES):
            piece = part[:, inner : inner + LANES]
            if start < 2 * width:
                piece = piece * cosine + half_swap(piece, lane) * sine
            if start < width:
                piece = piece * 0.125
            qkv_ref[:, start + inner : start + inner + LANES] = piece.astype(BF)


def project(frames_all, clip_col, mod_one, w_qkv, b_qkv, cosine, sine, clips):
    rows, width = frames_all.shape
    tile = 256
    return pl.pallas_call(
        lambda *refs: project_kernel(clips, *refs),
        grid=(rows // tile,),
        in_specs=[
            pl.BlockSpec((tile, 1), lambda i: (i, 0)),
            pl.BlockSpec((tile, width), lambda i: (i, 0)),
            pl.BlockSpec(mod_one.shape, lambda i: (0, 0)),
            pl.BlockSpec(w_qkv.shape, lambda i: (0, 0)),
            pl.BlockSpec((1, 3 * width), lambda i: (0, 0)),
            pl.BlockSpec((tile, LANES), lambda i: (i, 0)),
            pl.BlockSpec((tile, LANES), lambda i: (i, 0)),
        ],
        out_specs=[
            pl.BlockSpec((tile, width), lambda i: (i, 0)),
            pl.BlockSpec((tile, 3 * width), lambda i: (i, 0)),
        ],
        out_shape=[
            jax.ShapeDtypeStruct((rows, width), BF),
            jax.ShapeDtypeStruct((rows, 3 * width), BF),
        ],
        compiler_params=pltpu.CompilerParams(vmem_limit_bytes=40 * MIB),
        cost_estimate=pl.CostEstimate(
            flops=6 * rows * width * width, bytes_accessed=16 * MIB, transcendentals=0
        ),
    )(clip_col, frames_all, mod_one, w_qkv, b_qkv, cosine, sine)


def contract_last(left, right):
    return lax.dot_general(left, right, (((1,), (1,)), ((), ())), preferred_element_type=F32)


def softmax_keys(key_rows, queries, visible):
    scores = jnp.where(visible, contract_last(key_rows, queries), NEGATIVE)
    expo = jnp.exp(scores - jnp.max(scores, axis=0, keepdims=True))
    return expo * (1.0 / jnp.sum(expo, axis=0, keepdims=True))


def attend_kernel(keyclip_ref, rowclip_ref, q_ref, k_ref, v_ref, o_ref):
    visible = keyclip_ref[...] == rowclip_ref[...]
    q, k = q_ref[...], k_ref[...]
    v_turned = v_ref[...].T
    lane = lax.broadcasted_iota(jnp.int32, q.shape, 1)
    parts = []
    for h in range(2):
        own = jnp.where((lane // 64) == h, q, jnp.zeros_like(q))
        probs = softmax_keys(k, own, visible).astype(BF)
        parts.append(
            jnp.dot(v_turned[64 * h : 64 * h + 64, :], probs, preferred_element_type=F32)
        )
    o_ref[...] = jnp.concatenate(parts, axis=0).T.astype(BF)


def attend(qkv, clip_col, clip_row, own_rows):
    rows, width3 = qkv.shape
    width = width3 // 3
    pairs = width // LANES
    return pl.pallas_call(
        attend_kernel,
        grid=(pairs,),
        in_specs=[
            pl.BlockSpec((rows, 1), lambda p: (0, 0)),
            pl.BlockSpec((1, own_rows), lambda p: (0, 0)),
            pl.BlockSpec((own_rows, LANES), lambda p: (0, p)),
            pl.BlockSpec((rows, LANES), lambda p: (0, pairs + p)),
            pl.BlockSpec((rows, LANES), lambda p: (0, 2 * pairs + p)),
        ],
        out_specs=pl.BlockSpec((own_rows, LANES), lambda p: (0, p)),
        out_shape=jax.ShapeDtypeStruct((own_rows, width), BF),
        compiler_params=pltpu.CompilerParams(vmem_limit_bytes=32 * MIB),
        cost_estimate=pl.CostEstimate(
            flops=4 * own_rows * rows * width, bytes_accessed=5 * MIB, transcendentals=0
        ),
    )(clip_col, clip_row[:, :own_rows], qkv, qkv, qkv)


def attend_back_kernel(
    me_ref, keyclip_ref, rowclip_ref, q_ref, k_ref, v_ref, do_ref, cos_ref, sin_ref,
    out_ref, sent_ref, dk_ref, dv_ref,
):
    i, blocks = pl.program_id(0), pl.num_programs(0)
    rows = q_ref.shape[0]
    me = me_ref[0]

    @pl.when(i == 0)
    def _():
        dk_ref[...] = jnp.zeros_like(dk_ref)
        dv_ref[...] = jnp.zeros_like(dv_ref)

    visible = keyclip_ref[...] == rowclip_ref[...]
    q, k, v, upstream = q_ref[...], k_ref[...], v_ref[...], do_ref[0]
    k_turned = k.T
    lane = lax.broadcasted_iota(jnp.int32, q.shape, 1)
    probs_all, ds_all, q_all, up_all, dq_parts = [], [], [], [], []
    for h in range(2):
        mine = (lane // 64) == h
        own_q = jnp.where(mine, q, jnp.zeros_like(q))
        own_up = jnp.where(mine, upstream, jnp.zeros_like(upstream))
        probs = softmax_keys(k, own_q, visible)
        probs_low = probs.astype(BF)
        d_probs = contract_last(v, own_up)
        delta = jnp.sum(probs_low.astype(F32) * d_probs, axis=0, keepdims=True)
        ds = (probs * (d_probs - delta)).astype(BF)
        dq_parts.append(
            jnp.dot(k_turned[64 * h : 64 * h + 64, :], ds, preferred_element_type=F32)
        )
        probs_all.append(probs_low)
        ds_all.append(ds)
        q_all.append(own_q)
        up_all.append(own_up)
    dk_ref[...] += jnp.dot(
        jnp.concatenate(ds_all, axis=1), jnp.concatenate(q_all, axis=0), preferred_element_type=F32
    )
    dv_ref[...] += jnp.dot(
        jnp.concatenate(probs_all, axis=1),
        jnp.concatenate(up_all, axis=0),
        preferred_element_type=F32,
    )

    def turned_back(value, where):
        return (value * cos_ref[where, :] - half_swap(value, lane) * sin_ref[where, :]).astype(BF)

    here = pl.ds(pl.multiple_of(i * rows, rows), rows)
    dq = turned_back(jnp.concatenate(dq_parts, axis=0).T * 0.125, here)
    out_ref[here, 0:LANES] = dq
    sent_ref[me ^ i, :, 0:LANES] = dq

    @pl.when(i == blocks - 1)
    def _():
        @pl.loop(0, blocks)
        def _(j):
            there = pl.ds(pl.multiple_of(j * rows, rows), rows)
            dk = turned_back(dk_ref[there, :], there)
            dv = dv_ref[there, :].astype(BF)
            out_ref[there, LANES : 2 * LANES] = dk
            out_ref[there, 2 * LANES : 3 * LANES] = dv
            sent_ref[me ^ j, :, LANES : 2 * LANES] = dk
            sent_ref[me ^ j, :, 2 * LANES : 3 * LANES] = dv


def attend_back(me, qkv, d_o, clip_col, clip_row, cosine, sine):
    rows, width3 = qkv.shape
    pairs = width3 // 3 // LANES
    blocks, own_rows, _ = d_o.shape
    grid_spec = pltpu.PrefetchScalarGridSpec(
        num_scalar_prefetch=1,
        grid=(blocks,),
        in_specs=[
            pl.BlockSpec((rows, 1), lambda i, m: (0, 0)),
            pl.BlockSpec((1, own_rows), lambda i, m: (0, i)),
            pl.BlockSpec((own_rows, LANES), lambda i, m: (i, m[0])),
            pl.BlockSpec((rows, LANES), lambda i, m: (0, pairs + m[0])),
            pl.BlockSpec((rows, LANES), lambda i, m: (0, 2 * pairs + m[0])),
            pl.BlockSpec((1, own_rows, LANES), lambda i, m: (m[0] ^ i, 0, 0)),
            pl.BlockSpec((rows, LANES), lambda i, m: (0, 0)),
            pl.BlockSpec((rows, LANES), lambda i, m: (0, 0)),
        ],
        out_specs=[
            pl.BlockSpec((rows, 3 * LANES), lambda i, m: (0, 0)),
            pl.BlockSpec((blocks, own_rows, 3 * LANES), lambda i, m: (0, 0, 0)),
        ],
        scratch_shapes=[pltpu.VMEM((rows, LANES), F32), pltpu.VMEM((rows, LANES), F32)],
    )
    return pl.pallas_call(
        attend_back_kernel,
        grid_spec=grid_spec,
        out_shape=[
            jax.ShapeDtypeStruct((rows, 3 * LANES), BF),
            jax.ShapeDtypeStruct((blocks, own_rows, 3 * LANES), BF),
        ],
        compiler_params=pltpu.CompilerParams(vmem_limit_bytes=32 * MIB),
        cost_estimate=pl.CostEstimate(
            flops=10 * rows * rows * LANES, bytes_accessed=4 * MIB, transcendentals=0
        ),
    )(me, clip_col, clip_row, qkv, qkv, qkv, d_o, cosine, sine)


def norm_parts(inputs):
    centred = inputs - jnp.mean(inputs, axis=-1, keepdims=True)
    rstd = lax.rsqrt(jnp.mean(centred * centred, axis=-1, keepdims=True) + 1e-06)
    return centred * rstd, rstd


def norm_back(normed, rstd, gradient):
    return rstd * (
        gradient
        - jnp.mean(gradient, axis=-1, keepdims=True)
        - normed * jnp.mean(gradient * normed, axis=-1, keepdims=True)
    )


def dot_low(left, right):
    return jnp.dot(left, right, preferred_element_type=F32)


def dot_rows(left, right):
    return lax.dot_general(left, right, (((0,), (0,)), ((), ())), preferred_element_type=F32)


def gelu_parts(hidden):
    inner = 0.7978845608028654 * (hidden + 0.044715 * hidden * hidden * hidden)
    tanh = jnp.tanh(inner)
    slope = 0.5 * (1.0 + tanh) + 0.5 * hidden * (1.0 - tanh * tanh) * 0.7978845608028654 * (
        1.0 + 3.0 * 0.044715 * hidden * hidden
    )
    return 0.5 * hidden * (1.0 + tanh), slope


def batch_sum_scatter(chunks):
    place = lax.axis_index("batch")
    shape = chunks.shape[1:]
    halves = chunks.reshape((2, 2) + shape)
    core, far = place % 2, place // 2
    kept = lax.dynamic_index_in_dim(halves, core, 1, keepdims=False)
    sent = lax.dynamic_index_in_dim(halves, 1 - core, 1, keepdims=False).astype(BF)
    kept = kept + swapped_with(sent, "batch", 1).astype(F32)
    mine = lax.dynamic_index_in_dim(kept, far, 0, keepdims=False)
    sent = lax.dynamic_index_in_dim(kept, 1 - far, 0, keepdims=False).astype(BF)
    return (mine + swapped_with(sent, "batch", 2).astype(F32)).astype(BF)


def batch_gather(value):
    far_other = swapped_with(value, "batch", 2)
    near = swapped_with(value, "batch", 1)
    near_other = swapped_with(far_other, "batch", 1)
    place = lax.axis_index("batch")
    core, far = place % 2, place // 2

    def ordered(first, second, swap):
        return jnp.where(swap == 0, first, second), jnp.where(swap == 0, second, first)

    low_near, high_near = ordered(value, far_other, far)
    low_far, high_far = ordered(near, near_other, far)
    zero, one = ordered(low_near, low_far, core)
    two, three = ordered(high_near, high_far, core)
    return jnp.stack([zero, one, two, three])


def blk_sum(value, count):
    offset = 1
    while offset < count:
        value = value + swapped_with(value, "blk", offset)
        offset *= 2
    return value


def heads_body(
    frames, step_table, clip_lengths, clip_steps, w_mod, b_mod, w_qkv, b_qkv, w_out, b_out,
    w_up, b_up, w_down, b_down, cotangent,
):
    own_rows, width = frames.shape
    ffn = w_up.shape[1]
    count = lax.axis_size("blk")
    me = lax.axis_index("blk")
    lengths, steps = clip_lengths[0], clip_steps[0]
    clips = lengths.shape[0]
    clip_ends = jnp.cumsum(lengths)
    clip_starts = clip_ends - lengths
    rows = own_rows * count

    frames_all = jnp.concatenate(gathered_blocks(frames, count), axis=0)
    upstream_all = jnp.concatenate(gathered_blocks(cotangent, count), axis=0)
    steps_all = batch_gather(steps).reshape(-1)

    owner = me ^ jnp.arange(count, dtype=jnp.int32)
    places = (owner[:, None] * own_rows + jnp.arange(own_rows, dtype=jnp.int32)[None, :]).reshape(-1)
    clip_all = clip_index(places, clip_ends)
    clip_col, clip_row = clip_all[:, None], clip_all[None, :]
    starts = jnp.zeros_like(places)
    for c in range(clips):
        starts = jnp.where(clip_all == c, clip_starts[c], starts)
    head_size = width // HEADS
    freqs = 10000.0 ** (-2.0 * jnp.arange(head_size // 2, dtype=F32) / head_size)
    angles = (places - starts).astype(F32)[:, None] * freqs[None, :]
    half_cos, half_sin = jnp.cos(angles), jnp.sin(angles)
    cosine = jnp.concatenate([half_cos] * 4, axis=1)
    sine = jnp.concatenate([-half_sin, half_sin] * 2, axis=1)

    rows_of_table = jnp.arange(step_table.shape[0], dtype=jnp.int32)
    pick_all = (steps_all[:, None] == rows_of_table[None, :]).astype(F32)
    condition_all = exact_dot(pick_all, step_table)
    silu_all = jax.nn.silu(condition_all).astype(BF)
    pick = (steps[:, None] == rows_of_table[None, :]).astype(F32)
    silu_own = jax.nn.silu(exact_dot(pick, step_table)).astype(BF)
    modulation = dot_low(silu_own, w_mod) + b_mod

    mod_one = jnp.concatenate([modulation[:, :width], modulation[:, width : 2 * width]], axis=0)
    h1_all, qkv = project(
        frames_all, clip_col, mod_one, w_qkv, b_qkv[None, :], cosine, sine, clips
    )
    attended_low = attend(qkv, clip_col, clip_row, own_rows)

    own_clip = clip_col[:own_rows]
    member = (own_clip == jnp.arange(clips, dtype=jnp.int32)[None, :]).astype(F32)

    def frame_rows(index, clip):
        return by_clip(clip, modulation[:, index * width : (index + 1) * width], 0, clips)

    inputs = frames.astype(F32)
    attn_out = dot_low(attended_low, w_out) + b_out
    gate_one = frame_rows(2, own_clip)
    middle = inputs + gate_one * attn_out
    normed, rstd = norm_parts(middle)
    scale_two = frame_rows(4, own_clip)
    second_low = (normed * (1.0 + scale_two) + frame_rows(3, own_clip)).astype(BF)
    hidden = dot_low(second_low, w_up) + b_up
    activated, slope = gelu_parts(hidden)
    ffn_out = dot_low(activated.astype(BF), w_down) + b_down
    gate_two = frame_rows(5, own_clip)
    result = middle + gate_two * ffn_out
    upstream = cotangent.astype(F32)
    d_ffn = (gate_two * upstream).astype(BF)
    d_hidden = (contract_last(d_ffn, w_down) * slope).astype(BF)
    d_second = contract_last(d_hidden, w_up)
    d_middle = upstream + norm_back(normed, rstd, d_second * (1.0 + scale_two))
    d_attn = (gate_one * d_middle).astype(BF)
    d_attended = contract_last(d_attn, w_out).astype(BF)

    d_o = lax.all_to_all(d_attended, "blk", 1, 0, tiled=True).reshape(count, own_rows, LANES)
    d_qkv, d_qkv_sent = attend_back(
        me[None], qkv, d_o, clip_col, clip_row, cosine, sine
    )
    d_own = lax.all_to_all(d_qkv_sent, "blk", 0, 0, tiled=True)
    d_projected = jnp.transpose(
        d_own.reshape(count, own_rows, 3, LANES), (1, 2, 0, 3)
    ).reshape(own_rows, 3 * width)
    d_first = contract_last(d_projected, w_qkv)
    normed_one, rstd_one = norm_parts(inputs)
    scale_one = frame_rows(1, own_clip)
    d_inputs = d_middle + norm_back(normed_one, rstd_one, d_first * (1.0 + scale_one))

    def by_member(value):
        return exact_dot(member.T, value)

    d_mod = jnp.concatenate(
        [
            by_member(d_first),
            by_member(d_first * normed_one),
            by_member(d_middle * attn_out),
            by_member(d_second),
            by_member(d_second * normed),
            by_member(upstream * ffn_out),
        ],
        axis=1,
    )
    bias = jnp.concatenate(
        [
            jnp.sum(d_projected.astype(F32), axis=0),
            jnp.sum(d_attn.astype(F32), axis=0),
            jnp.sum(d_hidden.astype(F32), axis=0),
            jnp.sum(d_ffn.astype(F32), axis=0),
        ]
    )
    small = jnp.concatenate([d_mod.reshape(-1, LANES), bias.reshape(-1, LANES)], axis=0)
    small = batch_gather(blk_sum(small, count))
    mod_rows = d_mod.size // LANES
    d_mod_all = small[:, :mod_rows].reshape(-1, 6 * width)
    bias = jnp.sum(small[:, mod_rows:], axis=0).reshape(-1)
    d_b_mod = jnp.sum(d_mod_all, axis=0)
    d_silu = jnp.dot(d_mod_all, w_mod.T, precision=HIGH_PRECISION)
    d_condition = jax.vjp(jax.nn.silu, condition_all)[1](d_silu)[0]
    d_table = exact_dot(pick_all.T, d_condition)
    silu_cols = lax.dynamic_slice_in_dim(silu_all, me * own_rows, own_rows, 1).astype(F32)
    d_w_mod = exact_dot(silu_cols.T, d_mod_all)

    second_all = jnp.concatenate(gathered_blocks(second_low, count), axis=0)
    part = ffn // count
    up_cols = lax.dynamic_slice_in_dim(w_up, me * part, part, 1)
    down_rows = lax.dynamic_slice_in_dim(w_down, me * part, part, 0)
    up_bias = lax.dynamic_slice_in_dim(b_up, me * part, part, 0)
    d_ffn_all = (frame_rows(5, clip_col) * upstream_all.astype(F32)).astype(BF)
    part_act, part_slope = gelu_parts(dot_low(second_all, up_cols) + up_bias)
    part_d = (contract_last(d_ffn_all, down_rows) * part_slope).astype(BF)
    d_up_cols = dot_rows(second_all, part_d)
    d_down_rows = dot_rows(part_act.astype(BF), d_ffn_all)
    d_qkv_cols = dot_rows(h1_all, d_qkv)
    d_out_rows = lax.psum_scatter(
        dot_rows(attended_low, d_attn).astype(BF), "blk", scatter_dimension=0, tiled=True
    ).astype(F32)

    quarter = own_rows // 4

    def row_chunks(value):
        return value.reshape((4, value.shape[0] // 4) + value.shape[1:])

    def column_chunks(value):
        shaped = value.reshape(count, 4, quarter, value.shape[1])
        return jnp.transpose(shaped, (1, 0, 2, 3))

    def back_rows(value):
        return batch_gather(value).reshape(-1, value.shape[-1]).astype(F32)

    d_down = back_rows(batch_sum_scatter(row_chunks(d_down_rows)))
    d_out = back_rows(batch_sum_scatter(row_chunks(d_out_rows)))
    mine_up = lax.all_to_all(batch_sum_scatter(column_chunks(d_up_cols)), "blk", 0, 0, tiled=True)
    d_up = back_rows(jnp.transpose(mine_up, (1, 0, 2)).reshape(quarter, ffn))
    mine_qkv = lax.all_to_all(
        batch_sum_scatter(column_chunks(d_qkv_cols)), "blk", 0, 0, tiled=True
    )
    mine_qkv = jnp.transpose(mine_qkv.reshape(count, quarter, 3, LANES), (1, 2, 0, 3))
    d_w = back_rows(mine_qkv.reshape(quarter, 3 * width))

    bias_at = np.cumsum([3 * width, width, ffn])
    d_b_qkv, d_b_out, d_b_up, d_b_down = jnp.split(bias, bias_at)
    return (
        result.astype(BF),
        d_inputs.astype(BF),
        d_table,
        d_w_mod,
        d_b_mod,
        d_w,
        d_b_qkv,
        d_out,
        d_b_out,
        d_up,
        d_b_up,
        d_down,
        d_b_down,
    )


def solution(mesh):
    blk = mesh.shape["blk"]
    heads_fit = HEADS % (2 * blk) == 0 and mesh.shape["batch"] == 4
    chosen = heads_body if heads_fit else ring_body
    placed = (
        P(("batch", "blk"), None),
        P(),
        P("batch", None),
        P("batch", None),
        P(),
        P(),
        P(),
        P(),
        P(),
        P(),
        P(),
        P(),
        P(),
        P(),
        P(("batch", "blk"), None),
    )
    return jax.shard_map(
        chosen,
        mesh=mesh,
        in_specs=placed,
        out_specs=(
            P(("batch", "blk"), None),
            P(("batch", "blk"), None),
            P(),
            P("blk", None),
            P(),
            P("blk", None),
            P(),
            P("blk", None),
            P(),
            P("blk", None),
            P(),
            P("blk", None),
            P(),
        ),
        check_vma=False,
    )
```

```python
import jax
import jax.numpy as jnp
from jax import lax
from jax.experimental import pallas as pl
from jax.experimental.pallas import tpu as pltpu
from jax.sharding import PartitionSpec as P

HEADS = 16


HIGH_PRECISION = lax.Precision.HIGHEST
NEGATIVE = -1e30


def passed_along(value, axis, by):
    size = lax.axis_size(axis)
    return lax.ppermute(value, axis, [(i, (i + by) % size) for i in range(size)])


def norm_rows(inputs):
    average = jnp.mean(inputs, axis=-1, keepdims=True)
    centred = inputs - average
    variance = jnp.mean(centred * centred, axis=-1, keepdims=True)
    return centred * lax.rsqrt(variance + 1e-06)


def modulated(inputs, shift_part, scale_part):
    return norm_rows(inputs) * (1.0 + scale_part) + shift_part


def rotate(vectors, cosine, sine_part):
    half_size = vectors.shape[-1] // 2
    first_half = vectors[..., :half_size]
    second_half = vectors[..., half_size:]
    return jnp.concatenate(
        [
            first_half * cosine - second_half * sine_part,
            second_half * cosine + first_half * sine_part,
        ],
        axis=-1,
    )


def exact_dot(left_side, right_side):
    return jnp.dot(left_side, right_side, precision=HIGH_PRECISION)


def clip_index(positions, clip_ends):
    return jnp.sum((clip_ends[None, :] <= positions[:, None]).astype(jnp.int32), axis=1)


def attend_block(queries, key_rows, value_rows, visible, carry_state, scale):
    running_max, denominator, numerator = carry_state
    scores = (
        jnp.einsum("qhd,khd->hqk", queries, key_rows, preferred_element_type=jnp.float32) * scale
    )
    scores = jnp.where(visible[None], scores, NEGATIVE)
    new_max = jnp.maximum(running_max, jnp.max(scores, axis=-1))
    factor = jnp.exp(running_max - new_max)
    probabilities = jnp.where(visible[None], jnp.exp(scores - new_max[..., None]), 0.0)
    denominator = factor * denominator + jnp.sum(probabilities, axis=-1)
    numerator = numerator * jnp.transpose(factor)[:, :, None] + jnp.einsum(
        "hqk,khd->qhd",
        probabilities.astype(jnp.bfloat16),
        value_rows,
        preferred_element_type=jnp.float32,
    )
    return (new_max, denominator, numerator)


def grad_block(queries, upstream, log_total, row_delta, key_rows, value_rows, visible, scale):
    scores = (
        jnp.einsum("qhd,khd->hqk", queries, key_rows, preferred_element_type=jnp.float32) * scale
    )
    probabilities = jnp.where(
        visible[None],
        jnp.exp(jnp.where(visible[None], scores, NEGATIVE) - log_total[..., None]),
        0.0,
    )
    d_probs = jnp.einsum("qhd,khd->hqk", upstream, value_rows, preferred_element_type=jnp.float32)
    d_scores = (probabilities * (d_probs - row_delta[..., None])).astype(jnp.bfloat16)
    d_query = scale * jnp.einsum(
        "hqk,khd->qhd", d_scores, key_rows, preferred_element_type=jnp.float32
    )
    d_key = scale * jnp.einsum(
        "hqk,qhd->khd", d_scores, queries, preferred_element_type=jnp.float32
    )
    d_value = jnp.einsum(
        "hqk,qhd->khd",
        probabilities.astype(jnp.bfloat16),
        upstream,
        preferred_element_type=jnp.float32,
    )
    return (d_query, d_key, d_value)


def pass_key_grads(gradients):
    return (
        passed_along(gradients[0].astype(jnp.bfloat16), "blk", 1).astype(jnp.float32),
        passed_along(gradients[1].astype(jnp.bfloat16), "blk", 1).astype(jnp.float32),
    )


def ring_body(
    frames,
    step_table,
    clip_lengths,
    clip_steps,
    w_mod,
    b_mod,
    w_qkv,
    b_qkv,
    w_out,
    b_out,
    w_up,
    b_up,
    w_down,
    b_down,
    cotangent,
):
    frame_count, model_width = frames.shape
    ffn_width = w_up.shape[1]
    cycle_size = lax.axis_size("blk")
    cycle_place = lax.axis_index("blk")
    head_count = HEADS
    head_size = model_width // head_count
    scale = head_size ** (-0.5)
    lengths = clip_lengths[0]
    steps = clip_steps[0]
    clip_count = lengths.shape[0]
    clip_ends = jnp.cumsum(lengths)
    clip_starts = clip_ends - lengths
    local_rows = jnp.arange(frame_count, dtype=jnp.int32)
    places = cycle_place * frame_count + local_rows
    clip_own = clip_index(places, clip_ends)
    member = (clip_own[:, None] == jnp.arange(clip_count, dtype=jnp.int32)[None, :]).astype(
        jnp.float32
    )
    offsets = jnp.sum(member * clip_starts[None, :].astype(jnp.float32), axis=1)
    freqs = 10000.0 ** (-2.0 * jnp.arange(head_size // 2, dtype=jnp.float32) / head_size)
    angles = (places.astype(jnp.float32) - offsets)[:, None] * freqs[None, :]
    cosine = jnp.cos(angles)[:, None, :]
    sine_part = jnp.sin(angles)[:, None, :]

    def clip_of(turn_index):
        source = (cycle_place - turn_index) % cycle_size
        return clip_index(source * frame_count + local_rows, clip_ends)

    step_pick = (
        steps[:, None] == jnp.arange(step_table.shape[0], dtype=jnp.int32)[None, :]
    ).astype(jnp.float32)
    condition = exact_dot(step_pick, step_table)
    silu_low = jax.nn.silu(condition).astype(jnp.bfloat16)
    modulation = jnp.dot(silu_low, w_mod, preferred_element_type=jnp.float32) + b_mod
    frame_mod = exact_dot(member, modulation)
    shift_one, scale_one, gate_one, shift_two, scale_two, gate_two = jnp.split(frame_mod, 6, axis=1)
    inputs = frames.astype(jnp.float32)
    first, first_back = jax.vjp(modulated, inputs, shift_one, scale_one)
    first_low = first.astype(jnp.bfloat16)
    projected = jnp.dot(first_low, w_qkv, preferred_element_type=jnp.float32) + b_qkv
    query_part, key_part, value_part = jnp.split(projected, 3, axis=1)

    def spin(query_lin, key_lin):
        return (
            rotate(query_lin.reshape(frame_count, head_count, head_size), cosine, sine_part),
            rotate(key_lin.reshape(frame_count, head_count, head_size), cosine, sine_part),
        )

    (query_rot, key_rot), spin_back = jax.vjp(spin, query_part, key_part)
    queries = query_rot.astype(jnp.bfloat16)
    key_rows = key_rot.astype(jnp.bfloat16)
    value_rows = value_part.reshape(frame_count, head_count, head_size).astype(jnp.bfloat16)

    def forward_step(turn_index, key_value, carry_state):
        visible = clip_own[:, None] == clip_of(turn_index)[None, :]
        return attend_block(queries, key_value[0], key_value[1], visible, carry_state, scale)

    def forward_turn(turn_index, carry):
        key_value, carry_state = carry
        carry_state = forward_step(turn_index, key_value, carry_state)
        key_value = passed_along((key_value[0], key_value[1]), "blk", 1)
        return (key_value, carry_state)

    initial = (
        jnp.full((head_count, frame_count), NEGATIVE, jnp.float32),
        jnp.zeros((head_count, frame_count), jnp.float32),
        jnp.zeros((frame_count, head_count, head_size), jnp.float32),
    )
    key_value, carry_state = lax.fori_loop(
        0, cycle_size - 1, forward_turn, ((key_rows, value_rows), initial)
    )
    running_max, denominator, numerator = forward_step(cycle_size - 1, key_value, carry_state)
    attended = numerator / jnp.transpose(denominator)[:, :, None]
    log_total = running_max + jnp.log(denominator)
    attended_low = attended.reshape(frame_count, model_width).astype(jnp.bfloat16)
    attn_out = jnp.dot(attended_low, w_out, preferred_element_type=jnp.float32) + b_out
    middle = inputs + gate_one * attn_out
    second, second_back = jax.vjp(modulated, middle, shift_two, scale_two)
    second_low = second.astype(jnp.bfloat16)
    hidden = jnp.dot(second_low, w_up, preferred_element_type=jnp.float32) + b_up
    activated, gelu_back = jax.vjp(
        lambda values_in: jax.nn.gelu(values_in, approximate=True), hidden
    )
    activated_low = activated.astype(jnp.bfloat16)
    ffn_out = jnp.dot(activated_low, w_down, preferred_element_type=jnp.float32) + b_down
    result = middle + gate_two * ffn_out
    upstream_y = cotangent.astype(jnp.float32)
    d_ffn = (gate_two * upstream_y).astype(jnp.bfloat16)
    d_gate_two = upstream_y * ffn_out
    d_act = jnp.dot(d_ffn, w_down.T, preferred_element_type=jnp.float32)
    d_hidden = gelu_back(d_act)[0].astype(jnp.bfloat16)
    d_second = jnp.dot(d_hidden, w_up.T, preferred_element_type=jnp.float32)
    d_middle_norm, d_shift_two, d_scale_two = second_back(d_second)
    d_middle = upstream_y + d_middle_norm
    d_attn = (gate_one * d_middle).astype(jnp.bfloat16)
    d_gate_one = d_middle * attn_out
    d_attended = jnp.dot(d_attn, w_out.T, preferred_element_type=jnp.float32).astype(jnp.bfloat16)
    d_attended = d_attended.reshape(frame_count, head_count, head_size)
    row_delta = jnp.transpose(jnp.sum(d_attended.astype(jnp.float32) * attended, axis=-1))
    zeros_three = jnp.zeros((frame_count, head_count, head_size), jnp.float32)

    def key_step(turn_index, key_value, owed):
        visible = clip_own[:, None] == clip_of(turn_index)[None, :]
        d_query, d_key, d_value = grad_block(
            queries, d_attended, log_total, row_delta, key_value[0], key_value[1], visible, scale
        )
        return (owed[0] + d_query, (owed[1][0] + d_key, owed[1][1] + d_value))

    def key_turn(turn_index, carry):
        key_value, owed = carry
        d_query_sum, gradients = key_step(turn_index, key_value, owed)
        key_value = passed_along((key_value[0], key_value[1]), "blk", 1)
        gradients = pass_key_grads(gradients)
        return (key_value, (d_query_sum, gradients))

    key_value, owed = lax.fori_loop(
        0,
        cycle_size - 1,
        key_turn,
        ((key_rows, value_rows), (zeros_three, (zeros_three, zeros_three))),
    )
    d_query_rot, gradients = key_step(cycle_size - 1, key_value, owed)
    d_key_rot, d_value_all = pass_key_grads(gradients)
    d_query_lin, d_key_lin = spin_back((d_query_rot, d_key_rot))
    d_projected = jnp.concatenate(
        [d_query_lin, d_key_lin, d_value_all.reshape(frame_count, model_width)], axis=1
    ).astype(jnp.bfloat16)
    d_first = jnp.dot(d_projected, w_qkv.T, preferred_element_type=jnp.float32)
    d_input_norm, d_shift_one, d_scale_one = first_back(d_first)
    d_inputs = d_middle + d_input_norm
    d_frame_mod = jnp.concatenate(
        [d_shift_one, d_scale_one, d_gate_one, d_shift_two, d_scale_two, d_gate_two], axis=1
    )
    d_modulation = exact_dot(member.T, d_frame_mod)
    d_silu = jnp.dot(d_modulation, w_mod.T, precision=HIGH_PRECISION)
    d_condition = jax.vjp(jax.nn.silu, condition)[1](d_silu)[0]
    d_table_local = exact_dot(step_pick.T, d_condition)
    small = lax.psum(
        (
            jnp.sum(d_modulation, axis=0),
            jnp.sum(d_projected.astype(jnp.float32), axis=0),
            jnp.sum(d_attn.astype(jnp.float32), axis=0),
            jnp.sum(d_hidden.astype(jnp.float32), axis=0),
            jnp.sum(d_ffn.astype(jnp.float32), axis=0),
            d_table_local,
        ),
        ("batch", "blk"),
    )
    d_b_mod, d_b_qkv, d_b_out, d_b_up, d_b_down, d_table = small
    blocks_list = [
        jnp.dot(first_low.T, d_projected, preferred_element_type=jnp.float32),
        jnp.dot(attended_low.T, d_attn, preferred_element_type=jnp.float32),
        jnp.dot(second_low.T, d_hidden, preferred_element_type=jnp.float32),
    ]
    blocks_list.append(exact_dot(silu_low.T.astype(jnp.float32), d_modulation))
    wide_rows = lax.psum_scatter(
        jnp.concatenate(blocks_list, axis=1), "blk", scatter_dimension=0, tiled=True
    )
    down_part = lax.psum_scatter(
        jnp.dot(activated_low.T, d_ffn, preferred_element_type=jnp.float32),
        "blk",
        scatter_dimension=0,
        tiled=True,
    )
    wide_rows, down_part = (
        lax.psum(wide_rows.astype(jnp.bfloat16), "batch").astype(jnp.float32),
        lax.psum(down_part.astype(jnp.bfloat16), "batch").astype(jnp.float32),
    )
    qkv_end = 3 * model_width
    out_end = qkv_end + model_width
    up_end = out_end + ffn_width
    return (
        result.astype(jnp.bfloat16),
        d_inputs.astype(jnp.bfloat16),
        d_table,
        wide_rows[:, up_end:],
        d_b_mod,
        wide_rows[:, :qkv_end],
        d_b_qkv,
        wide_rows[:, qkv_end:out_end],
        d_b_out,
        wide_rows[:, out_end:up_end],
        d_b_up,
        down_part,
        d_b_down,
    )


BF = jnp.bfloat16
F32 = jnp.float32
LANES = 128
MIB = 1024 * 1024


def swapped_with(value, axis, offset):
    size = lax.axis_size(axis)
    return lax.ppermute(value, axis, [(i, i ^ offset) for i in range(size)])


def even_blocks(value, count):
    return [value] + [swapped_with(value, "blk", k) for k in range(2, count, 2)]


def gathered_blocks(value, count):
    evens = even_blocks(value, count)
    return evens, [swapped_with(e, "blk", 1) for e in evens]


def offset_of(index, count):
    return (2 * index) % count + (2 * index) // count


def after(value, *others):
    return lax.optimization_barrier((value,) + others)[0]


def half_swap(value, lane):
    return jnp.where((lane % 64) < 32, pltpu.roll(value, 96, 1), pltpu.roll(value, 32, 1))


def by_clip(clip, table, first, count):
    chosen = table[first : first + 1, :]
    for c in range(1, count):
        chosen = jnp.where(clip == c, table[first + c : first + c + 1, :], chosen)
    return chosen


def full(shape):
    return pl.BlockSpec(shape, lambda *_: (0,) * len(shape))


ANYWHERE = pl.BlockSpec(memory_space=pl.ANY)
SCALARS = pl.BlockSpec(memory_space=pltpu.SMEM)


KEPT = pl.BlockSpec(memory_space=pltpu.VMEM)


def in_hbm(value):
    return pltpu.with_memory_space_constraint(value, pltpu.HBM)


def all_in_hbm(values):
    return [in_hbm(v) for v in values]


def shape_of(shape, dtype=BF):
    return pltpu.HBM(shape, dtype)


def params(mib=24):
    return pltpu.CompilerParams(vmem_limit_bytes=mib * MIB)


def cost(flops, moved):
    return pl.CostEstimate(flops=flops, bytes_accessed=moved, transcendentals=0)


def prepare_kernel(
    count, me_ref, lengths_ref, steps_ref, table_ref, freq_ref, w_ref, b_ref, later_ref, *refs
):
    silu, sems = refs[-2:]
    kept = (len(refs) - 10) // 2
    sources, targets = refs[:kept], refs[-2 - kept : -2]
    out_ref, silu_ref, clip_ref, cliprow_ref, cos_ref, sin_ref, marks_ref, passed_ref = refs[
        kept : kept + 8
    ]
    clips = lengths_ref.shape[1]
    rows = cos_ref.shape[0] // count
    i = pl.program_id(0)

    def copies():
        return [
            pltpu.make_async_copy(
                source.at[:, pl.ds(0, target.shape[1])], target, sems.at[j]
            )
            for j, (source, target) in enumerate(zip(sources, targets))
        ]

    @pl.when(i == 0)
    def _():
        for copy in copies():
            copy.start()
        passed_ref[...] = later_ref[...]
        for c in range(clips):
            row = table_ref[pl.ds(steps_ref[0, c], 1), :]
            silu[c : c + 1, :] = row / (1.0 + jnp.exp(-row))
        silu_ref[...] = silu[:clips, :].astype(BF)

    out_ref[...] = dot_low(silu[...].astype(BF), w_ref[...])[:clips] + b_ref[...]

    @pl.when(i == 0)
    def _():
        def clip_and_start(places):
            clip, start, end = jnp.zeros_like(places), jnp.zeros_like(places), 0
            for c in range(clips):
                end = end + lengths_ref[0, c]
                clip = jnp.where(places >= end, c + 1, clip)
                start = jnp.where(places >= end, end, start)
            return clip, start

        for j in range(count):
            first = (me_ref[0] ^ offset_of(j, count)) * rows
            here = slice(j * rows, (j + 1) * rows)
            places = first + lax.broadcasted_iota(jnp.int32, (rows, LANES), 0)
            lane = lax.broadcasted_iota(jnp.int32, (rows, LANES), 1)
            clip, start = clip_and_start(places)
            angles = (places - start).astype(F32) * freq_ref[...]
            cos_ref[here, :] = jnp.cos(angles)
            sine = jnp.sin(angles)
            sin_ref[here, :] = jnp.where((lane % 64) < 32, -sine, sine)
            clip_ref[here, :] = clip[:, :1]
            places = first + lax.broadcasted_iota(jnp.int32, (1, rows), 1)
            cliprow_ref[:, here] = clip_and_start(places)[0]
            other = jnp.where((clip != lane) & (lane < clips), NEGATIVE, 0.0)
            marks_ref[here, :LANES] = other.astype(BF)
            marks_ref[here, LANES:] = jnp.where(clip == lane, 1.0, 0.0).astype(BF)

    @pl.when(i == pl.num_programs(0) - 1)
    def _():
        for copy in copies():
            copy.wait()


def prepare(me, lengths, steps, step_table, freqs, w_mod, b_mod, later, weights, own_rows, count):
    width = w_mod.shape[0]
    clips = lengths.shape[1]
    tile = width
    rows = own_rows * count
    shapes = [
        shape_of((clips, 2 * width), F32),
        shape_of((clips, width)),
        shape_of((rows, 1), jnp.int32),
        shape_of((1, rows), jnp.int32),
        shape_of((rows, LANES), F32),
        shape_of((rows, LANES), F32),
        shape_of((rows, 2 * LANES)),
        shape_of(later.shape, later.dtype),
    ]
    return pl.pallas_call(
        lambda *refs: prepare_kernel(count, *refs),
        grid=(2,),
        in_specs=[SCALARS] * 3
        + [
            full(step_table.shape),
            full(freqs.shape),
            pl.BlockSpec((width, tile), lambda i: (0, i)),
            pl.BlockSpec((1, tile), lambda i: (0, i)),
            full(later.shape),
        ]
        + [ANYWHERE] * len(weights),
        out_specs=[pl.BlockSpec((clips, tile), lambda i: (0, i))]
        + [full(v.shape) for v in shapes[1:]]
        + [KEPT] * len(weights),
        out_shape=shapes + [pltpu.VMEM(w.shape, w.dtype) for w in weights],
        scratch_shapes=[pltpu.VMEM((8, width), F32), pltpu.SemaphoreType.DMA((len(weights),))],
        compiler_params=params(),
        cost_estimate=cost(4 * clips * width * width, 5 * width * width),
    )(me, lengths, steps, *all_in_hbm([step_table, freqs, w_mod, b_mod, later, *weights]))


def modulate_kernel(silu_ref, w_ref, b_ref, out_ref):
    out_ref[...] = dot_low(silu_ref[...], w_ref[...]) + b_ref[...]


def modulate(silu, w_mod, b_mod):
    clips, width = silu.shape
    return pl.pallas_call(
        modulate_kernel,
        grid=(4,),
        in_specs=[
            full(silu.shape),
            pl.BlockSpec((width, width), lambda i: (0, 2 + i)),
            pl.BlockSpec((1, width), lambda i: (0, 2 + i)),
        ],
        out_specs=pl.BlockSpec((clips, width), lambda i: (0, i)),
        out_shape=shape_of((clips, 4 * width), F32),
        compiler_params=params(),
        cost_estimate=cost(8 * clips * width * width, 8 * width * width),
    )(*all_in_hbm([silu, w_mod, b_mod]))


def project_kernel(clips, with_own, me_ref, clip_ref, mod_ref, b_ref, cos_ref, sin_ref, w, *refs):
    blocks = refs[: len(refs) - (4 if with_own else 3)]
    h_ref, kv_ref, q_ref = refs[len(blocks) : len(blocks) + 3]
    rows, width = blocks[0].shape
    column = pl.multiple_of(me_ref[0] * LANES, LANES)
    if with_own:
        own_ref = refs[-1]

    mod = mod_ref[...]
    for pair in range(len(blocks) // 2):
        here = slice(2 * pair * rows, 2 * (pair + 1) * rows)
        x = jnp.concatenate([blocks[2 * pair][...], blocks[2 * pair + 1][...]], axis=0).astype(F32)
        normed, _ = norm_parts(x)
        clip = clip_ref[here, :]
        scale = by_clip(clip, mod[:, width:], 0, clips)
        h_ref[here, :] = (normed * (1.0 + scale) + by_clip(clip, mod[:, :width], 0, clips)).astype(BF)

    h = h_ref[...]
    cosine, sine = cos_ref[...], sin_ref[...]
    lane = lax.broadcasted_iota(jnp.int32, cosine.shape, 1)

    def turned(piece, some):
        return piece * cosine[:some] + half_swap(piece, lane[:some]) * sine[:some]

    part = dot_low(h, w[:, pl.ds(column, LANES)]) + b_ref[:, pl.ds(column, LANES)]
    q_ref[...] = (turned(part, h.shape[0]) * 0.125).astype(BF)
    step = 2 * LANES
    for start in range(0 if with_own else width, 3 * width, step):
        some = rows if start < width else h.shape[0]
        part = dot_low(h[:some], w[:, start : start + step]) + b_ref[:, start : start + step]
        for inner in range(0, step, LANES):
            piece = part[:, inner : inner + LANES]
            at = start + inner
            if start < 2 * width:
                piece = turned(piece, some)
            if start < width:
                own_ref[:, at : at + LANES] = (piece * 0.125).astype(BF)
            else:
                kv_ref[(at - width) // LANES] = piece.astype(BF)


def project(half, blocks, me, clip_col, modulation, w_qkv, b_qkv, cosine, sine, with_own):
    own_rows, width = blocks[0].shape
    rows = own_rows * len(blocks)
    clips = modulation.shape[0]
    out_shape = [
        shape_of((rows, width)),
        pltpu.VMEM((2 * width // LANES, rows, LANES), BF),
        shape_of((rows, LANES)),
    ]
    if with_own:
        out_shape.append(shape_of((own_rows, width)))
    return pl.pallas_call(
        lambda *refs: project_kernel(clips, with_own, *refs),
        grid=(1,),
        in_specs=[
            SCALARS,
            pl.BlockSpec((rows, 1), lambda *_: (half, 0)),
            pl.BlockSpec((clips, 2 * width), lambda *_: (0, 0)),
            full(b_qkv.shape),
            pl.BlockSpec((rows, LANES), lambda *_: (half, 0)),
            pl.BlockSpec((rows, LANES), lambda *_: (half, 0)),
            KEPT,
        ]
        + [full(v.shape) for v in blocks],
        out_specs=[full(out_shape[0].shape), KEPT] + [full(o.shape) for o in out_shape[2:]],
        out_shape=out_shape,
        compiler_params=params(),
        cost_estimate=cost(4 * rows * width * width, 6 * MIB),
    )(me, *all_in_hbm([clip_col, modulation, b_qkv, cosine, sine]), w_qkv, *all_in_hbm(blocks))


def contract_last(left, right):
    return lax.dot_general(left, right, (((1,), (1,)), ((), ())), preferred_element_type=F32)


def head_rows(value):
    lane = lax.broadcasted_iota(jnp.int32, value.shape, 1)
    zero = jnp.zeros_like(value)
    return jnp.concatenate(
        [jnp.where(lane < 64, value, zero), jnp.where(lane < 64, zero, value)], axis=0
    )


def head_diagonal(value):
    rows = value.shape[1] // 2
    return jnp.concatenate([value[:64, :rows], value[64:, rows:]], axis=0).T


def softmax_over_keys(keys, queries):
    scores = contract_last(keys, queries)
    expo = jnp.exp(scores - jnp.max(scores, axis=0, keepdims=True))
    return expo, 1.0 / jnp.sum(expo, axis=0, keepdims=True)


def attend_kernel(keymark_ref, rowmark_ref, q_ref, ka_ref, kb_ref, o_ref, keys, values, queries):
    half = ka_ref.shape[1]
    pair, pairs = pl.program_id(0), pl.num_programs(0)

    @pl.when(pair == 0)
    def _():
        keys[:, LANES:] = keymark_ref[...]
        marks = rowmark_ref[...]
        queries[:, LANES:] = jnp.concatenate([marks, marks], axis=0)

    keys[:half, :LANES] = ka_ref[pair]
    keys[half:, :LANES] = kb_ref[pair]
    values[:half] = ka_ref[pairs + pair]
    values[half:] = kb_ref[pairs + pair]
    queries[:, :LANES] = head_rows(q_ref[...])
    expo, inverse = softmax_over_keys(keys[...], queries[...])
    turned = jnp.dot(values[...].T, expo.astype(BF), preferred_element_type=F32) * inverse
    o_ref[...] = head_diagonal(turned).astype(BF)


def attend(q, kv_a, kv_b, marks):
    own_rows, width = q.shape
    rows = 2 * kv_a.shape[1]
    return pl.pallas_call(
        attend_kernel,
        grid=(width // LANES,),
        in_specs=[
            pl.BlockSpec((rows, LANES), lambda p: (0, 0)),
            pl.BlockSpec((own_rows, LANES), lambda p: (0, 1)),
            pl.BlockSpec((own_rows, LANES), lambda p: (0, p)),
            KEPT,
            KEPT,
        ],
        out_specs=pl.BlockSpec((own_rows, LANES), lambda p: (0, p)),
        out_shape=shape_of((own_rows, width)),
        scratch_shapes=[
            pltpu.VMEM((rows, 2 * LANES), BF),
            pltpu.VMEM((rows, LANES), BF),
            pltpu.VMEM((2 * own_rows, 2 * LANES), BF),
        ],
        compiler_params=params(),
        cost_estimate=cost(4 * own_rows * rows * width, MIB),
    )(*all_in_hbm([marks, marks, q]), kv_a, kv_b)


def probs_kernel(me_ref, keyclip_ref, rowclip_ref, qa_ref, qb_ref, ka_ref, kb_ref, *refs):
    out_ref, keys = refs[-2:]
    i, blocks = pl.program_id(0), pl.num_programs(0)
    half = ka_ref.shape[1]

    @pl.when(i == 0)
    def _():
        keys[:half] = ka_ref[me_ref[0]]
        keys[half:] = kb_ref[me_ref[0]]

    query = jnp.where(i < blocks // 2, qa_ref[...], qb_ref[...])
    visible = keyclip_ref[...] == rowclip_ref[...]
    visible = jnp.concatenate([visible, visible], axis=1)
    scores = jnp.where(visible, contract_last(keys[...], head_rows(query)), NEGATIVE)
    expo = jnp.exp(scores - jnp.max(scores, axis=0, keepdims=True))
    out_ref[...] = expo * (1.0 / jnp.sum(expo, axis=0, keepdims=True))


def heads_probs(me, q_a, q_b, kv_a, kv_b, clip_col, clip_row, blocks, earlier):
    half = kv_a.shape[1]
    rows = 2 * half
    own_rows = rows // blocks
    halfway = blocks // 2
    grid_spec = pltpu.PrefetchScalarGridSpec(
        num_scalar_prefetch=1,
        grid=(blocks,),
        in_specs=[
            pl.BlockSpec((rows, 1), lambda i, m: (0, 0)),
            pl.BlockSpec((1, own_rows), lambda i, m: (0, i)),
            pl.BlockSpec((own_rows, LANES), lambda i, m: (jnp.minimum(i, halfway - 1), 0)),
            pl.BlockSpec((own_rows, LANES), lambda i, m: (jnp.maximum(i - halfway, 0), 0)),
            KEPT,
            KEPT,
        ]
        + [ANYWHERE] * len(earlier),
        out_specs=pl.BlockSpec((rows, 2 * own_rows), lambda i, m: (0, i)),
        scratch_shapes=[pltpu.VMEM((rows, LANES), BF)],
    )
    return pl.pallas_call(
        probs_kernel,
        grid_spec=grid_spec,
        out_shape=shape_of((rows, 2 * rows), F32),
        compiler_params=params(),
        cost_estimate=cost(4 * rows * rows * LANES, 9 * MIB),
    )(me, *all_in_hbm([clip_col, clip_row, q_a, q_b]), kv_a, kv_b, *all_in_hbm(earlier))


def attend_back_kernel(
    me_ref, p_ref, qa_ref, qb_ref, ka_ref, kb_ref, do_ref, cos_ref, sin_ref, *refs
):
    out_ref, sent_ref = refs[-9:-7]
    dk_ref, dv_ref, values, keys_turned, d_probs = refs[-5:]
    i, blocks = pl.program_id(0), pl.num_programs(0)
    rows = do_ref.shape[1]
    half = ka_ref.shape[1]
    me = me_ref[0]

    @pl.when(i == 0)
    def _():
        dk_ref[...] = jnp.zeros_like(dk_ref)
        dv_ref[...] = jnp.zeros_like(dv_ref)
        for at, ref in ((0, ka_ref), (half, kb_ref)):
            values[at : at + half] = ref[ref.shape[0] // 2 + me]
            keys_turned[:, at : at + half] = ref[me].T

    query = jnp.where(i < blocks // 2, qa_ref[...], qb_ref[...])
    q_two, up_two = head_rows(query), head_rows(do_ref[0])
    delta = jnp.zeros((1, 2 * rows), F32)
    step = 256
    for start in range(0, 2 * half, step):
        part = slice(start, start + step)
        probs_low = p_ref[part, :].astype(BF)
        dv_ref[part, :] += dot_low(probs_low, up_two)
        products = contract_last(values[part, :], up_two)
        d_probs[part, :] = products
        delta += jnp.sum(probs_low.astype(F32) * products, axis=0, keepdims=True)
    d_query = jnp.zeros((LANES, 2 * rows), F32)
    for start in range(0, 2 * half, step):
        part = slice(start, start + step)
        ds = (p_ref[part, :] * (d_probs[part, :] - delta)).astype(BF)
        dk_ref[part, :] += dot_low(ds, q_two)
        d_query += dot_low(keys_turned[:, part], ds)
    lane = lax.broadcasted_iota(jnp.int32, (rows, LANES), 1)

    def turned_back(value, where):
        return (value * cos_ref[where, :] - half_swap(value, lane) * sin_ref[where, :]).astype(BF)

    here = pl.ds(pl.multiple_of(i * rows, rows), rows)
    dq = turned_back(head_diagonal(d_query) * 0.125, here)
    out_ref[here, 0:LANES] = dq
    sent_ref[me ^ offset_of(i, blocks), :, 0:LANES] = dq

    @pl.when(i == blocks - 1)
    def _():
        @pl.loop(0, blocks)
        def _(j):
            there = pl.ds(pl.multiple_of(j * rows, rows), rows)
            dk = turned_back(dk_ref[there, :], there)
            dv = dv_ref[there, :].astype(BF)
            out_ref[there, LANES : 2 * LANES] = dk
            out_ref[there, 2 * LANES : 3 * LANES] = dv
            owner = me ^ offset_of(j, blocks)
            sent_ref[owner, :, LANES : 2 * LANES] = dk
            sent_ref[owner, :, 2 * LANES : 3 * LANES] = dv


def attend_back(me, probs, q_a, q_b, kv_a, kv_b, d_o, cosine, sine, passed, earlier):
    half = kv_a.shape[1]
    rows = 2 * half
    blocks, own_rows, _ = d_o.shape
    halfway = blocks // 2
    grid_spec = pltpu.PrefetchScalarGridSpec(
        num_scalar_prefetch=1,
        grid=(blocks,),
        in_specs=[
            pl.BlockSpec((rows, 2 * own_rows), lambda i, m: (0, i)),
            pl.BlockSpec((own_rows, LANES), lambda i, m: (jnp.minimum(i, halfway - 1), 0)),
            pl.BlockSpec((own_rows, LANES), lambda i, m: (jnp.maximum(i - halfway, 0), 0)),
            KEPT,
            KEPT,
            pl.BlockSpec((1, own_rows, LANES), lambda i, m: (m[0] ^ offset_of(i, blocks), 0, 0)),
            pl.BlockSpec((rows, LANES), lambda i, m: (0, 0)),
            pl.BlockSpec((rows, LANES), lambda i, m: (0, 0)),
            ANYWHERE,
            ANYWHERE,
        ]
        + [ANYWHERE] * len(earlier),
        out_specs=[
            pl.BlockSpec((rows, 3 * LANES), lambda i, m: (0, 0)),
            pl.BlockSpec((blocks, own_rows, 3 * LANES), lambda i, m: (0, 0, 0)),
            ANYWHERE,
            ANYWHERE,
        ],
        scratch_shapes=[
            pltpu.VMEM((rows, LANES), F32),
            pltpu.VMEM((rows, LANES), F32),
            pltpu.VMEM((rows, LANES), BF),
            pltpu.VMEM((LANES, rows), BF),
            pltpu.VMEM((rows, 2 * own_rows), F32),
        ],
    )
    return pl.pallas_call(
        attend_back_kernel,
        grid_spec=grid_spec,
        out_shape=[
            shape_of((rows, 3 * LANES)),
            shape_of((blocks, own_rows, 3 * LANES)),
            shape_of(passed[0].shape, passed[0].dtype),
            shape_of(passed[1].shape, passed[1].dtype),
        ],
        input_output_aliases={9: 2, 10: 3},
        compiler_params=params(),
        cost_estimate=cost(8 * rows * rows * LANES, 12 * MIB),
    )(
        me,
        *all_in_hbm([probs, q_a, q_b]),
        kv_a,
        kv_b,
        *all_in_hbm([d_o, cosine, sine, *passed, *earlier]),
    )


def norm_parts(inputs):
    centred = inputs - jnp.mean(inputs, axis=-1, keepdims=True)
    rstd = lax.rsqrt(jnp.mean(centred * centred, axis=-1, keepdims=True) + 1e-06)
    return centred * rstd, rstd


def norm_back(normed, rstd, gradient):
    return rstd * (
        gradient
        - jnp.mean(gradient, axis=-1, keepdims=True)
        - normed * jnp.mean(gradient * normed, axis=-1, keepdims=True)
    )


def dot_low(left, right):
    return jnp.dot(left, right, preferred_element_type=F32)


def dot_rows(left, right):
    return lax.dot_general(left, right, (((0,), (0,)), ((), ())), preferred_element_type=F32)


def gelu_parts(hidden):
    square = hidden * hidden
    tanh = jnp.tanh(0.7978845608028654 * hidden * (1.0 + 0.044715 * square))
    upper = 0.5 * (1.0 + tanh)
    slope = upper + 0.5 * hidden * (1.0 - tanh * tanh) * (
        0.7978845608028654 * (1.0 + 3.0 * 0.044715 * square)
    )
    return hidden * upper, slope


def high_low(value):
    high = value.astype(BF)
    return high, (value - high.astype(F32)).astype(BF)


class RowSums:
    def __init__(self, clip_row, clips):
        self.place = lax.broadcasted_iota(jnp.int32, (8, clip_row.shape[1]), 0)
        self.member = ((self.place == clip_row) & (self.place < clips)).astype(F32).astype(BF)

    def by_clip(self, value):
        high, low = high_low(value)
        return dot_low(
            jnp.concatenate([self.member, self.member], axis=1),
            jnp.concatenate([high, low], axis=0),
        )

    def whole(self, value, row):
        return dot_low((self.place == row).astype(F32).astype(BF), value)


def middle_kernel(
    clips, steps_ref, clipc_ref, clipr_ref, x_ref, dy_ref, o_ref, mod_ref, bo_ref, bu_ref, bd_ref,
    wo_hbm, wu_hbm, wd_hbm, *refs,
):
    out_ref, h2_ref, dx_ref, da_ref, do_ref, sums_ref, wo, wu, wd, sems = refs[-10:]
    copies = [
        pltpu.make_async_copy(source, target, sems.at[i])
        for i, (source, target) in enumerate([(wo_hbm, wo), (wu_hbm, wu), (wd_hbm, wd)])
    ]
    for copy in copies:
        copy.start()
    width = x_ref.shape[1]
    ffn = wu.shape[1]
    clip = clipc_ref[...]

    def frame_rows(index):
        return by_clip(clip, mod_ref[:, (index - 2) * width : (index - 1) * width], 0, clips)

    gate_one, scale_two, gate_two = frame_rows(2), 1.0 + frame_rows(4), frame_rows(5)
    upstream = dy_ref[...].astype(F32)
    d_ffn = (gate_two * upstream).astype(BF)
    copies[0].wait()
    attn_out = dot_low(o_ref[...], wo[...]) + bo_ref[...]
    middle = x_ref[...].astype(F32) + gate_one * attn_out
    normed, rstd = norm_parts(middle)
    second = (normed * scale_two + frame_rows(3)).astype(BF)
    h2_ref[...] = second
    copies[1].wait()
    copies[2].wait()
    sums = RowSums(clipr_ref[...], clips)
    ffn_out = jnp.zeros(x_ref.shape, F32)
    d_second = jnp.zeros(x_ref.shape, F32)
    step = 512
    up_sums = []
    for start in range(0, ffn, step):
        here = slice(start, start + step)
        activated, slope = gelu_parts(dot_low(second, wu[:, here]) + bu_ref[:, here])
        ffn_out += dot_low(activated.astype(BF), wd[here, :])
        d_hidden = (contract_last(d_ffn, wd[here, :]) * slope).astype(BF)
        d_second += contract_last(d_hidden, wu[:, here])
        up_sums.append(sums.whole(d_hidden, clips))
    ffn_out += bd_ref[...]
    out_ref[...] = (middle + gate_two * ffn_out).astype(BF)
    d_middle = upstream + norm_back(normed, rstd, d_second * scale_two)
    dx_ref[...] = d_middle
    d_attn = (gate_one * d_middle).astype(BF)
    da_ref[...] = d_attn
    d_o = contract_last(d_attn, wo[...]).astype(BF)
    for k in range(width // LANES):
        do_ref[k] = d_o[:, k * LANES : (k + 1) * LANES]
    up_sums = jnp.concatenate(up_sums, axis=1)
    place = lax.broadcasted_iota(jnp.int32, (8, width), 0)
    lane = lax.broadcasted_iota(jnp.int32, (8, width), 1)
    steps = jnp.zeros((8, width), F32)
    for c in range(clips):
        here = (place == clips + 1) & (lane == c)
        steps = jnp.where(here, steps_ref[0, c].astype(F32), steps)
    sums_ref[:, :width] = (
        sums.by_clip(d_middle * attn_out) + sums.whole(d_attn, clips) + steps
    )
    sums_ref[:, width : 2 * width] = sums.by_clip(d_second) + up_sums[:, :width]
    sums_ref[:, 2 * width : 3 * width] = sums.by_clip(d_second * normed) + up_sums[:, width:]
    sums_ref[:, 3 * width :] = sums.by_clip(upstream * ffn_out) + sums.whole(d_ffn, clips)


def middle_part(
    steps, clip_col, clip_row, frames, cotangent, attended, modulation, b_out, b_up, b_down,
    w_out, w_up, w_down, earlier,
):
    rows, width = frames.shape
    clips = modulation.shape[0]
    small = [
        clip_col, clip_row, frames, cotangent, attended, modulation, b_out, b_up, b_down
    ]
    out_shape = [
        shape_of((rows, width)),
        shape_of((rows, width)),
        shape_of((rows, width), F32),
        shape_of((rows, width)),
        shape_of((width // LANES, rows, LANES)),
        shape_of((8, 4 * width), F32),
    ]
    return pl.pallas_call(
        lambda *refs: middle_kernel(clips, *refs),
        grid=(1,),
        in_specs=[SCALARS, full((rows, 1)), full((1, rows))]
        + [full(v.shape) for v in small[2:]]
        + [ANYWHERE] * 3
        + [ANYWHERE] * len(earlier),
        out_specs=[full(o.shape) for o in out_shape],
        out_shape=out_shape,
        scratch_shapes=[
            pltpu.VMEM(w_out.shape, BF),
            pltpu.VMEM(w_up.shape, BF),
            pltpu.VMEM(w_down.shape, BF),
            pltpu.SemaphoreType.DMA((3,)),
        ],
        compiler_params=params(32),
        cost_estimate=cost(20 * rows * width * width, 3 * MIB),
    )(steps, *all_in_hbm([*small, w_out, w_up, w_down, *earlier]))


def last_kernel(clips, clipc_ref, clipr_ref, x_ref, mod_ref, dx_ref, d_ref, w_hbm, *refs):
    out_ref, sums_ref, d_all, w, sems = refs[-5:]
    width = x_ref.shape[1]
    parts = 3
    copies = [
        pltpu.make_async_copy(
            w_hbm.at[:, pl.ds(i * width, width)], w.at[:, pl.ds(i * width, width)], sems.at[i]
        )
        for i in range(parts)
    ]
    for copy in copies:
        copy.start()
    for k in range(d_ref.shape[0]):
        for i in range(3):
            at = i * width + k * LANES
            d_all[:, at : at + LANES] = d_ref[k, :, i * LANES : (i + 1) * LANES]
    normed, rstd = norm_parts(x_ref[...].astype(F32))
    scale = 1.0 + by_clip(clipc_ref[...], mod_ref[...], 0, clips)
    d_first = jnp.zeros(x_ref.shape, F32)
    for i in range(parts):
        copies[i].wait()
        here = slice(i * width, (i + 1) * width)
        d_first += contract_last(d_all[:, here], w[:, here])
    out_ref[...] = (dx_ref[...] + norm_back(normed, rstd, d_first * scale)).astype(BF)
    sums = RowSums(clipr_ref[...], clips)
    sums_ref[:, :width] = (
        sums.by_clip(d_first)
        + sums.whole(d_all[:, :width], clips)
        + sums.whole(d_all[:, width : 2 * width], clips + 1)
    )
    sums_ref[:, width:] = sums.by_clip(d_first * normed) + sums.whole(d_all[:, 2 * width :], clips)


def last_part(clip_col, clip_row, frames, modulation, d_middle, d_own, w_qkv, earlier):
    rows, width = frames.shape
    clips = modulation.shape[0]
    return pl.pallas_call(
        lambda *refs: last_kernel(clips, *refs),
        grid=(1,),
        in_specs=[
            full((rows, 1)),
            full((1, rows)),
            full(frames.shape),
            pl.BlockSpec((clips, width), lambda *_: (0, 1)),
            full(d_middle.shape),
            full(d_own.shape),
        ]
        + [ANYWHERE] * (1 + len(earlier)),
        out_specs=[full((rows, width)), full((8, 2 * width))],
        out_shape=[shape_of((rows, width)), shape_of((8, 2 * width), F32)],
        scratch_shapes=[
            pltpu.VMEM((rows, 3 * width), BF),
            pltpu.VMEM(w_qkv.shape, BF),
            pltpu.SemaphoreType.DMA((3,)),
        ],
        compiler_params=params(),
        cost_estimate=cost(6 * rows * width * width, 2 * MIB),
    )(
        *all_in_hbm([clip_col, clip_row, frames, modulation, d_middle, d_own, w_qkv, *earlier]),
    )


def half_rows(core, value, kept_ref, sent_ref, at, columns):
    half = value.shape[0] // 2
    low, high = value[:half], value[half:]
    here = slice(at, at + half)
    kept_ref[here, columns] = jnp.where(core == 0, low, high)
    sent_ref[here, columns] = jnp.where(core == 0, high, low).astype(BF)


def weights_kernel(clips, count, who_ref, clip_ref, gate_ref, bu_ref, wu_hbm, wd_hbm, *refs):
    kept_ref, sent_ref, up_sum, down_sum, wu, wd, sems = refs[-7:]
    ha_ref, hb_ref, d_ref = refs[:3]
    blocks = refs[3 : 3 + count]
    seconds, upstreams = blocks[: len(blocks) // 2], blocks[len(blocks) // 2 :]
    me, core = who_ref[0], who_ref[1]
    rows, width = seconds[0].shape
    part = up_sum.shape[1]
    columns = d_ref.shape[1]
    half = ha_ref.shape[0]
    own = pl.ds(pl.multiple_of((me // 2) * part, part), part)
    copies = [
        pltpu.make_async_copy(wu_hbm.at[:, own], wu, sems.at[0]),
        pltpu.make_async_copy(wd_hbm.at[own, :], wd, sems.at[1]),
    ]
    for copy in copies:
        copy.start()
    shard = part // 2

    step = 2 * LANES
    for start in range(0, width, step):
        here = slice(start, start + step)
        value = dot_rows(ha_ref[:, here], d_ref[:half, :])
        value += dot_rows(hb_ref[:, here], d_ref[half:, :])
        for inner in range(0, step, LANES):
            half_rows(
                core, value[inner : inner + LANES], kept_ref, sent_ref, (start + inner) // 2,
                slice(0, columns),
            )

    for copy in copies:
        copy.wait()
    up_weights, down_weights = wu[...], wd[...]
    for pair in range(len(seconds) // 2):
        here = slice(2 * pair * rows, 2 * (pair + 1) * rows)
        second = jnp.concatenate([r[...] for r in seconds[2 * pair : 2 * pair + 2]], axis=0)
        upstream = jnp.concatenate([r[...] for r in upstreams[2 * pair : 2 * pair + 2]], axis=0)
        gate = by_clip(clip_ref[here, :], gate_ref[...], 0, clips)
        d_ffn = (gate * upstream.astype(F32)).astype(BF)
        activated, slope = gelu_parts(dot_low(second, up_weights) + bu_ref[:, own])
        d_hidden = (contract_last(d_ffn, down_weights) * slope).astype(BF)
        up, down = dot_rows(second, d_hidden), dot_rows(activated.astype(BF), d_ffn)
        if pair == 0:
            up_sum[...] = up
            down_sum[...] = down
        else:
            up_sum[...] += up
            down_sum[...] += down
    for y in range(2):
        mine = slice(y * shard, (y + 1) * shard)
        at = columns + 2 * y * shard
        for k in range(width // LANES):
            half_rows(
                core, up_sum[k * LANES : (k + 1) * LANES, mine], kept_ref, sent_ref,
                k * LANES // 2, slice(at, at + shard),
            )
        for c in range(width // shard):
            half_rows(
                core, down_sum[mine, c * shard : (c + 1) * shard], kept_ref, sent_ref,
                c * shard // 2, slice(at + shard, at + 2 * shard),
            )


def weights_part(who, clip_col, modulation, b_up, w_up, w_down, h1_a, h1_b, d_qkv, seconds, upstreams):
    width, ffn = w_up.shape
    count = 2 * len(seconds)
    part = 2 * ffn // count
    clips = modulation.shape[0]
    shape = (width // 2, d_qkv.shape[1] + 2 * part)
    rows = d_qkv.shape[0]
    arrays = [h1_a, h1_b, d_qkv, *seconds, *upstreams]
    return pl.pallas_call(
        lambda *refs: weights_kernel(clips, count, *refs),
        grid=(1,),
        in_specs=[
            SCALARS,
            pl.BlockSpec((rows // 2, 1), lambda *_: (0, 0)),
            pl.BlockSpec((clips, width), lambda *_: (0, 3)),
            full(b_up.shape),
            ANYWHERE,
            ANYWHERE,
        ]
        + [full(v.shape) for v in arrays],
        out_specs=[full(shape)] * 2,
        out_shape=[shape_of(shape, F32), shape_of(shape)],
        scratch_shapes=[
            pltpu.VMEM((width, part), F32),
            pltpu.VMEM((part, width), F32),
            pltpu.VMEM((width, part), BF),
            pltpu.VMEM((part, width), BF),
            pltpu.SemaphoreType.DMA((2,)),
        ],
        compiler_params=params(36),
        cost_estimate=cost(7 * rows * width * part, 10 * MIB),
    )(who, *all_in_hbm([clip_col, modulation, b_up, w_up, w_down, *arrays]))


def table_kernel(first, clips, place_ref, *refs):
    parts, refs = refs[:4], refs[4:]
    if first:
        silu_ref, w_ref = refs[:2]
        dw_ref, db_ref, out_ref, total, sums = refs[-5:]
    else:
        silu_ref, w_ref, cond_ref, pick_ref, earlier_ref, _, _ = refs[:7]
        dw_ref, db_ref, out_ref, total, sums = refs[7:]
    i = pl.program_id(0)

    @pl.when(i == 0)
    def _():
        total[...] = jnp.zeros_like(total) if first else earlier_ref[...]

    for j, part in enumerate(parts):
        value = part[...]
        valid = lax.broadcasted_iota(jnp.int32, value.shape, 0) < clips
        sums[pl.ds(pl.multiple_of((place_ref[0] ^ j) * 8, 8), 8), :] = jnp.where(valid, value, 0.0)
    high, low = high_low(sums[...])
    total[...] += contract_last(w_ref[...], jnp.concatenate([high, low], axis=0))
    silu = silu_ref[...]
    dw_ref[...] = dot_rows(
        jnp.concatenate([silu, silu], axis=0), jnp.concatenate([high, low], axis=0)
    )
    db_ref[...] = jnp.sum(sums[...], axis=0, keepdims=True)

    @pl.when(i == pl.num_programs(0) - 1)
    def _():
        if first:
            out_ref[...] = total[...]
        else:
            rows = high.shape[0]
            d_silu = total[:, :rows] + total[:, rows:]
            cond = cond_ref[...]
            gate = 1.0 / (1.0 + jnp.exp(-cond))
            d_cond = d_silu.T * (gate * (1.0 + cond * (1.0 - gate)))
            d_high, d_low = high_low(d_cond)
            lowest = (d_cond - d_high.astype(F32) - d_low.astype(F32)).astype(BF)
            pick = pick_ref[...].astype(BF)
            out_ref[...] = dot_rows(pick, d_high) + dot_rows(pick, d_low) + dot_rows(pick, lowest)


def table_part(place, sums, silu, w_mod, column, clips, rest=None, earlier=()):
    columns = sums[0].shape[1]
    width = w_mod.shape[0]
    all_columns = 6 * width
    rows, own = silu.shape
    tile = 1024
    skip = column // tile
    first = rest is None
    shapes = [
        shape_of((own, all_columns), F32),
        shape_of((1, all_columns), F32),
        shape_of((width, 2 * rows), F32),
    ]
    in_specs = [SCALARS] + [pl.BlockSpec((8, tile), lambda i: (0, i))] * 4 + [
        pl.BlockSpec((rows, own), lambda i: (0, 0)),
        pl.BlockSpec((width, tile), lambda i: (0, skip + i)),
    ]
    args = [place, *all_in_hbm([*sums, silu, w_mod])]
    aliases = {}
    if first:
        in_specs += [ANYWHERE] * len(earlier)
        args += all_in_hbm(earlier)
    else:
        condition, pick, earlier, d_w, d_b = rest
        in_specs += [
            pl.BlockSpec((rows, width), lambda i: (0, 0)),
            pl.BlockSpec(pick.shape, lambda i: (0, 0)),
            pl.BlockSpec((width, 2 * rows), lambda i: (0, 0)),
            ANYWHERE,
            ANYWHERE,
        ]
        args += all_in_hbm([condition, pick, earlier, d_w, d_b])
        aliases = {10: 0, 11: 1}
        shapes[2] = shape_of((pick.shape[1], width), F32)
    return pl.pallas_call(
        lambda *refs: table_kernel(first, clips, *refs),
        grid=(columns // tile,),
        in_specs=in_specs,
        out_specs=[
            pl.BlockSpec((own, tile), lambda i: (0, skip + i)),
            pl.BlockSpec((1, tile), lambda i: (0, skip + i)),
            pl.BlockSpec(shapes[2].shape, lambda i: (0, 0)),
        ],
        out_shape=shapes,
        scratch_shapes=[pltpu.VMEM((width, 2 * rows), F32), pltpu.VMEM((rows, tile), F32)],
        input_output_aliases=aliases,
        compiler_params=params(),
        cost_estimate=pl.CostEstimate(
            flops=4 * rows * width * columns, bytes_accessed=3 * width * columns, transcendentals=0
        ),
    )(*args)


def in_order(bit, mine, other):
    return jnp.stack([jnp.where(bit == 0, mine, other), jnp.where(bit == 0, other, mine)])


def everyone(sums, count):
    pairs = sums + swapped_with(sums, "blk", 1)
    others = [swapped_with(pairs, "blk", k) for k in range(2, count, 2)]
    level = [pairs] + others
    while len(level) > 1:
        level = [level[i] + level[i + 1] for i in range(0, len(level), 2)]
    sums = level[0]
    far = swapped_with(sums, "batch", 2)
    both = swapped_with(jnp.concatenate([sums, far], axis=0), "batch", 1)
    return [sums, both[:8], far, both[8:]]


def assemble_kernel(ffn, who_ref, *refs):
    qkv_ref, out_ref, up_ref, down_ref = refs[-4:]
    width = out_ref.shape[1]
    rows = qkv_ref.shape[0] // 4
    for j, ref in enumerate(refs[:4]):
        owner = who_ref[2] ^ j
        core, far = owner % 2, owner // 2
        at = pl.multiple_of(core * 2 * rows + far * rows, rows)
        piece = 0
        for target, count in ((qkv_ref, 3), (up_ref, ffn // width)):
            for i in range(count):
                here = slice(piece * rows, (piece + 1) * rows)
                target[pl.ds(at, rows), i * width : (i + 1) * width] = ref[here, :].astype(F32)
                piece += 1
        for g in range(2):
            here = slice(piece * rows, (piece + 1) * rows)
            there = pl.multiple_of(core * 4 * rows + g * 2 * rows + far * rows, rows)
            down_ref[pl.ds(there, rows), :] = ref[here, :].astype(F32)
            piece += 1
        part = width // 4
        for g in range(4):
            column = pl.multiple_of(owner * part, part)
            out_ref[g * rows : (g + 1) * rows, pl.ds(column, part)] = ref[
                piece * rows : (piece + 1) * rows, g * part : (g + 1) * part
            ].astype(F32)


def assemble(who, parts, own_rows, ffn):
    width = parts[0].shape[1]
    shapes = [
        shape_of((own_rows, 3 * width), F32),
        shape_of((own_rows, width), F32),
        shape_of((own_rows, ffn), F32),
        shape_of((2 * own_rows, width), F32),
    ]
    return pl.pallas_call(
        lambda *refs: assemble_kernel(ffn, *refs),
        grid=(1,),
        in_specs=[SCALARS] + [full(v.shape) for v in parts],
        out_specs=[full(o.shape) for o in shapes],
        out_shape=shapes,
        compiler_params=params(),
        cost_estimate=cost(0, 6 * MIB),
    )(who, *all_in_hbm(parts))


def heads_body(
    frames, step_table, clip_lengths, clip_steps, w_mod, b_mod, w_qkv, b_qkv, w_out, b_out,
    w_up, b_up, w_down, b_down, cotangent,
):
    own_rows, width = frames.shape
    ffn = w_up.shape[1]
    count = lax.axis_size("blk")
    me = lax.axis_index("blk")
    place = lax.axis_index("batch")
    core, far = place % 2, place // 2
    who = jnp.stack([me, core, place])
    clips = clip_lengths.shape[1]
    rows = own_rows * count

    evens, odds = gathered_blocks(frames, count)
    head_size = width // HEADS
    half = head_size // 2
    lane = jnp.arange(LANES, dtype=jnp.int32)
    freqs = 10000.0 ** (-2.0 * (lane % half).astype(F32) / head_size)
    rows_of_table = jnp.arange(step_table.shape[0], dtype=jnp.int32)
    (
        modulation, silu_own, clip_col, clip_row, cosine, sine, marks, later, kept_qkv,
    ) = prepare(
        me[None], clip_lengths, clip_steps, step_table, freqs[None, :], w_mod, b_mod[None, :],
        cotangent, [w_qkv], own_rows, count,
    )
    modulation_two = modulate(silu_own, w_mod, b_mod[None, :])

    shared = (me[None], clip_col, modulation, kept_qkv, b_qkv[None, :], cosine, sine)
    h1_a, kv_a, q_a, q_own = project(0, evens, *shared, True)
    upstreams = even_blocks(later, count)
    h1_b, kv_b, q_b = project(1, odds, *shared, False)
    attended = attend(q_own, kv_a, kv_b, marks)
    result, second, d_middle, d_attn, d_o, sums_two = middle_part(
        clip_steps, clip_col, clip_row, frames, cotangent, attended, modulation_two,
        b_out[None, :], b_up[None, :], b_down[None, :], w_out, w_up, w_down,
        upstreams,
    )
    d_o = lax.all_to_all(d_o, "blk", 0, 0, tiled=True)
    seconds = even_blocks(second, count)
    probs = heads_probs(
        me[None], q_a, q_b, kv_a, kv_b, clip_col, clip_row, count, [d_middle]
    )
    d_qkv, d_qkv_sent, sums_two, d_attn = attend_back(
        me[None], probs, q_a, q_b, kv_a, kv_b, d_o, cosine, sine, (sums_two, d_attn), seconds[:-1]
    )
    d_own = lax.all_to_all(d_qkv_sent, "blk", 0, 0, tiled=True)

    kept, sent = weights_part(
        who, clip_col, modulation_two, b_up[None, :], w_up, w_down, h1_a, h1_b, d_qkv,
        seconds, upstreams,
    )

    d_inputs, sums_one = last_part(
        clip_col, clip_row, frames, modulation, d_middle, d_own, w_qkv, []
    )
    sums_two = everyone(sums_two, count)
    steps_all = jnp.stack([v[clips + 1, :clips] for v in sums_two]) * (1.0 / count)
    steps_all = steps_all[place ^ jnp.arange(4, dtype=jnp.int32)].astype(jnp.int32)
    pick_all = (steps_all[:, :, None] == rows_of_table[None, None, :]).astype(F32)
    pick_all = jnp.pad(pick_all, ((0, 0), (0, 8 - clips), (0, 0))).reshape(32, -1)
    condition_all = exact_dot(pick_all, step_table)
    silu_all = jax.nn.silu(condition_all).astype(BF)
    silu_cols = lax.dynamic_slice_in_dim(silu_all, me * own_rows, own_rows, 1)
    d_w_mod, d_b_mod, d_silu = table_part(
        place[None], sums_two, silu_cols, w_mod, 2 * width, clips, earlier=[sums_one]
    )
    sums_one = everyone(sums_one, count)
    d_w_mod, d_b_mod, d_table = table_part(
        place[None], sums_one, silu_cols, w_mod, 0, clips,
        (condition_all, pick_all, d_silu, d_w_mod, d_b_mod),
    )

    def batch_total(parts):
        return (parts[0] + parts[1]) + (parts[2] + parts[3])

    bias_two = batch_total([v[clips] for v in sums_two])
    bias_one = batch_total([v[clips : clips + 2] for v in sums_one])
    d_b_qkv = jnp.concatenate(
        [bias_one[0, :width], bias_one[1, :width], bias_one[0, width:]], axis=0
    )
    d_b_out, d_b_up, d_b_down = jnp.split(bias_two, [width, width + ffn])

    quarter = own_rows // 4
    part = ffn // count
    mine = kept + swapped_with(sent, "batch", 1).astype(F32)
    first, even, odd = jnp.split(mine, [3 * LANES, 3 * LANES + 2 * part], axis=1)
    sent = jnp.where(me % 2 == 0, odd, even).astype(BF)
    both = jnp.where(me % 2 == 0, even, odd) + swapped_with(sent, "blk", 1).astype(F32)
    columns = 3 * LANES + 2 * part
    mine = jnp.concatenate([first, both], axis=1).reshape(count, 2, quarter, columns)
    low, high = mine[:, 0], mine[:, 1]
    sent = jnp.where(far == 0, high, low).astype(BF)
    mine = jnp.where(far == 0, low, high) + swapped_with(sent, "batch", 2).astype(F32)
    mine = mine.astype(BF)
    rows_mine = lax.all_to_all(mine[:, :, : columns - part], "blk", 0, 0, tiled=True)
    qkv_rows = [
        jnp.transpose(rows_mine[:, :, i * LANES : (i + 1) * LANES], (1, 0, 2)).reshape(quarter, width)
        for i in range(3)
    ]
    up_rows = jnp.transpose(rows_mine[:, :, 3 * LANES :], (1, 0, 2)).reshape(quarter, ffn)
    down_rows = mine[:, :, columns - part :].reshape(width // part, 2, quarter, part)
    down_rows = jnp.transpose(down_rows, (1, 2, 0, 3)).reshape(2 * quarter, width)

    wide = width // 2
    da_low, da_high = d_attn[:, :wide], d_attn[:, wide:]
    sent = jnp.concatenate([attended, jnp.where(far == 0, da_high, da_low)], axis=1)
    kept = jnp.concatenate([attended, jnp.where(far == 0, da_low, da_high)], axis=1)
    pair = jnp.concatenate([kept, swapped_with(sent, "batch", 2)], axis=0)
    left, low, high = pair[:, :width], pair[:, width : width + wide // 2], pair[:, width + wide // 2 :]
    sent = jnp.concatenate([left, jnp.where(core == 0, high, low)], axis=1)
    kept = jnp.concatenate([left, jnp.where(core == 0, low, high)], axis=1)
    pair = jnp.concatenate([kept, swapped_with(sent, "batch", 1)], axis=0)
    out_sums = dot_rows(pair[:, :width], pair[:, width:]).astype(BF).reshape(count, own_rows, -1)
    out_sums = lax.all_to_all(out_sums, "blk", 0, 0, tiled=True)
    out_sums = jnp.sum(out_sums.astype(F32), axis=0).astype(BF)
    out_rows = jnp.concatenate(
        [out_sums[g * quarter : (g + 1) * quarter] for g in range(4)], axis=1
    )

    pieces = qkv_rows + [up_rows[:, i * width : (i + 1) * width] for i in range(ffn // width)]
    mine = jnp.concatenate(pieces + [down_rows, out_rows], axis=0)
    other = swapped_with(mine, "batch", 2)
    d_w_qkv, d_w_out, d_w_up, d_w_down = assemble(
        who,
        [mine, swapped_with(mine, "batch", 1), other, swapped_with(other, "batch", 1)],
        own_rows,
        ffn,
    )

    return (
        result,
        d_inputs,
        d_table,
        d_w_mod,
        d_b_mod[0],
        d_w_qkv,
        d_b_qkv,
        d_w_out,
        d_b_out,
        d_w_up,
        d_b_up,
        d_w_down,
        d_b_down,
    )


def solution(mesh):
    blk = mesh.shape["blk"]
    heads_fit = HEADS % (2 * blk) == 0 and mesh.shape["batch"] == 4
    chosen = heads_body if heads_fit else ring_body
    placed = (
        P(("batch", "blk"), None),
        P(),
        P("batch", None),
        P("batch", None),
        P(),
        P(),
        P(),
        P(),
        P(),
        P(),
        P(),
        P(),
        P(),
        P(),
        P(("batch", "blk"), None),
    )
    return jax.shard_map(
        chosen,
        mesh=mesh,
        in_specs=placed,
        out_specs=(
            P(("batch", "blk"), None),
            P(("batch", "blk"), None),
            P(),
            P("blk", None),
            P(),
            P("blk", None),
            P(),
            P("blk", None),
            P(),
            P("blk", None),
            P(),
            P("blk", None),
            P(),
        ),
        check_vma=False,
    )
```

```python
import jax
import jax.numpy as jnp
from jax import lax
from jax.experimental import pallas as pl
from jax.experimental.pallas import tpu as pltpu
from jax.sharding import PartitionSpec as P

HEADS = 16


HIGH_PRECISION = lax.Precision.HIGHEST
NEGATIVE = -1e30


def passed_along(value, axis, by):
    size = lax.axis_size(axis)
    return lax.ppermute(value, axis, [(i, (i + by) % size) for i in range(size)])


def norm_rows(inputs):
    average = jnp.mean(inputs, axis=-1, keepdims=True)
    centred = inputs - average
    variance = jnp.mean(centred * centred, axis=-1, keepdims=True)
    return centred * lax.rsqrt(variance + 1e-06)


def modulated(inputs, shift_part, scale_part):
    return norm_rows(inputs) * (1.0 + scale_part) + shift_part


def rotate(vectors, cosine, sine_part):
    half_size = vectors.shape[-1] // 2
    first_half = vectors[..., :half_size]
    second_half = vectors[..., half_size:]
    return jnp.concatenate(
        [
            first_half * cosine - second_half * sine_part,
            second_half * cosine + first_half * sine_part,
        ],
        axis=-1,
    )


def exact_dot(left_side, right_side):
    return jnp.dot(left_side, right_side, precision=HIGH_PRECISION)


def clip_index(positions, clip_ends):
    return jnp.sum((clip_ends[None, :] <= positions[:, None]).astype(jnp.int32), axis=1)


def attend_block(queries, key_rows, value_rows, visible, carry_state, scale):
    running_max, denominator, numerator = carry_state
    scores = (
        jnp.einsum("qhd,khd->hqk", queries, key_rows, preferred_element_type=jnp.float32) * scale
    )
    scores = jnp.where(visible[None], scores, NEGATIVE)
    new_max = jnp.maximum(running_max, jnp.max(scores, axis=-1))
    factor = jnp.exp(running_max - new_max)
    probabilities = jnp.where(visible[None], jnp.exp(scores - new_max[..., None]), 0.0)
    denominator = factor * denominator + jnp.sum(probabilities, axis=-1)
    numerator = numerator * jnp.transpose(factor)[:, :, None] + jnp.einsum(
        "hqk,khd->qhd",
        probabilities.astype(jnp.bfloat16),
        value_rows,
        preferred_element_type=jnp.float32,
    )
    return (new_max, denominator, numerator)


def grad_block(queries, upstream, log_total, row_delta, key_rows, value_rows, visible, scale):
    scores = (
        jnp.einsum("qhd,khd->hqk", queries, key_rows, preferred_element_type=jnp.float32) * scale
    )
    probabilities = jnp.where(
        visible[None],
        jnp.exp(jnp.where(visible[None], scores, NEGATIVE) - log_total[..., None]),
        0.0,
    )
    d_probs = jnp.einsum("qhd,khd->hqk", upstream, value_rows, preferred_element_type=jnp.float32)
    d_scores = (probabilities * (d_probs - row_delta[..., None])).astype(jnp.bfloat16)
    d_query = scale * jnp.einsum(
        "hqk,khd->qhd", d_scores, key_rows, preferred_element_type=jnp.float32
    )
    d_key = scale * jnp.einsum(
        "hqk,qhd->khd", d_scores, queries, preferred_element_type=jnp.float32
    )
    d_value = jnp.einsum(
        "hqk,qhd->khd",
        probabilities.astype(jnp.bfloat16),
        upstream,
        preferred_element_type=jnp.float32,
    )
    return (d_query, d_key, d_value)


def pass_key_grads(gradients):
    return (
        passed_along(gradients[0].astype(jnp.bfloat16), "blk", 1).astype(jnp.float32),
        passed_along(gradients[1].astype(jnp.bfloat16), "blk", 1).astype(jnp.float32),
    )


def ring_body(
    frames,
    step_table,
    clip_lengths,
    clip_steps,
    w_mod,
    b_mod,
    w_qkv,
    b_qkv,
    w_out,
    b_out,
    w_up,
    b_up,
    w_down,
    b_down,
    cotangent,
):
    frame_count, model_width = frames.shape
    ffn_width = w_up.shape[1]
    cycle_size = lax.axis_size("blk")
    cycle_place = lax.axis_index("blk")
    head_count = HEADS
    head_size = model_width // head_count
    scale = head_size ** (-0.5)
    lengths = clip_lengths[0]
    steps = clip_steps[0]
    clip_count = lengths.shape[0]
    clip_ends = jnp.cumsum(lengths)
    clip_starts = clip_ends - lengths
    local_rows = jnp.arange(frame_count, dtype=jnp.int32)
    places = cycle_place * frame_count + local_rows
    clip_own = clip_index(places, clip_ends)
    member = (clip_own[:, None] == jnp.arange(clip_count, dtype=jnp.int32)[None, :]).astype(
        jnp.float32
    )
    offsets = jnp.sum(member * clip_starts[None, :].astype(jnp.float32), axis=1)
    freqs = 10000.0 ** (-2.0 * jnp.arange(head_size // 2, dtype=jnp.float32) / head_size)
    angles = (places.astype(jnp.float32) - offsets)[:, None] * freqs[None, :]
    cosine = jnp.cos(angles)[:, None, :]
    sine_part = jnp.sin(angles)[:, None, :]

    def clip_of(turn_index):
        source = (cycle_place - turn_index) % cycle_size
        return clip_index(source * frame_count + local_rows, clip_ends)

    step_pick = (
        steps[:, None] == jnp.arange(step_table.shape[0], dtype=jnp.int32)[None, :]
    ).astype(jnp.float32)
    condition = exact_dot(step_pick, step_table)
    silu_low = jax.nn.silu(condition).astype(jnp.bfloat16)
    modulation = jnp.dot(silu_low, w_mod, preferred_element_type=jnp.float32) + b_mod
    frame_mod = exact_dot(member, modulation)
    shift_one, scale_one, gate_one, shift_two, scale_two, gate_two = jnp.split(frame_mod, 6, axis=1)
    inputs = frames.astype(jnp.float32)
    first, first_back = jax.vjp(modulated, inputs, shift_one, scale_one)
    first_low = first.astype(jnp.bfloat16)
    projected = jnp.dot(first_low, w_qkv, preferred_element_type=jnp.float32) + b_qkv
    query_part, key_part, value_part = jnp.split(projected, 3, axis=1)

    def spin(query_lin, key_lin):
        return (
            rotate(query_lin.reshape(frame_count, head_count, head_size), cosine, sine_part),
            rotate(key_lin.reshape(frame_count, head_count, head_size), cosine, sine_part),
        )

    (query_rot, key_rot), spin_back = jax.vjp(spin, query_part, key_part)
    queries = query_rot.astype(jnp.bfloat16)
    key_rows = key_rot.astype(jnp.bfloat16)
    value_rows = value_part.reshape(frame_count, head_count, head_size).astype(jnp.bfloat16)

    def forward_step(turn_index, key_value, carry_state):
        visible = clip_own[:, None] == clip_of(turn_index)[None, :]
        return attend_block(queries, key_value[0], key_value[1], visible, carry_state, scale)

    def forward_turn(turn_index, carry):
        key_value, carry_state = carry
        carry_state = forward_step(turn_index, key_value, carry_state)
        key_value = passed_along((key_value[0], key_value[1]), "blk", 1)
        return (key_value, carry_state)

    initial = (
        jnp.full((head_count, frame_count), NEGATIVE, jnp.float32),
        jnp.zeros((head_count, frame_count), jnp.float32),
        jnp.zeros((frame_count, head_count, head_size), jnp.float32),
    )
    key_value, carry_state = lax.fori_loop(
        0, cycle_size - 1, forward_turn, ((key_rows, value_rows), initial)
    )
    running_max, denominator, numerator = forward_step(cycle_size - 1, key_value, carry_state)
    attended = numerator / jnp.transpose(denominator)[:, :, None]
    log_total = running_max + jnp.log(denominator)
    attended_low = attended.reshape(frame_count, model_width).astype(jnp.bfloat16)
    attn_out = jnp.dot(attended_low, w_out, preferred_element_type=jnp.float32) + b_out
    middle = inputs + gate_one * attn_out
    second, second_back = jax.vjp(modulated, middle, shift_two, scale_two)
    second_low = second.astype(jnp.bfloat16)
    hidden = jnp.dot(second_low, w_up, preferred_element_type=jnp.float32) + b_up
    activated, gelu_back = jax.vjp(
        lambda values_in: jax.nn.gelu(values_in, approximate=True), hidden
    )
    activated_low = activated.astype(jnp.bfloat16)
    ffn_out = jnp.dot(activated_low, w_down, preferred_element_type=jnp.float32) + b_down
    result = middle + gate_two * ffn_out
    upstream_y = cotangent.astype(jnp.float32)
    d_ffn = (gate_two * upstream_y).astype(jnp.bfloat16)
    d_gate_two = upstream_y * ffn_out
    d_act = jnp.dot(d_ffn, w_down.T, preferred_element_type=jnp.float32)
    d_hidden = gelu_back(d_act)[0].astype(jnp.bfloat16)
    d_second = jnp.dot(d_hidden, w_up.T, preferred_element_type=jnp.float32)
    d_middle_norm, d_shift_two, d_scale_two = second_back(d_second)
    d_middle = upstream_y + d_middle_norm
    d_attn = (gate_one * d_middle).astype(jnp.bfloat16)
    d_gate_one = d_middle * attn_out
    d_attended = jnp.dot(d_attn, w_out.T, preferred_element_type=jnp.float32).astype(jnp.bfloat16)
    d_attended = d_attended.reshape(frame_count, head_count, head_size)
    row_delta = jnp.transpose(jnp.sum(d_attended.astype(jnp.float32) * attended, axis=-1))
    zeros_three = jnp.zeros((frame_count, head_count, head_size), jnp.float32)

    def key_step(turn_index, key_value, owed):
        visible = clip_own[:, None] == clip_of(turn_index)[None, :]
        d_query, d_key, d_value = grad_block(
            queries, d_attended, log_total, row_delta, key_value[0], key_value[1], visible, scale
        )
        return (owed[0] + d_query, (owed[1][0] + d_key, owed[1][1] + d_value))

    def key_turn(turn_index, carry):
        key_value, owed = carry
        d_query_sum, gradients = key_step(turn_index, key_value, owed)
        key_value = passed_along((key_value[0], key_value[1]), "blk", 1)
        gradients = pass_key_grads(gradients)
        return (key_value, (d_query_sum, gradients))

    key_value, owed = lax.fori_loop(
        0,
        cycle_size - 1,
        key_turn,
        ((key_rows, value_rows), (zeros_three, (zeros_three, zeros_three))),
    )
    d_query_rot, gradients = key_step(cycle_size - 1, key_value, owed)
    d_key_rot, d_value_all = pass_key_grads(gradients)
    d_query_lin, d_key_lin = spin_back((d_query_rot, d_key_rot))
    d_projected = jnp.concatenate(
        [d_query_lin, d_key_lin, d_value_all.reshape(frame_count, model_width)], axis=1
    ).astype(jnp.bfloat16)
    d_first = jnp.dot(d_projected, w_qkv.T, preferred_element_type=jnp.float32)
    d_input_norm, d_shift_one, d_scale_one = first_back(d_first)
    d_inputs = d_middle + d_input_norm
    d_frame_mod = jnp.concatenate(
        [d_shift_one, d_scale_one, d_gate_one, d_shift_two, d_scale_two, d_gate_two], axis=1
    )
    d_modulation = exact_dot(member.T, d_frame_mod)
    d_silu = jnp.dot(d_modulation, w_mod.T, precision=HIGH_PRECISION)
    d_condition = jax.vjp(jax.nn.silu, condition)[1](d_silu)[0]
    d_table_local = exact_dot(step_pick.T, d_condition)
    small = lax.psum(
        (
            jnp.sum(d_modulation, axis=0),
            jnp.sum(d_projected.astype(jnp.float32), axis=0),
            jnp.sum(d_attn.astype(jnp.float32), axis=0),
            jnp.sum(d_hidden.astype(jnp.float32), axis=0),
            jnp.sum(d_ffn.astype(jnp.float32), axis=0),
            d_table_local,
        ),
        ("batch", "blk"),
    )
    d_b_mod, d_b_qkv, d_b_out, d_b_up, d_b_down, d_table = small
    blocks_list = [
        jnp.dot(first_low.T, d_projected, preferred_element_type=jnp.float32),
        jnp.dot(attended_low.T, d_attn, preferred_element_type=jnp.float32),
        jnp.dot(second_low.T, d_hidden, preferred_element_type=jnp.float32),
    ]
    blocks_list.append(exact_dot(silu_low.T.astype(jnp.float32), d_modulation))
    wide_rows = lax.psum_scatter(
        jnp.concatenate(blocks_list, axis=1), "blk", scatter_dimension=0, tiled=True
    )
    down_part = lax.psum_scatter(
        jnp.dot(activated_low.T, d_ffn, preferred_element_type=jnp.float32),
        "blk",
        scatter_dimension=0,
        tiled=True,
    )
    wide_rows, down_part = (
        lax.psum(wide_rows.astype(jnp.bfloat16), "batch").astype(jnp.float32),
        lax.psum(down_part.astype(jnp.bfloat16), "batch").astype(jnp.float32),
    )
    qkv_end = 3 * model_width
    out_end = qkv_end + model_width
    up_end = out_end + ffn_width
    return (
        result.astype(jnp.bfloat16),
        d_inputs.astype(jnp.bfloat16),
        d_table,
        wide_rows[:, up_end:],
        d_b_mod,
        wide_rows[:, :qkv_end],
        d_b_qkv,
        wide_rows[:, qkv_end:out_end],
        d_b_out,
        wide_rows[:, out_end:up_end],
        d_b_up,
        down_part,
        d_b_down,
    )


BF = jnp.bfloat16
F32 = jnp.float32
LANES = 128
MIB = 1024 * 1024


def swapped_with(value, axis, offset):
    size = lax.axis_size(axis)
    return lax.ppermute(value, axis, [(i, i ^ offset) for i in range(size)])


def even_blocks(value, count):
    return [value] + [swapped_with(value, "blk", k) for k in range(2, count, 2)]


def gathered_blocks(value, count, zero):
    evens = even_blocks(value, count)
    return evens, [swapped_with(e, "blk", 1) for e in evens[:1]] + [
        swapped_with(e + zero, "blk", 1) for e in evens[1:]
    ]


def offset_of(index, count):
    return (2 * index) % count + (2 * index) // count


def after(value, *others):
    return lax.optimization_barrier((value,) + others)[0]


def half_swap(value, lane):
    return jnp.where((lane % 64) < 32, pltpu.roll(value, 96, 1), pltpu.roll(value, 32, 1))


def by_clip(clip, table, first, count):
    chosen = table[first : first + 1, :]
    for c in range(1, count):
        chosen = jnp.where(clip == c, table[first + c : first + c + 1, :], chosen)
    return chosen


def full(shape):
    return pl.BlockSpec(shape, lambda *_: (0,) * len(shape))


ANYWHERE = pl.BlockSpec(memory_space=pl.ANY)
SCALARS = pl.BlockSpec(memory_space=pltpu.SMEM)


KEPT = pl.BlockSpec(memory_space=pltpu.VMEM)


def in_hbm(value):
    return pltpu.with_memory_space_constraint(value, pltpu.HBM)


def all_in_hbm(values):
    return [in_hbm(v) for v in values]


def shape_of(shape, dtype=BF):
    return pltpu.HBM(shape, dtype)


def params(mib=24):
    return pltpu.CompilerParams(vmem_limit_bytes=mib * MIB)


def cost(flops, moved):
    return pl.CostEstimate(flops=flops, bytes_accessed=moved, transcendentals=0)


def prepare_kernel(
    count, me_ref, lengths_ref, steps_ref, table_ref, freq_ref, w_ref, b_ref, *refs
):
    silu, sems = refs[-2:]
    kept = (len(refs) - 9) // 2
    sources, targets = refs[:kept], refs[-2 - kept : -2]
    out_ref, silu_ref, clip_ref, cliprow_ref, cos_ref, sin_ref, marks_ref = refs[kept : kept + 7]
    clips = lengths_ref.shape[1]
    rows = cos_ref.shape[0] // count
    i = pl.program_id(0)

    def copies():
        return [
            pltpu.make_async_copy(
                source.at[:, pl.ds(0, target.shape[1])], target, sems.at[j]
            )
            for j, (source, target) in enumerate(zip(sources, targets))
        ]

    @pl.when(i == 0)
    def _():
        for copy in copies():
            copy.start()
        for c in range(clips):
            row = table_ref[pl.ds(steps_ref[0, c], 1), :]
            silu[c : c + 1, :] = row / (1.0 + jnp.exp(-row))
        silu_ref[...] = silu[:clips, :].astype(BF)

    out_ref[...] = dot_low(silu[...].astype(BF), w_ref[...])[:clips] + b_ref[...]

    @pl.when(i == 0)
    def _():
        def clip_and_start(places):
            clip, start, end = jnp.zeros_like(places), jnp.zeros_like(places), 0
            for c in range(clips):
                end = end + lengths_ref[0, c]
                clip = jnp.where(places >= end, c + 1, clip)
                start = jnp.where(places >= end, end, start)
            return clip, start

        for j in range(count):
            first = (me_ref[0] ^ offset_of(j, count)) * rows
            here = slice(j * rows, (j + 1) * rows)
            places = first + lax.broadcasted_iota(jnp.int32, (rows, LANES), 0)
            lane = lax.broadcasted_iota(jnp.int32, (rows, LANES), 1)
            clip, start = clip_and_start(places)
            angles = (places - start).astype(F32) * freq_ref[...]
            cos_ref[here, :] = jnp.cos(angles)
            sine = jnp.sin(angles)
            sin_ref[here, :] = jnp.where((lane % 64) < 32, -sine, sine)
            clip_ref[here, :] = clip[:, :1]
            places = first + lax.broadcasted_iota(jnp.int32, (1, rows), 1)
            cliprow_ref[:, here] = clip_and_start(places)[0]
            other = jnp.where((clip != lane) & (lane < clips), NEGATIVE, 0.0)
            marks_ref[here, :LANES] = other.astype(BF)
            marks_ref[here, LANES:] = jnp.where(clip == lane, 1.0, 0.0).astype(BF)

    @pl.when(i == pl.num_programs(0) - 1)
    def _():
        for copy in copies():
            copy.wait()


def prepare(me, lengths, steps, step_table, freqs, w_mod, b_mod, weights, own_rows, count):
    width = w_mod.shape[0]
    clips = lengths.shape[1]
    tile = width
    rows = own_rows * count
    shapes = [
        shape_of((clips, 2 * width), F32),
        shape_of((clips, width)),
        shape_of((rows, 1), jnp.int32),
        shape_of((1, rows), jnp.int32),
        shape_of((rows, LANES), F32),
        shape_of((rows, LANES), F32),
        shape_of((rows, 2 * LANES)),
    ]
    return pl.pallas_call(
        lambda *refs: prepare_kernel(count, *refs),
        grid=(2,),
        in_specs=[SCALARS] * 3
        + [
            full(step_table.shape),
            full(freqs.shape),
            pl.BlockSpec((width, tile), lambda i: (0, i)),
            pl.BlockSpec((1, tile), lambda i: (0, i)),
        ]
        + [ANYWHERE] * len(weights),
        out_specs=[pl.BlockSpec((clips, tile), lambda i: (0, i))]
        + [full(v.shape) for v in shapes[1:]]
        + [KEPT] * len(weights),
        out_shape=shapes + [pltpu.VMEM(w.shape, w.dtype) for w in weights],
        scratch_shapes=[pltpu.VMEM((8, width), F32), pltpu.SemaphoreType.DMA((len(weights),))],
        compiler_params=params(),
        cost_estimate=cost(4 * clips * width * width, 5 * width * width),
    )(me, lengths, steps, *all_in_hbm([step_table, freqs, w_mod, b_mod, *weights]))


def modulate_kernel(silu_ref, w_ref, b_ref, out_ref):
    out_ref[...] = dot_low(silu_ref[...], w_ref[...]) + b_ref[...]


def modulate(silu, w_mod, b_mod):
    clips, width = silu.shape
    return pl.pallas_call(
        modulate_kernel,
        grid=(4,),
        in_specs=[
            full(silu.shape),
            pl.BlockSpec((width, width), lambda i: (0, 2 + i)),
            pl.BlockSpec((1, width), lambda i: (0, 2 + i)),
        ],
        out_specs=pl.BlockSpec((clips, width), lambda i: (0, i)),
        out_shape=shape_of((clips, 4 * width), F32),
        compiler_params=params(),
        cost_estimate=cost(8 * clips * width * width, 8 * width * width),
    )(*all_in_hbm([silu, w_mod, b_mod]))


def project_kernel(clips, with_own, me_ref, clip_ref, mod_ref, b_ref, cos_ref, sin_ref, w, *refs):
    blocks = refs[: len(refs) - (5 if with_own else 3)]
    h_ref, kv_ref, q_ref = refs[len(blocks) : len(blocks) + 3]
    rows, width = blocks[0].shape
    column = pl.multiple_of(me_ref[0] * LANES, LANES)
    if with_own:
        own_ref, passed_ref = refs[-2:]
        passed_ref[...] = blocks[-1][...]
        blocks = blocks[:-1]

    mod = mod_ref[...]
    for pair in range(len(blocks) // 2):
        here = slice(2 * pair * rows, 2 * (pair + 1) * rows)
        x = jnp.concatenate([blocks[2 * pair][...], blocks[2 * pair + 1][...]], axis=0).astype(F32)
        normed, _ = norm_parts(x)
        clip = clip_ref[here, :]
        scale = by_clip(clip, mod[:, width:], 0, clips)
        h_ref[here, :] = (normed * (1.0 + scale) + by_clip(clip, mod[:, :width], 0, clips)).astype(BF)

    h = h_ref[...]
    cosine, sine = cos_ref[...], sin_ref[...]
    lane = lax.broadcasted_iota(jnp.int32, cosine.shape, 1)

    def turned(piece, some):
        return piece * cosine[:some] + half_swap(piece, lane[:some]) * sine[:some]

    part = dot_low(h, w[:, pl.ds(column, LANES)]) + b_ref[:, pl.ds(column, LANES)]
    q_ref[...] = (turned(part, h.shape[0]) * 0.125).astype(BF)
    step = 2 * LANES
    for start in range(0 if with_own else width, 3 * width, step):
        some = rows if start < width else h.shape[0]
        part = dot_low(h[:some], w[:, start : start + step]) + b_ref[:, start : start + step]
        for inner in range(0, step, LANES):
            piece = part[:, inner : inner + LANES]
            at = start + inner
            if start < 2 * width:
                piece = turned(piece, some)
            if start < width:
                own_ref[:, at : at + LANES] = (piece * 0.125).astype(BF)
            else:
                kv_ref[(at - width) // LANES] = piece.astype(BF)


def project(half, blocks, me, clip_col, modulation, w_qkv, b_qkv, cosine, sine, passed=None):
    with_own = passed is not None
    own_rows, width = blocks[0].shape
    rows = own_rows * len(blocks)
    clips = modulation.shape[0]
    out_shape = [
        shape_of((rows, width)),
        pltpu.VMEM((2 * width // LANES, rows, LANES), BF),
        shape_of((rows, LANES)),
    ]
    if with_own:
        out_shape += [shape_of((own_rows, width)), shape_of(passed.shape)]
        blocks = blocks + [passed]
    return pl.pallas_call(
        lambda *refs: project_kernel(clips, with_own, *refs),
        grid=(1,),
        in_specs=[
            SCALARS,
            pl.BlockSpec((rows, 1), lambda *_: (half, 0)),
            pl.BlockSpec((clips, 2 * width), lambda *_: (0, 0)),
            full(b_qkv.shape),
            pl.BlockSpec((rows, LANES), lambda *_: (half, 0)),
            pl.BlockSpec((rows, LANES), lambda *_: (half, 0)),
            KEPT,
        ]
        + [full(v.shape) for v in blocks],
        out_specs=[full(out_shape[0].shape), KEPT] + [full(o.shape) for o in out_shape[2:]],
        out_shape=out_shape,
        compiler_params=params(),
        cost_estimate=cost(4 * rows * width * width, 6 * MIB),
    )(me, *all_in_hbm([clip_col, modulation, b_qkv, cosine, sine]), w_qkv, *all_in_hbm(blocks))


def contract_last(left, right):
    return lax.dot_general(left, right, (((1,), (1,)), ((), ())), preferred_element_type=F32)


def head_rows(value):
    lane = lax.broadcasted_iota(jnp.int32, value.shape, 1)
    zero = jnp.zeros_like(value)
    return jnp.concatenate(
        [jnp.where(lane < 64, value, zero), jnp.where(lane < 64, zero, value)], axis=0
    )


def head_diagonal(value):
    rows = value.shape[1] // 2
    return jnp.concatenate([value[:64, :rows], value[64:, rows:]], axis=0).T


def softmax_over_keys(keys, queries):
    scores = contract_last(keys, queries)
    expo = jnp.exp(scores - jnp.max(scores, axis=0, keepdims=True))
    return expo, 1.0 / jnp.sum(expo, axis=0, keepdims=True)


def attend_kernel(keymark_ref, rowmark_ref, q_ref, ka_ref, kb_ref, *refs):
    sources, o_ref, targets = refs[:3], refs[3], refs[4:7]
    keys, values, queries, sems = refs[7:]
    half = ka_ref.shape[1]
    pair, pairs = pl.program_id(0), pl.num_programs(0)

    def copies():
        return [
            pltpu.make_async_copy(source, target, sems.at[j])
            for j, (source, target) in enumerate(zip(sources, targets))
        ]

    @pl.when(pair == 0)
    def _():
        for copy in copies():
            copy.start()

    @pl.when(pair == pairs - 1)
    def _():
        for copy in copies():
            copy.wait()

    @pl.when(pair == 0)
    def _():
        keys[:, LANES:] = keymark_ref[...]
        marks = rowmark_ref[...]
        queries[:, LANES:] = jnp.concatenate([marks, marks], axis=0)

    keys[:half, :LANES] = ka_ref[pair]
    keys[half:, :LANES] = kb_ref[pair]
    values[:half] = ka_ref[pairs + pair]
    values[half:] = kb_ref[pairs + pair]
    queries[:, :LANES] = head_rows(q_ref[...])
    expo, inverse = softmax_over_keys(keys[...], queries[...])
    turned = jnp.dot(values[...].T, expo.astype(BF), preferred_element_type=F32) * inverse
    o_ref[...] = head_diagonal(turned).astype(BF)


def attend(q, kv_a, kv_b, marks, weights):
    own_rows, width = q.shape
    rows = 2 * kv_a.shape[1]
    return pl.pallas_call(
        attend_kernel,
        grid=(width // LANES,),
        in_specs=[
            pl.BlockSpec((rows, LANES), lambda p: (0, 0)),
            pl.BlockSpec((own_rows, LANES), lambda p: (0, 1)),
            pl.BlockSpec((own_rows, LANES), lambda p: (0, p)),
            KEPT,
            KEPT,
        ]
        + [ANYWHERE] * 3,
        out_specs=[pl.BlockSpec((own_rows, LANES), lambda p: (0, p))] + [KEPT] * 3,
        out_shape=[shape_of((own_rows, width))] + [pltpu.VMEM(w.shape, BF) for w in weights],
        scratch_shapes=[
            pltpu.VMEM((rows, 2 * LANES), BF),
            pltpu.VMEM((rows, LANES), BF),
            pltpu.VMEM((2 * own_rows, 2 * LANES), BF),
            pltpu.SemaphoreType.DMA((3,)),
        ],
        compiler_params=params(),
        cost_estimate=cost(4 * own_rows * rows * width, MIB),
    )(*all_in_hbm([marks, marks, q]), kv_a, kv_b, *all_in_hbm(weights))


def probs_kernel(me_ref, keyclip_ref, rowclip_ref, qa_ref, qb_ref, ka_ref, kb_ref, *refs):
    out_ref, keys = refs[-2:]
    i, blocks = pl.program_id(0), pl.num_programs(0)
    half = ka_ref.shape[1]

    @pl.when(i == 0)
    def _():
        keys[:half] = ka_ref[me_ref[0]]
        keys[half:] = kb_ref[me_ref[0]]

    query = jnp.where(i < blocks // 2, qa_ref[...], qb_ref[...])
    visible = keyclip_ref[...] == rowclip_ref[...]
    visible = jnp.concatenate([visible, visible], axis=1)
    scores = jnp.where(visible, contract_last(keys[...], head_rows(query)), NEGATIVE)
    expo = jnp.exp(scores - jnp.max(scores, axis=0, keepdims=True))
    out_ref[...] = expo * (1.0 / jnp.sum(expo, axis=0, keepdims=True))


def heads_probs(me, q_a, q_b, kv_a, kv_b, clip_col, clip_row, blocks, earlier):
    half = kv_a.shape[1]
    rows = 2 * half
    own_rows = rows // blocks
    halfway = blocks // 2
    grid_spec = pltpu.PrefetchScalarGridSpec(
        num_scalar_prefetch=1,
        grid=(blocks,),
        in_specs=[
            pl.BlockSpec((rows, 1), lambda i, m: (0, 0)),
            pl.BlockSpec((1, own_rows), lambda i, m: (0, i)),
            pl.BlockSpec((own_rows, LANES), lambda i, m: (jnp.minimum(i, halfway - 1), 0)),
            pl.BlockSpec((own_rows, LANES), lambda i, m: (jnp.maximum(i - halfway, 0), 0)),
            KEPT,
            KEPT,
        ]
        + [ANYWHERE] * len(earlier),
        out_specs=pl.BlockSpec((rows, 2 * own_rows), lambda i, m: (0, i)),
        scratch_shapes=[pltpu.VMEM((rows, LANES), BF)],
    )
    return pl.pallas_call(
        probs_kernel,
        grid_spec=grid_spec,
        out_shape=shape_of((rows, 2 * rows), F32),
        compiler_params=params(),
        cost_estimate=cost(4 * rows * rows * LANES, 9 * MIB),
    )(me, *all_in_hbm([clip_col, clip_row, q_a, q_b]), kv_a, kv_b, *all_in_hbm(earlier))


def attend_back_kernel(
    me_ref, p_ref, qa_ref, qb_ref, ka_ref, kb_ref, do_ref, cos_ref, sin_ref, *refs
):
    out_ref, sent_ref = refs[-9:-7]
    dk_ref, dv_ref, values, keys_turned, d_probs = refs[-5:]
    i, blocks = pl.program_id(0), pl.num_programs(0)
    rows = do_ref.shape[1]
    half = ka_ref.shape[1]
    me = me_ref[0]

    @pl.when(i == 0)
    def _():
        dk_ref[...] = jnp.zeros_like(dk_ref)
        dv_ref[...] = jnp.zeros_like(dv_ref)
        for at, ref in ((0, ka_ref), (half, kb_ref)):
            values[at : at + half] = ref[ref.shape[0] // 2 + me]
            keys_turned[:, at : at + half] = ref[me].T

    query = jnp.where(i < blocks // 2, qa_ref[...], qb_ref[...])
    q_two, up_two = head_rows(query), head_rows(do_ref[0])
    delta = jnp.zeros((1, 2 * rows), F32)
    step = 256
    for start in range(0, 2 * half, step):
        part = slice(start, start + step)
        probs_low = p_ref[part, :].astype(BF)
        dv_ref[part, :] += dot_low(probs_low, up_two)
        products = contract_last(values[part, :], up_two)
        d_probs[part, :] = products
        delta += jnp.sum(probs_low.astype(F32) * products, axis=0, keepdims=True)
    d_query = jnp.zeros((LANES, 2 * rows), F32)
    for start in range(0, 2 * half, step):
        part = slice(start, start + step)
        ds = (p_ref[part, :] * (d_probs[part, :] - delta)).astype(BF)
        dk_ref[part, :] += dot_low(ds, q_two)
        d_query += dot_low(keys_turned[:, part], ds)
    lane = lax.broadcasted_iota(jnp.int32, (rows, LANES), 1)

    def turned_back(value, where):
        return (value * cos_ref[where, :] - half_swap(value, lane) * sin_ref[where, :]).astype(BF)

    here = pl.ds(pl.multiple_of(i * rows, rows), rows)
    dq = turned_back(head_diagonal(d_query) * 0.125, here)
    out_ref[here, 0:LANES] = dq
    sent_ref[me ^ offset_of(i, blocks), :, 0:LANES] = dq

    @pl.when(i == blocks - 1)
    def _():
        @pl.loop(0, blocks)
        def _(j):
            there = pl.ds(pl.multiple_of(j * rows, rows), rows)
            dk = turned_back(dk_ref[there, :], there)
            dv = dv_ref[there, :].astype(BF)
            out_ref[there, LANES : 2 * LANES] = dk
            out_ref[there, 2 * LANES : 3 * LANES] = dv
            owner = me ^ offset_of(j, blocks)
            sent_ref[owner, :, LANES : 2 * LANES] = dk
            sent_ref[owner, :, 2 * LANES : 3 * LANES] = dv


def attend_back(me, probs, q_a, q_b, kv_a, kv_b, d_o, cosine, sine, passed, earlier):
    half = kv_a.shape[1]
    rows = 2 * half
    blocks, own_rows, _ = d_o.shape
    halfway = blocks // 2
    grid_spec = pltpu.PrefetchScalarGridSpec(
        num_scalar_prefetch=1,
        grid=(blocks,),
        in_specs=[
            pl.BlockSpec((rows, 2 * own_rows), lambda i, m: (0, i)),
            pl.BlockSpec((own_rows, LANES), lambda i, m: (jnp.minimum(i, halfway - 1), 0)),
            pl.BlockSpec((own_rows, LANES), lambda i, m: (jnp.maximum(i - halfway, 0), 0)),
            KEPT,
            KEPT,
            pl.BlockSpec((1, own_rows, LANES), lambda i, m: (m[0] ^ offset_of(i, blocks), 0, 0)),
            pl.BlockSpec((rows, LANES), lambda i, m: (0, 0)),
            pl.BlockSpec((rows, LANES), lambda i, m: (0, 0)),
            ANYWHERE,
            ANYWHERE,
        ]
        + [ANYWHERE] * len(earlier),
        out_specs=[
            pl.BlockSpec((rows, 3 * LANES), lambda i, m: (0, 0)),
            pl.BlockSpec((blocks, own_rows, 3 * LANES), lambda i, m: (0, 0, 0)),
            ANYWHERE,
            ANYWHERE,
        ],
        scratch_shapes=[
            pltpu.VMEM((rows, LANES), F32),
            pltpu.VMEM((rows, LANES), F32),
            pltpu.VMEM((rows, LANES), BF),
            pltpu.VMEM((LANES, rows), BF),
            pltpu.VMEM((rows, 2 * own_rows), F32),
        ],
    )
    return pl.pallas_call(
        attend_back_kernel,
        grid_spec=grid_spec,
        out_shape=[
            shape_of((rows, 3 * LANES)),
            shape_of((blocks, own_rows, 3 * LANES)),
            shape_of(passed[0].shape, passed[0].dtype),
            shape_of(passed[1].shape, passed[1].dtype),
        ],
        input_output_aliases={9: 2, 10: 3},
        compiler_params=params(),
        cost_estimate=cost(8 * rows * rows * LANES, 12 * MIB),
    )(
        me,
        *all_in_hbm([probs, q_a, q_b]),
        kv_a,
        kv_b,
        d_o,
        *all_in_hbm([cosine, sine, *passed, *earlier]),
    )


def norm_parts(inputs):
    centred = inputs - jnp.mean(inputs, axis=-1, keepdims=True)
    rstd = lax.rsqrt(jnp.mean(centred * centred, axis=-1, keepdims=True) + 1e-06)
    return centred * rstd, rstd


def norm_back(normed, rstd, gradient):
    return rstd * (
        gradient
        - jnp.mean(gradient, axis=-1, keepdims=True)
        - normed * jnp.mean(gradient * normed, axis=-1, keepdims=True)
    )


def dot_low(left, right):
    return jnp.dot(left, right, preferred_element_type=F32)


def dot_rows(left, right):
    return lax.dot_general(left, right, (((0,), (0,)), ((), ())), preferred_element_type=F32)


def gelu_parts(hidden):
    square = hidden * hidden
    tanh = jnp.tanh(0.7978845608028654 * hidden * (1.0 + 0.044715 * square))
    upper = 0.5 * (1.0 + tanh)
    slope = upper + 0.5 * hidden * (1.0 - tanh * tanh) * (
        0.7978845608028654 * (1.0 + 3.0 * 0.044715 * square)
    )
    return hidden * upper, slope


def high_low(value):
    high = value.astype(BF)
    return high, (value - high.astype(F32)).astype(BF)


class RowSums:
    def __init__(self, clip_row, clips):
        self.place = lax.broadcasted_iota(jnp.int32, (8, clip_row.shape[1]), 0)
        self.member = ((self.place == clip_row) & (self.place < clips)).astype(F32).astype(BF)

    def by_clip(self, value):
        high, low = high_low(value)
        return dot_low(
            jnp.concatenate([self.member, self.member], axis=1),
            jnp.concatenate([high, low], axis=0),
        )

    def whole(self, value, row):
        return dot_low((self.place == row).astype(F32).astype(BF), value)


def middle_kernel(
    clips, steps_ref, clipc_ref, clipr_ref, x_ref, dy_ref, o_ref, mod_ref, bo_ref, bu_ref, bd_ref,
    wo, wu, wd, *refs,
):
    out_ref, h2_ref, dx_ref, da_ref, do_ref, sums_ref = refs[-6:]
    width = x_ref.shape[1]
    ffn = wu.shape[1]
    clip = clipc_ref[...]

    def frame_rows(index):
        return by_clip(clip, mod_ref[:, (index - 2) * width : (index - 1) * width], 0, clips)

    gate_one, scale_two, gate_two = frame_rows(2), 1.0 + frame_rows(4), frame_rows(5)
    upstream = dy_ref[...].astype(F32)
    d_ffn = (gate_two * upstream).astype(BF)
    attn_out = dot_low(o_ref[...], wo[...]) + bo_ref[...]
    middle = x_ref[...].astype(F32) + gate_one * attn_out
    normed, rstd = norm_parts(middle)
    second = (normed * scale_two + frame_rows(3)).astype(BF)
    h2_ref[...] = second
    sums = RowSums(clipr_ref[...], clips)
    ffn_out = jnp.zeros(x_ref.shape, F32)
    d_second = jnp.zeros(x_ref.shape, F32)
    step = 512
    up_sums = []
    for start in range(0, ffn, step):
        here = slice(start, start + step)
        activated, slope = gelu_parts(dot_low(second, wu[:, here]) + bu_ref[:, here])
        ffn_out += dot_low(activated.astype(BF), wd[here, :])
        d_hidden = (contract_last(d_ffn, wd[here, :]) * slope).astype(BF)
        d_second += contract_last(d_hidden, wu[:, here])
        up_sums.append(sums.whole(d_hidden, clips))
    ffn_out += bd_ref[...]
    out_ref[...] = (middle + gate_two * ffn_out).astype(BF)
    d_middle = upstream + norm_back(normed, rstd, d_second * scale_two)
    dx_ref[...] = d_middle
    d_attn = (gate_one * d_middle).astype(BF)
    da_ref[...] = d_attn
    d_o = contract_last(d_attn, wo[...]).astype(BF)
    for k in range(width // LANES):
        do_ref[k] = d_o[:, k * LANES : (k + 1) * LANES]
    up_sums = jnp.concatenate(up_sums, axis=1)
    place = lax.broadcasted_iota(jnp.int32, (8, width), 0)
    lane = lax.broadcasted_iota(jnp.int32, (8, width), 1)
    steps = jnp.zeros((8, width), F32)
    for c in range(clips):
        here = (place == clips + 1) & (lane == c)
        steps = jnp.where(here, steps_ref[0, c].astype(F32), steps)
    sums_ref[:, :width] = (
        sums.by_clip(d_middle * attn_out) + sums.whole(d_attn, clips) + steps
    )
    sums_ref[:, width : 2 * width] = sums.by_clip(d_second) + up_sums[:, :width]
    sums_ref[:, 2 * width : 3 * width] = sums.by_clip(d_second * normed) + up_sums[:, width:]
    sums_ref[:, 3 * width :] = sums.by_clip(upstream * ffn_out) + sums.whole(d_ffn, clips)


def middle_part(
    steps, clip_col, clip_row, frames, cotangent, attended, modulation, b_out, b_up, b_down,
    w_out, w_up, w_down, earlier,
):
    rows, width = frames.shape
    clips = modulation.shape[0]
    small = [
        clip_col, clip_row, frames, cotangent, attended, modulation, b_out, b_up, b_down
    ]
    out_shape = [
        shape_of((rows, width)),
        shape_of((rows, width)),
        shape_of((rows, width), F32),
        shape_of((rows, width)),
        shape_of((width // LANES, rows, LANES)),
        shape_of((8, 4 * width), F32),
    ]
    return pl.pallas_call(
        lambda *refs: middle_kernel(clips, *refs),
        grid=(1,),
        in_specs=[SCALARS, full((rows, 1)), full((1, rows))]
        + [full(v.shape) for v in small[2:]]
        + [KEPT] * 3
        + [ANYWHERE] * len(earlier),
        out_specs=[full(o.shape) for o in out_shape],
        out_shape=out_shape,
        compiler_params=params(),
        cost_estimate=cost(20 * rows * width * width, 3 * MIB),
    )(steps, *all_in_hbm(small), w_out, w_up, w_down, *all_in_hbm(earlier))


def last_kernel(clips, clipc_ref, clipr_ref, x_ref, mod_ref, dx_ref, d_ref, w_hbm, *refs):
    passed = (len(refs) - 5) // 2
    out_ref, sums_ref = refs[passed : passed + 2]
    d_all, w, sems = refs[-3:]
    width = x_ref.shape[1]
    parts = 3
    copies = [
        pltpu.make_async_copy(
            w_hbm.at[:, pl.ds(i * width, width)], w.at[:, pl.ds(i * width, width)], sems.at[i]
        )
        for i in range(parts)
    ]
    for copy in copies:
        copy.start()
    for k in range(d_ref.shape[0]):
        for i in range(3):
            at = i * width + k * LANES
            d_all[:, at : at + LANES] = d_ref[k, :, i * LANES : (i + 1) * LANES]
    normed, rstd = norm_parts(x_ref[...].astype(F32))
    scale = 1.0 + by_clip(clipc_ref[...], mod_ref[...], 0, clips)
    d_first = jnp.zeros(x_ref.shape, F32)
    for i in range(parts):
        copies[i].wait()
        here = slice(i * width, (i + 1) * width)
        d_first += contract_last(d_all[:, here], w[:, here])
    out_ref[...] = (dx_ref[...] + norm_back(normed, rstd, d_first * scale)).astype(BF)
    sums = RowSums(clipr_ref[...], clips)
    sums_ref[:, :width] = (
        sums.by_clip(d_first)
        + sums.whole(d_all[:, :width], clips)
        + sums.whole(d_all[:, width : 2 * width], clips + 1)
    )
    sums_ref[:, width:] = sums.by_clip(d_first * normed) + sums.whole(d_all[:, 2 * width :], clips)


def last_part(clip_col, clip_row, frames, modulation, d_middle, d_own, w_qkv, passed):
    rows, width = frames.shape
    clips = modulation.shape[0]
    return pl.pallas_call(
        lambda *refs: last_kernel(clips, *refs),
        grid=(1,),
        in_specs=[
            full((rows, 1)),
            full((1, rows)),
            full(frames.shape),
            pl.BlockSpec((clips, width), lambda *_: (0, 1)),
            full(d_middle.shape),
            full(d_own.shape),
        ]
        + [ANYWHERE] * (1 + len(passed)),
        out_specs=[full((rows, width)), full((8, 2 * width))] + [ANYWHERE] * len(passed),
        out_shape=[shape_of((rows, width)), shape_of((8, 2 * width), F32)]
        + [shape_of(v.shape, v.dtype) for v in passed],
        input_output_aliases={7 + i: 2 + i for i in range(len(passed))},
        scratch_shapes=[
            pltpu.VMEM((rows, 3 * width), BF),
            pltpu.VMEM(w_qkv.shape, BF),
            pltpu.SemaphoreType.DMA((3,)),
        ],
        compiler_params=params(),
        cost_estimate=cost(6 * rows * width * width, 2 * MIB),
    )(
        *all_in_hbm([clip_col, clip_row, frames, modulation, d_middle]),
        d_own,
        *all_in_hbm([w_qkv, *passed]),
    )


def half_rows(core, value, kept_ref, sent_refs, at, columns):
    half = value.shape[0] // 2
    low, high = value[:half], value[half:]
    here = slice(at, at + half)
    kept_ref[here, columns] = jnp.where(core == 0, low, high)
    sent = jnp.where(core == 0, high, low).astype(BF)
    wide = sent_refs[0].shape[1]
    for i, ref in enumerate(sent_refs):
        start, stop = max(columns.start, i * wide), min(columns.stop, (i + 1) * wide)
        if start < stop:
            ref[here, start - i * wide : stop - i * wide] = sent[
                :, start - columns.start : stop - columns.start
            ]


def weights_kernel(clips, count, who_ref, clip_ref, gate_ref, bu_ref, wu_hbm, wd_hbm, *refs):
    kept_ref, sent_ref, (up_sum, down_sum, wu, wd, sems) = refs[-9], refs[-8:-5], refs[-5:]
    ha_ref, hb_ref, d_ref, mine_ref, theirs_ref = refs[:5]
    blocks = refs[5 : 5 + count]
    seconds, upstreams = blocks[: len(blocks) // 2], blocks[len(blocks) // 2 :]
    me, core = who_ref[0], who_ref[1]
    rows, width = seconds[0].shape
    part = up_sum.shape[1]
    columns = d_ref.shape[1]
    half = ha_ref.shape[0]
    own = pl.ds(pl.multiple_of((me // 2) * part, part), part)
    copies = [
        pltpu.make_async_copy(wu_hbm.at[:, own], wu, sems.at[0]),
        pltpu.make_async_copy(wd_hbm.at[own, :], wd, sems.at[1]),
    ]
    for copy in copies:
        copy.start()
    shard = part // 2

    step = 2 * LANES
    for start in range(0, width, step):
        here = slice(start, start + step)
        value = dot_rows(ha_ref[:, here], d_ref[:half, :])
        value += dot_rows(hb_ref[:, here], d_ref[half:, :])
        for inner in range(0, step, LANES):
            half_rows(
                core, value[inner : inner + LANES], kept_ref, sent_ref, (start + inner) // 2,
                slice(0, columns),
            )

    left = jnp.concatenate([mine_ref[:, :width], theirs_ref[:, :width]], axis=0)
    right = jnp.concatenate([mine_ref[:, width:], theirs_ref[:, width:]], axis=0)
    at = columns + 2 * part
    for start in range(0, width, step):
        value = dot_rows(left[:, start : start + step], right)
        for inner in range(0, step, LANES):
            half_rows(
                core, value[inner : inner + LANES], kept_ref, sent_ref, (start + inner) // 2,
                slice(at, at + width // 2),
            )

    for copy in copies:
        copy.wait()
    up_weights, down_weights = wu[...], wd[...]
    for pair in range(len(seconds) // 2):
        here = slice(2 * pair * rows, 2 * (pair + 1) * rows)
        second = jnp.concatenate([r[...] for r in seconds[2 * pair : 2 * pair + 2]], axis=0)
        upstream = jnp.concatenate([r[...] for r in upstreams[2 * pair : 2 * pair + 2]], axis=0)
        gate = by_clip(clip_ref[here, :], gate_ref[...], 0, clips)
        d_ffn = (gate * upstream.astype(F32)).astype(BF)
        activated, slope = gelu_parts(dot_low(second, up_weights) + bu_ref[:, own])
        d_hidden = (contract_last(d_ffn, down_weights) * slope).astype(BF)
        up, down = dot_rows(second, d_hidden), dot_rows(activated.astype(BF), d_ffn)
        if pair == 0:
            up_sum[...] = up
            down_sum[...] = down
        else:
            up_sum[...] += up
            down_sum[...] += down
    for y in range(2):
        mine = slice(y * shard, (y + 1) * shard)
        at = columns + 2 * y * shard
        for k in range(width // LANES):
            half_rows(
                core, up_sum[k * LANES : (k + 1) * LANES, mine], kept_ref, sent_ref,
                k * LANES // 2, slice(at, at + shard),
            )
        for c in range(width // shard):
            half_rows(
                core, down_sum[mine, c * shard : (c + 1) * shard], kept_ref, sent_ref,
                c * shard // 2, slice(at + shard, at + 2 * shard),
            )


def weights_part(who, clip_col, modulation, b_up, w_up, w_down, h1_a, h1_b, d_qkv, outs, seconds, upstreams):
    width, ffn = w_up.shape
    count = 2 * len(seconds)
    part = 2 * ffn // count
    clips = modulation.shape[0]
    shape = (width // 2, d_qkv.shape[1] + 2 * part + width // 2)
    rows = d_qkv.shape[0]
    arrays = [h1_a, h1_b, d_qkv, *outs, *seconds, *upstreams]
    return pl.pallas_call(
        lambda *refs: weights_kernel(clips, count, *refs),
        grid=(1,),
        in_specs=[
            SCALARS,
            pl.BlockSpec((rows // 2, 1), lambda *_: (0, 0)),
            pl.BlockSpec((clips, width), lambda *_: (0, 3)),
            full(b_up.shape),
            ANYWHERE,
            ANYWHERE,
        ]
        + [full(v.shape) for v in arrays],
        out_specs=[full(shape)] + [full((shape[0], shape[1] // 3))] * 3,
        out_shape=[shape_of(shape, F32)] + [shape_of((shape[0], shape[1] // 3))] * 3,
        scratch_shapes=[
            pltpu.VMEM((width, part), F32),
            pltpu.VMEM((part, width), F32),
            pltpu.VMEM((width, part), BF),
            pltpu.VMEM((part, width), BF),
            pltpu.SemaphoreType.DMA((2,)),
        ],
        compiler_params=params(36),
        cost_estimate=cost(7 * rows * width * part, 10 * MIB),
    )(who, *all_in_hbm([clip_col, modulation, b_up, w_up, w_down, *arrays]))


def table_kernel(first, clips, place_ref, *refs):
    parts, refs = refs[:4], refs[4:]
    if first:
        silu_ref, w_ref = refs[:2]
        dw_ref, db_ref, out_ref, total, sums = refs[-5:]
    else:
        silu_ref, w_ref, cond_ref, pick_ref, earlier_ref, _, _ = refs[:7]
        dw_ref, db_ref, out_ref, total, sums = refs[7:]
    i = pl.program_id(0)

    @pl.when(i == 0)
    def _():
        total[...] = jnp.zeros_like(total) if first else earlier_ref[...]

    for j, part in enumerate(parts):
        value = part[...]
        valid = lax.broadcasted_iota(jnp.int32, value.shape, 0) < clips
        sums[pl.ds(pl.multiple_of((place_ref[0] ^ j) * 8, 8), 8), :] = jnp.where(valid, value, 0.0)
    high, low = high_low(sums[...])
    total[...] += contract_last(w_ref[...], jnp.concatenate([high, low], axis=0))
    silu = silu_ref[...]
    dw_ref[...] = dot_rows(
        jnp.concatenate([silu, silu], axis=0), jnp.concatenate([high, low], axis=0)
    )
    db_ref[...] = jnp.sum(sums[...], axis=0, keepdims=True)

    @pl.when(i == pl.num_programs(0) - 1)
    def _():
        if first:
            out_ref[...] = total[...]
        else:
            rows = high.shape[0]
            d_silu = total[:, :rows] + total[:, rows:]
            cond = cond_ref[...]
            gate = 1.0 / (1.0 + jnp.exp(-cond))
            d_cond = d_silu.T * (gate * (1.0 + cond * (1.0 - gate)))
            d_high, d_low = high_low(d_cond)
            lowest = (d_cond - d_high.astype(F32) - d_low.astype(F32)).astype(BF)
            pick = pick_ref[...].astype(BF)
            out_ref[...] = dot_rows(pick, d_high) + dot_rows(pick, d_low) + dot_rows(pick, lowest)


def table_part(place, sums, silu, w_mod, column, clips, rest=None, earlier=()):
    columns = sums[0].shape[1]
    width = w_mod.shape[0]
    all_columns = 6 * width
    rows, own = silu.shape
    tile = 1024
    skip = column // tile
    first = rest is None
    shapes = [
        shape_of((own, all_columns), F32),
        shape_of((1, all_columns), F32),
        shape_of((width, 2 * rows), F32),
    ]
    in_specs = [SCALARS] + [pl.BlockSpec((8, tile), lambda i: (0, i))] * 4 + [
        pl.BlockSpec((rows, own), lambda i: (0, 0)),
        pl.BlockSpec((width, tile), lambda i: (0, skip + i)),
    ]
    args = [place, *all_in_hbm([*sums, silu]), in_hbm(w_mod)]
    aliases = {}
    if first:
        in_specs += [ANYWHERE] * len(earlier)
        args += all_in_hbm(earlier)
    else:
        condition, pick, earlier, d_w, d_b = rest
        in_specs += [
            pl.BlockSpec((rows, width), lambda i: (0, 0)),
            pl.BlockSpec(pick.shape, lambda i: (0, 0)),
            pl.BlockSpec((width, 2 * rows), lambda i: (0, 0)),
            ANYWHERE,
            ANYWHERE,
        ]
        args += all_in_hbm([condition, pick, earlier, d_w, d_b])
        aliases = {10: 0, 11: 1}
        shapes[2] = shape_of((pick.shape[1], width), F32)
    return pl.pallas_call(
        lambda *refs: table_kernel(first, clips, *refs),
        grid=(columns // tile,),
        in_specs=in_specs,
        out_specs=[
            pl.BlockSpec((own, tile), lambda i: (0, skip + i)),
            pl.BlockSpec((1, tile), lambda i: (0, skip + i)),
            pl.BlockSpec(shapes[2].shape, lambda i: (0, 0)),
        ],
        out_shape=shapes,
        scratch_shapes=[
            pltpu.VMEM((width, 2 * rows), F32),
            pltpu.VMEM((rows, tile), F32),
        ],
        input_output_aliases=aliases,
        compiler_params=params(),
        cost_estimate=cost(rows * width, width),
    )(*args)


def in_order(bit, mine, other):
    return jnp.stack([jnp.where(bit == 0, mine, other), jnp.where(bit == 0, other, mine)])


def batch_parts(sums):
    return [sums] + [swapped_with(sums, "batch", k) for k in range(1, 4)]


def share_kernel(columns, part, who_ref, kept_ref, *refs):
    others = refs[:3]
    own_ref, x_ref, y_ref, both_ref, out_ref = refs[-5:]
    far, odd = who_ref[2] // 2 == 1, who_ref[0] % 2 == 1
    rows = own_ref.shape[1]
    first, second = slice(columns, columns + part), slice(columns + part, columns + 2 * part)
    for k in range(own_ref.shape[0]):
        here = slice(2 * k * rows, 2 * (k + 1) * rows)
        other = jnp.concatenate([ref[here, :] for ref in others], axis=1)
        value = kept_ref[here, :] + other.astype(F32)
        low, high = value[:rows], value[rows:]
        near, away = jnp.where(far, high, low), jnp.where(far, low, high)
        own_ref[k, :, :columns] = near[:, :columns]
        own_ref[k, :, columns:] = jnp.where(odd, near[:, second], near[:, first])
        y_ref[k] = jnp.where(odd, near[:, first], near[:, second]).astype(BF)
        x_ref[k, :, :columns] = away[:, :columns].astype(BF)
        x_ref[k, :, columns:] = jnp.where(odd, away[:, second], away[:, first]).astype(BF)
        both_ref[k] = jnp.where(odd, away[:, first], away[:, second]).astype(BF)
        out_ref[k] = jnp.concatenate(
            [low[:, columns + 2 * part :], high[:, columns + 2 * part :]], axis=1
        ).astype(BF)


def share(who, kept, others, count, columns, part):
    rows = kept.shape[0] // count // 2
    width = 2 * (kept.shape[1] - columns - 2 * part)
    shapes = [
        shape_of((count, rows, columns + part), F32),
        shape_of((count, rows, columns + part)),
        shape_of((count, rows, part)),
        shape_of((count, rows, part)),
        shape_of((count, rows, width)),
    ]
    return pl.pallas_call(
        lambda *refs: share_kernel(columns, part, *refs),
        grid=(1,),
        in_specs=[SCALARS, full(kept.shape)] + [full(v.shape) for v in others],
        out_specs=[full(v.shape) for v in shapes],
        out_shape=shapes,
        compiler_params=params(),
        cost_estimate=cost(0, 8 * MIB),
    )(who, in_hbm(kept), *others)


def gather_sums_kernel(columns, own_ref, x_ref, y_ref, both_ref, out_ref, *refs):
    sent_ref, down_ref = refs[-2:]
    count, rows, _ = own_ref.shape
    shard = y_ref.shape[2] // 2
    ready = columns + shard
    for k in range(count):
        from_x = x_ref[k].astype(F32)
        sent_ref[k, :, :columns] = (own_ref[k, :, :columns] + from_x[:, :columns]).astype(BF)
        value = (own_ref[k, :, columns:] + from_x[:, columns:]) + (
            y_ref[k].astype(F32) + both_ref[k].astype(F32)
        )
        sent_ref[k, :, columns:ready] = value[:, :shard].astype(BF)
        group, at = k % 2, k // 2 * shard
        down_ref[group * rows : (group + 1) * rows, at : at + shard] = value[:, shard:].astype(BF)
        sent_ref[k, :, ready:] = out_ref[k]


def gather_sums(own, from_x, from_y, from_both, out_parts, columns, passed):
    count, rows, _ = own.shape
    width = out_parts.shape[2]
    args = [own, from_x, from_y, from_both, out_parts]
    shapes = [
        shape_of((count, rows, columns + from_y.shape[2] // 2 + width)),
        shape_of((2 * rows, width)),
    ]
    return pl.pallas_call(
        lambda *refs: gather_sums_kernel(columns, *refs),
        grid=(1,),
        in_specs=[full(v.shape) for v in args] + [ANYWHERE] * len(passed),
        out_specs=[ANYWHERE] * len(passed) + [full(v.shape) for v in shapes],
        out_shape=[shape_of(v.shape, v.dtype) for v in passed] + shapes,
        input_output_aliases={5 + i: i for i in range(len(passed))},
        compiler_params=params(),
        cost_estimate=cost(0, 4 * MIB),
    )(in_hbm(own), from_x, from_y, from_both, *all_in_hbm([out_parts, *passed]))


def rows_kernel(columns, rows_ref, down_ref, *refs):
    out_ref = refs[-1]
    count, rows, wide = rows_ref.shape
    width = out_ref.shape[1]
    shard = wide - width - columns
    total = jnp.zeros((rows, width), F32)
    for k in range(count):
        for i in range(columns // LANES):
            out_ref[i * rows : (i + 1) * rows, k * LANES : (k + 1) * LANES] = rows_ref[
                k, :, i * LANES : (i + 1) * LANES
            ]
        piece = columns // LANES + k * shard // width
        at = k * shard % width
        out_ref[piece * rows : (piece + 1) * rows, at : at + shard] = rows_ref[
            k, :, columns : columns + shard
        ]
        total += rows_ref[k, :, columns + shard :].astype(F32)
    piece = columns // LANES + count * shard // width
    out_ref[piece * rows : (piece + 2) * rows, :] = down_ref[...]
    out_ref[(piece + 2) * rows :, :] = total.astype(BF)


def gather_rows(rows_mine, down_rows, columns, passed, earlier):
    count, rows, wide = rows_mine.shape
    width = down_rows.shape[1]
    shard = wide - width - columns
    shape = ((columns // LANES + count * shard // width + 3) * rows, width)
    return pl.pallas_call(
        lambda *refs: rows_kernel(columns, *refs),
        grid=(1,),
        in_specs=[full(rows_mine.shape), full(down_rows.shape), ANYWHERE, ANYWHERE],
        out_specs=[ANYWHERE, full(shape)],
        out_shape=[shape_of(passed.shape, passed.dtype), shape_of(shape)],
        input_output_aliases={2: 0},
        compiler_params=params(),
        cost_estimate=cost(0, 2 * MIB),
    )(rows_mine, *all_in_hbm([down_rows, passed, earlier]))


def assemble_kernel(ffn, who_ref, *refs):
    qkv_ref, out_ref, up_ref, down_ref = refs[-4:]
    width = out_ref.shape[1]
    rows = qkv_ref.shape[0] // 4
    for j, ref in enumerate(refs[:4]):
        owner = who_ref[2] ^ j
        core, far = owner % 2, owner // 2
        at = pl.multiple_of(core * 2 * rows + far * rows, rows)
        piece = 0
        for target, count in ((qkv_ref, 3), (up_ref, ffn // width)):
            for i in range(count):
                here = slice(piece * rows, (piece + 1) * rows)
                target[pl.ds(at, rows), i * width : (i + 1) * width] = ref[here, :].astype(F32)
                piece += 1
        for g in range(2):
            here = slice(piece * rows, (piece + 1) * rows)
            there = pl.multiple_of(core * 4 * rows + g * 2 * rows + far * rows, rows)
            down_ref[pl.ds(there, rows), :] = ref[here, :].astype(F32)
            piece += 1
        part = width // 2
        column = pl.multiple_of(far * part, part)
        for g in range(2):
            there = pl.multiple_of(core * 2 * rows + g * rows, rows)
            out_ref[pl.ds(there, rows), pl.ds(column, part)] = ref[
                piece * rows : (piece + 1) * rows, g * part : (g + 1) * part
            ].astype(F32)


def assemble(who, parts, own_rows, ffn):
    width = parts[0].shape[1]
    shapes = [
        shape_of((own_rows, 3 * width), F32),
        shape_of((own_rows, width), F32),
        shape_of((own_rows, ffn), F32),
        shape_of((2 * own_rows, width), F32),
    ]
    return pl.pallas_call(
        lambda *refs: assemble_kernel(ffn, *refs),
        grid=(1,),
        in_specs=[SCALARS] + [full(v.shape) for v in parts],
        out_specs=[full(o.shape) for o in shapes],
        out_shape=shapes,
        compiler_params=params(),
        cost_estimate=cost(0, 6 * MIB),
    )(who, *parts)


def heads_body(
    frames, step_table, clip_lengths, clip_steps, w_mod, b_mod, w_qkv, b_qkv, w_out, b_out,
    w_up, b_up, w_down, b_down, cotangent,
):
    own_rows, width = frames.shape
    ffn = w_up.shape[1]
    count = lax.axis_size("blk")
    me = lax.axis_index("blk")
    place = lax.axis_index("batch")
    core, far = place % 2, place // 2
    who = jnp.stack([me, core, place])
    clips = clip_lengths.shape[1]
    rows = own_rows * count

    head_size = width // HEADS
    half = head_size // 2
    lane = jnp.arange(LANES, dtype=jnp.int32)
    freqs = 10000.0 ** (-2.0 * (lane % half).astype(F32) / head_size)
    rows_of_table = jnp.arange(step_table.shape[0], dtype=jnp.int32)
    (
        modulation, silu_own, clip_col, clip_row, cosine, sine, marks, kept_qkv,
    ) = prepare(
        me[None], clip_lengths, clip_steps, step_table, freqs[None, :], w_mod, b_mod[None, :],
        [w_qkv], own_rows, count,
    )
    modulation_two = modulate(silu_own, w_mod, b_mod[None, :])
    evens, odds = gathered_blocks(frames, count, (modulation_two[0, 0] * 0.0).astype(BF))

    shared = (me[None], clip_col, modulation, kept_qkv, b_qkv[None, :], cosine, sine)
    h1_a, kv_a, q_a, q_own, later = project(0, evens, *shared, cotangent)
    upstreams = even_blocks(later, count)
    h1_b, kv_b, q_b = project(1, odds, *shared)
    attended, kept_out, kept_up, kept_down = attend(
        q_own, kv_a, kv_b, marks, [w_out, w_up, w_down]
    )
    result, second, d_middle, d_attn, d_o, sums_two = middle_part(
        clip_steps, clip_col, clip_row, frames, cotangent, attended, modulation_two,
        b_out[None, :], b_up[None, :], b_down[None, :], kept_out, kept_up, kept_down,
        upstreams,
    )
    d_o = lax.all_to_all(d_o, "blk", 0, 0, tiled=True)
    seconds = even_blocks(second, count)
    probs = heads_probs(
        me[None], q_a, q_b, kv_a, kv_b, clip_col, clip_row, count, [d_middle]
    )
    sums_two = sums_two + swapped_with(sums_two, "blk", 1)
    sums_two = sums_two + swapped_with(sums_two, "blk", 2)

    wide = width // 2
    da_low, da_high = d_attn[:, :wide], d_attn[:, wide:]
    out_sent = jnp.concatenate([attended, jnp.where(far == 0, da_high, da_low)], axis=1)
    out_kept = jnp.concatenate([attended, jnp.where(far == 0, da_low, da_high)], axis=1)
    out_sent = swapped_with(out_sent, "batch", 2)

    d_qkv, d_qkv_sent, sums_two, out_sent = attend_back(
        me[None], probs, q_a, q_b, kv_a, kv_b, d_o, cosine, sine, (sums_two, out_sent), seconds
    )
    d_own = lax.all_to_all(d_qkv_sent, "blk", 0, 0, tiled=True)
    kept, *sent = weights_part(
        who, clip_col, modulation_two, b_up[None, :], w_up, w_down, h1_a, h1_b, d_qkv,
        [out_kept, out_sent], seconds, upstreams,
    )
    own_sums, for_x, for_y, for_both, out_parts = share(
        who, kept, [swapped_with(v, "batch", 1) for v in sent], count, 3 * LANES, 2 * ffn // count
    )

    d_inputs, sums_one, own_sums, sums_two = last_part(
        clip_col, clip_row, frames, modulation, d_middle, d_own, w_qkv,
        [own_sums, sums_two],
    )
    sums_one = sums_one + swapped_with(sums_one, "blk", 1)
    sums_two = sums_two + swapped_with(sums_two, "blk", 4)

    pairs = [
        (b * count + k, (b ^ 2) * count + (k ^ 1)) for b in range(4) for k in range(count)
    ]
    sums_one, sums_two, sent, down_rows = gather_sums(
        own_sums,
        swapped_with(for_x, "batch", 2),
        swapped_with(for_y, "blk", 1),
        lax.ppermute(for_both, ("batch", "blk"), pairs),
        out_parts,
        3 * LANES,
        [sums_one, sums_two],
    )
    rows_mine = lax.all_to_all(sent, "blk", 0, 0, tiled=True)
    sums_one = sums_one + swapped_with(sums_one, "blk", 2)
    sums_two = batch_parts(sums_two)
    steps_all = jnp.stack([v[clips + 1, :clips] for v in sums_two]) * (1.0 / count)
    steps_all = steps_all[place ^ jnp.arange(4, dtype=jnp.int32)].astype(jnp.int32)
    pick_all = (steps_all[:, :, None] == rows_of_table[None, None, :]).astype(F32)
    pick_all = jnp.pad(pick_all, ((0, 0), (0, 8 - clips), (0, 0))).reshape(32, -1)
    condition_all = exact_dot(pick_all, step_table)
    silu_all = jax.nn.silu(condition_all).astype(BF)
    silu_cols = lax.dynamic_slice_in_dim(silu_all, me * own_rows, own_rows, 1)
    d_w_mod, d_b_mod, d_silu = table_part(
        place[None], sums_two, silu_cols, w_mod, 2 * width, clips
    )
    sums_one, mine = gather_rows(rows_mine, down_rows, 3 * LANES, sums_one, d_silu)
    sums_one = batch_parts(sums_one + swapped_with(sums_one, "blk", 4))
    d_w_mod, d_b_mod, d_table = table_part(
        place[None], sums_one, silu_cols, w_mod, 0, clips,
        (condition_all, pick_all, d_silu, d_w_mod, d_b_mod),
    )

    def batch_total(parts):
        return (parts[0] + parts[1]) + (parts[2] + parts[3])

    bias_two = batch_total([v[clips] for v in sums_two])
    bias_one = batch_total([v[clips : clips + 2] for v in sums_one])
    d_b_qkv = jnp.concatenate(
        [bias_one[0, :width], bias_one[1, :width], bias_one[0, width:]], axis=0
    )
    d_b_out, d_b_up, d_b_down = jnp.split(bias_two, [width, width + ffn])

    other = swapped_with(mine, "batch", 2)
    d_w_qkv, d_w_out, d_w_up, d_w_down = assemble(
        who,
        [mine, swapped_with(mine, "batch", 1), other, swapped_with(other, "batch", 1)],
        own_rows,
        ffn,
    )

    return (
        result,
        d_inputs,
        d_table,
        d_w_mod,
        d_b_mod[0],
        d_w_qkv,
        d_b_qkv,
        d_w_out,
        d_b_out,
        d_w_up,
        d_b_up,
        d_w_down,
        d_b_down,
    )


def solution(mesh):
    blk = mesh.shape["blk"]
    heads_fit = HEADS % (2 * blk) == 0 and mesh.shape["batch"] == 4
    chosen = heads_body if heads_fit else ring_body
    placed = (
        P(("batch", "blk"), None),
        P(),
        P("batch", None),
        P("batch", None),
        P(),
        P(),
        P(),
        P(),
        P(),
        P(),
        P(),
        P(),
        P(),
        P(),
        P(("batch", "blk"), None),
    )
    return jax.shard_map(
        chosen,
        mesh=mesh,
        in_specs=placed,
        out_specs=(
            P(("batch", "blk"), None),
            P(("batch", "blk"), None),
            P(),
            P("blk", None),
            P(),
            P("blk", None),
            P(),
            P("blk", None),
            P(),
            P("blk", None),
            P(),
            P("blk", None),
            P(),
        ),
        check_vma=False,
    )
```

```python
import jax
import jax.numpy as jnp
from jax import lax
from jax.experimental import pallas as pl
from jax.experimental.pallas import tpu as pltpu
from jax.sharding import PartitionSpec as P

HEADS = 16


HIGH_PRECISION = lax.Precision.HIGHEST
NEGATIVE = -1e30


def passed_along(value, axis, by):
    size = lax.axis_size(axis)
    return lax.ppermute(value, axis, [(i, (i + by) % size) for i in range(size)])


def norm_rows(inputs):
    average = jnp.mean(inputs, axis=-1, keepdims=True)
    centred = inputs - average
    variance = jnp.mean(centred * centred, axis=-1, keepdims=True)
    return centred * lax.rsqrt(variance + 1e-06)


def modulated(inputs, shift_part, scale_part):
    return norm_rows(inputs) * (1.0 + scale_part) + shift_part


def rotate(vectors, cosine, sine_part):
    half_size = vectors.shape[-1] // 2
    first_half = vectors[..., :half_size]
    second_half = vectors[..., half_size:]
    return jnp.concatenate(
        [
            first_half * cosine - second_half * sine_part,
            second_half * cosine + first_half * sine_part,
        ],
        axis=-1,
    )


def exact_dot(left_side, right_side):
    return jnp.dot(left_side, right_side, precision=HIGH_PRECISION)


def clip_index(positions, clip_ends):
    return jnp.sum((clip_ends[None, :] <= positions[:, None]).astype(jnp.int32), axis=1)


def attend_block(queries, key_rows, value_rows, visible, carry_state, scale):
    running_max, denominator, numerator = carry_state
    scores = (
        jnp.einsum("qhd,khd->hqk", queries, key_rows, preferred_element_type=jnp.float32) * scale
    )
    scores = jnp.where(visible[None], scores, NEGATIVE)
    new_max = jnp.maximum(running_max, jnp.max(scores, axis=-1))
    factor = jnp.exp(running_max - new_max)
    probabilities = jnp.where(visible[None], jnp.exp(scores - new_max[..., None]), 0.0)
    denominator = factor * denominator + jnp.sum(probabilities, axis=-1)
    numerator = numerator * jnp.transpose(factor)[:, :, None] + jnp.einsum(
        "hqk,khd->qhd",
        probabilities.astype(jnp.bfloat16),
        value_rows,
        preferred_element_type=jnp.float32,
    )
    return (new_max, denominator, numerator)


def grad_block(queries, upstream, log_total, row_delta, key_rows, value_rows, visible, scale):
    scores = (
        jnp.einsum("qhd,khd->hqk", queries, key_rows, preferred_element_type=jnp.float32) * scale
    )
    probabilities = jnp.where(
        visible[None],
        jnp.exp(jnp.where(visible[None], scores, NEGATIVE) - log_total[..., None]),
        0.0,
    )
    d_probs = jnp.einsum("qhd,khd->hqk", upstream, value_rows, preferred_element_type=jnp.float32)
    d_scores = (probabilities * (d_probs - row_delta[..., None])).astype(jnp.bfloat16)
    d_query = scale * jnp.einsum(
        "hqk,khd->qhd", d_scores, key_rows, preferred_element_type=jnp.float32
    )
    d_key = scale * jnp.einsum(
        "hqk,qhd->khd", d_scores, queries, preferred_element_type=jnp.float32
    )
    d_value = jnp.einsum(
        "hqk,qhd->khd",
        probabilities.astype(jnp.bfloat16),
        upstream,
        preferred_element_type=jnp.float32,
    )
    return (d_query, d_key, d_value)


def pass_key_grads(gradients):
    return (
        passed_along(gradients[0].astype(jnp.bfloat16), "blk", 1).astype(jnp.float32),
        passed_along(gradients[1].astype(jnp.bfloat16), "blk", 1).astype(jnp.float32),
    )


def ring_body(
    frames,
    step_table,
    clip_lengths,
    clip_steps,
    w_mod,
    b_mod,
    w_qkv,
    b_qkv,
    w_out,
    b_out,
    w_up,
    b_up,
    w_down,
    b_down,
    cotangent,
):
    frame_count, model_width = frames.shape
    ffn_width = w_up.shape[1]
    cycle_size = lax.axis_size("blk")
    cycle_place = lax.axis_index("blk")
    head_count = HEADS
    head_size = model_width // head_count
    scale = head_size ** (-0.5)
    lengths = clip_lengths[0]
    steps = clip_steps[0]
    clip_count = lengths.shape[0]
    clip_ends = jnp.cumsum(lengths)
    clip_starts = clip_ends - lengths
    local_rows = jnp.arange(frame_count, dtype=jnp.int32)
    places = cycle_place * frame_count + local_rows
    clip_own = clip_index(places, clip_ends)
    member = (clip_own[:, None] == jnp.arange(clip_count, dtype=jnp.int32)[None, :]).astype(
        jnp.float32
    )
    offsets = jnp.sum(member * clip_starts[None, :].astype(jnp.float32), axis=1)
    freqs = 10000.0 ** (-2.0 * jnp.arange(head_size // 2, dtype=jnp.float32) / head_size)
    angles = (places.astype(jnp.float32) - offsets)[:, None] * freqs[None, :]
    cosine = jnp.cos(angles)[:, None, :]
    sine_part = jnp.sin(angles)[:, None, :]

    def clip_of(turn_index):
        source = (cycle_place - turn_index) % cycle_size
        return clip_index(source * frame_count + local_rows, clip_ends)

    step_pick = (
        steps[:, None] == jnp.arange(step_table.shape[0], dtype=jnp.int32)[None, :]
    ).astype(jnp.float32)
    condition = exact_dot(step_pick, step_table)
    silu_low = jax.nn.silu(condition).astype(jnp.bfloat16)
    modulation = jnp.dot(silu_low, w_mod, preferred_element_type=jnp.float32) + b_mod
    frame_mod = exact_dot(member, modulation)
    shift_one, scale_one, gate_one, shift_two, scale_two, gate_two = jnp.split(frame_mod, 6, axis=1)
    inputs = frames.astype(jnp.float32)
    first, first_back = jax.vjp(modulated, inputs, shift_one, scale_one)
    first_low = first.astype(jnp.bfloat16)
    projected = jnp.dot(first_low, w_qkv, preferred_element_type=jnp.float32) + b_qkv
    query_part, key_part, value_part = jnp.split(projected, 3, axis=1)

    def spin(query_lin, key_lin):
        return (
            rotate(query_lin.reshape(frame_count, head_count, head_size), cosine, sine_part),
            rotate(key_lin.reshape(frame_count, head_count, head_size), cosine, sine_part),
        )

    (query_rot, key_rot), spin_back = jax.vjp(spin, query_part, key_part)
    queries = query_rot.astype(jnp.bfloat16)
    key_rows = key_rot.astype(jnp.bfloat16)
    value_rows = value_part.reshape(frame_count, head_count, head_size).astype(jnp.bfloat16)

    def forward_step(turn_index, key_value, carry_state):
        visible = clip_own[:, None] == clip_of(turn_index)[None, :]
        return attend_block(queries, key_value[0], key_value[1], visible, carry_state, scale)

    def forward_turn(turn_index, carry):
        key_value, carry_state = carry
        carry_state = forward_step(turn_index, key_value, carry_state)
        key_value = passed_along((key_value[0], key_value[1]), "blk", 1)
        return (key_value, carry_state)

    initial = (
        jnp.full((head_count, frame_count), NEGATIVE, jnp.float32),
        jnp.zeros((head_count, frame_count), jnp.float32),
        jnp.zeros((frame_count, head_count, head_size), jnp.float32),
    )
    key_value, carry_state = lax.fori_loop(
        0, cycle_size - 1, forward_turn, ((key_rows, value_rows), initial)
    )
    running_max, denominator, numerator = forward_step(cycle_size - 1, key_value, carry_state)
    attended = numerator / jnp.transpose(denominator)[:, :, None]
    log_total = running_max + jnp.log(denominator)
    attended_low = attended.reshape(frame_count, model_width).astype(jnp.bfloat16)
    attn_out = jnp.dot(attended_low, w_out, preferred_element_type=jnp.float32) + b_out
    middle = inputs + gate_one * attn_out
    second, second_back = jax.vjp(modulated, middle, shift_two, scale_two)
    second_low = second.astype(jnp.bfloat16)
    hidden = jnp.dot(second_low, w_up, preferred_element_type=jnp.float32) + b_up
    activated, gelu_back = jax.vjp(
        lambda values_in: jax.nn.gelu(values_in, approximate=True), hidden
    )
    activated_low = activated.astype(jnp.bfloat16)
    ffn_out = jnp.dot(activated_low, w_down, preferred_element_type=jnp.float32) + b_down
    result = middle + gate_two * ffn_out
    upstream_y = cotangent.astype(jnp.float32)
    d_ffn = (gate_two * upstream_y).astype(jnp.bfloat16)
    d_gate_two = upstream_y * ffn_out
    d_act = jnp.dot(d_ffn, w_down.T, preferred_element_type=jnp.float32)
    d_hidden = gelu_back(d_act)[0].astype(jnp.bfloat16)
    d_second = jnp.dot(d_hidden, w_up.T, preferred_element_type=jnp.float32)
    d_middle_norm, d_shift_two, d_scale_two = second_back(d_second)
    d_middle = upstream_y + d_middle_norm
    d_attn = (gate_one * d_middle).astype(jnp.bfloat16)
    d_gate_one = d_middle * attn_out
    d_attended = jnp.dot(d_attn, w_out.T, preferred_element_type=jnp.float32).astype(jnp.bfloat16)
    d_attended = d_attended.reshape(frame_count, head_count, head_size)
    row_delta = jnp.transpose(jnp.sum(d_attended.astype(jnp.float32) * attended, axis=-1))
    zeros_three = jnp.zeros((frame_count, head_count, head_size), jnp.float32)

    def key_step(turn_index, key_value, owed):
        visible = clip_own[:, None] == clip_of(turn_index)[None, :]
        d_query, d_key, d_value = grad_block(
            queries, d_attended, log_total, row_delta, key_value[0], key_value[1], visible, scale
        )
        return (owed[0] + d_query, (owed[1][0] + d_key, owed[1][1] + d_value))

    def key_turn(turn_index, carry):
        key_value, owed = carry
        d_query_sum, gradients = key_step(turn_index, key_value, owed)
        key_value = passed_along((key_value[0], key_value[1]), "blk", 1)
        gradients = pass_key_grads(gradients)
        return (key_value, (d_query_sum, gradients))

    key_value, owed = lax.fori_loop(
        0,
        cycle_size - 1,
        key_turn,
        ((key_rows, value_rows), (zeros_three, (zeros_three, zeros_three))),
    )
    d_query_rot, gradients = key_step(cycle_size - 1, key_value, owed)
    d_key_rot, d_value_all = pass_key_grads(gradients)
    d_query_lin, d_key_lin = spin_back((d_query_rot, d_key_rot))
    d_projected = jnp.concatenate(
        [d_query_lin, d_key_lin, d_value_all.reshape(frame_count, model_width)], axis=1
    ).astype(jnp.bfloat16)
    d_first = jnp.dot(d_projected, w_qkv.T, preferred_element_type=jnp.float32)
    d_input_norm, d_shift_one, d_scale_one = first_back(d_first)
    d_inputs = d_middle + d_input_norm
    d_frame_mod = jnp.concatenate(
        [d_shift_one, d_scale_one, d_gate_one, d_shift_two, d_scale_two, d_gate_two], axis=1
    )
    d_modulation = exact_dot(member.T, d_frame_mod)
    d_silu = jnp.dot(d_modulation, w_mod.T, precision=HIGH_PRECISION)
    d_condition = jax.vjp(jax.nn.silu, condition)[1](d_silu)[0]
    d_table_local = exact_dot(step_pick.T, d_condition)
    small = lax.psum(
        (
            jnp.sum(d_modulation, axis=0),
            jnp.sum(d_projected.astype(jnp.float32), axis=0),
            jnp.sum(d_attn.astype(jnp.float32), axis=0),
            jnp.sum(d_hidden.astype(jnp.float32), axis=0),
            jnp.sum(d_ffn.astype(jnp.float32), axis=0),
            d_table_local,
        ),
        ("batch", "blk"),
    )
    d_b_mod, d_b_qkv, d_b_out, d_b_up, d_b_down, d_table = small
    blocks_list = [
        jnp.dot(first_low.T, d_projected, preferred_element_type=jnp.float32),
        jnp.dot(attended_low.T, d_attn, preferred_element_type=jnp.float32),
        jnp.dot(second_low.T, d_hidden, preferred_element_type=jnp.float32),
    ]
    blocks_list.append(exact_dot(silu_low.T.astype(jnp.float32), d_modulation))
    wide_rows = lax.psum_scatter(
        jnp.concatenate(blocks_list, axis=1), "blk", scatter_dimension=0, tiled=True
    )
    down_part = lax.psum_scatter(
        jnp.dot(activated_low.T, d_ffn, preferred_element_type=jnp.float32),
        "blk",
        scatter_dimension=0,
        tiled=True,
    )
    wide_rows, down_part = (
        lax.psum(wide_rows.astype(jnp.bfloat16), "batch").astype(jnp.float32),
        lax.psum(down_part.astype(jnp.bfloat16), "batch").astype(jnp.float32),
    )
    qkv_end = 3 * model_width
    out_end = qkv_end + model_width
    up_end = out_end + ffn_width
    return (
        result.astype(jnp.bfloat16),
        d_inputs.astype(jnp.bfloat16),
        d_table,
        wide_rows[:, up_end:],
        d_b_mod,
        wide_rows[:, :qkv_end],
        d_b_qkv,
        wide_rows[:, qkv_end:out_end],
        d_b_out,
        wide_rows[:, out_end:up_end],
        d_b_up,
        down_part,
        d_b_down,
    )


BF = jnp.bfloat16
F32 = jnp.float32
LANES = 128
MIB = 1024 * 1024


def swapped_with(value, axis, offset):
    size = lax.axis_size(axis)
    return lax.ppermute(value, axis, [(i, i ^ offset) for i in range(size)])


def even_blocks(value, count):
    return [value] + [swapped_with(value, "blk", k) for k in range(2, count, 2)]


def gathered_blocks(value, count, zero):
    evens = even_blocks(value, count)
    return evens, [swapped_with(e, "blk", 1) for e in evens[:1]] + [
        swapped_with(e + zero, "blk", 1) for e in evens[1:]
    ]


def offset_of(index, count):
    return (2 * index) % count + (2 * index) // count


def after(value, *others):
    return lax.optimization_barrier((value,) + others)[0]


def half_swap(value, lane):
    return jnp.where((lane % 64) < 32, pltpu.roll(value, 96, 1), pltpu.roll(value, 32, 1))


def by_clip(clip, table, first, count):
    chosen = table[first : first + 1, :]
    for c in range(1, count):
        chosen = jnp.where(clip == c, table[first + c : first + c + 1, :], chosen)
    return chosen


def full(shape):
    return pl.BlockSpec(shape, lambda *_: (0,) * len(shape))


ANYWHERE = pl.BlockSpec(memory_space=pl.ANY)
SCALARS = pl.BlockSpec(memory_space=pltpu.SMEM)


KEPT = pl.BlockSpec(memory_space=pltpu.VMEM)


def in_hbm(value):
    if value.size * value.dtype.itemsize < 140000:
        return value
    return pltpu.with_memory_space_constraint(value, pltpu.HBM)


def all_in_hbm(values):
    return [in_hbm(v) for v in values]


def shape_of(shape, dtype=BF):
    size = jnp.dtype(dtype).itemsize
    for n in shape:
        size *= n
    return jax.ShapeDtypeStruct(shape, dtype) if size < 140000 else pltpu.HBM(shape, dtype)


def params(mib=24):
    return pltpu.CompilerParams(vmem_limit_bytes=mib * MIB)


def cost(flops, moved):
    return pl.CostEstimate(flops=flops, bytes_accessed=moved, transcendentals=0)


def prepare_kernel(
    count, me_ref, lengths_ref, steps_ref, table_ref, freq_ref, w_ref, b_ref, *refs
):
    silu, sems = refs[-2:]
    kept = (len(refs) - 9) // 2
    sources, targets = refs[:kept], refs[-2 - kept : -2]
    out_ref, silu_ref, clip_ref, cliprow_ref, cos_ref, sin_ref, marks_ref = refs[kept : kept + 7]
    clips = lengths_ref.shape[1]
    rows = cos_ref.shape[0] // count
    i = pl.program_id(0)

    def copies():
        return [
            pltpu.make_async_copy(
                source.at[:, pl.ds(0, target.shape[1])], target, sems.at[j]
            )
            for j, (source, target) in enumerate(zip(sources, targets))
        ]

    @pl.when(i == 0)
    def _():
        for copy in copies():
            copy.start()
        for c in range(clips):
            row = table_ref[pl.ds(steps_ref[0, c], 1), :]
            silu[c : c + 1, :] = row / (1.0 + jnp.exp(-row))
        silu_ref[...] = silu[:clips, :].astype(BF)

    out_ref[...] = dot_low(silu[...].astype(BF), w_ref[...])[:clips] + b_ref[...]

    @pl.when(i == 0)
    def _():
        def clip_and_start(places):
            clip, start, end = jnp.zeros_like(places), jnp.zeros_like(places), 0
            for c in range(clips):
                end = end + lengths_ref[0, c]
                clip = jnp.where(places >= end, c + 1, clip)
                start = jnp.where(places >= end, end, start)
            return clip, start

        for j in range(count):
            first = (me_ref[0] ^ offset_of(j, count)) * rows
            here = slice(j * rows, (j + 1) * rows)
            places = first + lax.broadcasted_iota(jnp.int32, (rows, LANES), 0)
            lane = lax.broadcasted_iota(jnp.int32, (rows, LANES), 1)
            clip, start = clip_and_start(places)
            angles = (places - start).astype(F32) * freq_ref[...]
            cos_ref[here, :] = jnp.cos(angles)
            sine = jnp.sin(angles)
            sin_ref[here, :] = jnp.where((lane % 64) < 32, -sine, sine)
            clip_ref[here, :] = clip[:, :1]
            places = first + lax.broadcasted_iota(jnp.int32, (1, rows), 1)
            cliprow_ref[:, here] = clip_and_start(places)[0]
            other = jnp.where((clip != lane) & (lane < clips), NEGATIVE, 0.0)
            marks_ref[here, :LANES] = other.astype(BF)
            marks_ref[here, LANES:] = jnp.where(clip == lane, 1.0, 0.0).astype(BF)

    @pl.when(i == pl.num_programs(0) - 1)
    def _():
        for copy in copies():
            copy.wait()


def prepare(me, lengths, steps, step_table, freqs, w_mod, b_mod, weights, own_rows, count):
    width = w_mod.shape[0]
    clips = lengths.shape[1]
    tile = width
    rows = own_rows * count
    shapes = [
        shape_of((clips, 2 * width), F32),
        shape_of((clips, width)),
        shape_of((rows, 1), jnp.int32),
        shape_of((1, rows), jnp.int32),
        shape_of((rows, LANES), F32),
        shape_of((rows, LANES), F32),
        shape_of((rows, 2 * LANES)),
    ]
    return pl.pallas_call(
        lambda *refs: prepare_kernel(count, *refs),
        grid=(2,),
        in_specs=[SCALARS] * 3
        + [
            full(step_table.shape),
            full(freqs.shape),
            pl.BlockSpec((width, tile), lambda i: (0, i)),
            pl.BlockSpec((1, tile), lambda i: (0, i)),
        ]
        + [ANYWHERE] * len(weights),
        out_specs=[pl.BlockSpec((clips, tile), lambda i: (0, i))]
        + [full(v.shape) for v in shapes[1:]]
        + [KEPT] * len(weights),
        out_shape=shapes + [pltpu.VMEM(w.shape, w.dtype) for w in weights],
        scratch_shapes=[pltpu.VMEM((8, width), F32), pltpu.SemaphoreType.DMA((len(weights),))],
        compiler_params=params(),
        cost_estimate=cost(4 * clips * width * width, 5 * width * width),
    )(me, lengths, steps, *all_in_hbm([step_table, freqs, w_mod, b_mod, *weights]))


def modulate_kernel(silu_ref, w_ref, b_ref, out_ref):
    out_ref[...] = dot_low(silu_ref[...], w_ref[...]) + b_ref[...]


def modulate(silu, w_mod, b_mod):
    clips, width = silu.shape
    return pl.pallas_call(
        modulate_kernel,
        grid=(4,),
        in_specs=[
            full(silu.shape),
            pl.BlockSpec((width, width), lambda i: (0, 2 + i)),
            pl.BlockSpec((1, width), lambda i: (0, 2 + i)),
        ],
        out_specs=pl.BlockSpec((clips, width), lambda i: (0, i)),
        out_shape=shape_of((clips, 4 * width), F32),
        compiler_params=params(),
        cost_estimate=cost(8 * clips * width * width, 8 * width * width),
    )(*all_in_hbm([silu, w_mod, b_mod]))


def project_kernel(clips, with_own, me_ref, clip_ref, mod_ref, b_ref, cos_ref, sin_ref, w, *refs):
    copies = []
    if not with_own:
        source, (w, sems), refs = w, refs[-2:], refs[:-2]
        width, step = source.shape[0], 512
        column = pl.ds(pl.multiple_of(me_ref[0] * LANES, LANES), LANES)
        copies = [pltpu.make_async_copy(source.at[:, column], w.at[:, pl.ds(0, LANES)], sems.at[0])]
        for i, start in enumerate(range(width, 3 * width, step)):
            here = pl.ds(start, step)
            copies.append(
                pltpu.make_async_copy(source.at[:, here], w.at[:, here], sems.at[1 + i])
            )
        for copy in copies:
            copy.start()
    blocks = refs[: len(refs) - (5 if with_own else 3)]
    h_ref, kv_ref, q_ref = refs[len(blocks) : len(blocks) + 3]
    rows, width = blocks[0].shape
    column = pl.multiple_of(me_ref[0] * LANES, LANES)
    if with_own:
        own_ref, passed_ref = refs[-2:]
        passed_ref[...] = blocks[-1][...]
        blocks = blocks[:-1]

    mod = mod_ref[...]
    for pair in range(len(blocks) // 2):
        here = slice(2 * pair * rows, 2 * (pair + 1) * rows)
        x = jnp.concatenate([blocks[2 * pair][...], blocks[2 * pair + 1][...]], axis=0).astype(F32)
        normed, _ = norm_parts(x)
        clip = clip_ref[here, :]
        scale = by_clip(clip, mod[:, width:], 0, clips)
        h_ref[here, :] = (normed * (1.0 + scale) + by_clip(clip, mod[:, :width], 0, clips)).astype(BF)

    h = h_ref[...]
    cosine, sine = cos_ref[...], sin_ref[...]
    lane = lax.broadcasted_iota(jnp.int32, cosine.shape, 1)

    def turned(piece, some):
        return piece * cosine[:some] + half_swap(piece, lane[:some]) * sine[:some]

    if with_own:
        heads = w[:, pl.ds(column, LANES)]
    else:
        copies[0].wait()
        heads = w[:, :LANES]
    part = dot_low(h, heads) + b_ref[:, pl.ds(column, LANES)]
    q_ref[...] = (turned(part, h.shape[0]) * 0.125).astype(BF)
    step = 2 * LANES
    for start in range(0 if with_own else width, 3 * width, step):
        some = rows if start < width else h.shape[0]
        if copies and (start - width) % 512 == 0:
            copies[1 + (start - width) // 512].wait()
        part = dot_low(h[:some], w[:, start : start + step]) + b_ref[:, start : start + step]
        for inner in range(0, step, LANES):
            piece = part[:, inner : inner + LANES]
            at = start + inner
            if start < 2 * width:
                piece = turned(piece, some)
            if start < width:
                own_ref[:, at : at + LANES] = (piece * 0.125).astype(BF)
            else:
                kv_ref[(at - width) // LANES] = piece.astype(BF)


def project(half, blocks, me, clip_col, modulation, w_qkv, b_qkv, cosine, sine, passed=None):
    with_own = passed is not None
    own_rows, width = blocks[0].shape
    rows = own_rows * len(blocks)
    clips = modulation.shape[0]
    out_shape = [
        shape_of((rows, width)),
        pltpu.VMEM((2 * width // LANES, rows, LANES), BF),
        shape_of((rows, LANES)),
    ]
    if with_own:
        out_shape += [shape_of((own_rows, width)), shape_of(passed.shape)]
        blocks = blocks + [passed]
    return pl.pallas_call(
        lambda *refs: project_kernel(clips, with_own, *refs),
        grid=(1,),
        in_specs=[
            SCALARS,
            pl.BlockSpec((rows, 1), lambda *_: (half, 0)),
            pl.BlockSpec((clips, 2 * width), lambda *_: (0, 0)),
            full(b_qkv.shape),
            pl.BlockSpec((rows, LANES), lambda *_: (half, 0)),
            pl.BlockSpec((rows, LANES), lambda *_: (half, 0)),
            KEPT if with_own else ANYWHERE,
        ]
        + [full(v.shape) for v in blocks],
        out_specs=[full(out_shape[0].shape), KEPT] + [full(o.shape) for o in out_shape[2:]],
        out_shape=out_shape,
        scratch_shapes=[]
        if with_own
        else [pltpu.VMEM(w_qkv.shape, BF), pltpu.SemaphoreType.DMA((1 + 4 * width // 1024,))],
        compiler_params=params(),
        cost_estimate=cost(4 * rows * width * width, 6 * MIB),
    )(me, *all_in_hbm([clip_col, modulation, b_qkv, cosine, sine]), w_qkv if with_own else in_hbm(w_qkv), *all_in_hbm(blocks))


def contract_last(left, right):
    return lax.dot_general(left, right, (((1,), (1,)), ((), ())), preferred_element_type=F32)


def head_rows(value):
    lane = lax.broadcasted_iota(jnp.int32, value.shape, 1)
    zero = jnp.zeros_like(value)
    return jnp.concatenate(
        [jnp.where(lane < 64, value, zero), jnp.where(lane < 64, zero, value)], axis=0
    )


def head_diagonal(value):
    rows = value.shape[1] // 2
    return jnp.concatenate([value[:64, :rows], value[64:, rows:]], axis=0).T


def softmax_over_keys(keys, queries):
    scores = contract_last(keys, queries)
    expo = jnp.exp(scores - jnp.max(scores, axis=0, keepdims=True))
    return expo, 1.0 / jnp.sum(expo, axis=0, keepdims=True)


def attend_kernel(keymark_ref, rowmark_ref, q_ref, ka_ref, kb_ref, *refs):
    sources, o_ref, targets = refs[:3], refs[3], refs[4:7]
    keys, values, queries, sems = refs[7:]
    half = ka_ref.shape[1]
    pair, pairs = pl.program_id(0), pl.num_programs(0)

    def copies():
        return [
            pltpu.make_async_copy(source, target, sems.at[j])
            for j, (source, target) in enumerate(zip(sources, targets))
        ]

    @pl.when(pair == 0)
    def _():
        for copy in copies():
            copy.start()

    @pl.when(pair == pairs - 1)
    def _():
        for copy in copies():
            copy.wait()

    @pl.when(pair == 0)
    def _():
        keys[:, LANES:] = keymark_ref[...]
        marks = rowmark_ref[...]
        queries[:, LANES:] = jnp.concatenate([marks, marks], axis=0)

    keys[:half, :LANES] = ka_ref[pair]
    keys[half:, :LANES] = kb_ref[pair]
    values[:half] = ka_ref[pairs + pair]
    values[half:] = kb_ref[pairs + pair]
    queries[:, :LANES] = head_rows(q_ref[...])
    expo, inverse = softmax_over_keys(keys[...], queries[...])
    turned = jnp.dot(values[...].T, expo.astype(BF), preferred_element_type=F32) * inverse
    o_ref[...] = head_diagonal(turned).astype(BF)


def attend(q, kv_a, kv_b, marks, weights):
    own_rows, width = q.shape
    rows = 2 * kv_a.shape[1]
    return pl.pallas_call(
        attend_kernel,
        grid=(width // LANES,),
        in_specs=[
            pl.BlockSpec((rows, LANES), lambda p: (0, 0)),
            pl.BlockSpec((own_rows, LANES), lambda p: (0, 1)),
            pl.BlockSpec((own_rows, LANES), lambda p: (0, p)),
            KEPT,
            KEPT,
        ]
        + [ANYWHERE] * 3,
        out_specs=[pl.BlockSpec((own_rows, LANES), lambda p: (0, p))] + [KEPT] * 3,
        out_shape=[shape_of((own_rows, width))] + [pltpu.VMEM(w.shape, BF) for w in weights],
        scratch_shapes=[
            pltpu.VMEM((rows, 2 * LANES), BF),
            pltpu.VMEM((rows, LANES), BF),
            pltpu.VMEM((2 * own_rows, 2 * LANES), BF),
            pltpu.SemaphoreType.DMA((3,)),
        ],
        compiler_params=params(),
        cost_estimate=cost(4 * own_rows * rows * width, MIB),
    )(*all_in_hbm([marks, marks, q]), kv_a, kv_b, *all_in_hbm(weights))


def probs_kernel(me_ref, keyclip_ref, rowclip_ref, qa_ref, qb_ref, ka_ref, kb_ref, *refs):
    out_ref, keys = refs[-2:]
    i, blocks = pl.program_id(0), pl.num_programs(0)
    half = ka_ref.shape[1]

    @pl.when(i == 0)
    def _():
        keys[:half] = ka_ref[0]
        keys[half:] = kb_ref[0]

    query = jnp.where(i < blocks // 2, qa_ref[...], qb_ref[...])
    visible = keyclip_ref[...] == rowclip_ref[...]
    visible = jnp.concatenate([visible, visible], axis=1)
    scores = jnp.where(visible, contract_last(keys[...], head_rows(query)), NEGATIVE)
    expo = jnp.exp(scores - jnp.max(scores, axis=0, keepdims=True))
    out_ref[...] = expo * (1.0 / jnp.sum(expo, axis=0, keepdims=True))


def heads_probs(me, q_a, q_b, kv_a, kv_b, clip_col, clip_row, blocks, earlier):
    half = kv_a.shape[1]
    rows = 2 * half
    own_rows = rows // blocks
    halfway = blocks // 2
    grid_spec = pltpu.PrefetchScalarGridSpec(
        num_scalar_prefetch=1,
        grid=(blocks,),
        in_specs=[
            pl.BlockSpec((rows, 1), lambda i, m: (0, 0)),
            pl.BlockSpec((1, own_rows), lambda i, m: (0, i)),
            pl.BlockSpec((own_rows, LANES), lambda i, m: (jnp.minimum(i, halfway - 1), 0)),
            pl.BlockSpec((own_rows, LANES), lambda i, m: (jnp.maximum(i - halfway, 0), 0)),
            pl.BlockSpec((1, half, LANES), lambda i, m: (m[0], 0, 0)),
            pl.BlockSpec((1, half, LANES), lambda i, m: (m[0], 0, 0)),
        ]
        + [ANYWHERE] * len(earlier),
        out_specs=pl.BlockSpec((rows, 2 * own_rows), lambda i, m: (0, i)),
        scratch_shapes=[pltpu.VMEM((rows, LANES), BF)],
    )
    return pl.pallas_call(
        probs_kernel,
        grid_spec=grid_spec,
        out_shape=shape_of((rows, 2 * rows), F32),
        compiler_params=params(),
        cost_estimate=cost(4 * rows * rows * LANES, 9 * MIB),
    )(me, *all_in_hbm([clip_col, clip_row, q_a, q_b]), *all_in_hbm([kv_a, kv_b, *earlier]))


def attend_back_kernel(
    me_ref, p_ref, qa_ref, qb_ref, ka_ref, kb_ref, va_ref, vb_ref, do_ref, cos_ref, sin_ref, *refs
):
    out_ref, sent_ref = refs[-9:-7]
    dk_ref, dv_ref, values, keys_turned, d_probs = refs[-5:]
    i, blocks = pl.program_id(0), pl.num_programs(0)
    rows = do_ref.shape[1]
    half = ka_ref.shape[1]
    me = me_ref[0]

    @pl.when(i == 0)
    def _():
        dk_ref[...] = jnp.zeros_like(dk_ref)
        dv_ref[...] = jnp.zeros_like(dv_ref)
        for at, key_ref, value_ref in ((0, ka_ref, va_ref), (half, kb_ref, vb_ref)):
            values[at : at + half] = value_ref[0]
            keys_turned[:, at : at + half] = key_ref[0].T

    query = jnp.where(i < blocks // 2, qa_ref[...], qb_ref[...])
    q_two, up_two = head_rows(query), head_rows(do_ref[0])
    delta = jnp.zeros((1, 2 * rows), F32)
    step = 256
    for start in range(0, 2 * half, step):
        part = slice(start, start + step)
        probs_low = p_ref[part, :].astype(BF)
        dv_ref[part, :] += dot_low(probs_low, up_two)
        products = contract_last(values[part, :], up_two)
        d_probs[part, :] = products
        delta += jnp.sum(probs_low.astype(F32) * products, axis=0, keepdims=True)
    d_query = jnp.zeros((LANES, 2 * rows), F32)
    for start in range(0, 2 * half, step):
        part = slice(start, start + step)
        ds = (p_ref[part, :] * (d_probs[part, :] - delta)).astype(BF)
        dk_ref[part, :] += dot_low(ds, q_two)
        d_query += dot_low(keys_turned[:, part], ds)
    lane = lax.broadcasted_iota(jnp.int32, (rows, LANES), 1)

    def turned_back(value, where):
        return (value * cos_ref[where, :] - half_swap(value, lane) * sin_ref[where, :]).astype(BF)

    here = pl.ds(pl.multiple_of(i * rows, rows), rows)
    dq = turned_back(head_diagonal(d_query) * 0.125, here)
    out_ref[here, 0:LANES] = dq
    sent_ref[me ^ offset_of(i, blocks), :, 0:LANES] = dq

    @pl.when(i == blocks - 1)
    def _():
        @pl.loop(0, blocks)
        def _(j):
            there = pl.ds(pl.multiple_of(j * rows, rows), rows)
            dk = turned_back(dk_ref[there, :], there)
            dv = dv_ref[there, :].astype(BF)
            out_ref[there, LANES : 2 * LANES] = dk
            out_ref[there, 2 * LANES : 3 * LANES] = dv
            owner = me ^ offset_of(j, blocks)
            sent_ref[owner, :, LANES : 2 * LANES] = dk
            sent_ref[owner, :, 2 * LANES : 3 * LANES] = dv


def attend_back(me, probs, q_a, q_b, kv_a, kv_b, d_o, cosine, sine, passed, earlier):
    half = kv_a.shape[1]
    rows = 2 * half
    pairs = kv_a.shape[0] // 2
    blocks, own_rows, _ = d_o.shape
    halfway = blocks // 2
    grid_spec = pltpu.PrefetchScalarGridSpec(
        num_scalar_prefetch=1,
        grid=(blocks,),
        in_specs=[
            pl.BlockSpec((rows, 2 * own_rows), lambda i, m: (0, i)),
            pl.BlockSpec((own_rows, LANES), lambda i, m: (jnp.minimum(i, halfway - 1), 0)),
            pl.BlockSpec((own_rows, LANES), lambda i, m: (jnp.maximum(i - halfway, 0), 0)),
            pl.BlockSpec((1, half, LANES), lambda i, m: (m[0], 0, 0)),
            pl.BlockSpec((1, half, LANES), lambda i, m: (m[0], 0, 0)),
            pl.BlockSpec((1, half, LANES), lambda i, m: (pairs + m[0], 0, 0)),
            pl.BlockSpec((1, half, LANES), lambda i, m: (pairs + m[0], 0, 0)),
            pl.BlockSpec((1, own_rows, LANES), lambda i, m: (m[0] ^ offset_of(i, blocks), 0, 0)),
            pl.BlockSpec((rows, LANES), lambda i, m: (0, 0)),
            pl.BlockSpec((rows, LANES), lambda i, m: (0, 0)),
            ANYWHERE,
            ANYWHERE,
        ]
        + [ANYWHERE] * len(earlier),
        out_specs=[
            pl.BlockSpec((rows, 3 * LANES), lambda i, m: (0, 0)),
            pl.BlockSpec((blocks, own_rows, 3 * LANES), lambda i, m: (0, 0, 0)),
            ANYWHERE,
            ANYWHERE,
        ],
        scratch_shapes=[
            pltpu.VMEM((rows, LANES), F32),
            pltpu.VMEM((rows, LANES), F32),
            pltpu.VMEM((rows, LANES), BF),
            pltpu.VMEM((LANES, rows), BF),
            pltpu.VMEM((rows, 2 * own_rows), F32),
        ],
    )
    return pl.pallas_call(
        attend_back_kernel,
        grid_spec=grid_spec,
        out_shape=[
            shape_of((rows, 3 * LANES)),
            shape_of((blocks, own_rows, 3 * LANES)),
            shape_of(passed[0].shape, passed[0].dtype),
            shape_of(passed[1].shape, passed[1].dtype),
        ],
        input_output_aliases={11: 2, 12: 3},
        compiler_params=params(),
        cost_estimate=cost(8 * rows * rows * LANES, 12 * MIB),
    )(
        me,
        *all_in_hbm([probs, q_a, q_b]),
        *all_in_hbm([kv_a, kv_b, kv_a, kv_b]),
        d_o,
        *all_in_hbm([cosine, sine, *passed, *earlier]),
    )


def norm_parts(inputs):
    centred = inputs - jnp.mean(inputs, axis=-1, keepdims=True)
    rstd = lax.rsqrt(jnp.mean(centred * centred, axis=-1, keepdims=True) + 1e-06)
    return centred * rstd, rstd


def norm_back(normed, rstd, gradient):
    return rstd * (
        gradient
        - jnp.mean(gradient, axis=-1, keepdims=True)
        - normed * jnp.mean(gradient * normed, axis=-1, keepdims=True)
    )


def dot_low(left, right):
    return jnp.dot(left, right, preferred_element_type=F32)


def dot_rows(left, right):
    return lax.dot_general(left, right, (((0,), (0,)), ((), ())), preferred_element_type=F32)


def gelu_parts(hidden):
    square = hidden * hidden
    tanh = jnp.tanh(0.7978845608028654 * hidden * (1.0 + 0.044715 * square))
    upper = 0.5 * (1.0 + tanh)
    slope = upper + 0.5 * hidden * (1.0 - tanh * tanh) * (
        0.7978845608028654 * (1.0 + 3.0 * 0.044715 * square)
    )
    return hidden * upper, slope


def high_low(value):
    high = value.astype(BF)
    return high, (value - high.astype(F32)).astype(BF)


class RowSums:
    def __init__(self, clip_row, clips):
        self.place = lax.broadcasted_iota(jnp.int32, (8, clip_row.shape[1]), 0)
        self.member = ((self.place == clip_row) & (self.place < clips)).astype(F32).astype(BF)

    def by_clip(self, value):
        high, low = high_low(value)
        return dot_low(
            jnp.concatenate([self.member, self.member], axis=1),
            jnp.concatenate([high, low], axis=0),
        )

    def whole(self, value, row):
        return dot_low((self.place == row).astype(F32).astype(BF), value)


def middle_kernel(
    clips, steps_ref, clipc_ref, clipr_ref, x_ref, dy_ref, o_ref, mod_ref, bo_ref, bu_ref, bd_ref,
    wo, wu, wd, *refs,
):
    out_ref, h2_ref, dx_ref, da_ref, do_ref, sums_ref = refs[-6:]
    width = x_ref.shape[1]
    ffn = wu.shape[1]
    clip = clipc_ref[...]

    def frame_rows(index):
        return by_clip(clip, mod_ref[:, (index - 2) * width : (index - 1) * width], 0, clips)

    gate_one, scale_two, gate_two = frame_rows(2), 1.0 + frame_rows(4), frame_rows(5)
    upstream = dy_ref[...].astype(F32)
    d_ffn = (gate_two * upstream).astype(BF)
    attn_out = dot_low(o_ref[...], wo[...]) + bo_ref[...]
    middle = x_ref[...].astype(F32) + gate_one * attn_out
    normed, rstd = norm_parts(middle)
    second = (normed * scale_two + frame_rows(3)).astype(BF)
    h2_ref[...] = second
    sums = RowSums(clipr_ref[...], clips)
    ffn_out = jnp.zeros(x_ref.shape, F32)
    d_second = jnp.zeros(x_ref.shape, F32)
    step = 512
    up_sums = []
    for start in range(0, ffn, step):
        here = slice(start, start + step)
        activated, slope = gelu_parts(dot_low(second, wu[:, here]) + bu_ref[:, here])
        ffn_out += dot_low(activated.astype(BF), wd[here, :])
        d_hidden = (contract_last(d_ffn, wd[here, :]) * slope).astype(BF)
        d_second += contract_last(d_hidden, wu[:, here])
        up_sums.append(sums.whole(d_hidden, clips))
    ffn_out += bd_ref[...]
    out_ref[...] = (middle + gate_two * ffn_out).astype(BF)
    d_middle = upstream + norm_back(normed, rstd, d_second * scale_two)
    dx_ref[...] = d_middle
    d_attn = (gate_one * d_middle).astype(BF)
    da_ref[...] = d_attn
    d_o = contract_last(d_attn, wo[...]).astype(BF)
    for k in range(width // LANES):
        do_ref[k] = d_o[:, k * LANES : (k + 1) * LANES]
    up_sums = jnp.concatenate(up_sums, axis=1)
    place = lax.broadcasted_iota(jnp.int32, (8, width), 0)
    lane = lax.broadcasted_iota(jnp.int32, (8, width), 1)
    steps = jnp.zeros((8, width), F32)
    for c in range(clips):
        here = (place == clips + 1) & (lane == c)
        steps = jnp.where(here, steps_ref[0, c].astype(F32), steps)
    sums_ref[:, :width] = (
        sums.by_clip(d_middle * attn_out) + sums.whole(d_attn, clips) + steps
    )
    sums_ref[:, width : 2 * width] = sums.by_clip(d_second) + up_sums[:, :width]
    sums_ref[:, 2 * width : 3 * width] = sums.by_clip(d_second * normed) + up_sums[:, width:]
    sums_ref[:, 3 * width :] = sums.by_clip(upstream * ffn_out) + sums.whole(d_ffn, clips)


def middle_part(
    steps, clip_col, clip_row, frames, cotangent, attended, modulation, b_out, b_up, b_down,
    w_out, w_up, w_down, earlier,
):
    rows, width = frames.shape
    clips = modulation.shape[0]
    small = [
        clip_col, clip_row, frames, cotangent, attended, modulation, b_out, b_up, b_down
    ]
    out_shape = [
        shape_of((rows, width)),
        shape_of((rows, width)),
        shape_of((rows, width), F32),
        shape_of((rows, width)),
        shape_of((width // LANES, rows, LANES)),
        shape_of((8, 4 * width), F32),
    ]
    return pl.pallas_call(
        lambda *refs: middle_kernel(clips, *refs),
        grid=(1,),
        in_specs=[SCALARS, full((rows, 1)), full((1, rows))]
        + [full(v.shape) for v in small[2:]]
        + [KEPT] * 3
        + [ANYWHERE] * len(earlier),
        out_specs=[full(o.shape) for o in out_shape],
        out_shape=out_shape,
        compiler_params=params(),
        cost_estimate=cost(20 * rows * width * width, 3 * MIB),
    )(steps, *all_in_hbm(small), w_out, w_up, w_down, *all_in_hbm(earlier))


def last_kernel(clips, clipc_ref, clipr_ref, x_ref, mod_ref, dx_ref, d_ref, w_hbm, *refs):
    passed = (len(refs) - 5) // 2
    out_ref, sums_ref = refs[passed : passed + 2]
    d_all, w, sems = refs[-3:]
    width = x_ref.shape[1]
    parts = 3
    copies = [
        pltpu.make_async_copy(
            w_hbm.at[:, pl.ds(i * width, width)], w.at[:, pl.ds(i * width, width)], sems.at[i]
        )
        for i in range(parts)
    ]
    for copy in copies:
        copy.start()
    for k in range(d_ref.shape[0]):
        for i in range(3):
            at = i * width + k * LANES
            d_all[:, at : at + LANES] = d_ref[k, :, i * LANES : (i + 1) * LANES]
    normed, rstd = norm_parts(x_ref[...].astype(F32))
    scale = 1.0 + by_clip(clipc_ref[...], mod_ref[...], 0, clips)
    d_first = jnp.zeros(x_ref.shape, F32)
    for i in range(parts):
        copies[i].wait()
        here = slice(i * width, (i + 1) * width)
        d_first += contract_last(d_all[:, here], w[:, here])
    out_ref[...] = (dx_ref[...] + norm_back(normed, rstd, d_first * scale)).astype(BF)
    sums = RowSums(clipr_ref[...], clips)
    sums_ref[:, :width] = (
        sums.by_clip(d_first)
        + sums.whole(d_all[:, :width], clips)
        + sums.whole(d_all[:, width : 2 * width], clips + 1)
    )
    sums_ref[:, width:] = sums.by_clip(d_first * normed) + sums.whole(d_all[:, 2 * width :], clips)


def last_part(clip_col, clip_row, frames, modulation, d_middle, d_own, w_qkv, passed):
    rows, width = frames.shape
    clips = modulation.shape[0]
    return pl.pallas_call(
        lambda *refs: last_kernel(clips, *refs),
        grid=(1,),
        in_specs=[
            full((rows, 1)),
            full((1, rows)),
            full(frames.shape),
            pl.BlockSpec((clips, width), lambda *_: (0, 1)),
            full(d_middle.shape),
            full(d_own.shape),
        ]
        + [ANYWHERE] * (1 + len(passed)),
        out_specs=[full((rows, width)), full((8, 2 * width))] + [ANYWHERE] * len(passed),
        out_shape=[shape_of((rows, width)), shape_of((8, 2 * width), F32)]
        + [shape_of(v.shape, v.dtype) for v in passed],
        input_output_aliases={7 + i: 2 + i for i in range(len(passed))},
        scratch_shapes=[
            pltpu.VMEM((rows, 3 * width), BF),
            pltpu.VMEM(w_qkv.shape, BF),
            pltpu.SemaphoreType.DMA((3,)),
        ],
        compiler_params=params(),
        cost_estimate=cost(6 * rows * width * width, 2 * MIB),
    )(
        *all_in_hbm([clip_col, clip_row, frames, modulation, d_middle]),
        d_own,
        *all_in_hbm([w_qkv, *passed]),
    )


def half_rows(core, value, kept_ref, sent_refs, at, columns):
    half = value.shape[0] // 2
    low, high = value[:half], value[half:]
    here = slice(at, at + half)
    kept_ref[here, columns] = jnp.where(core == 0, low, high)
    sent = jnp.where(core == 0, high, low).astype(BF)
    wide = sent_refs[0].shape[1]
    for i, ref in enumerate(sent_refs):
        start, stop = max(columns.start, i * wide), min(columns.stop, (i + 1) * wide)
        if start < stop:
            ref[here, start - i * wide : stop - i * wide] = sent[
                :, start - columns.start : stop - columns.start
            ]


def weights_kernel(clips, count, who_ref, clip_ref, gate_ref, bu_ref, wu_hbm, wd_hbm, *refs):
    kept_ref, sent_ref, (up_sum, down_sum, wu, wd, sems) = refs[-9], refs[-8:-5], refs[-5:]
    ha_ref, hb_ref, d_ref, mine_ref, theirs_ref = refs[:5]
    blocks = refs[5 : 5 + count]
    seconds, upstreams = blocks[: len(blocks) // 2], blocks[len(blocks) // 2 :]
    me, core = who_ref[0], who_ref[1]
    rows, width = seconds[0].shape
    part = up_sum.shape[1]
    columns = d_ref.shape[1]
    half = ha_ref.shape[0]
    own = pl.ds(pl.multiple_of((me // 2) * part, part), part)
    copies = [
        pltpu.make_async_copy(wu_hbm.at[:, own], wu, sems.at[0]),
        pltpu.make_async_copy(wd_hbm.at[own, :], wd, sems.at[1]),
    ]
    for copy in copies:
        copy.start()
    shard = part // 2

    step = 2 * LANES
    for start in range(0, width, step):
        here = slice(start, start + step)
        value = dot_rows(ha_ref[:, here], d_ref[:half, :])
        value += dot_rows(hb_ref[:, here], d_ref[half:, :])
        for inner in range(0, step, LANES):
            half_rows(
                core, value[inner : inner + LANES], kept_ref, sent_ref, (start + inner) // 2,
                slice(0, columns),
            )

    left = jnp.concatenate([mine_ref[:, :width], theirs_ref[:, :width]], axis=0)
    right = jnp.concatenate([mine_ref[:, width:], theirs_ref[:, width:]], axis=0)
    at = columns + 2 * part
    for start in range(0, width, step):
        value = dot_rows(left[:, start : start + step], right)
        for inner in range(0, step, LANES):
            half_rows(
                core, value[inner : inner + LANES], kept_ref, sent_ref, (start + inner) // 2,
                slice(at, at + width // 2),
            )

    for copy in copies:
        copy.wait()
    up_weights, down_weights = wu[...], wd[...]
    for pair in range(len(seconds) // 2):
        here = slice(2 * pair * rows, 2 * (pair + 1) * rows)
        second = jnp.concatenate([r[...] for r in seconds[2 * pair : 2 * pair + 2]], axis=0)
        upstream = jnp.concatenate([r[...] for r in upstreams[2 * pair : 2 * pair + 2]], axis=0)
        gate = by_clip(clip_ref[here, :], gate_ref[...], 0, clips)
        d_ffn = (gate * upstream.astype(F32)).astype(BF)
        activated, slope = gelu_parts(dot_low(second, up_weights) + bu_ref[:, own])
        d_hidden = (contract_last(d_ffn, down_weights) * slope).astype(BF)
        up, down = dot_rows(second, d_hidden), dot_rows(activated.astype(BF), d_ffn)
        if pair == 0:
            up_sum[...] = up
            down_sum[...] = down
        else:
            up_sum[...] += up
            down_sum[...] += down
    for y in range(2):
        mine = slice(y * shard, (y + 1) * shard)
        at = columns + 2 * y * shard
        for k in range(width // LANES):
            half_rows(
                core, up_sum[k * LANES : (k + 1) * LANES, mine], kept_ref, sent_ref,
                k * LANES // 2, slice(at, at + shard),
            )
        for c in range(width // shard):
            half_rows(
                core, down_sum[mine, c * shard : (c + 1) * shard], kept_ref, sent_ref,
                c * shard // 2, slice(at + shard, at + 2 * shard),
            )


def weights_part(who, clip_col, modulation, b_up, w_up, w_down, h1_a, h1_b, d_qkv, outs, seconds, upstreams):
    width, ffn = w_up.shape
    count = 2 * len(seconds)
    part = 2 * ffn // count
    clips = modulation.shape[0]
    shape = (width // 2, d_qkv.shape[1] + 2 * part + width // 2)
    rows = d_qkv.shape[0]
    arrays = [h1_a, h1_b, d_qkv, *outs, *seconds, *upstreams]
    return pl.pallas_call(
        lambda *refs: weights_kernel(clips, count, *refs),
        grid=(1,),
        in_specs=[
            SCALARS,
            pl.BlockSpec((rows // 2, 1), lambda *_: (0, 0)),
            pl.BlockSpec((clips, width), lambda *_: (0, 3)),
            full(b_up.shape),
            ANYWHERE,
            ANYWHERE,
        ]
        + [full(v.shape) for v in arrays],
        out_specs=[full(shape)] + [full((shape[0], shape[1] // 3))] * 3,
        out_shape=[shape_of(shape, F32)] + [shape_of((shape[0], shape[1] // 3))] * 3,
        scratch_shapes=[
            pltpu.VMEM((width, part), F32),
            pltpu.VMEM((part, width), F32),
            pltpu.VMEM((width, part), BF),
            pltpu.VMEM((part, width), BF),
            pltpu.SemaphoreType.DMA((2,)),
        ],
        compiler_params=params(36),
        cost_estimate=cost(7 * rows * width * part, 10 * MIB),
    )(who, *all_in_hbm([clip_col, modulation, b_up, w_up, w_down, *arrays]))


def table_kernel(first, clips, place_ref, *refs):
    parts, refs = refs[:4], refs[4:]
    if first:
        silu_ref, w_ref = refs[:2]
        dw_ref, db_ref, out_ref, total, sums = refs[-5:]
    else:
        silu_ref, w_ref, cond_ref, pick_ref, earlier_ref, _, _ = refs[:7]
        dw_ref, db_ref, out_ref, total, sums = refs[7:]
    i = pl.program_id(0)

    @pl.when(i == 0)
    def _():
        total[...] = jnp.zeros_like(total) if first else earlier_ref[...]

    for j, part in enumerate(parts):
        value = part[...]
        valid = lax.broadcasted_iota(jnp.int32, value.shape, 0) < clips
        sums[pl.ds(pl.multiple_of((place_ref[0] ^ j) * 8, 8), 8), :] = jnp.where(valid, value, 0.0)
    high, low = high_low(sums[...])
    total[...] += contract_last(w_ref[...], jnp.concatenate([high, low], axis=0))
    silu = silu_ref[...]
    dw_ref[...] = dot_rows(
        jnp.concatenate([silu, silu], axis=0), jnp.concatenate([high, low], axis=0)
    )
    db_ref[...] = jnp.sum(sums[...], axis=0, keepdims=True)

    @pl.when(i == pl.num_programs(0) - 1)
    def _():
        if first:
            out_ref[...] = total[...]
        else:
            rows = high.shape[0]
            d_silu = total[:, :rows] + total[:, rows:]
            cond = cond_ref[...]
            gate = 1.0 / (1.0 + jnp.exp(-cond))
            d_cond = d_silu.T * (gate * (1.0 + cond * (1.0 - gate)))
            d_high, d_low = high_low(d_cond)
            lowest = (d_cond - d_high.astype(F32) - d_low.astype(F32)).astype(BF)
            pick = pick_ref[...].astype(BF)
            out_ref[...] = dot_rows(pick, d_high) + dot_rows(pick, d_low) + dot_rows(pick, lowest)


def table_part(place, sums, silu, w_mod, column, clips, rest=None, earlier=()):
    columns = sums[0].shape[1]
    width = w_mod.shape[0]
    all_columns = 6 * width
    rows, own = silu.shape
    tile = 1024
    skip = column // tile
    first = rest is None
    shapes = [
        shape_of((own, all_columns), F32),
        shape_of((1, all_columns), F32),
        shape_of((width, 2 * rows), F32),
    ]
    in_specs = [SCALARS] + [pl.BlockSpec((8, tile), lambda i: (0, i))] * 4 + [
        pl.BlockSpec((rows, own), lambda i: (0, 0)),
        pl.BlockSpec((width, tile), lambda i: (0, skip + i)),
    ]
    args = [place, *all_in_hbm([*sums, silu]), in_hbm(w_mod)]
    aliases = {}
    if first:
        in_specs += [ANYWHERE] * len(earlier)
        args += all_in_hbm(earlier)
    else:
        condition, pick, earlier, d_w, d_b = rest
        in_specs += [
            pl.BlockSpec((rows, width), lambda i: (0, 0)),
            pl.BlockSpec(pick.shape, lambda i: (0, 0)),
            pl.BlockSpec((width, 2 * rows), lambda i: (0, 0)),
            ANYWHERE,
            ANYWHERE,
        ]
        args += all_in_hbm([condition, pick, earlier, d_w, d_b])
        aliases = {10: 0, 11: 1}
        shapes[2] = shape_of((pick.shape[1], width), F32)
    return pl.pallas_call(
        lambda *refs: table_kernel(first, clips, *refs),
        grid=(columns // tile,),
        in_specs=in_specs,
        out_specs=[
            pl.BlockSpec((own, tile), lambda i: (0, skip + i)),
            pl.BlockSpec((1, tile), lambda i: (0, skip + i)),
            pl.BlockSpec(shapes[2].shape, lambda i: (0, 0)),
        ],
        out_shape=shapes,
        scratch_shapes=[
            pltpu.VMEM((width, 2 * rows), F32),
            pltpu.VMEM((rows, tile), F32),
        ],
        input_output_aliases=aliases,
        compiler_params=params(),
        cost_estimate=cost(rows * width, width),
    )(*args)


def in_order(bit, mine, other):
    return jnp.stack([jnp.where(bit == 0, mine, other), jnp.where(bit == 0, other, mine)])


def batch_parts(sums):
    return [sums] + [swapped_with(sums, "batch", k) for k in range(1, 4)]


def share_kernel(columns, part, who_ref, kept_ref, *refs):
    others = refs[:3]
    own_ref, x_ref, y_ref, both_ref, out_ref = refs[-5:]
    far, odd = who_ref[2] // 2 == 1, who_ref[0] % 2 == 1
    rows = own_ref.shape[1]
    first, second = slice(columns, columns + part), slice(columns + part, columns + 2 * part)
    for k in range(own_ref.shape[0]):
        here = slice(2 * k * rows, 2 * (k + 1) * rows)
        other = jnp.concatenate([ref[here, :] for ref in others], axis=1)
        value = kept_ref[here, :] + other.astype(F32)
        low, high = value[:rows], value[rows:]
        near, away = jnp.where(far, high, low), jnp.where(far, low, high)
        own_ref[k, :, :columns] = near[:, :columns]
        own_ref[k, :, columns:] = jnp.where(odd, near[:, second], near[:, first])
        y_ref[k] = jnp.where(odd, near[:, first], near[:, second]).astype(BF)
        x_ref[k, :, :columns] = away[:, :columns].astype(BF)
        x_ref[k, :, columns:] = jnp.where(odd, away[:, second], away[:, first]).astype(BF)
        both_ref[k] = jnp.where(odd, away[:, first], away[:, second]).astype(BF)
        out_ref[k] = jnp.concatenate(
            [low[:, columns + 2 * part :], high[:, columns + 2 * part :]], axis=1
        ).astype(BF)


def share(who, kept, others, count, columns, part):
    rows = kept.shape[0] // count // 2
    width = 2 * (kept.shape[1] - columns - 2 * part)
    shapes = [
        shape_of((count, rows, columns + part), F32),
        shape_of((count, rows, columns + part)),
        shape_of((count, rows, part)),
        shape_of((count, rows, part)),
        shape_of((count, rows, width)),
    ]
    return pl.pallas_call(
        lambda *refs: share_kernel(columns, part, *refs),
        grid=(1,),
        in_specs=[SCALARS, full(kept.shape)] + [full(v.shape) for v in others],
        out_specs=[full(v.shape) for v in shapes],
        out_shape=shapes,
        compiler_params=params(),
        cost_estimate=cost(0, 8 * MIB),
    )(who, in_hbm(kept), *others)


def gather_sums_kernel(columns, own_ref, x_ref, y_ref, both_ref, out_ref, *refs):
    sent_ref, down_ref = refs[-2:]
    count, rows, _ = own_ref.shape
    shard = y_ref.shape[2] // 2
    ready = columns + shard
    for k in range(count):
        from_x = x_ref[k].astype(F32)
        sent_ref[k, :, :columns] = (own_ref[k, :, :columns] + from_x[:, :columns]).astype(BF)
        value = (own_ref[k, :, columns:] + from_x[:, columns:]) + (
            y_ref[k].astype(F32) + both_ref[k].astype(F32)
        )
        sent_ref[k, :, columns:ready] = value[:, :shard].astype(BF)
        group, at = k % 2, k // 2 * shard
        down_ref[group * rows : (group + 1) * rows, at : at + shard] = value[:, shard:].astype(BF)
        sent_ref[k, :, ready:] = out_ref[k]


def gather_sums(own, from_x, from_y, from_both, out_parts, columns, passed):
    count, rows, _ = own.shape
    width = out_parts.shape[2]
    args = [own, from_x, from_y, from_both, out_parts]
    shapes = [
        shape_of((count, rows, columns + from_y.shape[2] // 2 + width)),
        shape_of((2 * rows, width)),
    ]
    return pl.pallas_call(
        lambda *refs: gather_sums_kernel(columns, *refs),
        grid=(1,),
        in_specs=[full(v.shape) for v in args] + [ANYWHERE] * len(passed),
        out_specs=[ANYWHERE] * len(passed) + [full(v.shape) for v in shapes],
        out_shape=[shape_of(v.shape, v.dtype) for v in passed] + shapes,
        input_output_aliases={5 + i: i for i in range(len(passed))},
        compiler_params=params(),
        cost_estimate=cost(0, 4 * MIB),
    )(in_hbm(own), from_x, from_y, from_both, *all_in_hbm([out_parts, *passed]))


def rows_kernel(columns, rows_ref, down_ref, *refs):
    out_ref = refs[-1]
    count, rows, wide = rows_ref.shape
    width = out_ref.shape[1]
    shard = wide - width - columns
    total = jnp.zeros((rows, width), F32)
    for k in range(count):
        for i in range(columns // LANES):
            out_ref[i * rows : (i + 1) * rows, k * LANES : (k + 1) * LANES] = rows_ref[
                k, :, i * LANES : (i + 1) * LANES
            ]
        piece = columns // LANES + k * shard // width
        at = k * shard % width
        out_ref[piece * rows : (piece + 1) * rows, at : at + shard] = rows_ref[
            k, :, columns : columns + shard
        ]
        total += rows_ref[k, :, columns + shard :].astype(F32)
    piece = columns // LANES + count * shard // width
    out_ref[piece * rows : (piece + 2) * rows, :] = down_ref[...]
    out_ref[(piece + 2) * rows :, :] = total.astype(BF)


def gather_rows(rows_mine, down_rows, columns, passed, earlier):
    count, rows, wide = rows_mine.shape
    width = down_rows.shape[1]
    shard = wide - width - columns
    shape = ((columns // LANES + count * shard // width + 3) * rows, width)
    return pl.pallas_call(
        lambda *refs: rows_kernel(columns, *refs),
        grid=(1,),
        in_specs=[full(rows_mine.shape), full(down_rows.shape), ANYWHERE, ANYWHERE],
        out_specs=[ANYWHERE, full(shape)],
        out_shape=[shape_of(passed.shape, passed.dtype), shape_of(shape)],
        input_output_aliases={2: 0},
        compiler_params=params(),
        cost_estimate=cost(0, 2 * MIB),
    )(rows_mine, *all_in_hbm([down_rows, passed, earlier]))


def assemble_kernel(ffn, who_ref, *refs):
    qkv_ref, out_ref, up_ref, down_ref = refs[-4:]
    width = out_ref.shape[1]
    rows = qkv_ref.shape[0] // 4
    for j, ref in enumerate(refs[:4]):
        owner = who_ref[2] ^ j
        core, far = owner % 2, owner // 2
        at = pl.multiple_of(core * 2 * rows + far * rows, rows)
        piece = 0
        for target, count in ((qkv_ref, 3), (up_ref, ffn // width)):
            for i in range(count):
                here = slice(piece * rows, (piece + 1) * rows)
                target[pl.ds(at, rows), i * width : (i + 1) * width] = ref[here, :].astype(F32)
                piece += 1
        for g in range(2):
            here = slice(piece * rows, (piece + 1) * rows)
            there = pl.multiple_of(core * 4 * rows + g * 2 * rows + far * rows, rows)
            down_ref[pl.ds(there, rows), :] = ref[here, :].astype(F32)
            piece += 1
        part = width // 2
        column = pl.multiple_of(far * part, part)
        for g in range(2):
            there = pl.multiple_of(core * 2 * rows + g * rows, rows)
            out_ref[pl.ds(there, rows), pl.ds(column, part)] = ref[
                piece * rows : (piece + 1) * rows, g * part : (g + 1) * part
            ].astype(F32)


def assemble(who, parts, own_rows, ffn):
    width = parts[0].shape[1]
    shapes = [
        shape_of((own_rows, 3 * width), F32),
        shape_of((own_rows, width), F32),
        shape_of((own_rows, ffn), F32),
        shape_of((2 * own_rows, width), F32),
    ]
    return pl.pallas_call(
        lambda *refs: assemble_kernel(ffn, *refs),
        grid=(1,),
        in_specs=[SCALARS] + [full(v.shape) for v in parts],
        out_specs=[full(o.shape) for o in shapes],
        out_shape=shapes,
        compiler_params=params(),
        cost_estimate=cost(0, 6 * MIB),
    )(who, *parts)


def heads_body(
    frames, step_table, clip_lengths, clip_steps, w_mod, b_mod, w_qkv, b_qkv, w_out, b_out,
    w_up, b_up, w_down, b_down, cotangent,
):
    own_rows, width = frames.shape
    ffn = w_up.shape[1]
    count = lax.axis_size("blk")
    me = lax.axis_index("blk")
    place = lax.axis_index("batch")
    core, far = place % 2, place // 2
    who = jnp.stack([me, core, place])
    clips = clip_lengths.shape[1]
    rows = own_rows * count

    head_size = width // HEADS
    half = head_size // 2
    lane = jnp.arange(LANES, dtype=jnp.int32)
    freqs = 10000.0 ** (-2.0 * (lane % half).astype(F32) / head_size)
    rows_of_table = jnp.arange(step_table.shape[0], dtype=jnp.int32)
    (
        modulation, silu_own, clip_col, clip_row, cosine, sine, marks, kept_qkv,
    ) = prepare(
        me[None], clip_lengths, clip_steps, step_table, freqs[None, :], w_mod, b_mod[None, :],
        [w_qkv], own_rows, count,
    )
    modulation_two = modulate(silu_own, w_mod, b_mod[None, :])
    evens, odds = gathered_blocks(frames, count, (modulation_two[0, 0] * 0.0).astype(BF))

    shared = (b_qkv[None, :], cosine, sine)
    first = (me[None], clip_col, modulation)
    h1_a, kv_a, q_a, q_own, later = project(0, evens, *first, kept_qkv, *shared, cotangent)
    upstreams = even_blocks(later, count)
    h1_b, kv_b, q_b = project(1, odds, *first, w_qkv, *shared)
    attended, kept_out, kept_up, kept_down = attend(
        q_own, kv_a, kv_b, marks, [w_out, w_up, w_down]
    )
    result, second, d_middle, d_attn, d_o, sums_two = middle_part(
        clip_steps, clip_col, clip_row, frames, cotangent, attended, modulation_two,
        b_out[None, :], b_up[None, :], b_down[None, :], kept_out, kept_up, kept_down,
        upstreams,
    )
    d_o = lax.all_to_all(d_o, "blk", 0, 0, tiled=True)
    seconds = even_blocks(second, count)
    probs = heads_probs(
        me[None], q_a, q_b, kv_a, kv_b, clip_col, clip_row, count, [d_middle]
    )
    sums_two = sums_two + swapped_with(sums_two, "blk", 1)
    sums_two = sums_two + swapped_with(sums_two, "blk", 2)

    wide = width // 2
    da_low, da_high = d_attn[:, :wide], d_attn[:, wide:]
    out_sent = jnp.concatenate([attended, jnp.where(far == 0, da_high, da_low)], axis=1)
    out_kept = jnp.concatenate([attended, jnp.where(far == 0, da_low, da_high)], axis=1)
    out_sent = swapped_with(out_sent, "batch", 2)

    d_qkv, d_qkv_sent, sums_two, out_sent = attend_back(
        me[None], probs, q_a, q_b, kv_a, kv_b, d_o, cosine, sine, (sums_two, out_sent), seconds
    )
    d_own = lax.all_to_all(d_qkv_sent, "blk", 0, 0, tiled=True)
    kept, *sent = weights_part(
        who, clip_col, modulation_two, b_up[None, :], w_up, w_down, h1_a, h1_b, d_qkv,
        [out_kept, out_sent], seconds, upstreams,
    )
    own_sums, for_x, for_y, for_both, out_parts = share(
        who, kept, [swapped_with(v, "batch", 1) for v in sent], count, 3 * LANES, 2 * ffn // count
    )

    d_inputs, sums_one, own_sums, sums_two = last_part(
        clip_col, clip_row, frames, modulation, d_middle, d_own, w_qkv,
        [own_sums, sums_two],
    )
    sums_one = sums_one + swapped_with(sums_one, "blk", 1)
    sums_two = sums_two + swapped_with(sums_two, "blk", 4)

    pairs = [
        (b * count + k, (b ^ 2) * count + (k ^ 1)) for b in range(4) for k in range(count)
    ]
    sums_one, sums_two, sent, down_rows = gather_sums(
        own_sums,
        swapped_with(for_x, "batch", 2),
        swapped_with(for_y, "blk", 1),
        lax.ppermute(for_both, ("batch", "blk"), pairs),
        out_parts,
        3 * LANES,
        [sums_one, sums_two],
    )
    rows_mine = lax.all_to_all(sent, "blk", 0, 0, tiled=True)
    sums_one = sums_one + swapped_with(sums_one, "blk", 2)
    sums_two = batch_parts(sums_two)
    steps_all = jnp.stack([v[clips + 1, :clips] for v in sums_two]) * (1.0 / count)
    steps_all = steps_all[place ^ jnp.arange(4, dtype=jnp.int32)].astype(jnp.int32)
    pick_all = (steps_all[:, :, None] == rows_of_table[None, None, :]).astype(F32)
    pick_all = jnp.pad(pick_all, ((0, 0), (0, 8 - clips), (0, 0))).reshape(32, -1)
    condition_all = exact_dot(pick_all, step_table)
    silu_all = jax.nn.silu(condition_all).astype(BF)
    silu_cols = lax.dynamic_slice_in_dim(silu_all, me * own_rows, own_rows, 1)
    d_w_mod, d_b_mod, d_silu = table_part(
        place[None], sums_two, silu_cols, w_mod, 2 * width, clips
    )
    sums_one, mine = gather_rows(rows_mine, down_rows, 3 * LANES, sums_one, d_silu)
    sums_one = batch_parts(sums_one + swapped_with(sums_one, "blk", 4))
    d_w_mod, d_b_mod, d_table = table_part(
        place[None], sums_one, silu_cols, w_mod, 0, clips,
        (condition_all, pick_all, d_silu, d_w_mod, d_b_mod),
    )

    def batch_total(parts):
        return (parts[0] + parts[1]) + (parts[2] + parts[3])

    bias_two = batch_total([v[clips] for v in sums_two])
    bias_one = batch_total([v[clips : clips + 2] for v in sums_one])
    d_b_qkv = jnp.concatenate(
        [bias_one[0, :width], bias_one[1, :width], bias_one[0, width:]], axis=0
    )
    d_b_out, d_b_up, d_b_down = jnp.split(bias_two, [width, width + ffn])

    other = swapped_with(mine, "batch", 2)
    d_w_qkv, d_w_out, d_w_up, d_w_down = assemble(
        who,
        [mine, swapped_with(mine, "batch", 1), other, swapped_with(other, "batch", 1)],
        own_rows,
        ffn,
    )

    return (
        result,
        d_inputs,
        d_table,
        d_w_mod,
        d_b_mod[0],
        d_w_qkv,
        d_b_qkv,
        d_w_out,
        d_b_out,
        d_w_up,
        d_b_up,
        d_w_down,
        d_b_down,
    )


def solution(mesh):
    blk = mesh.shape["blk"]
    heads_fit = HEADS % (2 * blk) == 0 and mesh.shape["batch"] == 4
    chosen = heads_body if heads_fit else ring_body
    placed = (
        P(("batch", "blk"), None),
        P(),
        P("batch", None),
        P("batch", None),
        P(),
        P(),
        P(),
        P(),
        P(),
        P(),
        P(),
        P(),
        P(),
        P(),
        P(("batch", "blk"), None),
    )
    return jax.shard_map(
        chosen,
        mesh=mesh,
        in_specs=placed,
        out_specs=(
            P(("batch", "blk"), None),
            P(("batch", "blk"), None),
            P(),
            P("blk", None),
            P(),
            P("blk", None),
            P(),
            P("blk", None),
            P(),
            P("blk", None),
            P(),
            P("blk", None),
            P(),
        ),
        check_vma=False,
    )
```

```python
import jax
import jax.numpy as jnp
from jax import lax
from jax.experimental import pallas as pl
from jax.experimental.pallas import tpu as pltpu
from jax.sharding import PartitionSpec as P

HEADS = 16


HIGH_PRECISION = lax.Precision.HIGHEST
NEGATIVE = -1e30


def passed_along(value, axis, by):
    size = lax.axis_size(axis)
    return lax.ppermute(value, axis, [(i, (i + by) % size) for i in range(size)])


def norm_rows(inputs):
    average = jnp.mean(inputs, axis=-1, keepdims=True)
    centred = inputs - average
    variance = jnp.mean(centred * centred, axis=-1, keepdims=True)
    return centred * lax.rsqrt(variance + 1e-06)


def modulated(inputs, shift_part, scale_part):
    return norm_rows(inputs) * (1.0 + scale_part) + shift_part


def rotate(vectors, cosine, sine_part):
    half_size = vectors.shape[-1] // 2
    first_half = vectors[..., :half_size]
    second_half = vectors[..., half_size:]
    return jnp.concatenate(
        [
            first_half * cosine - second_half * sine_part,
            second_half * cosine + first_half * sine_part,
        ],
        axis=-1,
    )


def exact_dot(left_side, right_side):
    return jnp.dot(left_side, right_side, precision=HIGH_PRECISION)


def clip_index(positions, clip_ends):
    return jnp.sum((clip_ends[None, :] <= positions[:, None]).astype(jnp.int32), axis=1)


def attend_block(queries, key_rows, value_rows, visible, carry_state, scale):
    running_max, denominator, numerator = carry_state
    scores = (
        jnp.einsum("qhd,khd->hqk", queries, key_rows, preferred_element_type=jnp.float32) * scale
    )
    scores = jnp.where(visible[None], scores, NEGATIVE)
    new_max = jnp.maximum(running_max, jnp.max(scores, axis=-1))
    factor = jnp.exp(running_max - new_max)
    probabilities = jnp.where(visible[None], jnp.exp(scores - new_max[..., None]), 0.0)
    denominator = factor * denominator + jnp.sum(probabilities, axis=-1)
    numerator = numerator * jnp.transpose(factor)[:, :, None] + jnp.einsum(
        "hqk,khd->qhd",
        probabilities.astype(jnp.bfloat16),
        value_rows,
        preferred_element_type=jnp.float32,
    )
    return (new_max, denominator, numerator)


def grad_block(queries, upstream, log_total, row_delta, key_rows, value_rows, visible, scale):
    scores = (
        jnp.einsum("qhd,khd->hqk", queries, key_rows, preferred_element_type=jnp.float32) * scale
    )
    probabilities = jnp.where(
        visible[None],
        jnp.exp(jnp.where(visible[None], scores, NEGATIVE) - log_total[..., None]),
        0.0,
    )
    d_probs = jnp.einsum("qhd,khd->hqk", upstream, value_rows, preferred_element_type=jnp.float32)
    d_scores = (probabilities * (d_probs - row_delta[..., None])).astype(jnp.bfloat16)
    d_query = scale * jnp.einsum(
        "hqk,khd->qhd", d_scores, key_rows, preferred_element_type=jnp.float32
    )
    d_key = scale * jnp.einsum(
        "hqk,qhd->khd", d_scores, queries, preferred_element_type=jnp.float32
    )
    d_value = jnp.einsum(
        "hqk,qhd->khd",
        probabilities.astype(jnp.bfloat16),
        upstream,
        preferred_element_type=jnp.float32,
    )
    return (d_query, d_key, d_value)


def pass_key_grads(gradients):
    return (
        passed_along(gradients[0].astype(jnp.bfloat16), "blk", 1).astype(jnp.float32),
        passed_along(gradients[1].astype(jnp.bfloat16), "blk", 1).astype(jnp.float32),
    )


def ring_body(
    frames,
    step_table,
    clip_lengths,
    clip_steps,
    w_mod,
    b_mod,
    w_qkv,
    b_qkv,
    w_out,
    b_out,
    w_up,
    b_up,
    w_down,
    b_down,
    cotangent,
):
    frame_count, model_width = frames.shape
    ffn_width = w_up.shape[1]
    cycle_size = lax.axis_size("blk")
    cycle_place = lax.axis_index("blk")
    head_count = HEADS
    head_size = model_width // head_count
    scale = head_size ** (-0.5)
    lengths = clip_lengths[0]
    steps = clip_steps[0]
    clip_count = lengths.shape[0]
    clip_ends = jnp.cumsum(lengths)
    clip_starts = clip_ends - lengths
    local_rows = jnp.arange(frame_count, dtype=jnp.int32)
    places = cycle_place * frame_count + local_rows
    clip_own = clip_index(places, clip_ends)
    member = (clip_own[:, None] == jnp.arange(clip_count, dtype=jnp.int32)[None, :]).astype(
        jnp.float32
    )
    offsets = jnp.sum(member * clip_starts[None, :].astype(jnp.float32), axis=1)
    freqs = 10000.0 ** (-2.0 * jnp.arange(head_size // 2, dtype=jnp.float32) / head_size)
    angles = (places.astype(jnp.float32) - offsets)[:, None] * freqs[None, :]
    cosine = jnp.cos(angles)[:, None, :]
    sine_part = jnp.sin(angles)[:, None, :]

    def clip_of(turn_index):
        source = (cycle_place - turn_index) % cycle_size
        return clip_index(source * frame_count + local_rows, clip_ends)

    step_pick = (
        steps[:, None] == jnp.arange(step_table.shape[0], dtype=jnp.int32)[None, :]
    ).astype(jnp.float32)
    condition = exact_dot(step_pick, step_table)
    silu_low = jax.nn.silu(condition).astype(jnp.bfloat16)
    modulation = jnp.dot(silu_low, w_mod, preferred_element_type=jnp.float32) + b_mod
    frame_mod = exact_dot(member, modulation)
    shift_one, scale_one, gate_one, shift_two, scale_two, gate_two = jnp.split(frame_mod, 6, axis=1)
    inputs = frames.astype(jnp.float32)
    first, first_back = jax.vjp(modulated, inputs, shift_one, scale_one)
    first_low = first.astype(jnp.bfloat16)
    projected = jnp.dot(first_low, w_qkv, preferred_element_type=jnp.float32) + b_qkv
    query_part, key_part, value_part = jnp.split(projected, 3, axis=1)

    def spin(query_lin, key_lin):
        return (
            rotate(query_lin.reshape(frame_count, head_count, head_size), cosine, sine_part),
            rotate(key_lin.reshape(frame_count, head_count, head_size), cosine, sine_part),
        )

    (query_rot, key_rot), spin_back = jax.vjp(spin, query_part, key_part)
    queries = query_rot.astype(jnp.bfloat16)
    key_rows = key_rot.astype(jnp.bfloat16)
    value_rows = value_part.reshape(frame_count, head_count, head_size).astype(jnp.bfloat16)

    def forward_step(turn_index, key_value, carry_state):
        visible = clip_own[:, None] == clip_of(turn_index)[None, :]
        return attend_block(queries, key_value[0], key_value[1], visible, carry_state, scale)

    def forward_turn(turn_index, carry):
        key_value, carry_state = carry
        carry_state = forward_step(turn_index, key_value, carry_state)
        key_value = passed_along((key_value[0], key_value[1]), "blk", 1)
        return (key_value, carry_state)

    initial = (
        jnp.full((head_count, frame_count), NEGATIVE, jnp.float32),
        jnp.zeros((head_count, frame_count), jnp.float32),
        jnp.zeros((frame_count, head_count, head_size), jnp.float32),
    )
    key_value, carry_state = lax.fori_loop(
        0, cycle_size - 1, forward_turn, ((key_rows, value_rows), initial)
    )
    running_max, denominator, numerator = forward_step(cycle_size - 1, key_value, carry_state)
    attended = numerator / jnp.transpose(denominator)[:, :, None]
    log_total = running_max + jnp.log(denominator)
    attended_low = attended.reshape(frame_count, model_width).astype(jnp.bfloat16)
    attn_out = jnp.dot(attended_low, w_out, preferred_element_type=jnp.float32) + b_out
    middle = inputs + gate_one * attn_out
    second, second_back = jax.vjp(modulated, middle, shift_two, scale_two)
    second_low = second.astype(jnp.bfloat16)
    hidden = jnp.dot(second_low, w_up, preferred_element_type=jnp.float32) + b_up
    activated, gelu_back = jax.vjp(
        lambda values_in: jax.nn.gelu(values_in, approximate=True), hidden
    )
    activated_low = activated.astype(jnp.bfloat16)
    ffn_out = jnp.dot(activated_low, w_down, preferred_element_type=jnp.float32) + b_down
    result = middle + gate_two * ffn_out
    upstream_y = cotangent.astype(jnp.float32)
    d_ffn = (gate_two * upstream_y).astype(jnp.bfloat16)
    d_gate_two = upstream_y * ffn_out
    d_act = jnp.dot(d_ffn, w_down.T, preferred_element_type=jnp.float32)
    d_hidden = gelu_back(d_act)[0].astype(jnp.bfloat16)
    d_second = jnp.dot(d_hidden, w_up.T, preferred_element_type=jnp.float32)
    d_middle_norm, d_shift_two, d_scale_two = second_back(d_second)
    d_middle = upstream_y + d_middle_norm
    d_attn = (gate_one * d_middle).astype(jnp.bfloat16)
    d_gate_one = d_middle * attn_out
    d_attended = jnp.dot(d_attn, w_out.T, preferred_element_type=jnp.float32).astype(jnp.bfloat16)
    d_attended = d_attended.reshape(frame_count, head_count, head_size)
    row_delta = jnp.transpose(jnp.sum(d_attended.astype(jnp.float32) * attended, axis=-1))
    zeros_three = jnp.zeros((frame_count, head_count, head_size), jnp.float32)

    def key_step(turn_index, key_value, owed):
        visible = clip_own[:, None] == clip_of(turn_index)[None, :]
        d_query, d_key, d_value = grad_block(
            queries, d_attended, log_total, row_delta, key_value[0], key_value[1], visible, scale
        )
        return (owed[0] + d_query, (owed[1][0] + d_key, owed[1][1] + d_value))

    def key_turn(turn_index, carry):
        key_value, owed = carry
        d_query_sum, gradients = key_step(turn_index, key_value, owed)
        key_value = passed_along((key_value[0], key_value[1]), "blk", 1)
        gradients = pass_key_grads(gradients)
        return (key_value, (d_query_sum, gradients))

    key_value, owed = lax.fori_loop(
        0,
        cycle_size - 1,
        key_turn,
        ((key_rows, value_rows), (zeros_three, (zeros_three, zeros_three))),
    )
    d_query_rot, gradients = key_step(cycle_size - 1, key_value, owed)
    d_key_rot, d_value_all = pass_key_grads(gradients)
    d_query_lin, d_key_lin = spin_back((d_query_rot, d_key_rot))
    d_projected = jnp.concatenate(
        [d_query_lin, d_key_lin, d_value_all.reshape(frame_count, model_width)], axis=1
    ).astype(jnp.bfloat16)
    d_first = jnp.dot(d_projected, w_qkv.T, preferred_element_type=jnp.float32)
    d_input_norm, d_shift_one, d_scale_one = first_back(d_first)
    d_inputs = d_middle + d_input_norm
    d_frame_mod = jnp.concatenate(
        [d_shift_one, d_scale_one, d_gate_one, d_shift_two, d_scale_two, d_gate_two], axis=1
    )
    d_modulation = exact_dot(member.T, d_frame_mod)
    d_silu = jnp.dot(d_modulation, w_mod.T, precision=HIGH_PRECISION)
    d_condition = jax.vjp(jax.nn.silu, condition)[1](d_silu)[0]
    d_table_local = exact_dot(step_pick.T, d_condition)
    small = lax.psum(
        (
            jnp.sum(d_modulation, axis=0),
            jnp.sum(d_projected.astype(jnp.float32), axis=0),
            jnp.sum(d_attn.astype(jnp.float32), axis=0),
            jnp.sum(d_hidden.astype(jnp.float32), axis=0),
            jnp.sum(d_ffn.astype(jnp.float32), axis=0),
            d_table_local,
        ),
        ("batch", "blk"),
    )
    d_b_mod, d_b_qkv, d_b_out, d_b_up, d_b_down, d_table = small
    blocks_list = [
        jnp.dot(first_low.T, d_projected, preferred_element_type=jnp.float32),
        jnp.dot(attended_low.T, d_attn, preferred_element_type=jnp.float32),
        jnp.dot(second_low.T, d_hidden, preferred_element_type=jnp.float32),
    ]
    blocks_list.append(exact_dot(silu_low.T.astype(jnp.float32), d_modulation))
    wide_rows = lax.psum_scatter(
        jnp.concatenate(blocks_list, axis=1), "blk", scatter_dimension=0, tiled=True
    )
    down_part = lax.psum_scatter(
        jnp.dot(activated_low.T, d_ffn, preferred_element_type=jnp.float32),
        "blk",
        scatter_dimension=0,
        tiled=True,
    )
    wide_rows, down_part = (
        lax.psum(wide_rows.astype(jnp.bfloat16), "batch").astype(jnp.float32),
        lax.psum(down_part.astype(jnp.bfloat16), "batch").astype(jnp.float32),
    )
    qkv_end = 3 * model_width
    out_end = qkv_end + model_width
    up_end = out_end + ffn_width
    return (
        result.astype(jnp.bfloat16),
        d_inputs.astype(jnp.bfloat16),
        d_table,
        wide_rows[:, up_end:],
        d_b_mod,
        wide_rows[:, :qkv_end],
        d_b_qkv,
        wide_rows[:, qkv_end:out_end],
        d_b_out,
        wide_rows[:, out_end:up_end],
        d_b_up,
        down_part,
        d_b_down,
    )


BF = jnp.bfloat16
F32 = jnp.float32
LANES = 128
MIB = 1024 * 1024


def swapped_with(value, axis, offset):
    size = lax.axis_size(axis)
    return lax.ppermute(value, axis, [(i, i ^ offset) for i in range(size)])


def even_blocks(value, count):
    return [value] + [swapped_with(value, "blk", k) for k in range(2, count, 2)]


def gathered_blocks(value, count, zero):
    evens = even_blocks(value, count)
    return evens, [swapped_with(e, "blk", 1) for e in evens[:1]] + [
        swapped_with(e + zero, "blk", 1) for e in evens[1:]
    ]


def offset_of(index, count):
    return (2 * index) % count + (2 * index) // count


def after(value, *others):
    return lax.optimization_barrier((value,) + others)[0]


def half_swap(value, lane):
    return jnp.where((lane % 64) < 32, pltpu.roll(value, 96, 1), pltpu.roll(value, 32, 1))


def by_clip(clip, table, first, count):
    chosen = table[first : first + 1, :]
    for c in range(1, count):
        chosen = jnp.where(clip == c, table[first + c : first + c + 1, :], chosen)
    return chosen


def full(shape):
    return pl.BlockSpec(shape, lambda *_: (0,) * len(shape))


ANYWHERE = pl.BlockSpec(memory_space=pl.ANY)
SCALARS = pl.BlockSpec(memory_space=pltpu.SMEM)


KEPT = pl.BlockSpec(memory_space=pltpu.VMEM)


def in_hbm(value):
    if value.size * value.dtype.itemsize < 140000:
        return value
    return pltpu.with_memory_space_constraint(value, pltpu.HBM)


def all_in_hbm(values):
    return [in_hbm(v) for v in values]


def shape_of(shape, dtype=BF):
    size = jnp.dtype(dtype).itemsize
    for n in shape:
        size *= n
    return jax.ShapeDtypeStruct(shape, dtype) if size < 140000 else pltpu.HBM(shape, dtype)


def params(mib=24):
    return pltpu.CompilerParams(vmem_limit_bytes=mib * MIB)


def cost(flops, moved):
    return pl.CostEstimate(flops=flops, bytes_accessed=moved, transcendentals=0)


def prepare_kernel(
    count, me_ref, lengths_ref, steps_ref, table_ref, freq_ref, w_ref, b_ref, *refs
):
    silu, sems = refs[-2:]
    kept = (len(refs) - 9) // 2
    sources, targets = refs[:kept], refs[-2 - kept : -2]
    out_ref, silu_ref, clip_ref, cliprow_ref, cos_ref, sin_ref, marks_ref = refs[kept : kept + 7]
    clips = lengths_ref.shape[1]
    rows = cos_ref.shape[0] // count
    i = pl.program_id(0)

    def copies():
        return [
            pltpu.make_async_copy(
                source.at[:, pl.ds(0, target.shape[1])], target, sems.at[j]
            )
            for j, (source, target) in enumerate(zip(sources, targets))
        ]

    @pl.when(i == 0)
    def _():
        for copy in copies():
            copy.start()
        for c in range(clips):
            row = table_ref[pl.ds(steps_ref[0, c], 1), :]
            silu[c : c + 1, :] = row / (1.0 + jnp.exp(-row))
        silu_ref[...] = silu[:clips, :].astype(BF)

    out_ref[...] = dot_low(silu[...].astype(BF), w_ref[...])[:clips] + b_ref[...]

    @pl.when(i == 0)
    def _():
        def clip_and_start(places):
            clip, start, end = jnp.zeros_like(places), jnp.zeros_like(places), 0
            for c in range(clips):
                end = end + lengths_ref[0, c]
                clip = jnp.where(places >= end, c + 1, clip)
                start = jnp.where(places >= end, end, start)
            return clip, start

        for j in range(count):
            first = (me_ref[0] ^ offset_of(j, count)) * rows
            here = slice(j * rows, (j + 1) * rows)
            places = first + lax.broadcasted_iota(jnp.int32, (rows, LANES), 0)
            lane = lax.broadcasted_iota(jnp.int32, (rows, LANES), 1)
            clip, start = clip_and_start(places)
            angles = (places - start).astype(F32) * freq_ref[...]
            cos_ref[here, :] = jnp.cos(angles)
            sine = jnp.sin(angles)
            sin_ref[here, :] = jnp.where((lane % 64) < 32, -sine, sine)
            clip_ref[here, :] = clip[:, :1]
            places = first + lax.broadcasted_iota(jnp.int32, (1, rows), 1)
            cliprow_ref[:, here] = clip_and_start(places)[0]
            other = jnp.where((clip != lane) & (lane < clips), NEGATIVE, 0.0)
            marks_ref[here, :LANES] = other.astype(BF)
            marks_ref[here, LANES:] = jnp.where(clip == lane, 1.0, 0.0).astype(BF)

    @pl.when(i == pl.num_programs(0) - 1)
    def _():
        for copy in copies():
            copy.wait()


def prepare(me, lengths, steps, step_table, freqs, w_mod, b_mod, weights, own_rows, count):
    width = w_mod.shape[0]
    clips = lengths.shape[1]
    tile = width
    rows = own_rows * count
    shapes = [
        shape_of((clips, 2 * width), F32),
        shape_of((clips, width)),
        shape_of((rows, 1), jnp.int32),
        shape_of((1, rows), jnp.int32),
        shape_of((rows, LANES), F32),
        shape_of((rows, LANES), F32),
        shape_of((rows, 2 * LANES)),
    ]
    return pl.pallas_call(
        lambda *refs: prepare_kernel(count, *refs),
        grid=(2,),
        in_specs=[SCALARS] * 3
        + [
            full(step_table.shape),
            full(freqs.shape),
            pl.BlockSpec((width, tile), lambda i: (0, i)),
            pl.BlockSpec((1, tile), lambda i: (0, i)),
        ]
        + [ANYWHERE] * len(weights),
        out_specs=[pl.BlockSpec((clips, tile), lambda i: (0, i))]
        + [full(v.shape) for v in shapes[1:]]
        + [KEPT] * len(weights),
        out_shape=shapes + [pltpu.VMEM(w.shape, w.dtype) for w in weights],
        scratch_shapes=[pltpu.VMEM((8, width), F32), pltpu.SemaphoreType.DMA((len(weights),))],
        compiler_params=params(),
        cost_estimate=cost(4 * clips * width * width, 5 * width * width),
    )(me, lengths, steps, *all_in_hbm([step_table, freqs, w_mod, b_mod, *weights]))


def modulate_kernel(silu_ref, w_ref, b_ref, out_ref):
    out_ref[...] = dot_low(silu_ref[...], w_ref[...]) + b_ref[...]


def modulate(silu, w_mod, b_mod):
    clips, width = silu.shape
    return pl.pallas_call(
        modulate_kernel,
        grid=(4,),
        in_specs=[
            full(silu.shape),
            pl.BlockSpec((width, width), lambda i: (0, 2 + i)),
            pl.BlockSpec((1, width), lambda i: (0, 2 + i)),
        ],
        out_specs=pl.BlockSpec((clips, width), lambda i: (0, i)),
        out_shape=shape_of((clips, 4 * width), F32),
        compiler_params=params(),
        cost_estimate=cost(8 * clips * width * width, 8 * width * width),
    )(*all_in_hbm([silu, w_mod, b_mod]))


def project_kernel(clips, with_own, me_ref, clip_ref, mod_ref, b_ref, cos_ref, sin_ref, w, *refs):
    copies = []
    if not with_own:
        source, (w, sems), refs = w, refs[-2:], refs[:-2]
        width, step = source.shape[0], 512
        column = pl.ds(pl.multiple_of(me_ref[0] * LANES, LANES), LANES)
        copies = [pltpu.make_async_copy(source.at[:, column], w.at[:, pl.ds(0, LANES)], sems.at[0])]
        for i, start in enumerate(range(width, 3 * width, step)):
            here = pl.ds(start, step)
            copies.append(
                pltpu.make_async_copy(source.at[:, here], w.at[:, here], sems.at[1 + i])
            )
        for copy in copies:
            copy.start()
    blocks = refs[: len(refs) - (5 if with_own else 3)]
    h_ref, kv_ref, q_ref = refs[len(blocks) : len(blocks) + 3]
    rows, width = blocks[0].shape
    column = pl.multiple_of(me_ref[0] * LANES, LANES)
    if with_own:
        own_ref, passed_ref = refs[-2:]
        passed_ref[...] = blocks[-1][...]
        blocks = blocks[:-1]

    mod = mod_ref[...]
    for pair in range(len(blocks) // 2):
        here = slice(2 * pair * rows, 2 * (pair + 1) * rows)
        x = jnp.concatenate([blocks[2 * pair][...], blocks[2 * pair + 1][...]], axis=0).astype(F32)
        normed, _ = norm_parts(x)
        clip = clip_ref[here, :]
        scale = by_clip(clip, mod[:, width:], 0, clips)
        h_ref[here, :] = (normed * (1.0 + scale) + by_clip(clip, mod[:, :width], 0, clips)).astype(BF)

    h = h_ref[...]
    cosine, sine = cos_ref[...], sin_ref[...]
    lane = lax.broadcasted_iota(jnp.int32, cosine.shape, 1)

    def turned(piece, some):
        return piece * cosine[:some] + half_swap(piece, lane[:some]) * sine[:some]

    if with_own:
        heads = w[:, pl.ds(column, LANES)]
    else:
        copies[0].wait()
        heads = w[:, :LANES]
    part = dot_low(h, heads) + b_ref[:, pl.ds(column, LANES)]
    q_ref[...] = (turned(part, h.shape[0]) * 0.125).astype(BF)
    step = 2 * LANES
    for start in range(0 if with_own else width, 3 * width, step):
        some = rows if start < width else h.shape[0]
        if copies and (start - width) % 512 == 0:
            copies[1 + (start - width) // 512].wait()
        part = dot_low(h[:some], w[:, start : start + step]) + b_ref[:, start : start + step]
        for inner in range(0, step, LANES):
            piece = part[:, inner : inner + LANES]
            at = start + inner
            if start < 2 * width:
                piece = turned(piece, some)
            if start < width:
                own_ref[:, at : at + LANES] = (piece * 0.125).astype(BF)
            else:
                kv_ref[(at - width) // LANES] = piece.astype(BF)


def project(half, blocks, me, clip_col, modulation, w_qkv, b_qkv, cosine, sine, passed=None):
    with_own = passed is not None
    own_rows, width = blocks[0].shape
    rows = own_rows * len(blocks)
    clips = modulation.shape[0]
    out_shape = [
        shape_of((rows, width)),
        pltpu.VMEM((2 * width // LANES, rows, LANES), BF),
        shape_of((rows, LANES)),
    ]
    if with_own:
        out_shape += [shape_of((own_rows, width)), shape_of(passed.shape)]
        blocks = blocks + [passed]
    return pl.pallas_call(
        lambda *refs: project_kernel(clips, with_own, *refs),
        grid=(1,),
        in_specs=[
            SCALARS,
            pl.BlockSpec((rows, 1), lambda *_: (half, 0)),
            pl.BlockSpec((clips, 2 * width), lambda *_: (0, 0)),
            full(b_qkv.shape),
            pl.BlockSpec((rows, LANES), lambda *_: (half, 0)),
            pl.BlockSpec((rows, LANES), lambda *_: (half, 0)),
            KEPT if with_own else ANYWHERE,
        ]
        + [full(v.shape) for v in blocks],
        out_specs=[full(out_shape[0].shape), KEPT] + [full(o.shape) for o in out_shape[2:]],
        out_shape=out_shape,
        scratch_shapes=[]
        if with_own
        else [pltpu.VMEM(w_qkv.shape, BF), pltpu.SemaphoreType.DMA((1 + 4 * width // 1024,))],
        compiler_params=params(),
        cost_estimate=cost(4 * rows * width * width, 6 * MIB),
    )(me, *all_in_hbm([clip_col, modulation, b_qkv, cosine, sine]), w_qkv if with_own else in_hbm(w_qkv), *all_in_hbm(blocks))


def contract_last(left, right):
    return lax.dot_general(left, right, (((1,), (1,)), ((), ())), preferred_element_type=F32)


def head_rows(value):
    lane = lax.broadcasted_iota(jnp.int32, value.shape, 1)
    zero = jnp.zeros_like(value)
    return jnp.concatenate(
        [jnp.where(lane < 64, value, zero), jnp.where(lane < 64, zero, value)], axis=0
    )


def head_diagonal(value):
    rows = value.shape[1] // 2
    return jnp.concatenate([value[:64, :rows], value[64:, rows:]], axis=0).T


def softmax_over_keys(keys, queries):
    scores = contract_last(keys, queries)
    expo = jnp.exp(scores - jnp.max(scores, axis=0, keepdims=True))
    return expo, 1.0 / jnp.sum(expo, axis=0, keepdims=True)


def attend_kernel(keymark_ref, rowmark_ref, q_ref, ka_ref, kb_ref, *refs):
    sources, o_ref, targets = refs[:3], refs[3], refs[4:7]
    keys, values, queries, sems = refs[7:]
    half = ka_ref.shape[1]
    pair, pairs = pl.program_id(0), pl.num_programs(0)

    def copies():
        return [
            pltpu.make_async_copy(source, target, sems.at[j])
            for j, (source, target) in enumerate(zip(sources, targets))
        ]

    @pl.when(pair == 0)
    def _():
        for copy in copies():
            copy.start()

    @pl.when(pair == pairs - 1)
    def _():
        for copy in copies():
            copy.wait()

    @pl.when(pair == 0)
    def _():
        keys[:, LANES:] = keymark_ref[...]
        marks = rowmark_ref[...]
        queries[:, LANES:] = jnp.concatenate([marks, marks], axis=0)

    keys[:half, :LANES] = ka_ref[pair]
    keys[half:, :LANES] = kb_ref[pair]
    values[:half] = ka_ref[pairs + pair]
    values[half:] = kb_ref[pairs + pair]
    queries[:, :LANES] = head_rows(q_ref[...])
    expo, inverse = softmax_over_keys(keys[...], queries[...])
    turned = jnp.dot(values[...].T, expo.astype(BF), preferred_element_type=F32) * inverse
    o_ref[...] = head_diagonal(turned).astype(BF)


def attend(q, kv_a, kv_b, marks, weights):
    own_rows, width = q.shape
    rows = 2 * kv_a.shape[1]
    return pl.pallas_call(
        attend_kernel,
        grid=(width // LANES,),
        in_specs=[
            pl.BlockSpec((rows, LANES), lambda p: (0, 0)),
            pl.BlockSpec((own_rows, LANES), lambda p: (0, 1)),
            pl.BlockSpec((own_rows, LANES), lambda p: (0, p)),
            KEPT,
            KEPT,
        ]
        + [ANYWHERE] * 3,
        out_specs=[pl.BlockSpec((own_rows, LANES), lambda p: (0, p))] + [KEPT] * 3,
        out_shape=[shape_of((own_rows, width))] + [pltpu.VMEM(w.shape, BF) for w in weights],
        scratch_shapes=[
            pltpu.VMEM((rows, 2 * LANES), BF),
            pltpu.VMEM((rows, LANES), BF),
            pltpu.VMEM((2 * own_rows, 2 * LANES), BF),
            pltpu.SemaphoreType.DMA((3,)),
        ],
        compiler_params=params(),
        cost_estimate=cost(4 * own_rows * rows * width, MIB),
    )(*all_in_hbm([marks, marks, q]), kv_a, kv_b, *all_in_hbm(weights))


def probs_kernel(me_ref, keyclip_ref, rowclip_ref, qa_ref, qb_ref, ka_ref, kb_ref, *refs):
    out_ref, keys = refs[-3], refs[-1]
    i, blocks = pl.program_id(0), pl.num_programs(0)
    half = ka_ref.shape[1]

    @pl.when(i == 0)
    def _():
        keys[:half] = ka_ref[0]
        keys[half:] = kb_ref[0]

    query = jnp.where(i < blocks // 2, qa_ref[...], qb_ref[...])
    visible = keyclip_ref[...] == rowclip_ref[...]
    visible = jnp.concatenate([visible, visible], axis=1)
    scores = jnp.where(visible, contract_last(keys[...], head_rows(query)), NEGATIVE)
    expo = jnp.exp(scores - jnp.max(scores, axis=0, keepdims=True))
    out_ref[...] = expo * (1.0 / jnp.sum(expo, axis=0, keepdims=True))


def heads_probs(me, q_a, q_b, kv_a, kv_b, clip_col, clip_row, blocks, earlier, passed):
    half = kv_a.shape[1]
    rows = 2 * half
    own_rows = rows // blocks
    halfway = blocks // 2
    grid_spec = pltpu.PrefetchScalarGridSpec(
        num_scalar_prefetch=1,
        grid=(blocks,),
        in_specs=[
            pl.BlockSpec((rows, 1), lambda i, m: (0, 0)),
            pl.BlockSpec((1, own_rows), lambda i, m: (0, i)),
            pl.BlockSpec((own_rows, LANES), lambda i, m: (jnp.minimum(i, halfway - 1), 0)),
            pl.BlockSpec((own_rows, LANES), lambda i, m: (jnp.maximum(i - halfway, 0), 0)),
            pl.BlockSpec((1, half, LANES), lambda i, m: (m[0], 0, 0)),
            pl.BlockSpec((1, half, LANES), lambda i, m: (m[0], 0, 0)),
        ]
        + [ANYWHERE] * 2,
        out_specs=[pl.BlockSpec((rows, 2 * own_rows), lambda i, m: (0, i)), ANYWHERE],
        scratch_shapes=[pltpu.VMEM((rows, LANES), BF)],
    )
    return pl.pallas_call(
        probs_kernel,
        grid_spec=grid_spec,
        out_shape=[shape_of((rows, 2 * rows), F32), shape_of(passed.shape, passed.dtype)],
        input_output_aliases={8: 1},
        compiler_params=params(),
        cost_estimate=cost(4 * rows * rows * LANES, 9 * MIB),
    )(me, *all_in_hbm([clip_col, clip_row, q_a, q_b]), *all_in_hbm([kv_a, kv_b, earlier, passed]))


def attend_back_kernel(
    me_ref, p_ref, qa_ref, qb_ref, ka_ref, kb_ref, va_ref, vb_ref, do_ref, cos_ref, sin_ref, *refs
):
    out_ref, sent_ref = refs[-8:-6]
    dk_ref, dv_ref, values, keys_turned, d_probs = refs[-5:]
    i, blocks = pl.program_id(0), pl.num_programs(0)
    rows = do_ref.shape[1]
    half = ka_ref.shape[1]
    me = me_ref[0]

    @pl.when(i == 0)
    def _():
        dk_ref[...] = jnp.zeros_like(dk_ref)
        dv_ref[...] = jnp.zeros_like(dv_ref)
        for at, key_ref, value_ref in ((0, ka_ref, va_ref), (half, kb_ref, vb_ref)):
            values[at : at + half] = value_ref[0]
            keys_turned[:, at : at + half] = key_ref[0].T

    query = jnp.where(i < blocks // 2, qa_ref[...], qb_ref[...])
    q_two, up_two = head_rows(query), head_rows(do_ref[0])
    delta = jnp.zeros((1, 2 * rows), F32)
    step = 256
    for start in range(0, 2 * half, step):
        part = slice(start, start + step)
        probs_low = p_ref[part, :].astype(BF)
        dv_ref[part, :] += dot_low(probs_low, up_two)
        products = contract_last(values[part, :], up_two)
        d_probs[part, :] = products
        delta += jnp.sum(probs_low.astype(F32) * products, axis=0, keepdims=True)
    d_query = jnp.zeros((LANES, 2 * rows), F32)
    for start in range(0, 2 * half, step):
        part = slice(start, start + step)
        ds = (p_ref[part, :] * (d_probs[part, :] - delta)).astype(BF)
        dk_ref[part, :] += dot_low(ds, q_two)
        d_query += dot_low(keys_turned[:, part], ds)
    lane = lax.broadcasted_iota(jnp.int32, (rows, LANES), 1)

    def turned_back(value, where):
        return (value * cos_ref[where, :] - half_swap(value, lane) * sin_ref[where, :]).astype(BF)

    here = pl.ds(pl.multiple_of(i * rows, rows), rows)
    dq = turned_back(head_diagonal(d_query) * 0.125, here)
    out_ref[here, 0:LANES] = dq
    sent_ref[me ^ offset_of(i, blocks), :, 0:LANES] = dq

    @pl.when(i == blocks - 1)
    def _():
        @pl.loop(0, blocks)
        def _(j):
            there = pl.ds(pl.multiple_of(j * rows, rows), rows)
            dk = turned_back(dk_ref[there, :], there)
            dv = dv_ref[there, :].astype(BF)
            out_ref[there, LANES : 2 * LANES] = dk
            out_ref[there, 2 * LANES : 3 * LANES] = dv
            owner = me ^ offset_of(j, blocks)
            sent_ref[owner, :, LANES : 2 * LANES] = dk
            sent_ref[owner, :, 2 * LANES : 3 * LANES] = dv


def attend_back(me, probs, q_a, q_b, kv_a, kv_b, d_o, cosine, sine, passed, earlier):
    half = kv_a.shape[1]
    rows = 2 * half
    pairs = kv_a.shape[0] // 2
    blocks, own_rows, _ = d_o.shape
    halfway = blocks // 2
    grid_spec = pltpu.PrefetchScalarGridSpec(
        num_scalar_prefetch=1,
        grid=(blocks,),
        in_specs=[
            pl.BlockSpec((rows, 2 * own_rows), lambda i, m: (0, i)),
            pl.BlockSpec((own_rows, LANES), lambda i, m: (jnp.minimum(i, halfway - 1), 0)),
            pl.BlockSpec((own_rows, LANES), lambda i, m: (jnp.maximum(i - halfway, 0), 0)),
            pl.BlockSpec((1, half, LANES), lambda i, m: (m[0], 0, 0)),
            pl.BlockSpec((1, half, LANES), lambda i, m: (m[0], 0, 0)),
            pl.BlockSpec((1, half, LANES), lambda i, m: (pairs + m[0], 0, 0)),
            pl.BlockSpec((1, half, LANES), lambda i, m: (pairs + m[0], 0, 0)),
            pl.BlockSpec((1, own_rows, LANES), lambda i, m: (m[0] ^ offset_of(i, blocks), 0, 0)),
            pl.BlockSpec((rows, LANES), lambda i, m: (0, 0)),
            pl.BlockSpec((rows, LANES), lambda i, m: (0, 0)),
            ANYWHERE,
        ]
        + [ANYWHERE] * len(earlier),
        out_specs=[
            pl.BlockSpec((rows, 3 * LANES), lambda i, m: (0, 0)),
            pl.BlockSpec((blocks, own_rows, 3 * LANES), lambda i, m: (0, 0, 0)),
            ANYWHERE,
        ],
        scratch_shapes=[
            pltpu.VMEM((rows, LANES), F32),
            pltpu.VMEM((rows, LANES), F32),
            pltpu.VMEM((rows, LANES), BF),
            pltpu.VMEM((LANES, rows), BF),
            pltpu.VMEM((rows, 2 * own_rows), F32),
        ],
    )
    return pl.pallas_call(
        attend_back_kernel,
        grid_spec=grid_spec,
        out_shape=[
            shape_of((rows, 3 * LANES)),
            shape_of((blocks, own_rows, 3 * LANES)),
            shape_of(passed.shape, passed.dtype),
        ],
        input_output_aliases={11: 2},
        compiler_params=params(),
        cost_estimate=cost(8 * rows * rows * LANES, 12 * MIB),
    )(
        me,
        *all_in_hbm([probs, q_a, q_b]),
        *all_in_hbm([kv_a, kv_b, kv_a, kv_b]),
        d_o,
        *all_in_hbm([cosine, sine, passed, *earlier]),
    )


def norm_parts(inputs):
    centred = inputs - jnp.mean(inputs, axis=-1, keepdims=True)
    rstd = lax.rsqrt(jnp.mean(centred * centred, axis=-1, keepdims=True) + 1e-06)
    return centred * rstd, rstd


def norm_back(normed, rstd, gradient):
    return rstd * (
        gradient
        - jnp.mean(gradient, axis=-1, keepdims=True)
        - normed * jnp.mean(gradient * normed, axis=-1, keepdims=True)
    )


def dot_low(left, right):
    return jnp.dot(left, right, preferred_element_type=F32)


def dot_rows(left, right):
    return lax.dot_general(left, right, (((0,), (0,)), ((), ())), preferred_element_type=F32)


def gelu_parts(hidden):
    square = hidden * hidden
    tanh = jnp.tanh(0.7978845608028654 * hidden * (1.0 + 0.044715 * square))
    upper = 0.5 * (1.0 + tanh)
    slope = upper + 0.5 * hidden * (1.0 - tanh * tanh) * (
        0.7978845608028654 * (1.0 + 3.0 * 0.044715 * square)
    )
    return hidden * upper, slope


def high_low(value):
    high = value.astype(BF)
    return high, (value - high.astype(F32)).astype(BF)


class RowSums:
    def __init__(self, clip_row, clips):
        self.place = lax.broadcasted_iota(jnp.int32, (8, clip_row.shape[1]), 0)
        self.member = ((self.place == clip_row) & (self.place < clips)).astype(F32).astype(BF)

    def by_clip(self, value):
        high, low = high_low(value)
        return dot_low(
            jnp.concatenate([self.member, self.member], axis=1),
            jnp.concatenate([high, low], axis=0),
        )

    def whole(self, value, row):
        return dot_low((self.place == row).astype(F32).astype(BF), value)


def middle_kernel(
    clips, steps_ref, clipc_ref, clipr_ref, x_ref, dy_ref, o_ref, mod_ref, bo_ref, bu_ref, bd_ref,
    wo, wu, wd, *refs,
):
    out_ref, h2_ref, dx_ref, da_ref, do_ref, sums_ref = refs[-6:]
    width = x_ref.shape[1]
    ffn = wu.shape[1]
    clip = clipc_ref[...]

    def frame_rows(index):
        return by_clip(clip, mod_ref[:, (index - 2) * width : (index - 1) * width], 0, clips)

    gate_one, scale_two, gate_two = frame_rows(2), 1.0 + frame_rows(4), frame_rows(5)
    upstream = dy_ref[...].astype(F32)
    d_ffn = (gate_two * upstream).astype(BF)
    attn_out = dot_low(o_ref[...], wo[...]) + bo_ref[...]
    middle = x_ref[...].astype(F32) + gate_one * attn_out
    normed, rstd = norm_parts(middle)
    second = (normed * scale_two + frame_rows(3)).astype(BF)
    h2_ref[...] = second
    sums = RowSums(clipr_ref[...], clips)
    ffn_out = jnp.zeros(x_ref.shape, F32)
    d_second = jnp.zeros(x_ref.shape, F32)
    step = 512
    up_sums = []
    for start in range(0, ffn, step):
        here = slice(start, start + step)
        activated, slope = gelu_parts(dot_low(second, wu[:, here]) + bu_ref[:, here])
        ffn_out += dot_low(activated.astype(BF), wd[here, :])
        d_hidden = (contract_last(d_ffn, wd[here, :]) * slope).astype(BF)
        d_second += contract_last(d_hidden, wu[:, here])
        up_sums.append(sums.whole(d_hidden, clips))
    ffn_out += bd_ref[...]
    out_ref[...] = (middle + gate_two * ffn_out).astype(BF)
    d_middle = upstream + norm_back(normed, rstd, d_second * scale_two)
    dx_ref[...] = d_middle
    d_attn = (gate_one * d_middle).astype(BF)
    da_ref[...] = d_attn
    d_o = contract_last(d_attn, wo[...]).astype(BF)
    for k in range(width // LANES):
        do_ref[k] = d_o[:, k * LANES : (k + 1) * LANES]
    up_sums = jnp.concatenate(up_sums, axis=1)
    place = lax.broadcasted_iota(jnp.int32, (8, width), 0)
    lane = lax.broadcasted_iota(jnp.int32, (8, width), 1)
    steps = jnp.zeros((8, width), F32)
    for c in range(clips):
        here = (place == clips + 1) & (lane == c)
        steps = jnp.where(here, steps_ref[0, c].astype(F32), steps)
    sums_ref[:, :width] = (
        sums.by_clip(d_middle * attn_out) + sums.whole(d_attn, clips) + steps
    )
    sums_ref[:, width : 2 * width] = sums.by_clip(d_second) + up_sums[:, :width]
    sums_ref[:, 2 * width : 3 * width] = sums.by_clip(d_second * normed) + up_sums[:, width:]
    sums_ref[:, 3 * width :] = sums.by_clip(upstream * ffn_out) + sums.whole(d_ffn, clips)


def middle_part(
    steps, clip_col, clip_row, frames, cotangent, attended, modulation, b_out, b_up, b_down,
    w_out, w_up, w_down, earlier,
):
    rows, width = frames.shape
    clips = modulation.shape[0]
    small = [
        clip_col, clip_row, frames, cotangent, attended, modulation, b_out, b_up, b_down
    ]
    out_shape = [
        shape_of((rows, width)),
        shape_of((rows, width)),
        shape_of((rows, width), F32),
        shape_of((rows, width)),
        shape_of((width // LANES, rows, LANES)),
        shape_of((8, 4 * width), F32),
    ]
    return pl.pallas_call(
        lambda *refs: middle_kernel(clips, *refs),
        grid=(1,),
        in_specs=[SCALARS, full((rows, 1)), full((1, rows))]
        + [full(v.shape) for v in small[2:]]
        + [KEPT] * 3
        + [ANYWHERE] * len(earlier),
        out_specs=[full(o.shape) for o in out_shape],
        out_shape=out_shape,
        compiler_params=params(),
        cost_estimate=cost(20 * rows * width * width, 3 * MIB),
    )(steps, *all_in_hbm(small), w_out, w_up, w_down, *all_in_hbm(earlier))


def last_kernel(clips, clipc_ref, clipr_ref, x_ref, mod_ref, dx_ref, d_ref, w_hbm, *refs):
    passed = (len(refs) - 5) // 2
    out_ref, sums_ref = refs[passed : passed + 2]
    d_all, w, sems = refs[-3:]
    width = x_ref.shape[1]
    parts = 3
    copies = [
        pltpu.make_async_copy(
            w_hbm.at[:, pl.ds(i * width, width)], w.at[:, pl.ds(i * width, width)], sems.at[i]
        )
        for i in range(parts)
    ]
    for copy in copies:
        copy.start()
    for k in range(d_ref.shape[0]):
        for i in range(3):
            at = i * width + k * LANES
            d_all[:, at : at + LANES] = d_ref[k, :, i * LANES : (i + 1) * LANES]
    normed, rstd = norm_parts(x_ref[...].astype(F32))
    scale = 1.0 + by_clip(clipc_ref[...], mod_ref[...], 0, clips)
    d_first = jnp.zeros(x_ref.shape, F32)
    for i in range(parts):
        copies[i].wait()
        here = slice(i * width, (i + 1) * width)
        d_first += contract_last(d_all[:, here], w[:, here])
    out_ref[...] = (dx_ref[...] + norm_back(normed, rstd, d_first * scale)).astype(BF)
    sums = RowSums(clipr_ref[...], clips)
    sums_ref[:, :width] = (
        sums.by_clip(d_first)
        + sums.whole(d_all[:, :width], clips)
        + sums.whole(d_all[:, width : 2 * width], clips + 1)
    )
    sums_ref[:, width:] = sums.by_clip(d_first * normed) + sums.whole(d_all[:, 2 * width :], clips)


def last_part(clip_col, clip_row, frames, modulation, d_middle, d_own, w_qkv, passed):
    rows, width = frames.shape
    clips = modulation.shape[0]
    return pl.pallas_call(
        lambda *refs: last_kernel(clips, *refs),
        grid=(1,),
        in_specs=[
            full((rows, 1)),
            full((1, rows)),
            full(frames.shape),
            pl.BlockSpec((clips, width), lambda *_: (0, 1)),
            full(d_middle.shape),
            full(d_own.shape),
        ]
        + [ANYWHERE] * (1 + len(passed)),
        out_specs=[full((rows, width)), full((8, 2 * width))] + [ANYWHERE] * len(passed),
        out_shape=[shape_of((rows, width)), shape_of((8, 2 * width), F32)]
        + [shape_of(v.shape, v.dtype) for v in passed],
        input_output_aliases={7 + i: 2 + i for i in range(len(passed))},
        scratch_shapes=[
            pltpu.VMEM((rows, 3 * width), BF),
            pltpu.VMEM(w_qkv.shape, BF),
            pltpu.SemaphoreType.DMA((3,)),
        ],
        compiler_params=params(),
        cost_estimate=cost(6 * rows * width * width, 2 * MIB),
    )(
        *all_in_hbm([clip_col, clip_row, frames, modulation, d_middle]),
        d_own,
        *all_in_hbm([w_qkv, *passed]),
    )


def half_rows(core, value, kept_ref, sent_refs, at, columns):
    half = value.shape[0] // 2
    low, high = value[:half], value[half:]
    here = slice(at, at + half)
    kept_ref[here, columns] = jnp.where(core == 0, low, high)
    sent = jnp.where(core == 0, high, low).astype(BF)
    wide = sent_refs[0].shape[1]
    for i, ref in enumerate(sent_refs):
        start, stop = max(columns.start, i * wide), min(columns.stop, (i + 1) * wide)
        if start < stop:
            ref[here, start - i * wide : stop - i * wide] = sent[
                :, start - columns.start : stop - columns.start
            ]


def weights_kernel(clips, count, who_ref, clip_ref, gate_ref, bu_ref, wu_hbm, wd_hbm, *refs):
    kept_ref, sent_ref, (up_sum, down_sum, wu, wd, sems) = refs[-9], refs[-8:-5], refs[-5:]
    ha_ref, hb_ref, d_ref, mine_ref, theirs_ref = refs[:5]
    blocks = refs[5 : 5 + count]
    seconds, upstreams = blocks[: len(blocks) // 2], blocks[len(blocks) // 2 :]
    me, core = who_ref[0], who_ref[1]
    rows, width = seconds[0].shape
    part = up_sum.shape[1]
    columns = d_ref.shape[1]
    half = ha_ref.shape[0]
    own = pl.ds(pl.multiple_of((me // 2) * part, part), part)
    copies = [
        pltpu.make_async_copy(wu_hbm.at[:, own], wu, sems.at[0]),
        pltpu.make_async_copy(wd_hbm.at[own, :], wd, sems.at[1]),
    ]
    for copy in copies:
        copy.start()
    shard = part // 2

    step = 2 * LANES
    for start in range(0, width, step):
        here = slice(start, start + step)
        value = dot_rows(ha_ref[:, here], d_ref[:half, :])
        value += dot_rows(hb_ref[:, here], d_ref[half:, :])
        for inner in range(0, step, LANES):
            half_rows(
                core, value[inner : inner + LANES], kept_ref, sent_ref, (start + inner) // 2,
                slice(0, columns),
            )

    left = jnp.concatenate([mine_ref[:, :width], theirs_ref[:, :width]], axis=0)
    right = jnp.concatenate([mine_ref[:, width:], theirs_ref[:, width:]], axis=0)
    at = columns + 2 * part
    for start in range(0, width, step):
        value = dot_rows(left[:, start : start + step], right)
        for inner in range(0, step, LANES):
            half_rows(
                core, value[inner : inner + LANES], kept_ref, sent_ref, (start + inner) // 2,
                slice(at, at + width // 2),
            )

    for copy in copies:
        copy.wait()
    up_weights, down_weights = wu[...], wd[...]
    for pair in range(len(seconds) // 2):
        here = slice(2 * pair * rows, 2 * (pair + 1) * rows)
        second = jnp.concatenate([r[...] for r in seconds[2 * pair : 2 * pair + 2]], axis=0)
        upstream = jnp.concatenate([r[...] for r in upstreams[2 * pair : 2 * pair + 2]], axis=0)
        gate = by_clip(clip_ref[here, :], gate_ref[...], 0, clips)
        d_ffn = (gate * upstream.astype(F32)).astype(BF)
        activated, slope = gelu_parts(dot_low(second, up_weights) + bu_ref[:, own])
        d_hidden = (contract_last(d_ffn, down_weights) * slope).astype(BF)
        up, down = dot_rows(second, d_hidden), dot_rows(activated.astype(BF), d_ffn)
        if pair == 0:
            up_sum[...] = up
            down_sum[...] = down
        else:
            up_sum[...] += up
            down_sum[...] += down
    for y in range(2):
        mine = slice(y * shard, (y + 1) * shard)
        at = columns + 2 * y * shard
        for k in range(width // LANES):
            half_rows(
                core, up_sum[k * LANES : (k + 1) * LANES, mine], kept_ref, sent_ref,
                k * LANES // 2, slice(at, at + shard),
            )
        for c in range(width // shard):
            half_rows(
                core, down_sum[mine, c * shard : (c + 1) * shard], kept_ref, sent_ref,
                c * shard // 2, slice(at + shard, at + 2 * shard),
            )


def weights_part(who, clip_col, modulation, b_up, w_up, w_down, h1_a, h1_b, d_qkv, outs, seconds, upstreams):
    width, ffn = w_up.shape
    count = 2 * len(seconds)
    part = 2 * ffn // count
    clips = modulation.shape[0]
    shape = (width // 2, d_qkv.shape[1] + 2 * part + width // 2)
    rows = d_qkv.shape[0]
    arrays = [h1_a, h1_b, d_qkv, *outs, *seconds, *upstreams]
    return pl.pallas_call(
        lambda *refs: weights_kernel(clips, count, *refs),
        grid=(1,),
        in_specs=[
            SCALARS,
            pl.BlockSpec((rows // 2, 1), lambda *_: (0, 0)),
            pl.BlockSpec((clips, width), lambda *_: (0, 3)),
            full(b_up.shape),
            ANYWHERE,
            ANYWHERE,
        ]
        + [full(v.shape) for v in arrays],
        out_specs=[full(shape)] + [full((shape[0], shape[1] // 3))] * 3,
        out_shape=[shape_of(shape, F32)] + [shape_of((shape[0], shape[1] // 3))] * 3,
        scratch_shapes=[
            pltpu.VMEM((width, part), F32),
            pltpu.VMEM((part, width), F32),
            pltpu.VMEM((width, part), BF),
            pltpu.VMEM((part, width), BF),
            pltpu.SemaphoreType.DMA((2,)),
        ],
        compiler_params=params(36),
        cost_estimate=cost(7 * rows * width * part, 10 * MIB),
    )(who, *all_in_hbm([clip_col, modulation, b_up, w_up, w_down, *arrays]))


def table_kernel(first, clips, place_ref, *refs):
    parts, refs = refs[:4], refs[4:]
    if first:
        silu_ref, w_ref = refs[:2]
        dw_ref, db_ref, out_ref, total, sums = refs[-5:]
    else:
        silu_ref, w_ref, cond_ref, pick_ref, earlier_ref, _, _ = refs[:7]
        dw_ref, db_ref, out_ref, total, sums = refs[7:]
    i = pl.program_id(0)

    @pl.when(i == 0)
    def _():
        total[...] = jnp.zeros_like(total) if first else earlier_ref[...]

    for j, part in enumerate(parts):
        value = part[...]
        valid = lax.broadcasted_iota(jnp.int32, value.shape, 0) < clips
        sums[pl.ds(pl.multiple_of((place_ref[0] ^ j) * 8, 8), 8), :] = jnp.where(valid, value, 0.0)
    high, low = high_low(sums[...])
    total[...] += contract_last(w_ref[...], jnp.concatenate([high, low], axis=0))
    silu = silu_ref[...]
    dw_ref[...] = dot_rows(
        jnp.concatenate([silu, silu], axis=0), jnp.concatenate([high, low], axis=0)
    )
    db_ref[...] = jnp.sum(sums[...], axis=0, keepdims=True)

    @pl.when(i == pl.num_programs(0) - 1)
    def _():
        if first:
            out_ref[...] = total[...]
        else:
            rows = high.shape[0]
            d_silu = total[:, :rows] + total[:, rows:]
            cond = cond_ref[...]
            gate = 1.0 / (1.0 + jnp.exp(-cond))
            d_cond = d_silu.T * (gate * (1.0 + cond * (1.0 - gate)))
            d_high, d_low = high_low(d_cond)
            lowest = (d_cond - d_high.astype(F32) - d_low.astype(F32)).astype(BF)
            pick = pick_ref[...].astype(BF)
            out_ref[...] = dot_rows(pick, d_high) + dot_rows(pick, d_low) + dot_rows(pick, lowest)


def table_part(place, sums, silu, w_mod, column, clips, rest=None, earlier=()):
    columns = sums[0].shape[1]
    width = w_mod.shape[0]
    all_columns = 6 * width
    rows, own = silu.shape
    tile = 1024
    skip = column // tile
    first = rest is None
    shapes = [
        shape_of((own, all_columns), F32),
        shape_of((1, all_columns), F32),
        shape_of((width, 2 * rows), F32),
    ]
    in_specs = [SCALARS] + [pl.BlockSpec((8, tile), lambda i: (0, i))] * 4 + [
        pl.BlockSpec((rows, own), lambda i: (0, 0)),
        pl.BlockSpec((width, tile), lambda i: (0, skip + i)),
    ]
    args = [place, *all_in_hbm([*sums, silu]), in_hbm(w_mod)]
    aliases = {}
    if first:
        in_specs += [ANYWHERE] * len(earlier)
        args += all_in_hbm(earlier)
    else:
        condition, pick, earlier, d_w, d_b = rest
        in_specs += [
            pl.BlockSpec((rows, width), lambda i: (0, 0)),
            pl.BlockSpec(pick.shape, lambda i: (0, 0)),
            pl.BlockSpec((width, 2 * rows), lambda i: (0, 0)),
            ANYWHERE,
            ANYWHERE,
        ]
        args += all_in_hbm([condition, pick, earlier, d_w, d_b])
        aliases = {10: 0, 11: 1}
        shapes[2] = shape_of((pick.shape[1], width), F32)
    return pl.pallas_call(
        lambda *refs: table_kernel(first, clips, *refs),
        grid=(columns // tile,),
        in_specs=in_specs,
        out_specs=[
            pl.BlockSpec((own, tile), lambda i: (0, skip + i)),
            pl.BlockSpec((1, tile), lambda i: (0, skip + i)),
            pl.BlockSpec(shapes[2].shape, lambda i: (0, 0)),
        ],
        out_shape=shapes,
        scratch_shapes=[
            pltpu.VMEM((width, 2 * rows), F32),
            pltpu.VMEM((rows, tile), F32),
        ],
        input_output_aliases=aliases,
        compiler_params=params(),
        cost_estimate=cost(rows * width, width),
    )(*args)


def in_order(bit, mine, other):
    return jnp.stack([jnp.where(bit == 0, mine, other), jnp.where(bit == 0, other, mine)])


def batch_parts(sums):
    return [sums] + [swapped_with(sums, "batch", k) for k in range(1, 4)]


def share_kernel(columns, part, who_ref, kept_ref, *refs):
    others = refs[:3]
    own_ref, x_ref, y_ref, both_ref, out_ref = refs[-5:]
    far, odd = who_ref[2] // 2 == 1, who_ref[0] % 2 == 1
    rows = own_ref.shape[1]
    first, second = slice(columns, columns + part), slice(columns + part, columns + 2 * part)
    for k in range(own_ref.shape[0]):
        here = slice(2 * k * rows, 2 * (k + 1) * rows)
        other = jnp.concatenate([ref[here, :] for ref in others], axis=1)
        value = kept_ref[here, :] + other.astype(F32)
        low, high = value[:rows], value[rows:]
        near, away = jnp.where(far, high, low), jnp.where(far, low, high)
        own_ref[k, :, :columns] = near[:, :columns]
        own_ref[k, :, columns:] = jnp.where(odd, near[:, second], near[:, first])
        y_ref[k] = jnp.where(odd, near[:, first], near[:, second]).astype(BF)
        x_ref[k, :, :columns] = away[:, :columns].astype(BF)
        x_ref[k, :, columns:] = jnp.where(odd, away[:, second], away[:, first]).astype(BF)
        both_ref[k] = jnp.where(odd, away[:, first], away[:, second]).astype(BF)
        out_ref[k] = jnp.concatenate(
            [low[:, columns + 2 * part :], high[:, columns + 2 * part :]], axis=1
        ).astype(BF)


def share(who, kept, others, count, columns, part):
    rows = kept.shape[0] // count // 2
    width = 2 * (kept.shape[1] - columns - 2 * part)
    shapes = [
        shape_of((count, rows, columns + part), F32),
        shape_of((count, rows, columns + part)),
        shape_of((count, rows, part)),
        shape_of((count, rows, part)),
        shape_of((count, rows, width)),
    ]
    return pl.pallas_call(
        lambda *refs: share_kernel(columns, part, *refs),
        grid=(1,),
        in_specs=[SCALARS, full(kept.shape)] + [full(v.shape) for v in others],
        out_specs=[full(v.shape) for v in shapes],
        out_shape=shapes,
        compiler_params=params(),
        cost_estimate=cost(0, 8 * MIB),
    )(who, in_hbm(kept), *others)


def gather_sums_kernel(columns, own_ref, x_ref, y_ref, both_ref, out_ref, *refs):
    sent_ref, down_ref = refs[-2:]
    count, rows, _ = own_ref.shape
    shard = y_ref.shape[2] // 2
    ready = columns + shard
    for k in range(count):
        from_x = x_ref[k].astype(F32)
        sent_ref[k, :, :columns] = (own_ref[k, :, :columns] + from_x[:, :columns]).astype(BF)
        value = (own_ref[k, :, columns:] + from_x[:, columns:]) + (
            y_ref[k].astype(F32) + both_ref[k].astype(F32)
        )
        sent_ref[k, :, columns:ready] = value[:, :shard].astype(BF)
        group, at = k % 2, k // 2 * shard
        down_ref[group * rows : (group + 1) * rows, at : at + shard] = value[:, shard:].astype(BF)
        sent_ref[k, :, ready:] = out_ref[k]


def gather_sums(own, from_x, from_y, from_both, out_parts, columns, passed):
    count, rows, _ = own.shape
    width = out_parts.shape[2]
    args = [own, from_x, from_y, from_both, out_parts]
    shapes = [
        shape_of((count, rows, columns + from_y.shape[2] // 2 + width)),
        shape_of((2 * rows, width)),
    ]
    return pl.pallas_call(
        lambda *refs: gather_sums_kernel(columns, *refs),
        grid=(1,),
        in_specs=[full(v.shape) for v in args] + [ANYWHERE] * len(passed),
        out_specs=[ANYWHERE] * len(passed) + [full(v.shape) for v in shapes],
        out_shape=[shape_of(v.shape, v.dtype) for v in passed] + shapes,
        input_output_aliases={5 + i: i for i in range(len(passed))},
        compiler_params=params(),
        cost_estimate=cost(0, 4 * MIB),
    )(in_hbm(own), from_x, from_y, from_both, *all_in_hbm([out_parts, *passed]))


def rows_kernel(columns, rows_ref, *refs):
    out_ref = refs[-1]
    count, rows, wide = rows_ref.shape
    width = out_ref.shape[1]
    shard = wide - width - columns
    total = jnp.zeros((rows, width), F32)
    for k in range(count):
        for i in range(columns // LANES):
            out_ref[i * rows : (i + 1) * rows, k * LANES : (k + 1) * LANES] = rows_ref[
                k, :, i * LANES : (i + 1) * LANES
            ]
        piece = columns // LANES + k * shard // width
        at = k * shard % width
        out_ref[piece * rows : (piece + 1) * rows, at : at + shard] = rows_ref[
            k, :, columns : columns + shard
        ]
        total += rows_ref[k, :, columns + shard :].astype(F32)
    piece = columns // LANES + count * shard // width
    out_ref[piece * rows :, :] = total.astype(BF)


def gather_rows(rows_mine, width, columns, passed, earlier):
    count, rows, wide = rows_mine.shape
    shard = wide - width - columns
    shape = ((columns // LANES + count * shard // width + 1) * rows, width)
    return pl.pallas_call(
        lambda *refs: rows_kernel(columns, *refs),
        grid=(1,),
        in_specs=[full(rows_mine.shape), ANYWHERE, ANYWHERE],
        out_specs=[ANYWHERE, full(shape)],
        out_shape=[shape_of(passed.shape, passed.dtype), shape_of(shape)],
        input_output_aliases={1: 0},
        compiler_params=params(),
        cost_estimate=cost(0, 2 * MIB),
    )(rows_mine, *all_in_hbm([passed, earlier]))


def assemble_kernel(ffn, who_ref, *refs):
    qkv_ref, out_ref, up_ref, down_ref = refs[-4:]
    width = out_ref.shape[1]
    rows = qkv_ref.shape[0] // 4
    for j, (ref, own_down) in enumerate(zip(refs[:4], refs[4:8])):
        owner = who_ref[2] ^ j
        core, far = owner % 2, owner // 2
        at = pl.multiple_of(core * 2 * rows + far * rows, rows)
        piece = 0
        for target, count in ((qkv_ref, 3), (up_ref, ffn // width)):
            for i in range(count):
                here = slice(piece * rows, (piece + 1) * rows)
                target[pl.ds(at, rows), i * width : (i + 1) * width] = ref[here, :].astype(F32)
                piece += 1
        for g in range(2):
            here = slice(g * rows, (g + 1) * rows)
            there = pl.multiple_of(core * 4 * rows + g * 2 * rows + far * rows, rows)
            down_ref[pl.ds(there, rows), :] = own_down[here, :].astype(F32)
        part = width // 2
        column = pl.multiple_of(far * part, part)
        for g in range(2):
            there = pl.multiple_of(core * 2 * rows + g * rows, rows)
            out_ref[pl.ds(there, rows), pl.ds(column, part)] = ref[
                piece * rows : (piece + 1) * rows, g * part : (g + 1) * part
            ].astype(F32)


def assemble(who, parts, own_rows, ffn):
    width = parts[0].shape[1]
    shapes = [
        shape_of((own_rows, 3 * width), F32),
        shape_of((own_rows, width), F32),
        shape_of((own_rows, ffn), F32),
        shape_of((2 * own_rows, width), F32),
    ]
    return pl.pallas_call(
        lambda *refs: assemble_kernel(ffn, *refs),
        grid=(1,),
        in_specs=[SCALARS] + [full(v.shape) for v in parts],
        out_specs=[full(o.shape) for o in shapes],
        out_shape=shapes,
        compiler_params=params(),
        cost_estimate=cost(0, 6 * MIB),
    )(who, *parts)


def heads_body(
    frames, step_table, clip_lengths, clip_steps, w_mod, b_mod, w_qkv, b_qkv, w_out, b_out,
    w_up, b_up, w_down, b_down, cotangent,
):
    own_rows, width = frames.shape
    ffn = w_up.shape[1]
    count = lax.axis_size("blk")
    me = lax.axis_index("blk")
    place = lax.axis_index("batch")
    core, far = place % 2, place // 2
    who = jnp.stack([me, core, place])
    clips = clip_lengths.shape[1]
    rows = own_rows * count

    head_size = width // HEADS
    half = head_size // 2
    lane = jnp.arange(LANES, dtype=jnp.int32)
    freqs = 10000.0 ** (-2.0 * (lane % half).astype(F32) / head_size)
    rows_of_table = jnp.arange(step_table.shape[0], dtype=jnp.int32)
    (
        modulation, silu_own, clip_col, clip_row, cosine, sine, marks, kept_qkv,
    ) = prepare(
        me[None], clip_lengths, clip_steps, step_table, freqs[None, :], w_mod, b_mod[None, :],
        [w_qkv], own_rows, count,
    )
    modulation_two = modulate(silu_own, w_mod, b_mod[None, :])
    evens, odds = gathered_blocks(frames, count, (modulation_two[0, 0] * 0.0).astype(BF))

    shared = (b_qkv[None, :], cosine, sine)
    first = (me[None], clip_col, modulation)
    h1_a, kv_a, q_a, q_own, later = project(0, evens, *first, kept_qkv, *shared, cotangent)
    upstreams = even_blocks(later, count)
    h1_b, kv_b, q_b = project(1, odds, *first, w_qkv, *shared)
    attended, kept_out, kept_up, kept_down = attend(
        q_own, kv_a, kv_b, marks, [w_out, w_up, w_down]
    )
    result, second, d_middle, d_attn, d_o, sums_two = middle_part(
        clip_steps, clip_col, clip_row, frames, cotangent, attended, modulation_two,
        b_out[None, :], b_up[None, :], b_down[None, :], kept_out, kept_up, kept_down,
        upstreams,
    )
    d_o = lax.all_to_all(d_o, "blk", 0, 0, tiled=True)
    seconds = even_blocks(second, count)
    probs, d_attn = heads_probs(
        me[None], q_a, q_b, kv_a, kv_b, clip_col, clip_row, count, d_middle, d_attn
    )
    sums_two = sums_two + swapped_with(sums_two, "blk", 1)
    sums_two = sums_two + swapped_with(sums_two, "blk", 2)

    wide = width // 2
    da_low, da_high = d_attn[:, :wide], d_attn[:, wide:]
    out_sent = jnp.concatenate([attended, jnp.where(far == 0, da_high, da_low)], axis=1)
    out_kept = jnp.concatenate([attended, jnp.where(far == 0, da_low, da_high)], axis=1)
    out_sent = swapped_with(out_sent, "batch", 2)

    d_qkv, d_qkv_sent, sums_two = attend_back(
        me[None], probs, q_a, q_b, kv_a, kv_b, d_o, cosine, sine, sums_two, seconds
    )
    d_own = lax.all_to_all(d_qkv_sent, "blk", 0, 0, tiled=True)
    kept, *sent = weights_part(
        who, clip_col, modulation_two, b_up[None, :], w_up, w_down, h1_a, h1_b, d_qkv,
        [out_kept, out_sent], seconds, upstreams,
    )
    own_sums, for_x, for_y, for_both, out_parts = share(
        who, kept, [swapped_with(v, "batch", 1) for v in sent], count, 3 * LANES, 2 * ffn // count
    )

    d_inputs, sums_one, own_sums, sums_two = last_part(
        clip_col, clip_row, frames, modulation, d_middle, d_own, w_qkv,
        [own_sums, sums_two],
    )
    sums_one = sums_one + swapped_with(sums_one, "blk", 2)
    sums_two = sums_two + swapped_with(sums_two, "blk", 4)

    pairs = [
        (b * count + k, (b ^ 2) * count + (k ^ 1)) for b in range(4) for k in range(count)
    ]
    sums_one, sums_two, sent, down_rows = gather_sums(
        own_sums,
        swapped_with(for_x, "batch", 2),
        swapped_with(for_y, "blk", 1),
        lax.ppermute(for_both, ("batch", "blk"), pairs),
        out_parts,
        3 * LANES,
        [sums_one, sums_two],
    )
    rows_mine = lax.all_to_all(sent, "blk", 0, 0, tiled=True)
    sums_one = sums_one + swapped_with(sums_one, "blk", 1)
    sums_two = batch_parts(sums_two)
    steps_all = jnp.stack([v[clips + 1, :clips] for v in sums_two]) * (1.0 / count)
    steps_all = steps_all[place ^ jnp.arange(4, dtype=jnp.int32)].astype(jnp.int32)
    pick_all = (steps_all[:, :, None] == rows_of_table[None, None, :]).astype(F32)
    pick_all = jnp.pad(pick_all, ((0, 0), (0, 8 - clips), (0, 0))).reshape(32, -1)
    condition_all = exact_dot(pick_all, step_table)
    silu_all = jax.nn.silu(condition_all).astype(BF)
    silu_cols = lax.dynamic_slice_in_dim(silu_all, me * own_rows, own_rows, 1)
    d_w_mod, d_b_mod, d_silu = table_part(
        place[None], sums_two, silu_cols, w_mod, 2 * width, clips
    )
    sums_one, mine = gather_rows(rows_mine, width, 3 * LANES, sums_one, d_silu)
    sums_one = batch_parts(sums_one + swapped_with(sums_one, "blk", 4))
    d_w_mod, d_b_mod, d_table = table_part(
        place[None], sums_one, silu_cols, w_mod, 0, clips,
        (condition_all, pick_all, d_silu, d_w_mod, d_b_mod),
    )

    def batch_total(parts):
        return (parts[0] + parts[1]) + (parts[2] + parts[3])

    bias_two = batch_total([v[clips] for v in sums_two])
    bias_one = batch_total([v[clips : clips + 2] for v in sums_one])
    d_b_qkv = jnp.concatenate(
        [bias_one[0, :width], bias_one[1, :width], bias_one[0, width:]], axis=0
    )
    d_b_out, d_b_up, d_b_down = jnp.split(bias_two, [width, width + ffn])

    def everyone(value):
        other = swapped_with(value, "batch", 2)
        return [value, swapped_with(value, "batch", 1), other, swapped_with(other, "batch", 1)]

    d_w_qkv, d_w_out, d_w_up, d_w_down = assemble(
        who, everyone(mine) + everyone(down_rows), own_rows, ffn
    )

    return (
        result,
        d_inputs,
        d_table,
        d_w_mod,
        d_b_mod[0],
        d_w_qkv,
        d_b_qkv,
        d_w_out,
        d_b_out,
        d_w_up,
        d_b_up,
        d_w_down,
        d_b_down,
    )


def solution(mesh):
    blk = mesh.shape["blk"]
    heads_fit = HEADS % (2 * blk) == 0 and mesh.shape["batch"] == 4
    chosen = heads_body if heads_fit else ring_body
    placed = (
        P(("batch", "blk"), None),
        P(),
        P("batch", None),
        P("batch", None),
        P(),
        P(),
        P(),
        P(),
        P(),
        P(),
        P(),
        P(),
        P(),
        P(),
        P(("batch", "blk"), None),
    )
    return jax.shard_map(
        chosen,
        mesh=mesh,
        in_specs=placed,
        out_specs=(
            P(("batch", "blk"), None),
            P(("batch", "blk"), None),
            P(),
            P("blk", None),
            P(),
            P("blk", None),
            P(),
            P("blk", None),
            P(),
            P("blk", None),
            P(),
            P("blk", None),
            P(),
        ),
        check_vma=False,
    )
```

```python
import jax
import jax.numpy as jnp
from jax import lax
from jax.experimental import pallas as pl
from jax.experimental.pallas import tpu as pltpu
from jax.sharding import PartitionSpec as P

HEADS = 16


HIGH_PRECISION = lax.Precision.HIGHEST
NEGATIVE = -1e30


def passed_along(value, axis, by):
    size = lax.axis_size(axis)
    return lax.ppermute(value, axis, [(i, (i + by) % size) for i in range(size)])


def norm_rows(inputs):
    average = jnp.mean(inputs, axis=-1, keepdims=True)
    centred = inputs - average
    variance = jnp.mean(centred * centred, axis=-1, keepdims=True)
    return centred * lax.rsqrt(variance + 1e-06)


def modulated(inputs, shift_part, scale_part):
    return norm_rows(inputs) * (1.0 + scale_part) + shift_part


def rotate(vectors, cosine, sine_part):
    half_size = vectors.shape[-1] // 2
    first_half = vectors[..., :half_size]
    second_half = vectors[..., half_size:]
    return jnp.concatenate(
        [
            first_half * cosine - second_half * sine_part,
            second_half * cosine + first_half * sine_part,
        ],
        axis=-1,
    )


def exact_dot(left_side, right_side):
    return jnp.dot(left_side, right_side, precision=HIGH_PRECISION)


def clip_index(positions, clip_ends):
    return jnp.sum((clip_ends[None, :] <= positions[:, None]).astype(jnp.int32), axis=1)


def attend_block(queries, key_rows, value_rows, visible, carry_state, scale):
    running_max, denominator, numerator = carry_state
    scores = (
        jnp.einsum("qhd,khd->hqk", queries, key_rows, preferred_element_type=jnp.float32) * scale
    )
    scores = jnp.where(visible[None], scores, NEGATIVE)
    new_max = jnp.maximum(running_max, jnp.max(scores, axis=-1))
    factor = jnp.exp(running_max - new_max)
    probabilities = jnp.where(visible[None], jnp.exp(scores - new_max[..., None]), 0.0)
    denominator = factor * denominator + jnp.sum(probabilities, axis=-1)
    numerator = numerator * jnp.transpose(factor)[:, :, None] + jnp.einsum(
        "hqk,khd->qhd",
        probabilities.astype(jnp.bfloat16),
        value_rows,
        preferred_element_type=jnp.float32,
    )
    return (new_max, denominator, numerator)


def grad_block(queries, upstream, log_total, row_delta, key_rows, value_rows, visible, scale):
    scores = (
        jnp.einsum("qhd,khd->hqk", queries, key_rows, preferred_element_type=jnp.float32) * scale
    )
    probabilities = jnp.where(
        visible[None],
        jnp.exp(jnp.where(visible[None], scores, NEGATIVE) - log_total[..., None]),
        0.0,
    )
    d_probs = jnp.einsum("qhd,khd->hqk", upstream, value_rows, preferred_element_type=jnp.float32)
    d_scores = (probabilities * (d_probs - row_delta[..., None])).astype(jnp.bfloat16)
    d_query = scale * jnp.einsum(
        "hqk,khd->qhd", d_scores, key_rows, preferred_element_type=jnp.float32
    )
    d_key = scale * jnp.einsum(
        "hqk,qhd->khd", d_scores, queries, preferred_element_type=jnp.float32
    )
    d_value = jnp.einsum(
        "hqk,qhd->khd",
        probabilities.astype(jnp.bfloat16),
        upstream,
        preferred_element_type=jnp.float32,
    )
    return (d_query, d_key, d_value)


def pass_key_grads(gradients):
    return (
        passed_along(gradients[0].astype(jnp.bfloat16), "blk", 1).astype(jnp.float32),
        passed_along(gradients[1].astype(jnp.bfloat16), "blk", 1).astype(jnp.float32),
    )


def ring_body(
    frames,
    step_table,
    clip_lengths,
    clip_steps,
    w_mod,
    b_mod,
    w_qkv,
    b_qkv,
    w_out,
    b_out,
    w_up,
    b_up,
    w_down,
    b_down,
    cotangent,
):
    frame_count, model_width = frames.shape
    ffn_width = w_up.shape[1]
    cycle_size = lax.axis_size("blk")
    cycle_place = lax.axis_index("blk")
    head_count = HEADS
    head_size = model_width // head_count
    scale = head_size ** (-0.5)
    lengths = clip_lengths[0]
    steps = clip_steps[0]
    clip_count = lengths.shape[0]
    clip_ends = jnp.cumsum(lengths)
    clip_starts = clip_ends - lengths
    local_rows = jnp.arange(frame_count, dtype=jnp.int32)
    places = cycle_place * frame_count + local_rows
    clip_own = clip_index(places, clip_ends)
    member = (clip_own[:, None] == jnp.arange(clip_count, dtype=jnp.int32)[None, :]).astype(
        jnp.float32
    )
    offsets = jnp.sum(member * clip_starts[None, :].astype(jnp.float32), axis=1)
    freqs = 10000.0 ** (-2.0 * jnp.arange(head_size // 2, dtype=jnp.float32) / head_size)
    angles = (places.astype(jnp.float32) - offsets)[:, None] * freqs[None, :]
    cosine = jnp.cos(angles)[:, None, :]
    sine_part = jnp.sin(angles)[:, None, :]

    def clip_of(turn_index):
        source = (cycle_place - turn_index) % cycle_size
        return clip_index(source * frame_count + local_rows, clip_ends)

    step_pick = (
        steps[:, None] == jnp.arange(step_table.shape[0], dtype=jnp.int32)[None, :]
    ).astype(jnp.float32)
    condition = exact_dot(step_pick, step_table)
    silu_low = jax.nn.silu(condition).astype(jnp.bfloat16)
    modulation = jnp.dot(silu_low, w_mod, preferred_element_type=jnp.float32) + b_mod
    frame_mod = exact_dot(member, modulation)
    shift_one, scale_one, gate_one, shift_two, scale_two, gate_two = jnp.split(frame_mod, 6, axis=1)
    inputs = frames.astype(jnp.float32)
    first, first_back = jax.vjp(modulated, inputs, shift_one, scale_one)
    first_low = first.astype(jnp.bfloat16)
    projected = jnp.dot(first_low, w_qkv, preferred_element_type=jnp.float32) + b_qkv
    query_part, key_part, value_part = jnp.split(projected, 3, axis=1)

    def spin(query_lin, key_lin):
        return (
            rotate(query_lin.reshape(frame_count, head_count, head_size), cosine, sine_part),
            rotate(key_lin.reshape(frame_count, head_count, head_size), cosine, sine_part),
        )

    (query_rot, key_rot), spin_back = jax.vjp(spin, query_part, key_part)
    queries = query_rot.astype(jnp.bfloat16)
    key_rows = key_rot.astype(jnp.bfloat16)
    value_rows = value_part.reshape(frame_count, head_count, head_size).astype(jnp.bfloat16)

    def forward_step(turn_index, key_value, carry_state):
        visible = clip_own[:, None] == clip_of(turn_index)[None, :]
        return attend_block(queries, key_value[0], key_value[1], visible, carry_state, scale)

    def forward_turn(turn_index, carry):
        key_value, carry_state = carry
        carry_state = forward_step(turn_index, key_value, carry_state)
        key_value = passed_along((key_value[0], key_value[1]), "blk", 1)
        return (key_value, carry_state)

    initial = (
        jnp.full((head_count, frame_count), NEGATIVE, jnp.float32),
        jnp.zeros((head_count, frame_count), jnp.float32),
        jnp.zeros((frame_count, head_count, head_size), jnp.float32),
    )
    key_value, carry_state = lax.fori_loop(
        0, cycle_size - 1, forward_turn, ((key_rows, value_rows), initial)
    )
    running_max, denominator, numerator = forward_step(cycle_size - 1, key_value, carry_state)
    attended = numerator / jnp.transpose(denominator)[:, :, None]
    log_total = running_max + jnp.log(denominator)
    attended_low = attended.reshape(frame_count, model_width).astype(jnp.bfloat16)
    attn_out = jnp.dot(attended_low, w_out, preferred_element_type=jnp.float32) + b_out
    middle = inputs + gate_one * attn_out
    second, second_back = jax.vjp(modulated, middle, shift_two, scale_two)
    second_low = second.astype(jnp.bfloat16)
    hidden = jnp.dot(second_low, w_up, preferred_element_type=jnp.float32) + b_up
    activated, gelu_back = jax.vjp(
        lambda values_in: jax.nn.gelu(values_in, approximate=True), hidden
    )
    activated_low = activated.astype(jnp.bfloat16)
    ffn_out = jnp.dot(activated_low, w_down, preferred_element_type=jnp.float32) + b_down
    result = middle + gate_two * ffn_out
    upstream_y = cotangent.astype(jnp.float32)
    d_ffn = (gate_two * upstream_y).astype(jnp.bfloat16)
    d_gate_two = upstream_y * ffn_out
    d_act = jnp.dot(d_ffn, w_down.T, preferred_element_type=jnp.float32)
    d_hidden = gelu_back(d_act)[0].astype(jnp.bfloat16)
    d_second = jnp.dot(d_hidden, w_up.T, preferred_element_type=jnp.float32)
    d_middle_norm, d_shift_two, d_scale_two = second_back(d_second)
    d_middle = upstream_y + d_middle_norm
    d_attn = (gate_one * d_middle).astype(jnp.bfloat16)
    d_gate_one = d_middle * attn_out
    d_attended = jnp.dot(d_attn, w_out.T, preferred_element_type=jnp.float32).astype(jnp.bfloat16)
    d_attended = d_attended.reshape(frame_count, head_count, head_size)
    row_delta = jnp.transpose(jnp.sum(d_attended.astype(jnp.float32) * attended, axis=-1))
    zeros_three = jnp.zeros((frame_count, head_count, head_size), jnp.float32)

    def key_step(turn_index, key_value, owed):
        visible = clip_own[:, None] == clip_of(turn_index)[None, :]
        d_query, d_key, d_value = grad_block(
            queries, d_attended, log_total, row_delta, key_value[0], key_value[1], visible, scale
        )
        return (owed[0] + d_query, (owed[1][0] + d_key, owed[1][1] + d_value))

    def key_turn(turn_index, carry):
        key_value, owed = carry
        d_query_sum, gradients = key_step(turn_index, key_value, owed)
        key_value = passed_along((key_value[0], key_value[1]), "blk", 1)
        gradients = pass_key_grads(gradients)
        return (key_value, (d_query_sum, gradients))

    key_value, owed = lax.fori_loop(
        0,
        cycle_size - 1,
        key_turn,
        ((key_rows, value_rows), (zeros_three, (zeros_three, zeros_three))),
    )
    d_query_rot, gradients = key_step(cycle_size - 1, key_value, owed)
    d_key_rot, d_value_all = pass_key_grads(gradients)
    d_query_lin, d_key_lin = spin_back((d_query_rot, d_key_rot))
    d_projected = jnp.concatenate(
        [d_query_lin, d_key_lin, d_value_all.reshape(frame_count, model_width)], axis=1
    ).astype(jnp.bfloat16)
    d_first = jnp.dot(d_projected, w_qkv.T, preferred_element_type=jnp.float32)
    d_input_norm, d_shift_one, d_scale_one = first_back(d_first)
    d_inputs = d_middle + d_input_norm
    d_frame_mod = jnp.concatenate(
        [d_shift_one, d_scale_one, d_gate_one, d_shift_two, d_scale_two, d_gate_two], axis=1
    )
    d_modulation = exact_dot(member.T, d_frame_mod)
    d_silu = jnp.dot(d_modulation, w_mod.T, precision=HIGH_PRECISION)
    d_condition = jax.vjp(jax.nn.silu, condition)[1](d_silu)[0]
    d_table_local = exact_dot(step_pick.T, d_condition)
    small = lax.psum(
        (
            jnp.sum(d_modulation, axis=0),
            jnp.sum(d_projected.astype(jnp.float32), axis=0),
            jnp.sum(d_attn.astype(jnp.float32), axis=0),
            jnp.sum(d_hidden.astype(jnp.float32), axis=0),
            jnp.sum(d_ffn.astype(jnp.float32), axis=0),
            d_table_local,
        ),
        ("batch", "blk"),
    )
    d_b_mod, d_b_qkv, d_b_out, d_b_up, d_b_down, d_table = small
    blocks_list = [
        jnp.dot(first_low.T, d_projected, preferred_element_type=jnp.float32),
        jnp.dot(attended_low.T, d_attn, preferred_element_type=jnp.float32),
        jnp.dot(second_low.T, d_hidden, preferred_element_type=jnp.float32),
    ]
    blocks_list.append(exact_dot(silu_low.T.astype(jnp.float32), d_modulation))
    wide_rows = lax.psum_scatter(
        jnp.concatenate(blocks_list, axis=1), "blk", scatter_dimension=0, tiled=True
    )
    down_part = lax.psum_scatter(
        jnp.dot(activated_low.T, d_ffn, preferred_element_type=jnp.float32),
        "blk",
        scatter_dimension=0,
        tiled=True,
    )
    wide_rows, down_part = (
        lax.psum(wide_rows.astype(jnp.bfloat16), "batch").astype(jnp.float32),
        lax.psum(down_part.astype(jnp.bfloat16), "batch").astype(jnp.float32),
    )
    qkv_end = 3 * model_width
    out_end = qkv_end + model_width
    up_end = out_end + ffn_width
    return (
        result.astype(jnp.bfloat16),
        d_inputs.astype(jnp.bfloat16),
        d_table,
        wide_rows[:, up_end:],
        d_b_mod,
        wide_rows[:, :qkv_end],
        d_b_qkv,
        wide_rows[:, qkv_end:out_end],
        d_b_out,
        wide_rows[:, out_end:up_end],
        d_b_up,
        down_part,
        d_b_down,
    )


BF = jnp.bfloat16
F32 = jnp.float32
LANES = 128
MIB = 1024 * 1024


def swapped_with(value, axis, offset):
    size = lax.axis_size(axis)
    return lax.ppermute(value, axis, [(i, i ^ offset) for i in range(size)])


def even_blocks(value, count):
    return [value] + [swapped_with(value, "blk", k) for k in range(2, count, 2)]


def gathered_blocks(value, count, zero):
    evens = even_blocks(value, count)
    return evens, [swapped_with(e, "blk", 1) for e in evens[:1]] + [
        swapped_with(e + zero, "blk", 1) for e in evens[1:]
    ]


def offset_of(index, count):
    return (2 * index) % count + (2 * index) // count


def after(value, *others):
    return lax.optimization_barrier((value,) + others)[0]


def half_swap(value, lane):
    return jnp.where((lane % 64) < 32, pltpu.roll(value, 96, 1), pltpu.roll(value, 32, 1))


def by_clip(clip, table, first, count):
    chosen = table[first : first + 1, :]
    for c in range(1, count):
        chosen = jnp.where(clip == c, table[first + c : first + c + 1, :], chosen)
    return chosen


def full(shape):
    return pl.BlockSpec(shape, lambda *_: (0,) * len(shape))


ANYWHERE = pl.BlockSpec(memory_space=pl.ANY)
SCALARS = pl.BlockSpec(memory_space=pltpu.SMEM)


KEPT = pl.BlockSpec(memory_space=pltpu.VMEM)


def in_hbm(value):
    if value.size * value.dtype.itemsize < 140000:
        return value
    return pltpu.with_memory_space_constraint(value, pltpu.HBM)


def all_in_hbm(values):
    return [in_hbm(v) for v in values]


def shape_of(shape, dtype=BF):
    size = jnp.dtype(dtype).itemsize
    for n in shape:
        size *= n
    return jax.ShapeDtypeStruct(shape, dtype) if size < 140000 else pltpu.HBM(shape, dtype)


def params(mib=24):
    return pltpu.CompilerParams(vmem_limit_bytes=mib * MIB)


def cost(flops, moved):
    return pl.CostEstimate(flops=flops, bytes_accessed=moved, transcendentals=0)


def prepare_kernel(
    count, me_ref, lengths_ref, steps_ref, table_ref, freq_ref, w_ref, b_ref, *refs
):
    silu, sems = refs[-2:]
    kept = (len(refs) - 9) // 2
    sources, targets = refs[:kept], refs[-2 - kept : -2]
    out_ref, silu_ref, clip_ref, cliprow_ref, cos_ref, sin_ref, marks_ref = refs[kept : kept + 7]
    clips = lengths_ref.shape[1]
    rows = cos_ref.shape[0] // count
    i = pl.program_id(0)

    def copies():
        return [
            pltpu.make_async_copy(
                source.at[:, pl.ds(0, target.shape[1])], target, sems.at[j]
            )
            for j, (source, target) in enumerate(zip(sources, targets))
        ]

    @pl.when(i == 0)
    def _():
        for copy in copies():
            copy.start()
        for c in range(clips):
            row = table_ref[pl.ds(steps_ref[0, c], 1), :]
            silu[c : c + 1, :] = row / (1.0 + jnp.exp(-row))
        silu_ref[...] = silu[:clips, :].astype(BF)

    out_ref[...] = dot_low(silu[...].astype(BF), w_ref[...])[:clips] + b_ref[...]

    @pl.when(i == 0)
    def _():
        def clip_and_start(places):
            clip, start, end = jnp.zeros_like(places), jnp.zeros_like(places), 0
            for c in range(clips):
                end = end + lengths_ref[0, c]
                clip = jnp.where(places >= end, c + 1, clip)
                start = jnp.where(places >= end, end, start)
            return clip, start

        for j in range(count):
            first = (me_ref[0] ^ offset_of(j, count)) * rows
            here = slice(j * rows, (j + 1) * rows)
            places = first + lax.broadcasted_iota(jnp.int32, (rows, LANES), 0)
            lane = lax.broadcasted_iota(jnp.int32, (rows, LANES), 1)
            clip, start = clip_and_start(places)
            angles = (places - start).astype(F32) * freq_ref[...]
            cos_ref[here, :] = jnp.cos(angles)
            sine = jnp.sin(angles)
            sin_ref[here, :] = jnp.where((lane % 64) < 32, -sine, sine)
            clip_ref[here, :] = clip[:, :1]
            places = first + lax.broadcasted_iota(jnp.int32, (1, rows), 1)
            cliprow_ref[:, here] = clip_and_start(places)[0]
            other = jnp.where((clip != lane) & (lane < clips), NEGATIVE, 0.0)
            marks_ref[here, :LANES] = other.astype(BF)
            marks_ref[here, LANES:] = jnp.where(clip == lane, 1.0, 0.0).astype(BF)

    @pl.when(i == pl.num_programs(0) - 1)
    def _():
        for copy in copies():
            copy.wait()


def prepare(me, lengths, steps, step_table, freqs, w_mod, b_mod, weights, own_rows, count):
    width = w_mod.shape[0]
    clips = lengths.shape[1]
    tile = width
    rows = own_rows * count
    shapes = [
        shape_of((clips, 2 * width), F32),
        shape_of((clips, width)),
        shape_of((rows, 1), jnp.int32),
        shape_of((1, rows), jnp.int32),
        shape_of((rows, LANES), F32),
        shape_of((rows, LANES), F32),
        shape_of((rows, 2 * LANES)),
    ]
    return pl.pallas_call(
        lambda *refs: prepare_kernel(count, *refs),
        grid=(2,),
        in_specs=[SCALARS] * 3
        + [
            full(step_table.shape),
            full(freqs.shape),
            pl.BlockSpec((width, tile), lambda i: (0, i)),
            pl.BlockSpec((1, tile), lambda i: (0, i)),
        ]
        + [ANYWHERE] * len(weights),
        out_specs=[pl.BlockSpec((clips, tile), lambda i: (0, i))]
        + [full(v.shape) for v in shapes[1:]]
        + [KEPT] * len(weights),
        out_shape=shapes + [pltpu.VMEM(w.shape, w.dtype) for w in weights],
        scratch_shapes=[pltpu.VMEM((8, width), F32), pltpu.SemaphoreType.DMA((len(weights),))],
        compiler_params=params(),
        cost_estimate=cost(4 * clips * width * width, 5 * width * width),
    )(me, lengths, steps, *all_in_hbm([step_table, freqs, w_mod, b_mod, *weights]))


def modulate_kernel(silu_ref, w_ref, b_ref, out_ref):
    out_ref[...] = dot_low(silu_ref[...], w_ref[...]) + b_ref[...]


def modulate(silu, w_mod, b_mod):
    clips, width = silu.shape
    return pl.pallas_call(
        modulate_kernel,
        grid=(4,),
        in_specs=[
            full(silu.shape),
            pl.BlockSpec((width, width), lambda i: (0, 2 + i)),
            pl.BlockSpec((1, width), lambda i: (0, 2 + i)),
        ],
        out_specs=pl.BlockSpec((clips, width), lambda i: (0, i)),
        out_shape=shape_of((clips, 4 * width), F32),
        compiler_params=params(),
        cost_estimate=cost(8 * clips * width * width, 8 * width * width),
    )(*all_in_hbm([silu, w_mod, b_mod]))


def project_kernel(clips, with_own, me_ref, clip_ref, mod_ref, b_ref, cos_ref, sin_ref, w, *refs):
    copies = []
    if not with_own:
        source, (w, sems), refs = w, refs[-2:], refs[:-2]
        width, step = source.shape[0], 512
        column = pl.ds(pl.multiple_of(me_ref[0] * LANES, LANES), LANES)
        copies = [pltpu.make_async_copy(source.at[:, column], w.at[:, pl.ds(0, LANES)], sems.at[0])]
        for i, start in enumerate(range(width, 3 * width, step)):
            here = pl.ds(start, step)
            copies.append(
                pltpu.make_async_copy(source.at[:, here], w.at[:, here], sems.at[1 + i])
            )
        for copy in copies:
            copy.start()
    blocks = refs[: len(refs) - (5 if with_own else 3)]
    h_ref, kv_ref, q_ref = refs[len(blocks) : len(blocks) + 3]
    rows, width = blocks[0].shape
    column = pl.multiple_of(me_ref[0] * LANES, LANES)
    if with_own:
        own_ref, passed_ref = refs[-2:]
        passed_ref[...] = blocks[-1][...]
        blocks = blocks[:-1]

    mod = mod_ref[...]
    for pair in range(len(blocks) // 2):
        here = slice(2 * pair * rows, 2 * (pair + 1) * rows)
        x = jnp.concatenate([blocks[2 * pair][...], blocks[2 * pair + 1][...]], axis=0).astype(F32)
        normed, _ = norm_parts(x)
        clip = clip_ref[here, :]
        scale = by_clip(clip, mod[:, width:], 0, clips)
        h_ref[here, :] = (normed * (1.0 + scale) + by_clip(clip, mod[:, :width], 0, clips)).astype(BF)

    h = h_ref[...]
    cosine, sine = cos_ref[...], sin_ref[...]
    lane = lax.broadcasted_iota(jnp.int32, cosine.shape, 1)

    def turned(piece, some):
        return piece * cosine[:some] + half_swap(piece, lane[:some]) * sine[:some]

    if with_own:
        heads = w[:, pl.ds(column, LANES)]
    else:
        copies[0].wait()
        heads = w[:, :LANES]
    part = dot_low(h, heads) + b_ref[:, pl.ds(column, LANES)]
    q_ref[...] = (turned(part, h.shape[0]) * 0.125).astype(BF)
    step = 2 * LANES
    for start in range(0 if with_own else width, 3 * width, step):
        some = rows if start < width else h.shape[0]
        if copies and (start - width) % 512 == 0:
            copies[1 + (start - width) // 512].wait()
        part = dot_low(h[:some], w[:, start : start + step]) + b_ref[:, start : start + step]
        for inner in range(0, step, LANES):
            piece = part[:, inner : inner + LANES]
            at = start + inner
            if start < 2 * width:
                piece = turned(piece, some)
            if start < width:
                own_ref[:, at : at + LANES] = (piece * 0.125).astype(BF)
            else:
                kv_ref[(at - width) // LANES] = piece.astype(BF)


def project(half, blocks, me, clip_col, modulation, w_qkv, b_qkv, cosine, sine, passed=None):
    with_own = passed is not None
    own_rows, width = blocks[0].shape
    rows = own_rows * len(blocks)
    clips = modulation.shape[0]
    out_shape = [
        shape_of((rows, width)),
        pltpu.VMEM((2 * width // LANES, rows, LANES), BF),
        shape_of((rows, LANES)),
    ]
    if with_own:
        out_shape += [shape_of((own_rows, width)), shape_of(passed.shape)]
        blocks = blocks + [passed]
    return pl.pallas_call(
        lambda *refs: project_kernel(clips, with_own, *refs),
        grid=(1,),
        in_specs=[
            SCALARS,
            pl.BlockSpec((rows, 1), lambda *_: (half, 0)),
            pl.BlockSpec((clips, 2 * width), lambda *_: (0, 0)),
            full(b_qkv.shape),
            pl.BlockSpec((rows, LANES), lambda *_: (half, 0)),
            pl.BlockSpec((rows, LANES), lambda *_: (half, 0)),
            KEPT if with_own else ANYWHERE,
        ]
        + [full(v.shape) for v in blocks],
        out_specs=[full(out_shape[0].shape), KEPT] + [full(o.shape) for o in out_shape[2:]],
        out_shape=out_shape,
        scratch_shapes=[]
        if with_own
        else [pltpu.VMEM(w_qkv.shape, BF), pltpu.SemaphoreType.DMA((1 + 4 * width // 1024,))],
        compiler_params=params(),
        cost_estimate=cost(4 * rows * width * width, 6 * MIB),
    )(me, *all_in_hbm([clip_col, modulation, b_qkv, cosine, sine]), w_qkv if with_own else in_hbm(w_qkv), *all_in_hbm(blocks))


def contract_last(left, right):
    return lax.dot_general(left, right, (((1,), (1,)), ((), ())), preferred_element_type=F32)


def head_rows(value):
    lane = lax.broadcasted_iota(jnp.int32, value.shape, 1)
    zero = jnp.zeros_like(value)
    return jnp.concatenate(
        [jnp.where(lane < 64, value, zero), jnp.where(lane < 64, zero, value)], axis=0
    )


def head_diagonal(value):
    rows = value.shape[1] // 2
    return jnp.concatenate([value[:64, :rows], value[64:, rows:]], axis=0).T


def softmax_over_keys(keys, queries):
    scores = contract_last(keys, queries)
    expo = jnp.exp(scores - jnp.max(scores, axis=0, keepdims=True))
    return expo, 1.0 / jnp.sum(expo, axis=0, keepdims=True)


def attend_kernel(keymark_ref, rowmark_ref, q_ref, ka_ref, kb_ref, *refs):
    sources, o_ref, targets = refs[:3], refs[3], refs[4:7]
    keys, values, queries, sems = refs[7:]
    half = ka_ref.shape[1]
    pair, pairs = pl.program_id(0), pl.num_programs(0)

    def copies():
        return [
            pltpu.make_async_copy(source, target, sems.at[j])
            for j, (source, target) in enumerate(zip(sources, targets))
        ]

    @pl.when(pair == 0)
    def _():
        for copy in copies():
            copy.start()

    @pl.when(pair == pairs - 1)
    def _():
        for copy in copies():
            copy.wait()

    @pl.when(pair == 0)
    def _():
        keys[:, LANES:] = keymark_ref[...]
        marks = rowmark_ref[...]
        queries[:, LANES:] = jnp.concatenate([marks, marks], axis=0)

    keys[:half, :LANES] = ka_ref[pair]
    keys[half:, :LANES] = kb_ref[pair]
    values[:half] = ka_ref[pairs + pair]
    values[half:] = kb_ref[pairs + pair]
    queries[:, :LANES] = head_rows(q_ref[...])
    expo, inverse = softmax_over_keys(keys[...], queries[...])
    turned = jnp.dot(values[...].T, expo.astype(BF), preferred_element_type=F32) * inverse
    o_ref[...] = head_diagonal(turned).astype(BF)


def attend(q, kv_a, kv_b, marks, weights):
    own_rows, width = q.shape
    rows = 2 * kv_a.shape[1]
    return pl.pallas_call(
        attend_kernel,
        grid=(width // LANES,),
        in_specs=[
            pl.BlockSpec((rows, LANES), lambda p: (0, 0)),
            pl.BlockSpec((own_rows, LANES), lambda p: (0, 1)),
            pl.BlockSpec((own_rows, LANES), lambda p: (0, p)),
            KEPT,
            KEPT,
        ]
        + [ANYWHERE] * 3,
        out_specs=[pl.BlockSpec((own_rows, LANES), lambda p: (0, p))] + [KEPT] * 3,
        out_shape=[shape_of((own_rows, width))] + [pltpu.VMEM(w.shape, BF) for w in weights],
        scratch_shapes=[
            pltpu.VMEM((rows, 2 * LANES), BF),
            pltpu.VMEM((rows, LANES), BF),
            pltpu.VMEM((2 * own_rows, 2 * LANES), BF),
            pltpu.SemaphoreType.DMA((3,)),
        ],
        compiler_params=params(),
        cost_estimate=cost(4 * own_rows * rows * width, MIB),
    )(*all_in_hbm([marks, marks, q]), kv_a, kv_b, *all_in_hbm(weights))


def probs_kernel(me_ref, keyclip_ref, rowclip_ref, qa_ref, qb_ref, ka_ref, kb_ref, *refs):
    out_ref, keys = refs[-3], refs[-1]
    i, blocks = pl.program_id(0), pl.num_programs(0)
    half = ka_ref.shape[1]

    @pl.when(i == 0)
    def _():
        keys[:half] = ka_ref[0]
        keys[half:] = kb_ref[0]

    query = jnp.where(i < blocks // 2, qa_ref[...], qb_ref[...])
    visible = keyclip_ref[...] == rowclip_ref[...]
    visible = jnp.concatenate([visible, visible], axis=1)
    scores = jnp.where(visible, contract_last(keys[...], head_rows(query)), NEGATIVE)
    expo = jnp.exp(scores - jnp.max(scores, axis=0, keepdims=True))
    out_ref[...] = expo * (1.0 / jnp.sum(expo, axis=0, keepdims=True))


def heads_probs(me, q_a, q_b, kv_a, kv_b, clip_col, clip_row, blocks, earlier, passed):
    half = kv_a.shape[1]
    rows = 2 * half
    own_rows = rows // blocks
    halfway = blocks // 2
    grid_spec = pltpu.PrefetchScalarGridSpec(
        num_scalar_prefetch=1,
        grid=(blocks,),
        in_specs=[
            pl.BlockSpec((rows, 1), lambda i, m: (0, 0)),
            pl.BlockSpec((1, own_rows), lambda i, m: (0, i)),
            pl.BlockSpec((own_rows, LANES), lambda i, m: (jnp.minimum(i, halfway - 1), 0)),
            pl.BlockSpec((own_rows, LANES), lambda i, m: (jnp.maximum(i - halfway, 0), 0)),
            pl.BlockSpec((1, half, LANES), lambda i, m: (m[0], 0, 0)),
            pl.BlockSpec((1, half, LANES), lambda i, m: (m[0], 0, 0)),
        ]
        + [ANYWHERE] * 2,
        out_specs=[pl.BlockSpec((rows, 2 * own_rows), lambda i, m: (0, i)), ANYWHERE],
        scratch_shapes=[pltpu.VMEM((rows, LANES), BF)],
    )
    return pl.pallas_call(
        probs_kernel,
        grid_spec=grid_spec,
        out_shape=[shape_of((rows, 2 * rows), F32), shape_of(passed.shape, passed.dtype)],
        input_output_aliases={8: 1},
        compiler_params=params(),
        cost_estimate=cost(4 * rows * rows * LANES, 9 * MIB),
    )(me, *all_in_hbm([clip_col, clip_row, q_a, q_b]), *all_in_hbm([kv_a, kv_b, earlier, passed]))


def attend_back_kernel(
    me_ref, p_ref, qa_ref, qb_ref, ka_ref, kb_ref, va_ref, vb_ref, do_ref, cos_ref, sin_ref, *refs
):
    out_ref, sent_ref = refs[-8:-6]
    dk_ref, dv_ref, values, keys_turned, d_probs = refs[-5:]
    i, blocks = pl.program_id(0), pl.num_programs(0)
    rows = do_ref.shape[1]
    half = ka_ref.shape[1]
    me = me_ref[0]

    @pl.when(i == 0)
    def _():
        dk_ref[...] = jnp.zeros_like(dk_ref)
        dv_ref[...] = jnp.zeros_like(dv_ref)
        for at, key_ref, value_ref in ((0, ka_ref, va_ref), (half, kb_ref, vb_ref)):
            values[at : at + half] = value_ref[0]
            keys_turned[:, at : at + half] = key_ref[0].T

    query = jnp.where(i < blocks // 2, qa_ref[...], qb_ref[...])
    q_two, up_two = head_rows(query), head_rows(do_ref[0])
    delta = jnp.zeros((1, 2 * rows), F32)
    step = 256
    for start in range(0, 2 * half, step):
        part = slice(start, start + step)
        probs_low = p_ref[part, :].astype(BF)
        dv_ref[part, :] += dot_low(probs_low, up_two)
        products = contract_last(values[part, :], up_two)
        d_probs[part, :] = products
        delta += jnp.sum(probs_low.astype(F32) * products, axis=0, keepdims=True)
    d_query = jnp.zeros((LANES, 2 * rows), F32)
    for start in range(0, 2 * half, step):
        part = slice(start, start + step)
        ds = (p_ref[part, :] * (d_probs[part, :] - delta)).astype(BF)
        dk_ref[part, :] += dot_low(ds, q_two)
        d_query += dot_low(keys_turned[:, part], ds)
    lane = lax.broadcasted_iota(jnp.int32, (rows, LANES), 1)

    def turned_back(value, where):
        return (value * cos_ref[where, :] - half_swap(value, lane) * sin_ref[where, :]).astype(BF)

    here = pl.ds(pl.multiple_of(i * rows, rows), rows)
    dq = turned_back(head_diagonal(d_query) * 0.125, here)
    out_ref[here, 0:LANES] = dq
    sent_ref[me ^ offset_of(i, blocks), :, 0:LANES] = dq

    @pl.when(i == blocks - 1)
    def _():
        @pl.loop(0, blocks)
        def _(j):
            there = pl.ds(pl.multiple_of(j * rows, rows), rows)
            dk = turned_back(dk_ref[there, :], there)
            dv = dv_ref[there, :].astype(BF)
            out_ref[there, LANES : 2 * LANES] = dk
            out_ref[there, 2 * LANES : 3 * LANES] = dv
            owner = me ^ offset_of(j, blocks)
            sent_ref[owner, :, LANES : 2 * LANES] = dk
            sent_ref[owner, :, 2 * LANES : 3 * LANES] = dv


def attend_back(me, probs, q_a, q_b, kv_a, kv_b, d_o, cosine, sine, passed, earlier):
    half = kv_a.shape[1]
    rows = 2 * half
    pairs = kv_a.shape[0] // 2
    blocks, own_rows, _ = d_o.shape
    halfway = blocks // 2
    grid_spec = pltpu.PrefetchScalarGridSpec(
        num_scalar_prefetch=1,
        grid=(blocks,),
        in_specs=[
            pl.BlockSpec((rows, 2 * own_rows), lambda i, m: (0, i)),
            pl.BlockSpec((own_rows, LANES), lambda i, m: (jnp.minimum(i, halfway - 1), 0)),
            pl.BlockSpec((own_rows, LANES), lambda i, m: (jnp.maximum(i - halfway, 0), 0)),
            pl.BlockSpec((1, half, LANES), lambda i, m: (m[0], 0, 0)),
            pl.BlockSpec((1, half, LANES), lambda i, m: (m[0], 0, 0)),
            pl.BlockSpec((1, half, LANES), lambda i, m: (pairs + m[0], 0, 0)),
            pl.BlockSpec((1, half, LANES), lambda i, m: (pairs + m[0], 0, 0)),
            pl.BlockSpec((1, own_rows, LANES), lambda i, m: (m[0] ^ offset_of(i, blocks), 0, 0)),
            pl.BlockSpec((rows, LANES), lambda i, m: (0, 0)),
            pl.BlockSpec((rows, LANES), lambda i, m: (0, 0)),
            ANYWHERE,
        ]
        + [ANYWHERE] * len(earlier),
        out_specs=[
            pl.BlockSpec((rows, 3 * LANES), lambda i, m: (0, 0)),
            pl.BlockSpec((blocks, own_rows, 3 * LANES), lambda i, m: (0, 0, 0)),
            ANYWHERE,
        ],
        scratch_shapes=[
            pltpu.VMEM((rows, LANES), F32),
            pltpu.VMEM((rows, LANES), F32),
            pltpu.VMEM((rows, LANES), BF),
            pltpu.VMEM((LANES, rows), BF),
            pltpu.VMEM((rows, 2 * own_rows), F32),
        ],
    )
    return pl.pallas_call(
        attend_back_kernel,
        grid_spec=grid_spec,
        out_shape=[
            shape_of((rows, 3 * LANES)),
            shape_of((blocks, own_rows, 3 * LANES)),
            shape_of(passed.shape, passed.dtype),
        ],
        input_output_aliases={11: 2},
        compiler_params=params(),
        cost_estimate=cost(8 * rows * rows * LANES, 12 * MIB),
    )(
        me,
        *all_in_hbm([probs, q_a, q_b]),
        *all_in_hbm([kv_a, kv_b, kv_a, kv_b]),
        d_o,
        *all_in_hbm([cosine, sine, passed, *earlier]),
    )


def norm_parts(inputs):
    centred = inputs - jnp.mean(inputs, axis=-1, keepdims=True)
    rstd = lax.rsqrt(jnp.mean(centred * centred, axis=-1, keepdims=True) + 1e-06)
    return centred * rstd, rstd


def norm_back(normed, rstd, gradient):
    return rstd * (
        gradient
        - jnp.mean(gradient, axis=-1, keepdims=True)
        - normed * jnp.mean(gradient * normed, axis=-1, keepdims=True)
    )


def dot_low(left, right):
    return jnp.dot(left, right, preferred_element_type=F32)


def dot_rows(left, right):
    return lax.dot_general(left, right, (((0,), (0,)), ((), ())), preferred_element_type=F32)


def gelu_parts(hidden):
    square = hidden * hidden
    tanh = jnp.tanh(0.7978845608028654 * hidden * (1.0 + 0.044715 * square))
    upper = 0.5 * (1.0 + tanh)
    slope = upper + 0.5 * hidden * (1.0 - tanh * tanh) * (
        0.7978845608028654 * (1.0 + 3.0 * 0.044715 * square)
    )
    return hidden * upper, slope


def high_low(value):
    high = value.astype(BF)
    return high, (value - high.astype(F32)).astype(BF)


class RowSums:
    def __init__(self, clip_row, clips):
        self.place = lax.broadcasted_iota(jnp.int32, (8, clip_row.shape[1]), 0)
        self.member = ((self.place == clip_row) & (self.place < clips)).astype(F32).astype(BF)

    def by_clip(self, value):
        high, low = high_low(value)
        return dot_low(
            jnp.concatenate([self.member, self.member], axis=1),
            jnp.concatenate([high, low], axis=0),
        )

    def whole(self, value, row):
        return dot_low((self.place == row).astype(F32).astype(BF), value)


def middle_kernel(
    clips, steps_ref, clipc_ref, clipr_ref, x_ref, dy_ref, o_ref, mod_ref, bo_ref, bu_ref, bd_ref,
    wo, wu, wd, *refs,
):
    out_ref, h2_ref, dx_ref, da_ref, do_ref, sums_ref = refs[-6:]
    width = x_ref.shape[1]
    ffn = wu.shape[1]
    clip = clipc_ref[...]

    def frame_rows(index):
        return by_clip(clip, mod_ref[:, (index - 2) * width : (index - 1) * width], 0, clips)

    gate_one, scale_two, gate_two = frame_rows(2), 1.0 + frame_rows(4), frame_rows(5)
    upstream = dy_ref[...].astype(F32)
    d_ffn = (gate_two * upstream).astype(BF)
    attn_out = dot_low(o_ref[...], wo[...]) + bo_ref[...]
    middle = x_ref[...].astype(F32) + gate_one * attn_out
    normed, rstd = norm_parts(middle)
    second = (normed * scale_two + frame_rows(3)).astype(BF)
    h2_ref[...] = second
    sums = RowSums(clipr_ref[...], clips)
    ffn_out = jnp.zeros(x_ref.shape, F32)
    d_second = jnp.zeros(x_ref.shape, F32)
    step = 512
    up_sums = []
    for start in range(0, ffn, step):
        here = slice(start, start + step)
        activated, slope = gelu_parts(dot_low(second, wu[:, here]) + bu_ref[:, here])
        ffn_out += dot_low(activated.astype(BF), wd[here, :])
        d_hidden = (contract_last(d_ffn, wd[here, :]) * slope).astype(BF)
        d_second += contract_last(d_hidden, wu[:, here])
        up_sums.append(sums.whole(d_hidden, clips))
    ffn_out += bd_ref[...]
    out_ref[...] = (middle + gate_two * ffn_out).astype(BF)
    d_middle = upstream + norm_back(normed, rstd, d_second * scale_two)
    dx_ref[...] = d_middle
    d_attn = (gate_one * d_middle).astype(BF)
    da_ref[...] = d_attn
    d_o = contract_last(d_attn, wo[...]).astype(BF)
    for k in range(width // LANES):
        do_ref[k] = d_o[:, k * LANES : (k + 1) * LANES]
    up_sums = jnp.concatenate(up_sums, axis=1)
    place = lax.broadcasted_iota(jnp.int32, (8, width), 0)
    lane = lax.broadcasted_iota(jnp.int32, (8, width), 1)
    steps = jnp.zeros((8, width), F32)
    for c in range(clips):
        here = (place == clips + 1) & (lane == c)
        steps = jnp.where(here, steps_ref[0, c].astype(F32), steps)
    sums_ref[:, :width] = (
        sums.by_clip(d_middle * attn_out) + sums.whole(d_attn, clips) + steps
    )
    sums_ref[:, width : 2 * width] = sums.by_clip(d_second) + up_sums[:, :width]
    sums_ref[:, 2 * width : 3 * width] = sums.by_clip(d_second * normed) + up_sums[:, width:]
    sums_ref[:, 3 * width :] = sums.by_clip(upstream * ffn_out) + sums.whole(d_ffn, clips)


def middle_part(
    steps, clip_col, clip_row, frames, cotangent, attended, modulation, b_out, b_up, b_down,
    w_out, w_up, w_down, earlier,
):
    rows, width = frames.shape
    clips = modulation.shape[0]
    small = [
        clip_col, clip_row, frames, cotangent, attended, modulation, b_out, b_up, b_down
    ]
    out_shape = [
        shape_of((rows, width)),
        shape_of((rows, width)),
        shape_of((rows, width), F32),
        shape_of((rows, width)),
        shape_of((width // LANES, rows, LANES)),
        shape_of((8, 4 * width), F32),
    ]
    return pl.pallas_call(
        lambda *refs: middle_kernel(clips, *refs),
        grid=(1,),
        in_specs=[SCALARS, full((rows, 1)), full((1, rows))]
        + [full(v.shape) for v in small[2:]]
        + [KEPT] * 3
        + [ANYWHERE] * len(earlier),
        out_specs=[full(o.shape) for o in out_shape],
        out_shape=out_shape,
        compiler_params=params(),
        cost_estimate=cost(20 * rows * width * width, 3 * MIB),
    )(steps, *all_in_hbm(small), w_out, w_up, w_down, *all_in_hbm(earlier))


def last_kernel(clips, clipc_ref, clipr_ref, x_ref, mod_ref, dx_ref, d_ref, w_hbm, *refs):
    passed = (len(refs) - 5) // 2
    out_ref, sums_ref = refs[passed : passed + 2]
    d_all, w, sems = refs[-3:]
    width = x_ref.shape[1]
    parts = 3
    copies = [
        pltpu.make_async_copy(
            w_hbm.at[:, pl.ds(i * width, width)], w.at[:, pl.ds(i * width, width)], sems.at[i]
        )
        for i in range(parts)
    ]
    for copy in copies:
        copy.start()
    for k in range(d_ref.shape[0]):
        for i in range(3):
            at = i * width + k * LANES
            d_all[:, at : at + LANES] = d_ref[k, :, i * LANES : (i + 1) * LANES]
    normed, rstd = norm_parts(x_ref[...].astype(F32))
    scale = 1.0 + by_clip(clipc_ref[...], mod_ref[...], 0, clips)
    d_first = jnp.zeros(x_ref.shape, F32)
    for i in range(parts):
        copies[i].wait()
        here = slice(i * width, (i + 1) * width)
        d_first += contract_last(d_all[:, here], w[:, here])
    out_ref[...] = (dx_ref[...] + norm_back(normed, rstd, d_first * scale)).astype(BF)
    sums = RowSums(clipr_ref[...], clips)
    sums_ref[:, :width] = (
        sums.by_clip(d_first)
        + sums.whole(d_all[:, :width], clips)
        + sums.whole(d_all[:, width : 2 * width], clips + 1)
    )
    sums_ref[:, width:] = sums.by_clip(d_first * normed) + sums.whole(d_all[:, 2 * width :], clips)


def last_part(clip_col, clip_row, frames, modulation, d_middle, d_own, w_qkv, passed):
    rows, width = frames.shape
    clips = modulation.shape[0]
    return pl.pallas_call(
        lambda *refs: last_kernel(clips, *refs),
        grid=(1,),
        in_specs=[
            full((rows, 1)),
            full((1, rows)),
            full(frames.shape),
            pl.BlockSpec((clips, width), lambda *_: (0, 1)),
            full(d_middle.shape),
            full(d_own.shape),
        ]
        + [ANYWHERE] * (1 + len(passed)),
        out_specs=[full((rows, width)), full((8, 2 * width))] + [ANYWHERE] * len(passed),
        out_shape=[shape_of((rows, width)), shape_of((8, 2 * width), F32)]
        + [shape_of(v.shape, v.dtype) for v in passed],
        input_output_aliases={7 + i: 2 + i for i in range(len(passed))},
        scratch_shapes=[
            pltpu.VMEM((rows, 3 * width), BF),
            pltpu.VMEM(w_qkv.shape, BF),
            pltpu.SemaphoreType.DMA((3,)),
        ],
        compiler_params=params(),
        cost_estimate=cost(6 * rows * width * width, 2 * MIB),
    )(
        *all_in_hbm([clip_col, clip_row, frames, modulation, d_middle]),
        d_own,
        *all_in_hbm([w_qkv, *passed]),
    )


def half_rows(core, value, kept_ref, sent_refs, at, columns):
    half = value.shape[0] // 2
    low, high = value[:half], value[half:]
    here = slice(at, at + half)
    kept_ref[here, columns] = jnp.where(core == 0, low, high)
    sent = jnp.where(core == 0, high, low).astype(BF)
    wide = sent_refs[0].shape[1]
    for i, ref in enumerate(sent_refs):
        start, stop = max(columns.start, i * wide), min(columns.stop, (i + 1) * wide)
        if start < stop:
            ref[here, start - i * wide : stop - i * wide] = sent[
                :, start - columns.start : stop - columns.start
            ]


def weights_kernel(clips, count, who_ref, clip_ref, gate_ref, bu_ref, wu_hbm, wd_hbm, *refs):
    kept_ref, sent_ref, (up_sum, down_sum, wu, wd, sems) = refs[-9], refs[-8:-5], refs[-5:]
    ha_ref, hb_ref, d_ref, mine_ref, theirs_ref = refs[:5]
    blocks = refs[5 : 5 + count]
    seconds, upstreams = blocks[: len(blocks) // 2], blocks[len(blocks) // 2 :]
    me, core = who_ref[0], who_ref[1]
    rows, width = seconds[0].shape
    part = up_sum.shape[1]
    columns = d_ref.shape[1]
    half = ha_ref.shape[0]
    own = pl.ds(pl.multiple_of((me // 2) * part, part), part)
    copies = [
        pltpu.make_async_copy(wu_hbm.at[:, own], wu, sems.at[0]),
        pltpu.make_async_copy(wd_hbm.at[own, :], wd, sems.at[1]),
    ]
    for copy in copies:
        copy.start()
    shard = part // 2

    step = 2 * LANES
    for start in range(0, width, step):
        here = slice(start, start + step)
        value = dot_rows(ha_ref[:, here], d_ref[:half, :])
        value += dot_rows(hb_ref[:, here], d_ref[half:, :])
        for inner in range(0, step, LANES):
            half_rows(
                core, value[inner : inner + LANES], kept_ref, sent_ref, (start + inner) // 2,
                slice(0, columns),
            )

    left = jnp.concatenate([mine_ref[:, :width], theirs_ref[:, :width]], axis=0)
    right = jnp.concatenate([mine_ref[:, width:], theirs_ref[:, width:]], axis=0)
    at = columns + 2 * part
    for start in range(0, width, step):
        value = dot_rows(left[:, start : start + step], right)
        for inner in range(0, step, LANES):
            half_rows(
                core, value[inner : inner + LANES], kept_ref, sent_ref, (start + inner) // 2,
                slice(at, at + width // 2),
            )

    for copy in copies:
        copy.wait()
    up_weights, down_weights = wu[...], wd[...]
    for pair in range(len(seconds) // 2):
        here = slice(2 * pair * rows, 2 * (pair + 1) * rows)
        second = jnp.concatenate([r[...] for r in seconds[2 * pair : 2 * pair + 2]], axis=0)
        upstream = jnp.concatenate([r[...] for r in upstreams[2 * pair : 2 * pair + 2]], axis=0)
        gate = by_clip(clip_ref[here, :], gate_ref[...], 0, clips)
        d_ffn = (gate * upstream.astype(F32)).astype(BF)
        activated, slope = gelu_parts(dot_low(second, up_weights) + bu_ref[:, own])
        d_hidden = (contract_last(d_ffn, down_weights) * slope).astype(BF)
        up, down = dot_rows(second, d_hidden), dot_rows(activated.astype(BF), d_ffn)
        if pair == 0:
            up_sum[...] = up
            down_sum[...] = down
        else:
            up_sum[...] += up
            down_sum[...] += down
    for y in range(2):
        mine = slice(y * shard, (y + 1) * shard)
        at = columns + 2 * y * shard
        for k in range(width // LANES):
            half_rows(
                core, up_sum[k * LANES : (k + 1) * LANES, mine], kept_ref, sent_ref,
                k * LANES // 2, slice(at, at + shard),
            )
        for c in range(width // shard):
            half_rows(
                core, down_sum[mine, c * shard : (c + 1) * shard], kept_ref, sent_ref,
                c * shard // 2, slice(at + shard, at + 2 * shard),
            )


def weights_part(who, clip_col, modulation, b_up, w_up, w_down, h1_a, h1_b, d_qkv, outs, seconds, upstreams):
    width, ffn = w_up.shape
    count = 2 * len(seconds)
    part = 2 * ffn // count
    clips = modulation.shape[0]
    shape = (width // 2, d_qkv.shape[1] + 2 * part + width // 2)
    rows = d_qkv.shape[0]
    arrays = [h1_a, h1_b, d_qkv, *outs, *seconds, *upstreams]
    return pl.pallas_call(
        lambda *refs: weights_kernel(clips, count, *refs),
        grid=(1,),
        in_specs=[
            SCALARS,
            pl.BlockSpec((rows // 2, 1), lambda *_: (0, 0)),
            pl.BlockSpec((clips, width), lambda *_: (0, 3)),
            full(b_up.shape),
            ANYWHERE,
            ANYWHERE,
        ]
        + [full(v.shape) for v in arrays],
        out_specs=[full(shape)] + [full((shape[0], shape[1] // 3))] * 3,
        out_shape=[shape_of(shape, F32)] + [shape_of((shape[0], shape[1] // 3))] * 3,
        scratch_shapes=[
            pltpu.VMEM((width, part), F32),
            pltpu.VMEM((part, width), F32),
            pltpu.VMEM((width, part), BF),
            pltpu.VMEM((part, width), BF),
            pltpu.SemaphoreType.DMA((2,)),
        ],
        compiler_params=params(36),
        cost_estimate=cost(7 * rows * width * part, 10 * MIB),
    )(who, *all_in_hbm([clip_col, modulation, b_up, w_up, w_down, *arrays]))


def table_kernel(first, clips, place_ref, *refs):
    parts, refs = refs[:4], refs[4:]
    if first:
        silu_ref, w_ref = refs[:2]
        dw_ref, db_ref, out_ref, total, sums = refs[-5:]
    else:
        silu_ref, w_ref, cond_ref, pick_ref, earlier_ref, _, _ = refs[:7]
        dw_ref, db_ref, out_ref, total, sums = refs[7:]
    i = pl.program_id(0)

    @pl.when(i == 0)
    def _():
        total[...] = jnp.zeros_like(total) if first else earlier_ref[...]

    for j, part in enumerate(parts):
        value = part[...]
        valid = lax.broadcasted_iota(jnp.int32, value.shape, 0) < clips
        sums[pl.ds(pl.multiple_of((place_ref[0] ^ j) * 8, 8), 8), :] = jnp.where(valid, value, 0.0)
    high, low = high_low(sums[...])
    total[...] += contract_last(w_ref[...], jnp.concatenate([high, low], axis=0))
    silu = silu_ref[...]
    dw_ref[...] = dot_rows(
        jnp.concatenate([silu, silu], axis=0), jnp.concatenate([high, low], axis=0)
    )
    db_ref[...] = jnp.sum(sums[...], axis=0, keepdims=True)

    @pl.when(i == pl.num_programs(0) - 1)
    def _():
        if first:
            out_ref[...] = total[...]
        else:
            rows = high.shape[0]
            d_silu = total[:, :rows] + total[:, rows:]
            cond = cond_ref[...]
            gate = 1.0 / (1.0 + jnp.exp(-cond))
            d_cond = d_silu.T * (gate * (1.0 + cond * (1.0 - gate)))
            d_high, d_low = high_low(d_cond)
            lowest = (d_cond - d_high.astype(F32) - d_low.astype(F32)).astype(BF)
            pick = pick_ref[...].astype(BF)
            out_ref[...] = dot_rows(pick, d_high) + dot_rows(pick, d_low) + dot_rows(pick, lowest)


def table_part(place, sums, silu, w_mod, column, clips, rest=None, earlier=()):
    columns = sums[0].shape[1]
    width = w_mod.shape[0]
    all_columns = 6 * width
    rows, own = silu.shape
    tile = 1024
    skip = column // tile
    first = rest is None
    shapes = [
        shape_of((own, all_columns), F32),
        shape_of((1, all_columns), F32),
        shape_of((width, 2 * rows), F32),
    ]
    in_specs = [SCALARS] + [pl.BlockSpec((8, tile), lambda i: (0, i))] * 4 + [
        pl.BlockSpec((rows, own), lambda i: (0, 0)),
        pl.BlockSpec((width, tile), lambda i: (0, skip + i)),
    ]
    args = [place, *all_in_hbm([*sums, silu]), in_hbm(w_mod)]
    aliases = {}
    if first:
        in_specs += [ANYWHERE] * len(earlier)
        args += all_in_hbm(earlier)
    else:
        condition, pick, earlier, d_w, d_b = rest
        in_specs += [
            pl.BlockSpec((rows, width), lambda i: (0, 0)),
            pl.BlockSpec(pick.shape, lambda i: (0, 0)),
            pl.BlockSpec((width, 2 * rows), lambda i: (0, 0)),
            ANYWHERE,
            ANYWHERE,
        ]
        args += all_in_hbm([condition, pick, earlier, d_w, d_b])
        aliases = {10: 0, 11: 1}
        shapes[2] = shape_of((pick.shape[1], width), F32)
    return pl.pallas_call(
        lambda *refs: table_kernel(first, clips, *refs),
        grid=(columns // tile,),
        in_specs=in_specs,
        out_specs=[
            pl.BlockSpec((own, tile), lambda i: (0, skip + i)),
            pl.BlockSpec((1, tile), lambda i: (0, skip + i)),
            pl.BlockSpec(shapes[2].shape, lambda i: (0, 0)),
        ],
        out_shape=shapes,
        scratch_shapes=[
            pltpu.VMEM((width, 2 * rows), F32),
            pltpu.VMEM((rows, tile), F32),
        ],
        input_output_aliases=aliases,
        compiler_params=params(),
        cost_estimate=cost(rows * width, width),
    )(*args)


def in_order(bit, mine, other):
    return jnp.stack([jnp.where(bit == 0, mine, other), jnp.where(bit == 0, other, mine)])


def batch_parts(sums):
    return [sums] + [swapped_with(sums, "batch", k) for k in range(1, 4)]


def share_kernel(columns, part, who_ref, kept_ref, *refs):
    others = refs[:3]
    own_ref, x_ref, y_ref, both_ref, out_ref = refs[-5:]
    far, odd = who_ref[2] // 2 == 1, who_ref[0] % 2 == 1
    rows = own_ref.shape[1]
    first, second = slice(columns, columns + part), slice(columns + part, columns + 2 * part)
    for k in range(own_ref.shape[0]):
        here = slice(2 * k * rows, 2 * (k + 1) * rows)
        other = jnp.concatenate([ref[here, :] for ref in others], axis=1)
        value = kept_ref[here, :] + other.astype(F32)
        low, high = value[:rows], value[rows:]
        near, away = jnp.where(far, high, low), jnp.where(far, low, high)
        own_ref[k, :, :columns] = near[:, :columns]
        own_ref[k, :, columns:] = jnp.where(odd, near[:, second], near[:, first])
        y_ref[k] = jnp.where(odd, near[:, first], near[:, second]).astype(BF)
        x_ref[k, :, :columns] = away[:, :columns].astype(BF)
        x_ref[k, :, columns:] = jnp.where(odd, away[:, second], away[:, first]).astype(BF)
        both_ref[k] = jnp.where(odd, away[:, first], away[:, second]).astype(BF)
        out_ref[k] = jnp.concatenate(
            [low[:, columns + 2 * part :], high[:, columns + 2 * part :]], axis=1
        ).astype(BF)


def share(who, kept, others, count, columns, part):
    rows = kept.shape[0] // count // 2
    width = 2 * (kept.shape[1] - columns - 2 * part)
    shapes = [
        shape_of((count, rows, columns + part), F32),
        shape_of((count, rows, columns + part)),
        shape_of((count, rows, part)),
        shape_of((count, rows, part)),
        shape_of((count, rows, width)),
    ]
    return pl.pallas_call(
        lambda *refs: share_kernel(columns, part, *refs),
        grid=(1,),
        in_specs=[SCALARS, full(kept.shape)] + [full(v.shape) for v in others],
        out_specs=[full(v.shape) for v in shapes],
        out_shape=shapes,
        compiler_params=params(),
        cost_estimate=cost(0, 8 * MIB),
    )(who, in_hbm(kept), *others)


def gather_sums_kernel(columns, own_ref, x_ref, y_ref, both_ref, out_ref, *refs):
    sent_ref, down_ref = refs[-2:]
    count, rows, _ = own_ref.shape
    shard = y_ref.shape[2] // 2
    ready = columns + shard
    for k in range(count):
        from_x = x_ref[k].astype(F32)
        sent_ref[k, :, :columns] = (own_ref[k, :, :columns] + from_x[:, :columns]).astype(BF)
        value = (own_ref[k, :, columns:] + from_x[:, columns:]) + (
            y_ref[k].astype(F32) + both_ref[k].astype(F32)
        )
        sent_ref[k, :, columns:ready] = value[:, :shard].astype(BF)
        group, at = k % 2, k // 2 * shard
        down_ref[group * rows : (group + 1) * rows, at : at + shard] = value[:, shard:].astype(BF)
        sent_ref[k, :, ready:] = out_ref[k]


def gather_sums(own, from_x, from_y, from_both, out_parts, columns, passed):
    count, rows, _ = own.shape
    width = out_parts.shape[2]
    args = [own, from_x, from_y, from_both, out_parts]
    shapes = [
        shape_of((count, rows, columns + from_y.shape[2] // 2 + width)),
        shape_of((2 * rows, width)),
    ]
    return pl.pallas_call(
        lambda *refs: gather_sums_kernel(columns, *refs),
        grid=(1,),
        in_specs=[full(v.shape) for v in args] + [ANYWHERE] * len(passed),
        out_specs=[ANYWHERE] * len(passed) + [full(v.shape) for v in shapes],
        out_shape=[shape_of(v.shape, v.dtype) for v in passed] + shapes,
        input_output_aliases={5 + i: i for i in range(len(passed))},
        compiler_params=params(),
        cost_estimate=cost(0, 4 * MIB),
    )(in_hbm(own), from_x, from_y, from_both, *all_in_hbm([out_parts, *passed]))


def rows_kernel(columns, rows_ref, *refs):
    out_ref = refs[-1]
    count, rows, wide = rows_ref.shape
    width = out_ref.shape[1]
    shard = wide - width - columns
    total = jnp.zeros((rows, width), F32)
    for k in range(count):
        for i in range(columns // LANES):
            out_ref[i * rows : (i + 1) * rows, k * LANES : (k + 1) * LANES] = rows_ref[
                k, :, i * LANES : (i + 1) * LANES
            ]
        piece = columns // LANES + k * shard // width
        at = k * shard % width
        out_ref[piece * rows : (piece + 1) * rows, at : at + shard] = rows_ref[
            k, :, columns : columns + shard
        ]
        total += rows_ref[k, :, columns + shard :].astype(F32)
    piece = columns // LANES + count * shard // width
    out_ref[piece * rows :, :] = total.astype(BF)


def gather_rows(rows_mine, width, columns, passed, earlier):
    count, rows, wide = rows_mine.shape
    shard = wide - width - columns
    shape = ((columns // LANES + count * shard // width + 1) * rows, width)
    return pl.pallas_call(
        lambda *refs: rows_kernel(columns, *refs),
        grid=(1,),
        in_specs=[full(rows_mine.shape), ANYWHERE, ANYWHERE],
        out_specs=[ANYWHERE, full(shape)],
        out_shape=[shape_of(passed.shape, passed.dtype), shape_of(shape)],
        input_output_aliases={1: 0},
        compiler_params=params(),
        cost_estimate=cost(0, 2 * MIB),
    )(rows_mine, *all_in_hbm([passed, earlier]))


def assemble_kernel(ffn, who_ref, *refs):
    qkv_ref, out_ref, up_ref, down_ref = refs[-4:]
    width = out_ref.shape[1]
    rows = qkv_ref.shape[0] // 4
    for j, (ref, own_down) in enumerate(zip(refs[:4], refs[4:8])):
        owner = who_ref[2] ^ j
        core, far = owner % 2, owner // 2
        at = pl.multiple_of(core * 2 * rows + far * rows, rows)
        piece = 0
        for target, count in ((qkv_ref, 3), (up_ref, ffn // width)):
            for i in range(count):
                here = slice(piece * rows, (piece + 1) * rows)
                target[pl.ds(at, rows), i * width : (i + 1) * width] = ref[here, :].astype(F32)
                piece += 1
        for g in range(2):
            here = slice(g * rows, (g + 1) * rows)
            there = pl.multiple_of(core * 4 * rows + g * 2 * rows + far * rows, rows)
            down_ref[pl.ds(there, rows), :] = own_down[here, :].astype(F32)
        part = width // 2
        column = pl.multiple_of(far * part, part)
        for g in range(2):
            there = pl.multiple_of(core * 2 * rows + g * rows, rows)
            out_ref[pl.ds(there, rows), pl.ds(column, part)] = ref[
                piece * rows : (piece + 1) * rows, g * part : (g + 1) * part
            ].astype(F32)


def assemble(who, parts, own_rows, ffn):
    width = parts[0].shape[1]
    shapes = [
        shape_of((own_rows, 3 * width), F32),
        shape_of((own_rows, width), F32),
        shape_of((own_rows, ffn), F32),
        shape_of((2 * own_rows, width), F32),
    ]
    return pl.pallas_call(
        lambda *refs: assemble_kernel(ffn, *refs),
        grid=(1,),
        in_specs=[SCALARS] + [full(v.shape) for v in parts],
        out_specs=[full(o.shape) for o in shapes],
        out_shape=shapes,
        compiler_params=params(),
        cost_estimate=cost(0, 6 * MIB),
    )(who, *parts)


def heads_body(
    frames, step_table, clip_lengths, clip_steps, w_mod, b_mod, w_qkv, b_qkv, w_out, b_out,
    w_up, b_up, w_down, b_down, cotangent,
):
    own_rows, width = frames.shape
    ffn = w_up.shape[1]
    count = lax.axis_size("blk")
    me = lax.axis_index("blk")
    place = lax.axis_index("batch")
    core, far = place % 2, place // 2
    who = jnp.stack([me, core, place])
    clips = clip_lengths.shape[1]
    rows = own_rows * count

    head_size = width // HEADS
    half = head_size // 2
    lane = jnp.arange(LANES, dtype=jnp.int32)
    freqs = 10000.0 ** (-2.0 * (lane % half).astype(F32) / head_size)
    rows_of_table = jnp.arange(step_table.shape[0], dtype=jnp.int32)
    (
        modulation, silu_own, clip_col, clip_row, cosine, sine, marks, kept_qkv,
    ) = prepare(
        me[None], clip_lengths, clip_steps, step_table, freqs[None, :], w_mod, b_mod[None, :],
        [w_qkv], own_rows, count,
    )
    modulation_two = modulate(silu_own, w_mod, b_mod[None, :])
    evens, odds = gathered_blocks(frames, count, (modulation_two[0, 0] * 0.0).astype(BF))

    shared = (b_qkv[None, :], cosine, sine)
    first = (me[None], clip_col, modulation)
    h1_a, kv_a, q_a, q_own, later = project(0, evens, *first, kept_qkv, *shared, cotangent)
    upstreams = even_blocks(later, count)
    h1_b, kv_b, q_b = project(1, odds, *first, w_qkv, *shared)
    attended, kept_out, kept_up, kept_down = attend(
        q_own, kv_a, kv_b, marks, [w_out, w_up, w_down]
    )
    result, second, d_middle, d_attn, d_o, sums_two = middle_part(
        clip_steps, clip_col, clip_row, frames, cotangent, attended, modulation_two,
        b_out[None, :], b_up[None, :], b_down[None, :], kept_out, kept_up, kept_down,
        upstreams,
    )
    d_o = lax.all_to_all(d_o, "blk", 0, 0, tiled=True)
    seconds = even_blocks(second, count)
    probs, d_attn = heads_probs(
        me[None], q_a, q_b, kv_a, kv_b, clip_col, clip_row, count, d_middle, d_attn
    )
    sums_two = sums_two + swapped_with(sums_two, "blk", 1)
    sums_two = sums_two + swapped_with(sums_two, "blk", 2)

    wide = width // 2
    da_low, da_high = d_attn[:, :wide], d_attn[:, wide:]
    out_sent = jnp.concatenate([attended, jnp.where(far == 0, da_high, da_low)], axis=1)
    out_kept = jnp.concatenate([attended, jnp.where(far == 0, da_low, da_high)], axis=1)
    out_sent = swapped_with(out_sent, "batch", 2)

    d_qkv, d_qkv_sent, sums_two = attend_back(
        me[None], probs, q_a, q_b, kv_a, kv_b, d_o, cosine, sine, sums_two, seconds[:3]
    )
    d_own = lax.all_to_all(d_qkv_sent, "blk", 0, 0, tiled=True)
    kept, *sent = weights_part(
        who, clip_col, modulation_two, b_up[None, :], w_up, w_down, h1_a, h1_b, d_qkv,
        [out_kept, out_sent], seconds, upstreams,
    )
    own_sums, for_x, for_y, for_both, out_parts = share(
        who, kept, [swapped_with(v, "batch", 1) for v in sent], count, 3 * LANES, 2 * ffn // count
    )

    d_inputs, sums_one, own_sums, sums_two = last_part(
        clip_col, clip_row, frames, modulation, d_middle, d_own, w_qkv,
        [own_sums, sums_two],
    )
    sums_one = sums_one + swapped_with(sums_one, "blk", 2)
    sums_two = sums_two + swapped_with(sums_two, "blk", 4)

    pairs = [
        (b * count + k, (b ^ 2) * count + (k ^ 1)) for b in range(4) for k in range(count)
    ]
    sums_one, sums_two, sent, down_rows = gather_sums(
        own_sums,
        swapped_with(for_x, "batch", 2),
        swapped_with(for_y, "blk", 1),
        lax.ppermute(for_both, ("batch", "blk"), pairs),
        out_parts,
        3 * LANES,
        [sums_one, sums_two],
    )
    rows_mine = lax.all_to_all(sent, "blk", 0, 0, tiled=True)
    sums_one = sums_one + swapped_with(sums_one, "blk", 1)
    sums_two = batch_parts(sums_two)
    steps_all = jnp.stack([v[clips + 1, :clips] for v in sums_two]) * (1.0 / count)
    steps_all = steps_all[place ^ jnp.arange(4, dtype=jnp.int32)].astype(jnp.int32)
    pick_all = (steps_all[:, :, None] == rows_of_table[None, None, :]).astype(F32)
    pick_all = jnp.pad(pick_all, ((0, 0), (0, 8 - clips), (0, 0))).reshape(32, -1)
    condition_all = exact_dot(pick_all, step_table)
    silu_all = jax.nn.silu(condition_all).astype(BF)
    silu_cols = lax.dynamic_slice_in_dim(silu_all, me * own_rows, own_rows, 1)
    d_w_mod, d_b_mod, d_silu = table_part(
        place[None], sums_two, silu_cols, w_mod, 2 * width, clips
    )
    sums_one, mine = gather_rows(rows_mine, width, 3 * LANES, sums_one, d_silu)
    sums_one = batch_parts(sums_one + swapped_with(sums_one, "blk", 4))
    d_w_mod, d_b_mod, d_table = table_part(
        place[None], sums_one, silu_cols, w_mod, 0, clips,
        (condition_all, pick_all, d_silu, d_w_mod, d_b_mod),
    )

    def batch_total(parts):
        return (parts[0] + parts[1]) + (parts[2] + parts[3])

    bias_two = batch_total([v[clips] for v in sums_two])
    bias_one = batch_total([v[clips : clips + 2] for v in sums_one])
    d_b_qkv = jnp.concatenate(
        [bias_one[0, :width], bias_one[1, :width], bias_one[0, width:]], axis=0
    )
    d_b_out, d_b_up, d_b_down = jnp.split(bias_two, [width, width + ffn])

    def everyone(value):
        other = swapped_with(value, "batch", 2)
        return [value, swapped_with(value, "batch", 1), other, swapped_with(other, "batch", 1)]

    d_w_qkv, d_w_out, d_w_up, d_w_down = assemble(
        who, everyone(mine) + everyone(down_rows), own_rows, ffn
    )

    return (
        result,
        d_inputs,
        d_table,
        d_w_mod,
        d_b_mod[0],
        d_w_qkv,
        d_b_qkv,
        d_w_out,
        d_b_out,
        d_w_up,
        d_b_up,
        d_w_down,
        d_b_down,
    )


def solution(mesh):
    blk = mesh.shape["blk"]
    heads_fit = HEADS == 2 * blk and mesh.shape["batch"] == 4
    chosen = heads_body if heads_fit else ring_body
    placed = (
        P(("batch", "blk"), None),
        P(),
        P("batch", None),
        P("batch", None),
        P(),
        P(),
        P(),
        P(),
        P(),
        P(),
        P(),
        P(),
        P(),
        P(),
        P(("batch", "blk"), None),
    )
    return jax.shard_map(
        chosen,
        mesh=mesh,
        in_specs=placed,
        out_specs=(
            P(("batch", "blk"), None),
            P(("batch", "blk"), None),
            P(),
            P("blk", None),
            P(),
            P("blk", None),
            P(),
            P("blk", None),
            P(),
            P("blk", None),
            P(),
            P("blk", None),
            P(),
        ),
        check_vma=False,
    )
```

```python
import jax
import jax.numpy as jnp
from jax import lax
from jax.experimental import pallas as pl
from jax.experimental.pallas import tpu as pltpu
from jax.sharding import PartitionSpec as P

HEADS = 16


HIGH_PRECISION = lax.Precision.HIGHEST
NEGATIVE = -1e30


def passed_along(value, axis, by):
    size = lax.axis_size(axis)
    return lax.ppermute(value, axis, [(i, (i + by) % size) for i in range(size)])


def norm_rows(inputs):
    average = jnp.mean(inputs, axis=-1, keepdims=True)
    centred = inputs - average
    variance = jnp.mean(centred * centred, axis=-1, keepdims=True)
    return centred * lax.rsqrt(variance + 1e-06)


def modulated(inputs, shift_part, scale_part):
    return norm_rows(inputs) * (1.0 + scale_part) + shift_part


def rotate(vectors, cosine, sine_part):
    half_size = vectors.shape[-1] // 2
    first_half = vectors[..., :half_size]
    second_half = vectors[..., half_size:]
    return jnp.concatenate(
        [
            first_half * cosine - second_half * sine_part,
            second_half * cosine + first_half * sine_part,
        ],
        axis=-1,
    )


def exact_dot(left_side, right_side):
    return jnp.dot(left_side, right_side, precision=HIGH_PRECISION)


def clip_index(positions, clip_ends):
    return jnp.sum((clip_ends[None, :] <= positions[:, None]).astype(jnp.int32), axis=1)


def attend_block(queries, key_rows, value_rows, visible, carry_state, scale):
    running_max, denominator, numerator = carry_state
    scores = (
        jnp.einsum("qhd,khd->hqk", queries, key_rows, preferred_element_type=jnp.float32) * scale
    )
    scores = jnp.where(visible[None], scores, NEGATIVE)
    new_max = jnp.maximum(running_max, jnp.max(scores, axis=-1))
    factor = jnp.exp(running_max - new_max)
    probabilities = jnp.where(visible[None], jnp.exp(scores - new_max[..., None]), 0.0)
    denominator = factor * denominator + jnp.sum(probabilities, axis=-1)
    numerator = numerator * jnp.transpose(factor)[:, :, None] + jnp.einsum(
        "hqk,khd->qhd",
        probabilities.astype(jnp.bfloat16),
        value_rows,
        preferred_element_type=jnp.float32,
    )
    return (new_max, denominator, numerator)


def grad_block(queries, upstream, log_total, row_delta, key_rows, value_rows, visible, scale):
    scores = (
        jnp.einsum("qhd,khd->hqk", queries, key_rows, preferred_element_type=jnp.float32) * scale
    )
    probabilities = jnp.where(
        visible[None],
        jnp.exp(jnp.where(visible[None], scores, NEGATIVE) - log_total[..., None]),
        0.0,
    )
    d_probs = jnp.einsum("qhd,khd->hqk", upstream, value_rows, preferred_element_type=jnp.float32)
    d_scores = (probabilities * (d_probs - row_delta[..., None])).astype(jnp.bfloat16)
    d_query = scale * jnp.einsum(
        "hqk,khd->qhd", d_scores, key_rows, preferred_element_type=jnp.float32
    )
    d_key = scale * jnp.einsum(
        "hqk,qhd->khd", d_scores, queries, preferred_element_type=jnp.float32
    )
    d_value = jnp.einsum(
        "hqk,qhd->khd",
        probabilities.astype(jnp.bfloat16),
        upstream,
        preferred_element_type=jnp.float32,
    )
    return (d_query, d_key, d_value)


def pass_key_grads(gradients):
    return (
        passed_along(gradients[0].astype(jnp.bfloat16), "blk", 1).astype(jnp.float32),
        passed_along(gradients[1].astype(jnp.bfloat16), "blk", 1).astype(jnp.float32),
    )


def ring_body(
    frames,
    step_table,
    clip_lengths,
    clip_steps,
    w_mod,
    b_mod,
    w_qkv,
    b_qkv,
    w_out,
    b_out,
    w_up,
    b_up,
    w_down,
    b_down,
    cotangent,
):
    frame_count, model_width = frames.shape
    ffn_width = w_up.shape[1]
    cycle_size = lax.axis_size("blk")
    cycle_place = lax.axis_index("blk")
    head_count = HEADS
    head_size = model_width // head_count
    scale = head_size ** (-0.5)
    lengths = clip_lengths[0]
    steps = clip_steps[0]
    clip_count = lengths.shape[0]
    clip_ends = jnp.cumsum(lengths)
    clip_starts = clip_ends - lengths
    local_rows = jnp.arange(frame_count, dtype=jnp.int32)
    places = cycle_place * frame_count + local_rows
    clip_own = clip_index(places, clip_ends)
    member = (clip_own[:, None] == jnp.arange(clip_count, dtype=jnp.int32)[None, :]).astype(
        jnp.float32
    )
    offsets = jnp.sum(member * clip_starts[None, :].astype(jnp.float32), axis=1)
    freqs = 10000.0 ** (-2.0 * jnp.arange(head_size // 2, dtype=jnp.float32) / head_size)
    angles = (places.astype(jnp.float32) - offsets)[:, None] * freqs[None, :]
    cosine = jnp.cos(angles)[:, None, :]
    sine_part = jnp.sin(angles)[:, None, :]

    def clip_of(turn_index):
        source = (cycle_place - turn_index) % cycle_size
        return clip_index(source * frame_count + local_rows, clip_ends)

    step_pick = (
        steps[:, None] == jnp.arange(step_table.shape[0], dtype=jnp.int32)[None, :]
    ).astype(jnp.float32)
    condition = exact_dot(step_pick, step_table)
    silu_low = jax.nn.silu(condition).astype(jnp.bfloat16)
    modulation = jnp.dot(silu_low, w_mod, preferred_element_type=jnp.float32) + b_mod
    frame_mod = exact_dot(member, modulation)
    shift_one, scale_one, gate_one, shift_two, scale_two, gate_two = jnp.split(frame_mod, 6, axis=1)
    inputs = frames.astype(jnp.float32)
    first, first_back = jax.vjp(modulated, inputs, shift_one, scale_one)
    first_low = first.astype(jnp.bfloat16)
    projected = jnp.dot(first_low, w_qkv, preferred_element_type=jnp.float32) + b_qkv
    query_part, key_part, value_part = jnp.split(projected, 3, axis=1)

    def spin(query_lin, key_lin):
        return (
            rotate(query_lin.reshape(frame_count, head_count, head_size), cosine, sine_part),
            rotate(key_lin.reshape(frame_count, head_count, head_size), cosine, sine_part),
        )

    (query_rot, key_rot), spin_back = jax.vjp(spin, query_part, key_part)
    queries = query_rot.astype(jnp.bfloat16)
    key_rows = key_rot.astype(jnp.bfloat16)
    value_rows = value_part.reshape(frame_count, head_count, head_size).astype(jnp.bfloat16)

    def forward_step(turn_index, key_value, carry_state):
        visible = clip_own[:, None] == clip_of(turn_index)[None, :]
        return attend_block(queries, key_value[0], key_value[1], visible, carry_state, scale)

    def forward_turn(turn_index, carry):
        key_value, carry_state = carry
        carry_state = forward_step(turn_index, key_value, carry_state)
        key_value = passed_along((key_value[0], key_value[1]), "blk", 1)
        return (key_value, carry_state)

    initial = (
        jnp.full((head_count, frame_count), NEGATIVE, jnp.float32),
        jnp.zeros((head_count, frame_count), jnp.float32),
        jnp.zeros((frame_count, head_count, head_size), jnp.float32),
    )
    key_value, carry_state = lax.fori_loop(
        0, cycle_size - 1, forward_turn, ((key_rows, value_rows), initial)
    )
    running_max, denominator, numerator = forward_step(cycle_size - 1, key_value, carry_state)
    attended = numerator / jnp.transpose(denominator)[:, :, None]
    log_total = running_max + jnp.log(denominator)
    attended_low = attended.reshape(frame_count, model_width).astype(jnp.bfloat16)
    attn_out = jnp.dot(attended_low, w_out, preferred_element_type=jnp.float32) + b_out
    middle = inputs + gate_one * attn_out
    second, second_back = jax.vjp(modulated, middle, shift_two, scale_two)
    second_low = second.astype(jnp.bfloat16)
    hidden = jnp.dot(second_low, w_up, preferred_element_type=jnp.float32) + b_up
    activated, gelu_back = jax.vjp(
        lambda values_in: jax.nn.gelu(values_in, approximate=True), hidden
    )
    activated_low = activated.astype(jnp.bfloat16)
    ffn_out = jnp.dot(activated_low, w_down, preferred_element_type=jnp.float32) + b_down
    result = middle + gate_two * ffn_out
    upstream_y = cotangent.astype(jnp.float32)
    d_ffn = (gate_two * upstream_y).astype(jnp.bfloat16)
    d_gate_two = upstream_y * ffn_out
    d_act = jnp.dot(d_ffn, w_down.T, preferred_element_type=jnp.float32)
    d_hidden = gelu_back(d_act)[0].astype(jnp.bfloat16)
    d_second = jnp.dot(d_hidden, w_up.T, preferred_element_type=jnp.float32)
    d_middle_norm, d_shift_two, d_scale_two = second_back(d_second)
    d_middle = upstream_y + d_middle_norm
    d_attn = (gate_one * d_middle).astype(jnp.bfloat16)
    d_gate_one = d_middle * attn_out
    d_attended = jnp.dot(d_attn, w_out.T, preferred_element_type=jnp.float32).astype(jnp.bfloat16)
    d_attended = d_attended.reshape(frame_count, head_count, head_size)
    row_delta = jnp.transpose(jnp.sum(d_attended.astype(jnp.float32) * attended, axis=-1))
    zeros_three = jnp.zeros((frame_count, head_count, head_size), jnp.float32)

    def key_step(turn_index, key_value, owed):
        visible = clip_own[:, None] == clip_of(turn_index)[None, :]
        d_query, d_key, d_value = grad_block(
            queries, d_attended, log_total, row_delta, key_value[0], key_value[1], visible, scale
        )
        return (owed[0] + d_query, (owed[1][0] + d_key, owed[1][1] + d_value))

    def key_turn(turn_index, carry):
        key_value, owed = carry
        d_query_sum, gradients = key_step(turn_index, key_value, owed)
        key_value = passed_along((key_value[0], key_value[1]), "blk", 1)
        gradients = pass_key_grads(gradients)
        return (key_value, (d_query_sum, gradients))

    key_value, owed = lax.fori_loop(
        0,
        cycle_size - 1,
        key_turn,
        ((key_rows, value_rows), (zeros_three, (zeros_three, zeros_three))),
    )
    d_query_rot, gradients = key_step(cycle_size - 1, key_value, owed)
    d_key_rot, d_value_all = pass_key_grads(gradients)
    d_query_lin, d_key_lin = spin_back((d_query_rot, d_key_rot))
    d_projected = jnp.concatenate(
        [d_query_lin, d_key_lin, d_value_all.reshape(frame_count, model_width)], axis=1
    ).astype(jnp.bfloat16)
    d_first = jnp.dot(d_projected, w_qkv.T, preferred_element_type=jnp.float32)
    d_input_norm, d_shift_one, d_scale_one = first_back(d_first)
    d_inputs = d_middle + d_input_norm
    d_frame_mod = jnp.concatenate(
        [d_shift_one, d_scale_one, d_gate_one, d_shift_two, d_scale_two, d_gate_two], axis=1
    )
    d_modulation = exact_dot(member.T, d_frame_mod)
    d_silu = jnp.dot(d_modulation, w_mod.T, precision=HIGH_PRECISION)
    d_condition = jax.vjp(jax.nn.silu, condition)[1](d_silu)[0]
    d_table_local = exact_dot(step_pick.T, d_condition)
    small = lax.psum(
        (
            jnp.sum(d_modulation, axis=0),
            jnp.sum(d_projected.astype(jnp.float32), axis=0),
            jnp.sum(d_attn.astype(jnp.float32), axis=0),
            jnp.sum(d_hidden.astype(jnp.float32), axis=0),
            jnp.sum(d_ffn.astype(jnp.float32), axis=0),
            d_table_local,
        ),
        ("batch", "blk"),
    )
    d_b_mod, d_b_qkv, d_b_out, d_b_up, d_b_down, d_table = small
    blocks_list = [
        jnp.dot(first_low.T, d_projected, preferred_element_type=jnp.float32),
        jnp.dot(attended_low.T, d_attn, preferred_element_type=jnp.float32),
        jnp.dot(second_low.T, d_hidden, preferred_element_type=jnp.float32),
    ]
    blocks_list.append(exact_dot(silu_low.T.astype(jnp.float32), d_modulation))
    wide_rows = lax.psum_scatter(
        jnp.concatenate(blocks_list, axis=1), "blk", scatter_dimension=0, tiled=True
    )
    down_part = lax.psum_scatter(
        jnp.dot(activated_low.T, d_ffn, preferred_element_type=jnp.float32),
        "blk",
        scatter_dimension=0,
        tiled=True,
    )
    wide_rows, down_part = (
        lax.psum(wide_rows.astype(jnp.bfloat16), "batch").astype(jnp.float32),
        lax.psum(down_part.astype(jnp.bfloat16), "batch").astype(jnp.float32),
    )
    qkv_end = 3 * model_width
    out_end = qkv_end + model_width
    up_end = out_end + ffn_width
    return (
        result.astype(jnp.bfloat16),
        d_inputs.astype(jnp.bfloat16),
        d_table,
        wide_rows[:, up_end:],
        d_b_mod,
        wide_rows[:, :qkv_end],
        d_b_qkv,
        wide_rows[:, qkv_end:out_end],
        d_b_out,
        wide_rows[:, out_end:up_end],
        d_b_up,
        down_part,
        d_b_down,
    )


BF = jnp.bfloat16
F32 = jnp.float32
LANES = 128
MIB = 1024 * 1024


def swapped_with(value, axis, offset):
    size = lax.axis_size(axis)
    return lax.ppermute(value, axis, [(i, i ^ offset) for i in range(size)])


def even_blocks(value, count):
    return [value] + [swapped_with(value, "blk", k) for k in range(2, count, 2)]


def gathered_blocks(value, count, zero):
    evens = even_blocks(value, count)
    return evens, [swapped_with(e, "blk", 1) for e in evens[:1]] + [
        swapped_with(e + zero, "blk", 1) for e in evens[1:]
    ]


def offset_of(index, count):
    return (2 * index) % count + (2 * index) // count


def after(value, *others):
    return lax.optimization_barrier((value,) + others)[0]


def half_swap(value, lane):
    return jnp.where((lane % 64) < 32, pltpu.roll(value, 96, 1), pltpu.roll(value, 32, 1))


def by_clip(clip, table, first, count):
    chosen = table[first : first + 1, :]
    for c in range(1, count):
        chosen = jnp.where(clip == c, table[first + c : first + c + 1, :], chosen)
    return chosen


def full(shape):
    return pl.BlockSpec(shape, lambda *_: (0,) * len(shape))


ANYWHERE = pl.BlockSpec(memory_space=pl.ANY)
SCALARS = pl.BlockSpec(memory_space=pltpu.SMEM)


KEPT = pl.BlockSpec(memory_space=pltpu.VMEM)


def in_hbm(value):
    if value.size * value.dtype.itemsize < 140000:
        return value
    return pltpu.with_memory_space_constraint(value, pltpu.HBM)


def all_in_hbm(values):
    return [in_hbm(v) for v in values]


def shape_of(shape, dtype=BF):
    size = jnp.dtype(dtype).itemsize
    for n in shape:
        size *= n
    return jax.ShapeDtypeStruct(shape, dtype) if size < 140000 else pltpu.HBM(shape, dtype)


def params(mib=24):
    return pltpu.CompilerParams(vmem_limit_bytes=mib * MIB)


def cost(flops, moved):
    return pl.CostEstimate(flops=flops, bytes_accessed=moved, transcendentals=0)


def prepare_kernel(
    count, me_ref, lengths_ref, steps_ref, table_ref, freq_ref, w_ref, b_ref, *refs
):
    silu, sems = refs[-2:]
    kept = (len(refs) - 9) // 2
    sources, targets = refs[:kept], refs[-2 - kept : -2]
    out_ref, silu_ref, clip_ref, cliprow_ref, cos_ref, sin_ref, marks_ref = refs[kept : kept + 7]
    clips = lengths_ref.shape[1]
    rows = cos_ref.shape[0] // count
    i = pl.program_id(0)

    def copies():
        return [
            pltpu.make_async_copy(
                source.at[:, pl.ds(0, target.shape[1])], target, sems.at[j]
            )
            for j, (source, target) in enumerate(zip(sources, targets))
        ]

    @pl.when(i == 0)
    def _():
        for copy in copies():
            copy.start()
        for c in range(clips):
            row = table_ref[pl.ds(steps_ref[0, c], 1), :]
            silu[c : c + 1, :] = row / (1.0 + jnp.exp(-row))
        silu_ref[...] = silu[:clips, :].astype(BF)

    out_ref[...] = dot_low(silu[...].astype(BF), w_ref[...])[:clips] + b_ref[...]

    @pl.when(i == 0)
    def _():
        def clip_and_start(places):
            clip, start, end = jnp.zeros_like(places), jnp.zeros_like(places), 0
            for c in range(clips):
                end = end + lengths_ref[0, c]
                clip = jnp.where(places >= end, c + 1, clip)
                start = jnp.where(places >= end, end, start)
            return clip, start

        for j in range(count):
            first = (me_ref[0] ^ offset_of(j, count)) * rows
            here = slice(j * rows, (j + 1) * rows)
            places = first + lax.broadcasted_iota(jnp.int32, (rows, LANES), 0)
            lane = lax.broadcasted_iota(jnp.int32, (rows, LANES), 1)
            clip, start = clip_and_start(places)
            angles = (places - start).astype(F32) * freq_ref[...]
            cos_ref[here, :] = jnp.cos(angles)
            sine = jnp.sin(angles)
            sin_ref[here, :] = jnp.where((lane % 64) < 32, -sine, sine)
            clip_ref[here, :] = clip[:, :1]
            places = first + lax.broadcasted_iota(jnp.int32, (1, rows), 1)
            cliprow_ref[:, here] = clip_and_start(places)[0]
            other = jnp.where((clip != lane) & (lane < clips), NEGATIVE, 0.0)
            marks_ref[here, :LANES] = other.astype(BF)
            marks_ref[here, LANES:] = jnp.where(clip == lane, 1.0, 0.0).astype(BF)

    @pl.when(i == pl.num_programs(0) - 1)
    def _():
        for copy in copies():
            copy.wait()


def prepare(me, lengths, steps, step_table, freqs, w_mod, b_mod, weights, own_rows, count):
    width = w_mod.shape[0]
    clips = lengths.shape[1]
    tile = width
    rows = own_rows * count
    shapes = [
        shape_of((clips, 2 * width), F32),
        shape_of((clips, width)),
        shape_of((rows, 1), jnp.int32),
        shape_of((1, rows), jnp.int32),
        shape_of((rows, LANES), F32),
        shape_of((rows, LANES), F32),
        shape_of((rows, 2 * LANES)),
    ]
    return pl.pallas_call(
        lambda *refs: prepare_kernel(count, *refs),
        grid=(2,),
        in_specs=[SCALARS] * 3
        + [
            full(step_table.shape),
            full(freqs.shape),
            pl.BlockSpec((width, tile), lambda i: (0, i)),
            pl.BlockSpec((1, tile), lambda i: (0, i)),
        ]
        + [ANYWHERE] * len(weights),
        out_specs=[pl.BlockSpec((clips, tile), lambda i: (0, i))]
        + [full(v.shape) for v in shapes[1:]]
        + [KEPT] * len(weights),
        out_shape=shapes + [pltpu.VMEM(w.shape, w.dtype) for w in weights],
        scratch_shapes=[pltpu.VMEM((8, width), F32), pltpu.SemaphoreType.DMA((len(weights),))],
        compiler_params=params(),
        cost_estimate=cost(4 * clips * width * width, 5 * width * width),
    )(me, lengths, steps, *all_in_hbm([step_table, freqs, w_mod, b_mod, *weights]))


def modulate_kernel(silu_ref, w_ref, b_ref, out_ref):
    out_ref[...] = dot_low(silu_ref[...], w_ref[...]) + b_ref[...]


def modulate(silu, w_mod, b_mod):
    clips, width = silu.shape
    return pl.pallas_call(
        modulate_kernel,
        grid=(4,),
        in_specs=[
            full(silu.shape),
            pl.BlockSpec((width, width), lambda i: (0, 2 + i)),
            pl.BlockSpec((1, width), lambda i: (0, 2 + i)),
        ],
        out_specs=pl.BlockSpec((clips, width), lambda i: (0, i)),
        out_shape=shape_of((clips, 4 * width), F32),
        compiler_params=params(),
        cost_estimate=cost(8 * clips * width * width, 8 * width * width),
    )(*all_in_hbm([silu, w_mod, b_mod]))


def project_kernel(clips, with_own, me_ref, clip_ref, mod_ref, b_ref, cos_ref, sin_ref, w, *refs):
    copies = []
    if not with_own:
        source, (w, sems), refs = w, refs[-2:], refs[:-2]
        width, step = source.shape[0], 512
        column = pl.ds(pl.multiple_of(me_ref[0] * LANES, LANES), LANES)
        copies = [pltpu.make_async_copy(source.at[:, column], w.at[:, pl.ds(0, LANES)], sems.at[0])]
        for i, start in enumerate(range(width, 3 * width, step)):
            here = pl.ds(start, step)
            copies.append(
                pltpu.make_async_copy(source.at[:, here], w.at[:, here], sems.at[1 + i])
            )
        for copy in copies:
            copy.start()
    blocks = refs[: len(refs) - (5 if with_own else 3)]
    h_ref, kv_ref, q_ref = refs[len(blocks) : len(blocks) + 3]
    rows, width = blocks[0].shape
    column = pl.multiple_of(me_ref[0] * LANES, LANES)
    if with_own:
        own_ref, passed_ref = refs[-2:]
        passed_ref[...] = blocks[-1][...]
        blocks = blocks[:-1]

    mod = mod_ref[...]
    for pair in range(len(blocks) // 2):
        here = slice(2 * pair * rows, 2 * (pair + 1) * rows)
        x = jnp.concatenate([blocks[2 * pair][...], blocks[2 * pair + 1][...]], axis=0).astype(F32)
        normed, _ = norm_parts(x)
        clip = clip_ref[here, :]
        scale = by_clip(clip, mod[:, width:], 0, clips)
        h_ref[here, :] = (normed * (1.0 + scale) + by_clip(clip, mod[:, :width], 0, clips)).astype(BF)

    h = h_ref[...]
    cosine, sine = cos_ref[...], sin_ref[...]
    lane = lax.broadcasted_iota(jnp.int32, cosine.shape, 1)

    def turned(piece, some):
        return piece * cosine[:some] + half_swap(piece, lane[:some]) * sine[:some]

    if with_own:
        heads = w[:, pl.ds(column, LANES)]
    else:
        copies[0].wait()
        heads = w[:, :LANES]
    part = dot_low(h, heads) + b_ref[:, pl.ds(column, LANES)]
    q_ref[...] = (turned(part, h.shape[0]) * 0.125).astype(BF)
    step = 2 * LANES
    for start in range(0 if with_own else width, 3 * width, step):
        some = rows if start < width else h.shape[0]
        if copies and (start - width) % 512 == 0:
            copies[1 + (start - width) // 512].wait()
        part = dot_low(h[:some], w[:, start : start + step]) + b_ref[:, start : start + step]
        for inner in range(0, step, LANES):
            piece = part[:, inner : inner + LANES]
            at = start + inner
            if start < 2 * width:
                piece = turned(piece, some)
            if start < width:
                own_ref[:, at : at + LANES] = (piece * 0.125).astype(BF)
            else:
                kv_ref[(at - width) // LANES] = piece.astype(BF)


def project(half, blocks, me, clip_col, modulation, w_qkv, b_qkv, cosine, sine, passed=None):
    with_own = passed is not None
    own_rows, width = blocks[0].shape
    rows = own_rows * len(blocks)
    clips = modulation.shape[0]
    out_shape = [
        shape_of((rows, width)),
        pltpu.VMEM((2 * width // LANES, rows, LANES), BF),
        shape_of((rows, LANES)),
    ]
    if with_own:
        out_shape += [shape_of((own_rows, width)), shape_of(passed.shape)]
        blocks = blocks + [passed]
    return pl.pallas_call(
        lambda *refs: project_kernel(clips, with_own, *refs),
        grid=(1,),
        in_specs=[
            SCALARS,
            pl.BlockSpec((rows, 1), lambda *_: (half, 0)),
            pl.BlockSpec((clips, 2 * width), lambda *_: (0, 0)),
            full(b_qkv.shape),
            pl.BlockSpec((rows, LANES), lambda *_: (half, 0)),
            pl.BlockSpec((rows, LANES), lambda *_: (half, 0)),
            KEPT if with_own else ANYWHERE,
        ]
        + [full(v.shape) for v in blocks],
        out_specs=[full(out_shape[0].shape), KEPT] + [full(o.shape) for o in out_shape[2:]],
        out_shape=out_shape,
        scratch_shapes=[]
        if with_own
        else [pltpu.VMEM(w_qkv.shape, BF), pltpu.SemaphoreType.DMA((1 + 4 * width // 1024,))],
        compiler_params=params(),
        cost_estimate=cost(4 * rows * width * width, 6 * MIB),
    )(me, *all_in_hbm([clip_col, modulation, b_qkv, cosine, sine]), w_qkv if with_own else in_hbm(w_qkv), *all_in_hbm(blocks))


def contract_last(left, right):
    return lax.dot_general(left, right, (((1,), (1,)), ((), ())), preferred_element_type=F32)


def head_rows(value):
    lane = lax.broadcasted_iota(jnp.int32, value.shape, 1)
    zero = jnp.zeros_like(value)
    return jnp.concatenate(
        [jnp.where(lane < 64, value, zero), jnp.where(lane < 64, zero, value)], axis=0
    )


def head_diagonal(value):
    rows = value.shape[1] // 2
    return jnp.concatenate([value[:64, :rows], value[64:, rows:]], axis=0).T


def softmax_over_keys(keys, queries):
    scores = contract_last(keys, queries)
    expo = jnp.exp(scores - jnp.max(scores, axis=0, keepdims=True))
    return expo, 1.0 / jnp.sum(expo, axis=0, keepdims=True)


def attend_kernel(keymark_ref, rowmark_ref, q_ref, ka_ref, kb_ref, *refs):
    sources, o_ref, targets = refs[:3], refs[3], refs[4:7]
    keys, values, queries, sems = refs[7:]
    half = ka_ref.shape[1]
    pair, pairs = pl.program_id(0), pl.num_programs(0)

    def copies():
        return [
            pltpu.make_async_copy(source, target, sems.at[j])
            for j, (source, target) in enumerate(zip(sources, targets))
        ]

    @pl.when(pair == 0)
    def _():
        for copy in copies():
            copy.start()

    @pl.when(pair == pairs - 1)
    def _():
        for copy in copies():
            copy.wait()

    @pl.when(pair == 0)
    def _():
        keys[:, LANES:] = keymark_ref[...]
        marks = rowmark_ref[...]
        queries[:, LANES:] = jnp.concatenate([marks, marks], axis=0)

    keys[:half, :LANES] = ka_ref[pair]
    keys[half:, :LANES] = kb_ref[pair]
    values[:half] = ka_ref[pairs + pair]
    values[half:] = kb_ref[pairs + pair]
    queries[:, :LANES] = head_rows(q_ref[...])
    expo, inverse = softmax_over_keys(keys[...], queries[...])
    turned = jnp.dot(values[...].T, expo.astype(BF), preferred_element_type=F32) * inverse
    o_ref[...] = head_diagonal(turned).astype(BF)


def attend(q, kv_a, kv_b, marks, weights):
    own_rows, width = q.shape
    rows = 2 * kv_a.shape[1]
    return pl.pallas_call(
        attend_kernel,
        grid=(width // LANES,),
        in_specs=[
            pl.BlockSpec((rows, LANES), lambda p: (0, 0)),
            pl.BlockSpec((own_rows, LANES), lambda p: (0, 1)),
            pl.BlockSpec((own_rows, LANES), lambda p: (0, p)),
            KEPT,
            KEPT,
        ]
        + [ANYWHERE] * 3,
        out_specs=[pl.BlockSpec((own_rows, LANES), lambda p: (0, p))] + [KEPT] * 3,
        out_shape=[shape_of((own_rows, width))] + [pltpu.VMEM(w.shape, BF) for w in weights],
        scratch_shapes=[
            pltpu.VMEM((rows, 2 * LANES), BF),
            pltpu.VMEM((rows, LANES), BF),
            pltpu.VMEM((2 * own_rows, 2 * LANES), BF),
            pltpu.SemaphoreType.DMA((3,)),
        ],
        compiler_params=params(),
        cost_estimate=cost(4 * own_rows * rows * width, MIB),
    )(*all_in_hbm([marks, marks, q]), kv_a, kv_b, *all_in_hbm(weights))


def probs_kernel(me_ref, keyclip_ref, rowclip_ref, qa_ref, qb_ref, ka_ref, kb_ref, *refs):
    out_ref, keys = refs[-3], refs[-1]
    i, blocks = pl.program_id(0), pl.num_programs(0)
    half = ka_ref.shape[1]

    @pl.when(i == 0)
    def _():
        keys[:half] = ka_ref[0]
        keys[half:] = kb_ref[0]

    query = jnp.where(i < blocks // 2, qa_ref[...], qb_ref[...])
    visible = keyclip_ref[...] == rowclip_ref[...]
    visible = jnp.concatenate([visible, visible], axis=1)
    scores = jnp.where(visible, contract_last(keys[...], head_rows(query)), NEGATIVE)
    expo = jnp.exp(scores - jnp.max(scores, axis=0, keepdims=True))
    out_ref[...] = expo * (1.0 / jnp.sum(expo, axis=0, keepdims=True))


def heads_probs(me, q_a, q_b, kv_a, kv_b, clip_col, clip_row, blocks, earlier, passed):
    half = kv_a.shape[1]
    rows = 2 * half
    own_rows = rows // blocks
    halfway = blocks // 2
    grid_spec = pltpu.PrefetchScalarGridSpec(
        num_scalar_prefetch=1,
        grid=(blocks,),
        in_specs=[
            pl.BlockSpec((rows, 1), lambda i, m: (0, 0)),
            pl.BlockSpec((1, own_rows), lambda i, m: (0, i)),
            pl.BlockSpec((own_rows, LANES), lambda i, m: (jnp.minimum(i, halfway - 1), 0)),
            pl.BlockSpec((own_rows, LANES), lambda i, m: (jnp.maximum(i - halfway, 0), 0)),
            pl.BlockSpec((1, half, LANES), lambda i, m: (m[0], 0, 0)),
            pl.BlockSpec((1, half, LANES), lambda i, m: (m[0], 0, 0)),
        ]
        + [ANYWHERE] * 2,
        out_specs=[pl.BlockSpec((rows, 2 * own_rows), lambda i, m: (0, i)), ANYWHERE],
        scratch_shapes=[pltpu.VMEM((rows, LANES), BF)],
    )
    return pl.pallas_call(
        probs_kernel,
        grid_spec=grid_spec,
        out_shape=[shape_of((rows, 2 * rows), F32), shape_of(passed.shape, passed.dtype)],
        input_output_aliases={8: 1},
        compiler_params=params(),
        cost_estimate=cost(4 * rows * rows * LANES, 9 * MIB),
    )(me, *all_in_hbm([clip_col, clip_row, q_a, q_b]), *all_in_hbm([kv_a, kv_b, earlier, passed]))


def attend_back_kernel(
    me_ref, p_ref, qa_ref, qb_ref, ka_ref, kb_ref, va_ref, vb_ref, do_ref, cos_ref, sin_ref, *refs
):
    out_ref, sent_ref = refs[-8:-6]
    dk_ref, dv_ref, values, keys_turned, d_probs = refs[-5:]
    i, blocks = pl.program_id(0), pl.num_programs(0)
    rows = do_ref.shape[1]
    half = ka_ref.shape[1]
    me = me_ref[0]

    @pl.when(i == 0)
    def _():
        dk_ref[...] = jnp.zeros_like(dk_ref)
        dv_ref[...] = jnp.zeros_like(dv_ref)
        for at, key_ref, value_ref in ((0, ka_ref, va_ref), (half, kb_ref, vb_ref)):
            values[at : at + half] = value_ref[0]
            keys_turned[:, at : at + half] = key_ref[0].T

    query = jnp.where(i < blocks // 2, qa_ref[...], qb_ref[...])
    q_two, up_two = head_rows(query), head_rows(do_ref[0])
    delta = jnp.zeros((1, 2 * rows), F32)
    step = 256
    for start in range(0, 2 * half, step):
        part = slice(start, start + step)
        probs_low = p_ref[part, :].astype(BF)
        dv_ref[part, :] += dot_low(probs_low, up_two)
        products = contract_last(values[part, :], up_two)
        d_probs[part, :] = products
        delta += jnp.sum(probs_low.astype(F32) * products, axis=0, keepdims=True)
    d_query = jnp.zeros((LANES, 2 * rows), F32)
    for start in range(0, 2 * half, step):
        part = slice(start, start + step)
        ds = (p_ref[part, :] * (d_probs[part, :] - delta)).astype(BF)
        dk_ref[part, :] += dot_low(ds, q_two)
        d_query += dot_low(keys_turned[:, part], ds)
    lane = lax.broadcasted_iota(jnp.int32, (rows, LANES), 1)

    def turned_back(value, where):
        return (value * cos_ref[where, :] - half_swap(value, lane) * sin_ref[where, :]).astype(BF)

    here = pl.ds(pl.multiple_of(i * rows, rows), rows)
    dq = turned_back(head_diagonal(d_query) * 0.125, here)
    out_ref[here, 0:LANES] = dq
    sent_ref[me ^ offset_of(i, blocks), :, 0:LANES] = dq

    @pl.when(i == blocks - 1)
    def _():
        @pl.loop(0, blocks)
        def _(j):
            there = pl.ds(pl.multiple_of(j * rows, rows), rows)
            dk = turned_back(dk_ref[there, :], there)
            dv = dv_ref[there, :].astype(BF)
            out_ref[there, LANES : 2 * LANES] = dk
            out_ref[there, 2 * LANES : 3 * LANES] = dv
            owner = me ^ offset_of(j, blocks)
            sent_ref[owner, :, LANES : 2 * LANES] = dk
            sent_ref[owner, :, 2 * LANES : 3 * LANES] = dv


def attend_back(me, probs, q_a, q_b, kv_a, kv_b, d_o, cosine, sine, passed, earlier):
    half = kv_a.shape[1]
    rows = 2 * half
    pairs = kv_a.shape[0] // 2
    blocks, own_rows, _ = d_o.shape
    halfway = blocks // 2
    grid_spec = pltpu.PrefetchScalarGridSpec(
        num_scalar_prefetch=1,
        grid=(blocks,),
        in_specs=[
            pl.BlockSpec((rows, 2 * own_rows), lambda i, m: (0, i)),
            pl.BlockSpec((own_rows, LANES), lambda i, m: (jnp.minimum(i, halfway - 1), 0)),
            pl.BlockSpec((own_rows, LANES), lambda i, m: (jnp.maximum(i - halfway, 0), 0)),
            pl.BlockSpec((1, half, LANES), lambda i, m: (m[0], 0, 0)),
            pl.BlockSpec((1, half, LANES), lambda i, m: (m[0], 0, 0)),
            pl.BlockSpec((1, half, LANES), lambda i, m: (pairs + m[0], 0, 0)),
            pl.BlockSpec((1, half, LANES), lambda i, m: (pairs + m[0], 0, 0)),
            pl.BlockSpec((1, own_rows, LANES), lambda i, m: (m[0] ^ offset_of(i, blocks), 0, 0)),
            pl.BlockSpec((rows, LANES), lambda i, m: (0, 0)),
            pl.BlockSpec((rows, LANES), lambda i, m: (0, 0)),
            ANYWHERE,
        ]
        + [ANYWHERE] * len(earlier),
        out_specs=[
            pl.BlockSpec((rows, 3 * LANES), lambda i, m: (0, 0)),
            pl.BlockSpec((blocks, own_rows, 3 * LANES), lambda i, m: (0, 0, 0)),
            ANYWHERE,
        ],
        scratch_shapes=[
            pltpu.VMEM((rows, LANES), F32),
            pltpu.VMEM((rows, LANES), F32),
            pltpu.VMEM((rows, LANES), BF),
            pltpu.VMEM((LANES, rows), BF),
            pltpu.VMEM((rows, 2 * own_rows), F32),
        ],
    )
    return pl.pallas_call(
        attend_back_kernel,
        grid_spec=grid_spec,
        out_shape=[
            shape_of((rows, 3 * LANES)),
            shape_of((blocks, own_rows, 3 * LANES)),
            shape_of(passed.shape, passed.dtype),
        ],
        input_output_aliases={11: 2},
        compiler_params=params(),
        cost_estimate=cost(8 * rows * rows * LANES, 12 * MIB),
    )(
        me,
        *all_in_hbm([probs, q_a, q_b]),
        *all_in_hbm([kv_a, kv_b, kv_a, kv_b]),
        d_o,
        *all_in_hbm([cosine, sine, passed, *earlier]),
    )


def norm_parts(inputs):
    centred = inputs - jnp.mean(inputs, axis=-1, keepdims=True)
    rstd = lax.rsqrt(jnp.mean(centred * centred, axis=-1, keepdims=True) + 1e-06)
    return centred * rstd, rstd


def norm_back(normed, rstd, gradient):
    return rstd * (
        gradient
        - jnp.mean(gradient, axis=-1, keepdims=True)
        - normed * jnp.mean(gradient * normed, axis=-1, keepdims=True)
    )


def dot_low(left, right):
    return jnp.dot(left, right, preferred_element_type=F32)


def dot_rows(left, right):
    return lax.dot_general(left, right, (((0,), (0,)), ((), ())), preferred_element_type=F32)


def gelu_parts(hidden):
    square = hidden * hidden
    tanh = jnp.tanh(0.7978845608028654 * hidden * (1.0 + 0.044715 * square))
    upper = 0.5 * (1.0 + tanh)
    slope = upper + 0.5 * hidden * (1.0 - tanh * tanh) * (
        0.7978845608028654 * (1.0 + 3.0 * 0.044715 * square)
    )
    return hidden * upper, slope


def high_low(value):
    high = value.astype(BF)
    return high, (value - high.astype(F32)).astype(BF)


class RowSums:
    def __init__(self, clip_row, clips):
        self.place = lax.broadcasted_iota(jnp.int32, (8, clip_row.shape[1]), 0)
        self.member = ((self.place == clip_row) & (self.place < clips)).astype(F32).astype(BF)

    def by_clip(self, value):
        high, low = high_low(value)
        return dot_low(
            jnp.concatenate([self.member, self.member], axis=1),
            jnp.concatenate([high, low], axis=0),
        )

    def whole(self, value, row):
        total = jnp.sum(value.astype(F32), axis=0, keepdims=True)
        place = lax.broadcasted_iota(jnp.int32, (8, value.shape[1]), 0)
        return jnp.where(place == row, total, 0.0)


def middle_kernel(
    clips, steps_ref, clipc_ref, clipr_ref, x_ref, dy_ref, o_ref, mod_ref, bo_ref, bu_ref, bd_ref,
    wo, wu, wd, *refs,
):
    out_ref, h2_ref, dx_ref, da_ref, do_ref, sums_ref = refs[-6:]
    width = x_ref.shape[1]
    ffn = wu.shape[1]
    clip = clipc_ref[...]

    def frame_rows(index):
        return by_clip(clip, mod_ref[:, (index - 2) * width : (index - 1) * width], 0, clips)

    gate_one, scale_two, gate_two = frame_rows(2), 1.0 + frame_rows(4), frame_rows(5)
    upstream = dy_ref[...].astype(F32)
    d_ffn = (gate_two * upstream).astype(BF)
    attn_out = dot_low(o_ref[...], wo[...]) + bo_ref[...]
    middle = x_ref[...].astype(F32) + gate_one * attn_out
    normed, rstd = norm_parts(middle)
    second = (normed * scale_two + frame_rows(3)).astype(BF)
    h2_ref[...] = second
    sums = RowSums(clipr_ref[...], clips)
    ffn_out = jnp.zeros(x_ref.shape, F32)
    d_second = jnp.zeros(x_ref.shape, F32)
    step = 512
    up_sums = []
    for start in range(0, ffn, step):
        here = slice(start, start + step)
        activated, slope = gelu_parts(dot_low(second, wu[:, here]) + bu_ref[:, here])
        ffn_out += dot_low(activated.astype(BF), wd[here, :])
        d_hidden = (contract_last(d_ffn, wd[here, :]) * slope).astype(BF)
        d_second += contract_last(d_hidden, wu[:, here])
        up_sums.append(sums.whole(d_hidden, clips))
    ffn_out += bd_ref[...]
    out_ref[...] = (middle + gate_two * ffn_out).astype(BF)
    d_middle = upstream + norm_back(normed, rstd, d_second * scale_two)
    dx_ref[...] = d_middle
    d_attn = (gate_one * d_middle).astype(BF)
    da_ref[...] = d_attn
    d_o = contract_last(d_attn, wo[...]).astype(BF)
    for k in range(width // LANES):
        do_ref[k] = d_o[:, k * LANES : (k + 1) * LANES]
    up_sums = jnp.concatenate(up_sums, axis=1)
    place = lax.broadcasted_iota(jnp.int32, (8, width), 0)
    lane = lax.broadcasted_iota(jnp.int32, (8, width), 1)
    steps = jnp.zeros((8, width), F32)
    for c in range(clips):
        here = (place == clips + 1) & (lane == c)
        steps = jnp.where(here, steps_ref[0, c].astype(F32), steps)
    sums_ref[:, :width] = (
        sums.by_clip(d_middle * attn_out) + sums.whole(d_attn, clips) + steps
    )
    sums_ref[:, width : 2 * width] = sums.by_clip(d_second) + up_sums[:, :width]
    sums_ref[:, 2 * width : 3 * width] = sums.by_clip(d_second * normed) + up_sums[:, width:]
    sums_ref[:, 3 * width :] = sums.by_clip(upstream * ffn_out) + sums.whole(d_ffn, clips)


def middle_part(
    steps, clip_col, clip_row, frames, cotangent, attended, modulation, b_out, b_up, b_down,
    w_out, w_up, w_down, earlier,
):
    rows, width = frames.shape
    clips = modulation.shape[0]
    small = [
        clip_col, clip_row, frames, cotangent, attended, modulation, b_out, b_up, b_down
    ]
    out_shape = [
        shape_of((rows, width)),
        shape_of((rows, width)),
        shape_of((rows, width), F32),
        shape_of((rows, width)),
        shape_of((width // LANES, rows, LANES)),
        shape_of((8, 4 * width), F32),
    ]
    return pl.pallas_call(
        lambda *refs: middle_kernel(clips, *refs),
        grid=(1,),
        in_specs=[SCALARS, full((rows, 1)), full((1, rows))]
        + [full(v.shape) for v in small[2:]]
        + [KEPT] * 3
        + [ANYWHERE] * len(earlier),
        out_specs=[full(o.shape) for o in out_shape],
        out_shape=out_shape,
        compiler_params=params(),
        cost_estimate=cost(20 * rows * width * width, 3 * MIB),
    )(steps, *all_in_hbm(small), w_out, w_up, w_down, *all_in_hbm(earlier))


def last_kernel(clips, clipc_ref, clipr_ref, x_ref, mod_ref, dx_ref, d_ref, w_hbm, *refs):
    passed = (len(refs) - 5) // 2
    out_ref, sums_ref = refs[passed : passed + 2]
    d_all, w, sems = refs[-3:]
    width = x_ref.shape[1]
    parts = 3
    copies = [
        pltpu.make_async_copy(
            w_hbm.at[:, pl.ds(i * width, width)], w.at[:, pl.ds(i * width, width)], sems.at[i]
        )
        for i in range(parts)
    ]
    for copy in copies:
        copy.start()
    for k in range(d_ref.shape[0]):
        for i in range(3):
            at = i * width + k * LANES
            d_all[:, at : at + LANES] = d_ref[k, :, i * LANES : (i + 1) * LANES]
    normed, rstd = norm_parts(x_ref[...].astype(F32))
    scale = 1.0 + by_clip(clipc_ref[...], mod_ref[...], 0, clips)
    d_first = jnp.zeros(x_ref.shape, F32)
    for i in range(parts):
        copies[i].wait()
        here = slice(i * width, (i + 1) * width)
        d_first += contract_last(d_all[:, here], w[:, here])
    out_ref[...] = (dx_ref[...] + norm_back(normed, rstd, d_first * scale)).astype(BF)
    sums = RowSums(clipr_ref[...], clips)
    sums_ref[:, :width] = (
        sums.by_clip(d_first)
        + sums.whole(d_all[:, :width], clips)
        + sums.whole(d_all[:, width : 2 * width], clips + 1)
    )
    sums_ref[:, width:] = sums.by_clip(d_first * normed) + sums.whole(d_all[:, 2 * width :], clips)


def last_part(clip_col, clip_row, frames, modulation, d_middle, d_own, w_qkv, passed):
    rows, width = frames.shape
    clips = modulation.shape[0]
    return pl.pallas_call(
        lambda *refs: last_kernel(clips, *refs),
        grid=(1,),
        in_specs=[
            full((rows, 1)),
            full((1, rows)),
            full(frames.shape),
            pl.BlockSpec((clips, width), lambda *_: (0, 1)),
            full(d_middle.shape),
            full(d_own.shape),
        ]
        + [ANYWHERE] * (1 + len(passed)),
        out_specs=[full((rows, width)), full((8, 2 * width))] + [ANYWHERE] * len(passed),
        out_shape=[shape_of((rows, width)), shape_of((8, 2 * width), F32)]
        + [shape_of(v.shape, v.dtype) for v in passed],
        input_output_aliases={7 + i: 2 + i for i in range(len(passed))},
        scratch_shapes=[
            pltpu.VMEM((rows, 3 * width), BF),
            pltpu.VMEM(w_qkv.shape, BF),
            pltpu.SemaphoreType.DMA((3,)),
        ],
        compiler_params=params(),
        cost_estimate=cost(6 * rows * width * width, 2 * MIB),
    )(
        *all_in_hbm([clip_col, clip_row, frames, modulation, d_middle]),
        d_own,
        *all_in_hbm([w_qkv, *passed]),
    )


def half_rows(core, value, kept_ref, sent_refs, at, columns):
    half = value.shape[0] // 2
    low, high = value[:half], value[half:]
    here = slice(at, at + half)
    kept_ref[here, columns] = jnp.where(core == 0, low, high)
    sent = jnp.where(core == 0, high, low).astype(BF)
    wide = sent_refs[0].shape[1]
    for i, ref in enumerate(sent_refs):
        start, stop = max(columns.start, i * wide), min(columns.stop, (i + 1) * wide)
        if start < stop:
            ref[here, start - i * wide : stop - i * wide] = sent[
                :, start - columns.start : stop - columns.start
            ]


def weights_kernel(clips, count, who_ref, clip_ref, gate_ref, bu_ref, wu_hbm, wd_hbm, *refs):
    kept_ref, sent_ref, (up_sum, down_sum, wu, wd, sems) = refs[-9], refs[-8:-5], refs[-5:]
    ha_ref, hb_ref, d_ref, mine_ref, theirs_ref = refs[:5]
    blocks = refs[5 : 5 + count]
    seconds, upstreams = blocks[: len(blocks) // 2], blocks[len(blocks) // 2 :]
    me, core = who_ref[0], who_ref[1]
    rows, width = seconds[0].shape
    part = up_sum.shape[1]
    columns = d_ref.shape[1]
    half = ha_ref.shape[0]
    own = pl.ds(pl.multiple_of((me // 2) * part, part), part)
    copies = [
        pltpu.make_async_copy(wu_hbm.at[:, own], wu, sems.at[0]),
        pltpu.make_async_copy(wd_hbm.at[own, :], wd, sems.at[1]),
    ]
    for copy in copies:
        copy.start()
    shard = part // 2

    step = 2 * LANES
    for start in range(0, width, step):
        here = slice(start, start + step)
        value = dot_rows(ha_ref[:, here], d_ref[:half, :])
        value += dot_rows(hb_ref[:, here], d_ref[half:, :])
        for inner in range(0, step, LANES):
            half_rows(
                core, value[inner : inner + LANES], kept_ref, sent_ref, (start + inner) // 2,
                slice(0, columns),
            )

    left = jnp.concatenate([mine_ref[:, :width], theirs_ref[:, :width]], axis=0)
    right = jnp.concatenate([mine_ref[:, width:], theirs_ref[:, width:]], axis=0)
    at = columns + 2 * part
    for start in range(0, width, step):
        value = dot_rows(left[:, start : start + step], right)
        for inner in range(0, step, LANES):
            half_rows(
                core, value[inner : inner + LANES], kept_ref, sent_ref, (start + inner) // 2,
                slice(at, at + width // 2),
            )

    for copy in copies:
        copy.wait()
    up_weights, down_weights = wu[...], wd[...]
    for pair in range(len(seconds) // 2):
        here = slice(2 * pair * rows, 2 * (pair + 1) * rows)
        second = jnp.concatenate([r[...] for r in seconds[2 * pair : 2 * pair + 2]], axis=0)
        upstream = jnp.concatenate([r[...] for r in upstreams[2 * pair : 2 * pair + 2]], axis=0)
        gate = by_clip(clip_ref[here, :], gate_ref[...], 0, clips)
        d_ffn = (gate * upstream.astype(F32)).astype(BF)
        activated, slope = gelu_parts(dot_low(second, up_weights) + bu_ref[:, own])
        d_hidden = (contract_last(d_ffn, down_weights) * slope).astype(BF)
        up, down = dot_rows(second, d_hidden), dot_rows(activated.astype(BF), d_ffn)
        if pair == 0:
            up_sum[...] = up
            down_sum[...] = down
        else:
            up_sum[...] += up
            down_sum[...] += down
    for y in range(2):
        mine = slice(y * shard, (y + 1) * shard)
        at = columns + 2 * y * shard
        for k in range(width // LANES):
            half_rows(
                core, up_sum[k * LANES : (k + 1) * LANES, mine], kept_ref, sent_ref,
                k * LANES // 2, slice(at, at + shard),
            )
        for c in range(width // shard):
            half_rows(
                core, down_sum[mine, c * shard : (c + 1) * shard], kept_ref, sent_ref,
                c * shard // 2, slice(at + shard, at + 2 * shard),
            )


def weights_part(who, clip_col, modulation, b_up, w_up, w_down, h1_a, h1_b, d_qkv, outs, seconds, upstreams):
    width, ffn = w_up.shape
    count = 2 * len(seconds)
    part = 2 * ffn // count
    clips = modulation.shape[0]
    shape = (width // 2, d_qkv.shape[1] + 2 * part + width // 2)
    rows = d_qkv.shape[0]
    arrays = [h1_a, h1_b, d_qkv, *outs, *seconds, *upstreams]
    return pl.pallas_call(
        lambda *refs: weights_kernel(clips, count, *refs),
        grid=(1,),
        in_specs=[
            SCALARS,
            pl.BlockSpec((rows // 2, 1), lambda *_: (0, 0)),
            pl.BlockSpec((clips, width), lambda *_: (0, 3)),
            full(b_up.shape),
            ANYWHERE,
            ANYWHERE,
        ]
        + [full(v.shape) for v in arrays],
        out_specs=[full(shape)] + [full((shape[0], shape[1] // 3))] * 3,
        out_shape=[shape_of(shape, F32)] + [shape_of((shape[0], shape[1] // 3))] * 3,
        scratch_shapes=[
            pltpu.VMEM((width, part), F32),
            pltpu.VMEM((part, width), F32),
            pltpu.VMEM((width, part), BF),
            pltpu.VMEM((part, width), BF),
            pltpu.SemaphoreType.DMA((2,)),
        ],
        compiler_params=params(36),
        cost_estimate=cost(7 * rows * width * part, 10 * MIB),
    )(who, *all_in_hbm([clip_col, modulation, b_up, w_up, w_down, *arrays]))


def table_kernel(first, clips, place_ref, *refs):
    parts, refs = refs[:4], refs[4:]
    if first:
        silu_ref, w_ref = refs[:2]
        dw_ref, db_ref, out_ref, total, sums = refs[-5:]
    else:
        silu_ref, w_ref, cond_ref, pick_ref, earlier_ref, _, _ = refs[:7]
        dw_ref, db_ref, out_ref, total, sums = refs[7:]
    i = pl.program_id(0)

    @pl.when(i == 0)
    def _():
        total[...] = jnp.zeros_like(total) if first else earlier_ref[...]

    for j, part in enumerate(parts):
        value = part[...]
        valid = lax.broadcasted_iota(jnp.int32, value.shape, 0) < clips
        sums[pl.ds(pl.multiple_of((place_ref[0] ^ j) * 8, 8), 8), :] = jnp.where(valid, value, 0.0)
    high, low = high_low(sums[...])
    total[...] += contract_last(w_ref[...], jnp.concatenate([high, low], axis=0))
    silu = silu_ref[...]
    dw_ref[...] = dot_rows(
        jnp.concatenate([silu, silu], axis=0), jnp.concatenate([high, low], axis=0)
    )
    db_ref[...] = jnp.sum(sums[...], axis=0, keepdims=True)

    @pl.when(i == pl.num_programs(0) - 1)
    def _():
        if first:
            out_ref[...] = total[...]
        else:
            rows = high.shape[0]
            d_silu = total[:, :rows] + total[:, rows:]
            cond = cond_ref[...]
            gate = 1.0 / (1.0 + jnp.exp(-cond))
            d_cond = d_silu.T * (gate * (1.0 + cond * (1.0 - gate)))
            d_high, d_low = high_low(d_cond)
            lowest = (d_cond - d_high.astype(F32) - d_low.astype(F32)).astype(BF)
            pick = pick_ref[...].astype(BF)
            out_ref[...] = dot_rows(pick, d_high) + dot_rows(pick, d_low) + dot_rows(pick, lowest)


def table_part(place, sums, silu, w_mod, column, clips, rest=None, earlier=()):
    columns = sums[0].shape[1]
    width = w_mod.shape[0]
    all_columns = 6 * width
    rows, own = silu.shape
    tile = 2048
    skip = column // tile
    first = rest is None
    shapes = [
        shape_of((own, all_columns), F32),
        shape_of((1, all_columns), F32),
        shape_of((width, 2 * rows), F32),
    ]
    in_specs = [SCALARS] + [pl.BlockSpec((8, tile), lambda i: (0, i))] * 4 + [
        pl.BlockSpec((rows, own), lambda i: (0, 0)),
        pl.BlockSpec((width, tile), lambda i: (0, skip + i)),
    ]
    args = [place, *all_in_hbm([*sums, silu]), in_hbm(w_mod)]
    aliases = {}
    if first:
        in_specs += [ANYWHERE] * len(earlier)
        args += all_in_hbm(earlier)
    else:
        condition, pick, earlier, d_w, d_b = rest
        in_specs += [
            pl.BlockSpec((rows, width), lambda i: (0, 0)),
            pl.BlockSpec(pick.shape, lambda i: (0, 0)),
            pl.BlockSpec((width, 2 * rows), lambda i: (0, 0)),
            ANYWHERE,
            ANYWHERE,
        ]
        args += all_in_hbm([condition, pick, earlier, d_w, d_b])
        aliases = {10: 0, 11: 1}
        shapes[2] = shape_of((pick.shape[1], width), F32)
    return pl.pallas_call(
        lambda *refs: table_kernel(first, clips, *refs),
        grid=(columns // tile,),
        in_specs=in_specs,
        out_specs=[
            pl.BlockSpec((own, tile), lambda i: (0, skip + i)),
            pl.BlockSpec((1, tile), lambda i: (0, skip + i)),
            pl.BlockSpec(shapes[2].shape, lambda i: (0, 0)),
        ],
        out_shape=shapes,
        scratch_shapes=[
            pltpu.VMEM((width, 2 * rows), F32),
            pltpu.VMEM((rows, tile), F32),
        ],
        input_output_aliases=aliases,
        compiler_params=params(),
        cost_estimate=cost(rows * width, width),
    )(*args)


def in_order(bit, mine, other):
    return jnp.stack([jnp.where(bit == 0, mine, other), jnp.where(bit == 0, other, mine)])


def batch_parts(sums):
    return [sums] + [swapped_with(sums, "batch", k) for k in range(1, 4)]


def share_kernel(columns, part, who_ref, kept_ref, *refs):
    others = refs[:3]
    own_ref, x_ref, y_ref, both_ref, out_ref = refs[-5:]
    far, odd = who_ref[2] // 2 == 1, who_ref[0] % 2 == 1
    rows = own_ref.shape[1]
    first, second = slice(columns, columns + part), slice(columns + part, columns + 2 * part)
    for k in range(own_ref.shape[0]):
        here = slice(2 * k * rows, 2 * (k + 1) * rows)
        other = jnp.concatenate([ref[here, :] for ref in others], axis=1)
        value = kept_ref[here, :] + other.astype(F32)
        low, high = value[:rows], value[rows:]
        near, away = jnp.where(far, high, low), jnp.where(far, low, high)
        own_ref[k, :, :columns] = near[:, :columns]
        own_ref[k, :, columns:] = jnp.where(odd, near[:, second], near[:, first])
        y_ref[k] = jnp.where(odd, near[:, first], near[:, second]).astype(BF)
        x_ref[k, :, :columns] = away[:, :columns].astype(BF)
        x_ref[k, :, columns:] = jnp.where(odd, away[:, second], away[:, first]).astype(BF)
        both_ref[k] = jnp.where(odd, away[:, first], away[:, second]).astype(BF)
        out_ref[k] = jnp.concatenate(
            [low[:, columns + 2 * part :], high[:, columns + 2 * part :]], axis=1
        ).astype(BF)


def share(who, kept, others, count, columns, part):
    rows = kept.shape[0] // count // 2
    width = 2 * (kept.shape[1] - columns - 2 * part)
    shapes = [
        shape_of((count, rows, columns + part), F32),
        shape_of((count, rows, columns + part)),
        shape_of((count, rows, part)),
        shape_of((count, rows, part)),
        shape_of((count, rows, width)),
    ]
    return pl.pallas_call(
        lambda *refs: share_kernel(columns, part, *refs),
        grid=(1,),
        in_specs=[SCALARS, full(kept.shape)] + [full(v.shape) for v in others],
        out_specs=[full(v.shape) for v in shapes],
        out_shape=shapes,
        compiler_params=params(),
        cost_estimate=cost(0, 8 * MIB),
    )(who, in_hbm(kept), *others)


def gather_sums_kernel(columns, own_ref, x_ref, y_ref, both_ref, out_ref, *refs):
    sent_ref, down_ref = refs[-2:]
    count, rows, _ = own_ref.shape
    shard = y_ref.shape[2] // 2
    ready = columns + shard
    for k in range(count):
        from_x = x_ref[k].astype(F32)
        sent_ref[k, :, :columns] = (own_ref[k, :, :columns] + from_x[:, :columns]).astype(BF)
        value = (own_ref[k, :, columns:] + from_x[:, columns:]) + (
            y_ref[k].astype(F32) + both_ref[k].astype(F32)
        )
        sent_ref[k, :, columns:ready] = value[:, :shard].astype(BF)
        group, at = k % 2, k // 2 * shard
        down_ref[group * rows : (group + 1) * rows, at : at + shard] = value[:, shard:].astype(BF)
        sent_ref[k, :, ready:] = out_ref[k]


def gather_sums(own, from_x, from_y, from_both, out_parts, columns, passed):
    count, rows, _ = own.shape
    width = out_parts.shape[2]
    args = [own, from_x, from_y, from_both, out_parts]
    shapes = [
        shape_of((count, rows, columns + from_y.shape[2] // 2 + width)),
        shape_of((2 * rows, width)),
    ]
    return pl.pallas_call(
        lambda *refs: gather_sums_kernel(columns, *refs),
        grid=(1,),
        in_specs=[full(v.shape) for v in args] + [ANYWHERE] * len(passed),
        out_specs=[ANYWHERE] * len(passed) + [full(v.shape) for v in shapes],
        out_shape=[shape_of(v.shape, v.dtype) for v in passed] + shapes,
        input_output_aliases={5 + i: i for i in range(len(passed))},
        compiler_params=params(),
        cost_estimate=cost(0, 4 * MIB),
    )(in_hbm(own), from_x, from_y, from_both, *all_in_hbm([out_parts, *passed]))


def rows_kernel(columns, rows_ref, *refs):
    out_ref = refs[-1]
    count, rows, wide = rows_ref.shape
    width = out_ref.shape[1]
    shard = wide - width - columns
    total = jnp.zeros((rows, width), F32)
    for k in range(count):
        for i in range(columns // LANES):
            out_ref[i * rows : (i + 1) * rows, k * LANES : (k + 1) * LANES] = rows_ref[
                k, :, i * LANES : (i + 1) * LANES
            ]
        piece = columns // LANES + k * shard // width
        at = k * shard % width
        out_ref[piece * rows : (piece + 1) * rows, at : at + shard] = rows_ref[
            k, :, columns : columns + shard
        ]
        total += rows_ref[k, :, columns + shard :].astype(F32)
    piece = columns // LANES + count * shard // width
    out_ref[piece * rows :, :] = total.astype(BF)


def gather_rows(rows_mine, width, columns, passed, earlier):
    count, rows, wide = rows_mine.shape
    shard = wide - width - columns
    shape = ((columns // LANES + count * shard // width + 1) * rows, width)
    return pl.pallas_call(
        lambda *refs: rows_kernel(columns, *refs),
        grid=(1,),
        in_specs=[full(rows_mine.shape), ANYWHERE, ANYWHERE],
        out_specs=[ANYWHERE, full(shape)],
        out_shape=[shape_of(passed.shape, passed.dtype), shape_of(shape)],
        input_output_aliases={1: 0},
        compiler_params=params(),
        cost_estimate=cost(0, 2 * MIB),
    )(rows_mine, *all_in_hbm([passed, earlier]))


def assemble_kernel(ffn, who_ref, *refs):
    qkv_ref, out_ref, up_ref, down_ref = refs[-4:]
    width = out_ref.shape[1]
    rows = qkv_ref.shape[0] // 4
    for j, (ref, own_down) in enumerate(zip(refs[:4], refs[4:8])):
        owner = who_ref[2] ^ j
        core, far = owner % 2, owner // 2
        at = pl.multiple_of(core * 2 * rows + far * rows, rows)
        piece = 0
        for target, count in ((qkv_ref, 3), (up_ref, ffn // width)):
            for i in range(count):
                here = slice(piece * rows, (piece + 1) * rows)
                target[pl.ds(at, rows), i * width : (i + 1) * width] = ref[here, :].astype(F32)
                piece += 1
        for g in range(2):
            here = slice(g * rows, (g + 1) * rows)
            there = pl.multiple_of(core * 4 * rows + g * 2 * rows + far * rows, rows)
            down_ref[pl.ds(there, rows), :] = own_down[here, :].astype(F32)
        part = width // 2
        column = pl.multiple_of(far * part, part)
        for g in range(2):
            there = pl.multiple_of(core * 2 * rows + g * rows, rows)
            out_ref[pl.ds(there, rows), pl.ds(column, part)] = ref[
                piece * rows : (piece + 1) * rows, g * part : (g + 1) * part
            ].astype(F32)


def assemble(who, parts, own_rows, ffn):
    width = parts[0].shape[1]
    shapes = [
        shape_of((own_rows, 3 * width), F32),
        shape_of((own_rows, width), F32),
        shape_of((own_rows, ffn), F32),
        shape_of((2 * own_rows, width), F32),
    ]
    return pl.pallas_call(
        lambda *refs: assemble_kernel(ffn, *refs),
        grid=(1,),
        in_specs=[SCALARS] + [full(v.shape) for v in parts],
        out_specs=[full(o.shape) for o in shapes],
        out_shape=shapes,
        compiler_params=params(),
        cost_estimate=cost(0, 6 * MIB),
    )(who, *parts)


def heads_body(
    frames, step_table, clip_lengths, clip_steps, w_mod, b_mod, w_qkv, b_qkv, w_out, b_out,
    w_up, b_up, w_down, b_down, cotangent,
):
    own_rows, width = frames.shape
    ffn = w_up.shape[1]
    count = lax.axis_size("blk")
    me = lax.axis_index("blk")
    place = lax.axis_index("batch")
    core, far = place % 2, place // 2
    who = jnp.stack([me, core, place])
    clips = clip_lengths.shape[1]
    rows = own_rows * count

    head_size = width // HEADS
    half = head_size // 2
    lane = jnp.arange(LANES, dtype=jnp.int32)
    freqs = 10000.0 ** (-2.0 * (lane % half).astype(F32) / head_size)
    rows_of_table = jnp.arange(step_table.shape[0], dtype=jnp.int32)
    (
        modulation, silu_own, clip_col, clip_row, cosine, sine, marks, kept_qkv,
    ) = prepare(
        me[None], clip_lengths, clip_steps, step_table, freqs[None, :], w_mod, b_mod[None, :],
        [w_qkv], own_rows, count,
    )
    modulation_two = modulate(silu_own, w_mod, b_mod[None, :])
    evens, odds = gathered_blocks(frames, count, (modulation_two[0, 0] * 0.0).astype(BF))

    shared = (b_qkv[None, :], cosine, sine)
    first = (me[None], clip_col, modulation)
    h1_a, kv_a, q_a, q_own, later = project(0, evens, *first, kept_qkv, *shared, cotangent)
    upstreams = even_blocks(later, count)
    h1_b, kv_b, q_b = project(1, odds, *first, w_qkv, *shared)
    attended, kept_out, kept_up, kept_down = attend(
        q_own, kv_a, kv_b, marks, [w_out, w_up, w_down]
    )
    result, second, d_middle, d_attn, d_o, sums_two = middle_part(
        clip_steps, clip_col, clip_row, frames, cotangent, attended, modulation_two,
        b_out[None, :], b_up[None, :], b_down[None, :], kept_out, kept_up, kept_down,
        upstreams,
    )
    d_o = lax.all_to_all(d_o, "blk", 0, 0, tiled=True)
    seconds = even_blocks(second, count)
    probs, d_attn = heads_probs(
        me[None], q_a, q_b, kv_a, kv_b, clip_col, clip_row, count, d_middle, d_attn
    )
    sums_two = sums_two + swapped_with(sums_two, "blk", 1)
    sums_two = sums_two + swapped_with(sums_two, "blk", 2)

    wide = width // 2
    da_low, da_high = d_attn[:, :wide], d_attn[:, wide:]
    out_sent = jnp.concatenate([attended, jnp.where(far == 0, da_high, da_low)], axis=1)
    out_kept = jnp.concatenate([attended, jnp.where(far == 0, da_low, da_high)], axis=1)
    out_sent = swapped_with(out_sent, "batch", 2)

    d_qkv, d_qkv_sent, sums_two = attend_back(
        me[None], probs, q_a, q_b, kv_a, kv_b, d_o, cosine, sine, sums_two, seconds[:3]
    )
    d_own = lax.all_to_all(d_qkv_sent, "blk", 0, 0, tiled=True)
    kept, *sent = weights_part(
        who, clip_col, modulation_two, b_up[None, :], w_up, w_down, h1_a, h1_b, d_qkv,
        [out_kept, out_sent], seconds, upstreams,
    )
    own_sums, for_x, for_y, for_both, out_parts = share(
        who, kept, [swapped_with(v, "batch", 1) for v in sent], count, 3 * LANES, 2 * ffn // count
    )

    d_inputs, sums_one, own_sums, sums_two = last_part(
        clip_col, clip_row, frames, modulation, d_middle, d_own, w_qkv,
        [own_sums, sums_two],
    )
    sums_one = sums_one + swapped_with(sums_one, "blk", 2)
    sums_two = sums_two + swapped_with(sums_two, "blk", 4)

    pairs = [
        (b * count + k, (b ^ 2) * count + (k ^ 1)) for b in range(4) for k in range(count)
    ]
    sums_one, sums_two, sent, down_rows = gather_sums(
        own_sums,
        swapped_with(for_x, "batch", 2),
        swapped_with(for_y, "blk", 1),
        lax.ppermute(for_both, ("batch", "blk"), pairs),
        out_parts,
        3 * LANES,
        [sums_one, sums_two],
    )
    rows_mine = lax.all_to_all(sent, "blk", 0, 0, tiled=True)
    sums_one = sums_one + swapped_with(sums_one, "blk", 1)
    sums_two = batch_parts(sums_two)
    steps_all = jnp.stack([v[clips + 1, :clips] for v in sums_two]) * (1.0 / count)
    steps_all = steps_all[place ^ jnp.arange(4, dtype=jnp.int32)].astype(jnp.int32)
    pick_all = (steps_all[:, :, None] == rows_of_table[None, None, :]).astype(F32)
    pick_all = jnp.pad(pick_all, ((0, 0), (0, 8 - clips), (0, 0))).reshape(32, -1)
    condition_all = exact_dot(pick_all, step_table)
    silu_all = jax.nn.silu(condition_all).astype(BF)
    silu_cols = lax.dynamic_slice_in_dim(silu_all, me * own_rows, own_rows, 1)
    d_w_mod, d_b_mod, d_silu = table_part(
        place[None], sums_two, silu_cols, w_mod, 2 * width, clips
    )
    sums_one, mine = gather_rows(rows_mine, width, 3 * LANES, sums_one, d_silu)
    sums_one = batch_parts(sums_one + swapped_with(sums_one, "blk", 4))
    d_w_mod, d_b_mod, d_table = table_part(
        place[None], sums_one, silu_cols, w_mod, 0, clips,
        (condition_all, pick_all, d_silu, d_w_mod, d_b_mod),
    )

    def batch_total(parts):
        return (parts[0] + parts[1]) + (parts[2] + parts[3])

    bias_two = batch_total([v[clips] for v in sums_two])
    bias_one = batch_total([v[clips : clips + 2] for v in sums_one])
    d_b_qkv = jnp.concatenate(
        [bias_one[0, :width], bias_one[1, :width], bias_one[0, width:]], axis=0
    )
    d_b_out, d_b_up, d_b_down = jnp.split(bias_two, [width, width + ffn])

    def everyone(value):
        other = swapped_with(value, "batch", 2)
        return [value, swapped_with(value, "batch", 1), other, swapped_with(other, "batch", 1)]

    d_w_qkv, d_w_out, d_w_up, d_w_down = assemble(
        who, everyone(mine) + everyone(down_rows), own_rows, ffn
    )

    return (
        result,
        d_inputs,
        d_table,
        d_w_mod,
        d_b_mod[0],
        d_w_qkv,
        d_b_qkv,
        d_w_out,
        d_b_out,
        d_w_up,
        d_b_up,
        d_w_down,
        d_b_down,
    )


def solution(mesh):
    blk = mesh.shape["blk"]
    heads_fit = HEADS == 2 * blk and mesh.shape["batch"] == 4
    chosen = heads_body if heads_fit else ring_body
    placed = (
        P(("batch", "blk"), None),
        P(),
        P("batch", None),
        P("batch", None),
        P(),
        P(),
        P(),
        P(),
        P(),
        P(),
        P(),
        P(),
        P(),
        P(),
        P(("batch", "blk"), None),
    )
    return jax.shard_map(
        chosen,
        mesh=mesh,
        in_specs=placed,
        out_specs=(
            P(("batch", "blk"), None),
            P(("batch", "blk"), None),
            P(),
            P("blk", None),
            P(),
            P("blk", None),
            P(),
            P("blk", None),
            P(),
            P("blk", None),
            P(),
            P("blk", None),
            P(),
        ),
        check_vma=False,
    )
```

```python
import jax
import jax.numpy as jnp
from jax import lax
from jax.experimental import pallas as pl
from jax.experimental.pallas import tpu as pltpu
from jax.sharding import PartitionSpec as P

HEADS = 16


HIGH_PRECISION = lax.Precision.HIGHEST
NEGATIVE = -1e30


def passed_along(value, axis, by):
    size = lax.axis_size(axis)
    return lax.ppermute(value, axis, [(i, (i + by) % size) for i in range(size)])


def norm_rows(inputs):
    average = jnp.mean(inputs, axis=-1, keepdims=True)
    centred = inputs - average
    variance = jnp.mean(centred * centred, axis=-1, keepdims=True)
    return centred * lax.rsqrt(variance + 1e-06)


def modulated(inputs, shift_part, scale_part):
    return norm_rows(inputs) * (1.0 + scale_part) + shift_part


def rotate(vectors, cosine, sine_part):
    half_size = vectors.shape[-1] // 2
    first_half = vectors[..., :half_size]
    second_half = vectors[..., half_size:]
    return jnp.concatenate(
        [
            first_half * cosine - second_half * sine_part,
            second_half * cosine + first_half * sine_part,
        ],
        axis=-1,
    )


def exact_dot(left_side, right_side):
    return jnp.dot(left_side, right_side, precision=HIGH_PRECISION)


def clip_index(positions, clip_ends):
    return jnp.sum((clip_ends[None, :] <= positions[:, None]).astype(jnp.int32), axis=1)


def attend_block(queries, key_rows, value_rows, visible, carry_state, scale):
    running_max, denominator, numerator = carry_state
    scores = (
        jnp.einsum("qhd,khd->hqk", queries, key_rows, preferred_element_type=jnp.float32) * scale
    )
    scores = jnp.where(visible[None], scores, NEGATIVE)
    new_max = jnp.maximum(running_max, jnp.max(scores, axis=-1))
    factor = jnp.exp(running_max - new_max)
    probabilities = jnp.where(visible[None], jnp.exp(scores - new_max[..., None]), 0.0)
    denominator = factor * denominator + jnp.sum(probabilities, axis=-1)
    numerator = numerator * jnp.transpose(factor)[:, :, None] + jnp.einsum(
        "hqk,khd->qhd",
        probabilities.astype(jnp.bfloat16),
        value_rows,
        preferred_element_type=jnp.float32,
    )
    return (new_max, denominator, numerator)


def grad_block(queries, upstream, log_total, row_delta, key_rows, value_rows, visible, scale):
    scores = (
        jnp.einsum("qhd,khd->hqk", queries, key_rows, preferred_element_type=jnp.float32) * scale
    )
    probabilities = jnp.where(
        visible[None],
        jnp.exp(jnp.where(visible[None], scores, NEGATIVE) - log_total[..., None]),
        0.0,
    )
    d_probs = jnp.einsum("qhd,khd->hqk", upstream, value_rows, preferred_element_type=jnp.float32)
    d_scores = (probabilities * (d_probs - row_delta[..., None])).astype(jnp.bfloat16)
    d_query = scale * jnp.einsum(
        "hqk,khd->qhd", d_scores, key_rows, preferred_element_type=jnp.float32
    )
    d_key = scale * jnp.einsum(
        "hqk,qhd->khd", d_scores, queries, preferred_element_type=jnp.float32
    )
    d_value = jnp.einsum(
        "hqk,qhd->khd",
        probabilities.astype(jnp.bfloat16),
        upstream,
        preferred_element_type=jnp.float32,
    )
    return (d_query, d_key, d_value)


def pass_key_grads(gradients):
    return (
        passed_along(gradients[0].astype(jnp.bfloat16), "blk", 1).astype(jnp.float32),
        passed_along(gradients[1].astype(jnp.bfloat16), "blk", 1).astype(jnp.float32),
    )


def ring_body(
    frames,
    step_table,
    clip_lengths,
    clip_steps,
    w_mod,
    b_mod,
    w_qkv,
    b_qkv,
    w_out,
    b_out,
    w_up,
    b_up,
    w_down,
    b_down,
    cotangent,
):
    frame_count, model_width = frames.shape
    ffn_width = w_up.shape[1]
    cycle_size = lax.axis_size("blk")
    cycle_place = lax.axis_index("blk")
    head_count = HEADS
    head_size = model_width // head_count
    scale = head_size ** (-0.5)
    lengths = clip_lengths[0]
    steps = clip_steps[0]
    clip_count = lengths.shape[0]
    clip_ends = jnp.cumsum(lengths)
    clip_starts = clip_ends - lengths
    local_rows = jnp.arange(frame_count, dtype=jnp.int32)
    places = cycle_place * frame_count + local_rows
    clip_own = clip_index(places, clip_ends)
    member = (clip_own[:, None] == jnp.arange(clip_count, dtype=jnp.int32)[None, :]).astype(
        jnp.float32
    )
    offsets = jnp.sum(member * clip_starts[None, :].astype(jnp.float32), axis=1)
    freqs = 10000.0 ** (-2.0 * jnp.arange(head_size // 2, dtype=jnp.float32) / head_size)
    angles = (places.astype(jnp.float32) - offsets)[:, None] * freqs[None, :]
    cosine = jnp.cos(angles)[:, None, :]
    sine_part = jnp.sin(angles)[:, None, :]

    def clip_of(turn_index):
        source = (cycle_place - turn_index) % cycle_size
        return clip_index(source * frame_count + local_rows, clip_ends)

    step_pick = (
        steps[:, None] == jnp.arange(step_table.shape[0], dtype=jnp.int32)[None, :]
    ).astype(jnp.float32)
    condition = exact_dot(step_pick, step_table)
    silu_low = jax.nn.silu(condition).astype(jnp.bfloat16)
    modulation = jnp.dot(silu_low, w_mod, preferred_element_type=jnp.float32) + b_mod
    frame_mod = exact_dot(member, modulation)
    shift_one, scale_one, gate_one, shift_two, scale_two, gate_two = jnp.split(frame_mod, 6, axis=1)
    inputs = frames.astype(jnp.float32)
    first, first_back = jax.vjp(modulated, inputs, shift_one, scale_one)
    first_low = first.astype(jnp.bfloat16)
    projected = jnp.dot(first_low, w_qkv, preferred_element_type=jnp.float32) + b_qkv
    query_part, key_part, value_part = jnp.split(projected, 3, axis=1)

    def spin(query_lin, key_lin):
        return (
            rotate(query_lin.reshape(frame_count, head_count, head_size), cosine, sine_part),
            rotate(key_lin.reshape(frame_count, head_count, head_size), cosine, sine_part),
        )

    (query_rot, key_rot), spin_back = jax.vjp(spin, query_part, key_part)
    queries = query_rot.astype(jnp.bfloat16)
    key_rows = key_rot.astype(jnp.bfloat16)
    value_rows = value_part.reshape(frame_count, head_count, head_size).astype(jnp.bfloat16)

    def forward_step(turn_index, key_value, carry_state):
        visible = clip_own[:, None] == clip_of(turn_index)[None, :]
        return attend_block(queries, key_value[0], key_value[1], visible, carry_state, scale)

    def forward_turn(turn_index, carry):
        key_value, carry_state = carry
        carry_state = forward_step(turn_index, key_value, carry_state)
        key_value = passed_along((key_value[0], key_value[1]), "blk", 1)
        return (key_value, carry_state)

    initial = (
        jnp.full((head_count, frame_count), NEGATIVE, jnp.float32),
        jnp.zeros((head_count, frame_count), jnp.float32),
        jnp.zeros((frame_count, head_count, head_size), jnp.float32),
    )
    key_value, carry_state = lax.fori_loop(
        0, cycle_size - 1, forward_turn, ((key_rows, value_rows), initial)
    )
    running_max, denominator, numerator = forward_step(cycle_size - 1, key_value, carry_state)
    attended = numerator / jnp.transpose(denominator)[:, :, None]
    log_total = running_max + jnp.log(denominator)
    attended_low = attended.reshape(frame_count, model_width).astype(jnp.bfloat16)
    attn_out = jnp.dot(attended_low, w_out, preferred_element_type=jnp.float32) + b_out
    middle = inputs + gate_one * attn_out
    second, second_back = jax.vjp(modulated, middle, shift_two, scale_two)
    second_low = second.astype(jnp.bfloat16)
    hidden = jnp.dot(second_low, w_up, preferred_element_type=jnp.float32) + b_up
    activated, gelu_back = jax.vjp(
        lambda values_in: jax.nn.gelu(values_in, approximate=True), hidden
    )
    activated_low = activated.astype(jnp.bfloat16)
    ffn_out = jnp.dot(activated_low, w_down, preferred_element_type=jnp.float32) + b_down
    result = middle + gate_two * ffn_out
    upstream_y = cotangent.astype(jnp.float32)
    d_ffn = (gate_two * upstream_y).astype(jnp.bfloat16)
    d_gate_two = upstream_y * ffn_out
    d_act = jnp.dot(d_ffn, w_down.T, preferred_element_type=jnp.float32)
    d_hidden = gelu_back(d_act)[0].astype(jnp.bfloat16)
    d_second = jnp.dot(d_hidden, w_up.T, preferred_element_type=jnp.float32)
    d_middle_norm, d_shift_two, d_scale_two = second_back(d_second)
    d_middle = upstream_y + d_middle_norm
    d_attn = (gate_one * d_middle).astype(jnp.bfloat16)
    d_gate_one = d_middle * attn_out
    d_attended = jnp.dot(d_attn, w_out.T, preferred_element_type=jnp.float32).astype(jnp.bfloat16)
    d_attended = d_attended.reshape(frame_count, head_count, head_size)
    row_delta = jnp.transpose(jnp.sum(d_attended.astype(jnp.float32) * attended, axis=-1))
    zeros_three = jnp.zeros((frame_count, head_count, head_size), jnp.float32)

    def key_step(turn_index, key_value, owed):
        visible = clip_own[:, None] == clip_of(turn_index)[None, :]
        d_query, d_key, d_value = grad_block(
            queries, d_attended, log_total, row_delta, key_value[0], key_value[1], visible, scale
        )
        return (owed[0] + d_query, (owed[1][0] + d_key, owed[1][1] + d_value))

    def key_turn(turn_index, carry):
        key_value, owed = carry
        d_query_sum, gradients = key_step(turn_index, key_value, owed)
        key_value = passed_along((key_value[0], key_value[1]), "blk", 1)
        gradients = pass_key_grads(gradients)
        return (key_value, (d_query_sum, gradients))

    key_value, owed = lax.fori_loop(
        0,
        cycle_size - 1,
        key_turn,
        ((key_rows, value_rows), (zeros_three, (zeros_three, zeros_three))),
    )
    d_query_rot, gradients = key_step(cycle_size - 1, key_value, owed)
    d_key_rot, d_value_all = pass_key_grads(gradients)
    d_query_lin, d_key_lin = spin_back((d_query_rot, d_key_rot))
    d_projected = jnp.concatenate(
        [d_query_lin, d_key_lin, d_value_all.reshape(frame_count, model_width)], axis=1
    ).astype(jnp.bfloat16)
    d_first = jnp.dot(d_projected, w_qkv.T, preferred_element_type=jnp.float32)
    d_input_norm, d_shift_one, d_scale_one = first_back(d_first)
    d_inputs = d_middle + d_input_norm
    d_frame_mod = jnp.concatenate(
        [d_shift_one, d_scale_one, d_gate_one, d_shift_two, d_scale_two, d_gate_two], axis=1
    )
    d_modulation = exact_dot(member.T, d_frame_mod)
    d_silu = jnp.dot(d_modulation, w_mod.T, precision=HIGH_PRECISION)
    d_condition = jax.vjp(jax.nn.silu, condition)[1](d_silu)[0]
    d_table_local = exact_dot(step_pick.T, d_condition)
    small = lax.psum(
        (
            jnp.sum(d_modulation, axis=0),
            jnp.sum(d_projected.astype(jnp.float32), axis=0),
            jnp.sum(d_attn.astype(jnp.float32), axis=0),
            jnp.sum(d_hidden.astype(jnp.float32), axis=0),
            jnp.sum(d_ffn.astype(jnp.float32), axis=0),
            d_table_local,
        ),
        ("batch", "blk"),
    )
    d_b_mod, d_b_qkv, d_b_out, d_b_up, d_b_down, d_table = small
    blocks_list = [
        jnp.dot(first_low.T, d_projected, preferred_element_type=jnp.float32),
        jnp.dot(attended_low.T, d_attn, preferred_element_type=jnp.float32),
        jnp.dot(second_low.T, d_hidden, preferred_element_type=jnp.float32),
    ]
    blocks_list.append(exact_dot(silu_low.T.astype(jnp.float32), d_modulation))
    wide_rows = lax.psum_scatter(
        jnp.concatenate(blocks_list, axis=1), "blk", scatter_dimension=0, tiled=True
    )
    down_part = lax.psum_scatter(
        jnp.dot(activated_low.T, d_ffn, preferred_element_type=jnp.float32),
        "blk",
        scatter_dimension=0,
        tiled=True,
    )
    wide_rows, down_part = (
        lax.psum(wide_rows.astype(jnp.bfloat16), "batch").astype(jnp.float32),
        lax.psum(down_part.astype(jnp.bfloat16), "batch").astype(jnp.float32),
    )
    qkv_end = 3 * model_width
    out_end = qkv_end + model_width
    up_end = out_end + ffn_width
    return (
        result.astype(jnp.bfloat16),
        d_inputs.astype(jnp.bfloat16),
        d_table,
        wide_rows[:, up_end:],
        d_b_mod,
        wide_rows[:, :qkv_end],
        d_b_qkv,
        wide_rows[:, qkv_end:out_end],
        d_b_out,
        wide_rows[:, out_end:up_end],
        d_b_up,
        down_part,
        d_b_down,
    )


BF = jnp.bfloat16
F32 = jnp.float32
LANES = 128
MIB = 1024 * 1024


def swapped_with(value, axis, offset):
    size = lax.axis_size(axis)
    return lax.ppermute(value, axis, [(i, i ^ offset) for i in range(size)])


def even_blocks(value, count):
    return [value] + [swapped_with(value, "blk", k) for k in range(2, count, 2)]


def gathered_blocks(value, count, zero):
    evens = even_blocks(value, count)
    waiting = [e if i in (0, count // 2 - 1) else e + zero for i, e in enumerate(evens)]
    return evens, [swapped_with(e, "blk", 1) for e in waiting]


def offset_of(index, count):
    return (2 * index) % count + (2 * index) // count


def after(value, *others):
    return lax.optimization_barrier((value,) + others)[0]


def half_swap(value, lane):
    return jnp.where((lane % 64) < 32, pltpu.roll(value, 96, 1), pltpu.roll(value, 32, 1))


def by_clip(clip, table, first, count):
    chosen = table[first : first + 1, :]
    for c in range(1, count):
        chosen = jnp.where(clip == c, table[first + c : first + c + 1, :], chosen)
    return chosen


def full(shape):
    return pl.BlockSpec(shape, lambda *_: (0,) * len(shape))


ANYWHERE = pl.BlockSpec(memory_space=pl.ANY)
SCALARS = pl.BlockSpec(memory_space=pltpu.SMEM)


KEPT = pl.BlockSpec(memory_space=pltpu.VMEM)


def in_hbm(value):
    if value.size * value.dtype.itemsize < 140000:
        return value
    return pltpu.with_memory_space_constraint(value, pltpu.HBM)


def all_in_hbm(values):
    return [in_hbm(v) for v in values]


def shape_of(shape, dtype=BF):
    size = jnp.dtype(dtype).itemsize
    for n in shape:
        size *= n
    return jax.ShapeDtypeStruct(shape, dtype) if size < 140000 else pltpu.HBM(shape, dtype)


def params(mib=24):
    return pltpu.CompilerParams(vmem_limit_bytes=mib * MIB)


def cost(flops, moved):
    return pl.CostEstimate(flops=flops, bytes_accessed=moved, transcendentals=0)


def prepare_kernel(
    count, me_ref, lengths_ref, steps_ref, table_ref, freq_ref, w_ref, b_ref, *refs
):
    silu, sems = refs[-2:]
    kept = (len(refs) - 9) // 2
    sources, targets = refs[:kept], refs[-2 - kept : -2]
    out_ref, silu_ref, clip_ref, cliprow_ref, cos_ref, sin_ref, marks_ref = refs[kept : kept + 7]
    clips = lengths_ref.shape[1]
    rows = cos_ref.shape[0] // count
    i = pl.program_id(0)

    def copies():
        return [
            pltpu.make_async_copy(
                source.at[:, pl.ds(0, target.shape[1])], target, sems.at[j]
            )
            for j, (source, target) in enumerate(zip(sources, targets))
        ]

    @pl.when(i == 0)
    def _():
        for copy in copies():
            copy.start()
        for c in range(clips):
            row = table_ref[pl.ds(steps_ref[0, c], 1), :]
            silu[c : c + 1, :] = row / (1.0 + jnp.exp(-row))
        silu_ref[...] = silu[:clips, :].astype(BF)

    out_ref[...] = dot_low(silu[...].astype(BF), w_ref[...])[:clips] + b_ref[...]

    @pl.when(i == 0)
    def _():
        def clip_and_start(places):
            clip, start, end = jnp.zeros_like(places), jnp.zeros_like(places), 0
            for c in range(clips):
                end = end + lengths_ref[0, c]
                clip = jnp.where(places >= end, c + 1, clip)
                start = jnp.where(places >= end, end, start)
            return clip, start

        for j in range(count):
            first = (me_ref[0] ^ offset_of(j, count)) * rows
            here = slice(j * rows, (j + 1) * rows)
            places = first + lax.broadcasted_iota(jnp.int32, (rows, LANES), 0)
            lane = lax.broadcasted_iota(jnp.int32, (rows, LANES), 1)
            clip, start = clip_and_start(places)
            angles = (places - start).astype(F32) * freq_ref[...]
            cos_ref[here, :] = jnp.cos(angles)
            sine = jnp.sin(angles)
            sin_ref[here, :] = jnp.where((lane % 64) < 32, -sine, sine)
            clip_ref[here, :] = clip[:, :1]
            places = first + lax.broadcasted_iota(jnp.int32, (1, rows), 1)
            cliprow_ref[:, here] = clip_and_start(places)[0]
            other = jnp.where((clip != lane) & (lane < clips), NEGATIVE, 0.0)
            marks_ref[here, :LANES] = other.astype(BF)
            marks_ref[here, LANES:] = jnp.where(clip == lane, 1.0, 0.0).astype(BF)

    @pl.when(i == pl.num_programs(0) - 1)
    def _():
        for copy in copies():
            copy.wait()


def prepare(me, lengths, steps, step_table, freqs, w_mod, b_mod, weights, own_rows, count):
    width = w_mod.shape[0]
    clips = lengths.shape[1]
    tile = width
    rows = own_rows * count
    shapes = [
        shape_of((clips, 2 * width), F32),
        shape_of((clips, width)),
        shape_of((rows, 1), jnp.int32),
        shape_of((1, rows), jnp.int32),
        shape_of((rows, LANES), F32),
        shape_of((rows, LANES), F32),
        shape_of((rows, 2 * LANES)),
    ]
    return pl.pallas_call(
        lambda *refs: prepare_kernel(count, *refs),
        grid=(2,),
        in_specs=[SCALARS] * 3
        + [
            full(step_table.shape),
            full(freqs.shape),
            pl.BlockSpec((width, tile), lambda i: (0, i)),
            pl.BlockSpec((1, tile), lambda i: (0, i)),
        ]
        + [ANYWHERE] * len(weights),
        out_specs=[pl.BlockSpec((clips, tile), lambda i: (0, i))]
        + [full(v.shape) for v in shapes[1:]]
        + [KEPT] * len(weights),
        out_shape=shapes + [pltpu.VMEM(w.shape, w.dtype) for w in weights],
        scratch_shapes=[pltpu.VMEM((8, width), F32), pltpu.SemaphoreType.DMA((len(weights),))],
        compiler_params=params(),
        cost_estimate=cost(4 * clips * width * width, 5 * width * width),
    )(me, lengths, steps, *all_in_hbm([step_table, freqs, w_mod, b_mod, *weights]))


def modulate_kernel(silu_ref, w_ref, b_ref, out_ref):
    out_ref[...] = dot_low(silu_ref[...], w_ref[...]) + b_ref[...]


def modulate(silu, w_mod, b_mod):
    clips, width = silu.shape
    return pl.pallas_call(
        modulate_kernel,
        grid=(4,),
        in_specs=[
            full(silu.shape),
            pl.BlockSpec((width, width), lambda i: (0, 2 + i)),
            pl.BlockSpec((1, width), lambda i: (0, 2 + i)),
        ],
        out_specs=pl.BlockSpec((clips, width), lambda i: (0, i)),
        out_shape=shape_of((clips, 4 * width), F32),
        compiler_params=params(),
        cost_estimate=cost(8 * clips * width * width, 8 * width * width),
    )(*all_in_hbm([silu, w_mod, b_mod]))


def project_kernel(clips, with_own, me_ref, clip_ref, mod_ref, b_ref, cos_ref, sin_ref, w, *refs):
    copies = []
    if not with_own:
        source, (w, sems), refs = w, refs[-2:], refs[:-2]
        width, step = source.shape[0], 512
        column = pl.ds(pl.multiple_of(me_ref[0] * LANES, LANES), LANES)
        copies = [pltpu.make_async_copy(source.at[:, column], w.at[:, pl.ds(0, LANES)], sems.at[0])]
        for i, start in enumerate(range(width, 3 * width, step)):
            here = pl.ds(start, step)
            copies.append(
                pltpu.make_async_copy(source.at[:, here], w.at[:, here], sems.at[1 + i])
            )
        for copy in copies:
            copy.start()
    blocks = refs[: len(refs) - (5 if with_own else 3)]
    h_ref, kv_ref, q_ref = refs[len(blocks) : len(blocks) + 3]
    rows, width = blocks[0].shape
    column = pl.multiple_of(me_ref[0] * LANES, LANES)
    if with_own:
        own_ref, passed_ref = refs[-2:]
        passed_ref[...] = blocks[-1][...]
        blocks = blocks[:-1]

    mod = mod_ref[...]
    for pair in range(len(blocks) // 2):
        here = slice(2 * pair * rows, 2 * (pair + 1) * rows)
        x = jnp.concatenate([blocks[2 * pair][...], blocks[2 * pair + 1][...]], axis=0).astype(F32)
        normed, _ = norm_parts(x)
        clip = clip_ref[here, :]
        scale = by_clip(clip, mod[:, width:], 0, clips)
        h_ref[here, :] = (normed * (1.0 + scale) + by_clip(clip, mod[:, :width], 0, clips)).astype(BF)

    h = h_ref[...]
    cosine, sine = cos_ref[...], sin_ref[...]
    lane = lax.broadcasted_iota(jnp.int32, cosine.shape, 1)

    def turned(piece, some):
        return piece * cosine[:some] + half_swap(piece, lane[:some]) * sine[:some]

    if with_own:
        heads = w[:, pl.ds(column, LANES)]
    else:
        copies[0].wait()
        heads = w[:, :LANES]
    part = dot_low(h, heads) + b_ref[:, pl.ds(column, LANES)]
    q_ref[...] = (turned(part, h.shape[0]) * 0.125).astype(BF)
    step = 2 * LANES
    for start in range(0 if with_own else width, 3 * width, step):
        some = rows if start < width else h.shape[0]
        if copies and (start - width) % 512 == 0:
            copies[1 + (start - width) // 512].wait()
        part = dot_low(h[:some], w[:, start : start + step]) + b_ref[:, start : start + step]
        for inner in range(0, step, LANES):
            piece = part[:, inner : inner + LANES]
            at = start + inner
            if start < 2 * width:
                piece = turned(piece, some)
            if start < width:
                own_ref[:, at : at + LANES] = (piece * 0.125).astype(BF)
            else:
                kv_ref[(at - width) // LANES] = piece.astype(BF)


def project(half, blocks, me, clip_col, modulation, w_qkv, b_qkv, cosine, sine, passed=None):
    with_own = passed is not None
    own_rows, width = blocks[0].shape
    rows = own_rows * len(blocks)
    clips = modulation.shape[0]
    out_shape = [
        shape_of((rows, width)),
        pltpu.VMEM((2 * width // LANES, rows, LANES), BF),
        shape_of((rows, LANES)),
    ]
    if with_own:
        out_shape += [shape_of((own_rows, width)), shape_of(passed.shape)]
        blocks = blocks + [passed]
    return pl.pallas_call(
        lambda *refs: project_kernel(clips, with_own, *refs),
        grid=(1,),
        in_specs=[
            SCALARS,
            pl.BlockSpec((rows, 1), lambda *_: (half, 0)),
            pl.BlockSpec((clips, 2 * width), lambda *_: (0, 0)),
            full(b_qkv.shape),
            pl.BlockSpec((rows, LANES), lambda *_: (half, 0)),
            pl.BlockSpec((rows, LANES), lambda *_: (half, 0)),
            KEPT if with_own else ANYWHERE,
        ]
        + [full(v.shape) for v in blocks],
        out_specs=[full(out_shape[0].shape), KEPT] + [full(o.shape) for o in out_shape[2:]],
        out_shape=out_shape,
        scratch_shapes=[]
        if with_own
        else [pltpu.VMEM(w_qkv.shape, BF), pltpu.SemaphoreType.DMA((1 + 4 * width // 1024,))],
        compiler_params=params(),
        cost_estimate=cost(4 * rows * width * width, 6 * MIB),
    )(me, *all_in_hbm([clip_col, modulation, b_qkv, cosine, sine]), w_qkv if with_own else in_hbm(w_qkv), *all_in_hbm(blocks))


def contract_last(left, right):
    return lax.dot_general(left, right, (((1,), (1,)), ((), ())), preferred_element_type=F32)


def head_rows(value):
    lane = lax.broadcasted_iota(jnp.int32, value.shape, 1)
    zero = jnp.zeros_like(value)
    return jnp.concatenate(
        [jnp.where(lane < 64, value, zero), jnp.where(lane < 64, zero, value)], axis=0
    )


def head_diagonal(value):
    rows = value.shape[1] // 2
    return jnp.concatenate([value[:64, :rows], value[64:, rows:]], axis=0).T


def softmax_over_keys(keys, queries):
    scores = contract_last(keys, queries)
    expo = jnp.exp(scores - jnp.max(scores, axis=0, keepdims=True))
    return expo, 1.0 / jnp.sum(expo, axis=0, keepdims=True)


def attend_kernel(keymark_ref, rowmark_ref, q_ref, ka_ref, kb_ref, *refs):
    sources, o_ref, targets = refs[:3], refs[3], refs[4:7]
    keys, values, queries, sems = refs[7:]
    half = ka_ref.shape[1]
    pair, pairs = pl.program_id(0), pl.num_programs(0)

    def copies():
        return [
            pltpu.make_async_copy(source, target, sems.at[j])
            for j, (source, target) in enumerate(zip(sources, targets))
        ]

    @pl.when(pair == 0)
    def _():
        for copy in copies():
            copy.start()

    @pl.when(pair == pairs - 1)
    def _():
        for copy in copies():
            copy.wait()

    @pl.when(pair == 0)
    def _():
        keys[:, LANES:] = keymark_ref[...]
        marks = rowmark_ref[...]
        queries[:, LANES:] = jnp.concatenate([marks, marks], axis=0)

    keys[:half, :LANES] = ka_ref[pair]
    keys[half:, :LANES] = kb_ref[pair]
    values[:half] = ka_ref[pairs + pair]
    values[half:] = kb_ref[pairs + pair]
    queries[:, :LANES] = head_rows(q_ref[...])
    expo, inverse = softmax_over_keys(keys[...], queries[...])
    turned = jnp.dot(values[...].T, expo.astype(BF), preferred_element_type=F32) * inverse
    o_ref[...] = head_diagonal(turned).astype(BF)


def attend(q, kv_a, kv_b, marks, weights):
    own_rows, width = q.shape
    rows = 2 * kv_a.shape[1]
    return pl.pallas_call(
        attend_kernel,
        grid=(width // LANES,),
        in_specs=[
            pl.BlockSpec((rows, LANES), lambda p: (0, 0)),
            pl.BlockSpec((own_rows, LANES), lambda p: (0, 1)),
            pl.BlockSpec((own_rows, LANES), lambda p: (0, p)),
            KEPT,
            KEPT,
        ]
        + [ANYWHERE] * 3,
        out_specs=[pl.BlockSpec((own_rows, LANES), lambda p: (0, p))] + [KEPT] * 3,
        out_shape=[shape_of((own_rows, width))] + [pltpu.VMEM(w.shape, BF) for w in weights],
        scratch_shapes=[
            pltpu.VMEM((rows, 2 * LANES), BF),
            pltpu.VMEM((rows, LANES), BF),
            pltpu.VMEM((2 * own_rows, 2 * LANES), BF),
            pltpu.SemaphoreType.DMA((3,)),
        ],
        compiler_params=params(),
        cost_estimate=cost(4 * own_rows * rows * width, MIB),
    )(*all_in_hbm([marks, marks, q]), kv_a, kv_b, *all_in_hbm(weights))


def probs_kernel(me_ref, keyclip_ref, rowclip_ref, qa_ref, qb_ref, ka_ref, kb_ref, *refs):
    out_ref, keys = refs[-3], refs[-1]
    i, blocks = pl.program_id(0), pl.num_programs(0)
    half = ka_ref.shape[1]

    @pl.when(i == 0)
    def _():
        keys[:half] = ka_ref[0]
        keys[half:] = kb_ref[0]

    query = jnp.where(i < blocks // 2, qa_ref[...], qb_ref[...])
    visible = keyclip_ref[...] == rowclip_ref[...]
    visible = jnp.concatenate([visible, visible], axis=1)
    scores = jnp.where(visible, contract_last(keys[...], head_rows(query)), NEGATIVE)
    expo = jnp.exp(scores - jnp.max(scores, axis=0, keepdims=True))
    out_ref[...] = expo * (1.0 / jnp.sum(expo, axis=0, keepdims=True))


def heads_probs(me, q_a, q_b, kv_a, kv_b, clip_col, clip_row, blocks, earlier, passed):
    half = kv_a.shape[1]
    rows = 2 * half
    own_rows = rows // blocks
    halfway = blocks // 2
    grid_spec = pltpu.PrefetchScalarGridSpec(
        num_scalar_prefetch=1,
        grid=(blocks,),
        in_specs=[
            pl.BlockSpec((rows, 1), lambda i, m: (0, 0)),
            pl.BlockSpec((1, own_rows), lambda i, m: (0, i)),
            pl.BlockSpec((own_rows, LANES), lambda i, m: (jnp.minimum(i, halfway - 1), 0)),
            pl.BlockSpec((own_rows, LANES), lambda i, m: (jnp.maximum(i - halfway, 0), 0)),
            pl.BlockSpec((1, half, LANES), lambda i, m: (m[0], 0, 0)),
            pl.BlockSpec((1, half, LANES), lambda i, m: (m[0], 0, 0)),
        ]
        + [ANYWHERE] * 2,
        out_specs=[pl.BlockSpec((rows, 2 * own_rows), lambda i, m: (0, i)), ANYWHERE],
        scratch_shapes=[pltpu.VMEM((rows, LANES), BF)],
    )
    return pl.pallas_call(
        probs_kernel,
        grid_spec=grid_spec,
        out_shape=[shape_of((rows, 2 * rows), F32), shape_of(passed.shape, passed.dtype)],
        input_output_aliases={8: 1},
        compiler_params=params(),
        cost_estimate=cost(4 * rows * rows * LANES, 9 * MIB),
    )(me, *all_in_hbm([clip_col, clip_row, q_a, q_b]), *all_in_hbm([kv_a, kv_b, earlier, passed]))


def attend_back_kernel(
    me_ref, p_ref, qa_ref, qb_ref, ka_ref, kb_ref, va_ref, vb_ref, do_ref, cos_ref, sin_ref, *refs
):
    out_ref, sent_ref = refs[-8:-6]
    dk_ref, dv_ref, values, keys_turned, d_probs = refs[-5:]
    i, blocks = pl.program_id(0), pl.num_programs(0)
    rows = do_ref.shape[1]
    half = ka_ref.shape[1]
    me = me_ref[0]

    @pl.when(i == 0)
    def _():
        dk_ref[...] = jnp.zeros_like(dk_ref)
        dv_ref[...] = jnp.zeros_like(dv_ref)
        for at, key_ref, value_ref in ((0, ka_ref, va_ref), (half, kb_ref, vb_ref)):
            values[at : at + half] = value_ref[0]
            keys_turned[:, at : at + half] = key_ref[0].T

    query = jnp.where(i < blocks // 2, qa_ref[...], qb_ref[...])
    q_two, up_two = head_rows(query), head_rows(do_ref[0])
    delta = jnp.zeros((1, 2 * rows), F32)
    step = 256
    for start in range(0, 2 * half, step):
        part = slice(start, start + step)
        probs_low = p_ref[part, :].astype(BF)
        dv_ref[part, :] += dot_low(probs_low, up_two)
        products = contract_last(values[part, :], up_two)
        d_probs[part, :] = products
        delta += jnp.sum(probs_low.astype(F32) * products, axis=0, keepdims=True)
    d_query = jnp.zeros((LANES, 2 * rows), F32)
    for start in range(0, 2 * half, step):
        part = slice(start, start + step)
        ds = (p_ref[part, :] * (d_probs[part, :] - delta)).astype(BF)
        dk_ref[part, :] += dot_low(ds, q_two)
        d_query += dot_low(keys_turned[:, part], ds)
    lane = lax.broadcasted_iota(jnp.int32, (rows, LANES), 1)

    def turned_back(value, where):
        return (value * cos_ref[where, :] - half_swap(value, lane) * sin_ref[where, :]).astype(BF)

    here = pl.ds(pl.multiple_of(i * rows, rows), rows)
    dq = turned_back(head_diagonal(d_query) * 0.125, here)
    out_ref[here, 0:LANES] = dq
    sent_ref[me ^ offset_of(i, blocks), :, 0:LANES] = dq

    @pl.when(i == blocks - 1)
    def _():
        @pl.loop(0, blocks)
        def _(j):
            there = pl.ds(pl.multiple_of(j * rows, rows), rows)
            dk = turned_back(dk_ref[there, :], there)
            dv = dv_ref[there, :].astype(BF)
            out_ref[there, LANES : 2 * LANES] = dk
            out_ref[there, 2 * LANES : 3 * LANES] = dv
            owner = me ^ offset_of(j, blocks)
            sent_ref[owner, :, LANES : 2 * LANES] = dk
            sent_ref[owner, :, 2 * LANES : 3 * LANES] = dv


def attend_back(me, probs, q_a, q_b, kv_a, kv_b, d_o, cosine, sine, passed, earlier):
    half = kv_a.shape[1]
    rows = 2 * half
    pairs = kv_a.shape[0] // 2
    blocks, own_rows, _ = d_o.shape
    halfway = blocks // 2
    grid_spec = pltpu.PrefetchScalarGridSpec(
        num_scalar_prefetch=1,
        grid=(blocks,),
        in_specs=[
            pl.BlockSpec((rows, 2 * own_rows), lambda i, m: (0, i)),
            pl.BlockSpec((own_rows, LANES), lambda i, m: (jnp.minimum(i, halfway - 1), 0)),
            pl.BlockSpec((own_rows, LANES), lambda i, m: (jnp.maximum(i - halfway, 0), 0)),
            pl.BlockSpec((1, half, LANES), lambda i, m: (m[0], 0, 0)),
            pl.BlockSpec((1, half, LANES), lambda i, m: (m[0], 0, 0)),
            pl.BlockSpec((1, half, LANES), lambda i, m: (pairs + m[0], 0, 0)),
            pl.BlockSpec((1, half, LANES), lambda i, m: (pairs + m[0], 0, 0)),
            pl.BlockSpec((1, own_rows, LANES), lambda i, m: (m[0] ^ offset_of(i, blocks), 0, 0)),
            pl.BlockSpec((rows, LANES), lambda i, m: (0, 0)),
            pl.BlockSpec((rows, LANES), lambda i, m: (0, 0)),
            ANYWHERE,
        ]
        + [ANYWHERE] * len(earlier),
        out_specs=[
            pl.BlockSpec((rows, 3 * LANES), lambda i, m: (0, 0)),
            pl.BlockSpec((blocks, own_rows, 3 * LANES), lambda i, m: (0, 0, 0)),
            ANYWHERE,
        ],
        scratch_shapes=[
            pltpu.VMEM((rows, LANES), F32),
            pltpu.VMEM((rows, LANES), F32),
            pltpu.VMEM((rows, LANES), BF),
            pltpu.VMEM((LANES, rows), BF),
            pltpu.VMEM((rows, 2 * own_rows), F32),
        ],
    )
    return pl.pallas_call(
        attend_back_kernel,
        grid_spec=grid_spec,
        out_shape=[
            shape_of((rows, 3 * LANES)),
            shape_of((blocks, own_rows, 3 * LANES)),
            shape_of(passed.shape, passed.dtype),
        ],
        input_output_aliases={11: 2},
        compiler_params=params(),
        cost_estimate=cost(8 * rows * rows * LANES, 12 * MIB),
    )(
        me,
        *all_in_hbm([probs, q_a, q_b]),
        *all_in_hbm([kv_a, kv_b, kv_a, kv_b]),
        d_o,
        *all_in_hbm([cosine, sine, passed, *earlier]),
    )


def norm_parts(inputs):
    centred = inputs - jnp.mean(inputs, axis=-1, keepdims=True)
    rstd = lax.rsqrt(jnp.mean(centred * centred, axis=-1, keepdims=True) + 1e-06)
    return centred * rstd, rstd


def norm_back(normed, rstd, gradient):
    return rstd * (
        gradient
        - jnp.mean(gradient, axis=-1, keepdims=True)
        - normed * jnp.mean(gradient * normed, axis=-1, keepdims=True)
    )


def dot_low(left, right):
    return jnp.dot(left, right, preferred_element_type=F32)


def dot_rows(left, right):
    return lax.dot_general(left, right, (((0,), (0,)), ((), ())), preferred_element_type=F32)


def gelu_parts(hidden):
    square = hidden * hidden
    tanh = jnp.tanh(0.7978845608028654 * hidden * (1.0 + 0.044715 * square))
    upper = 0.5 * (1.0 + tanh)
    slope = upper + 0.5 * hidden * (1.0 - tanh * tanh) * (
        0.7978845608028654 * (1.0 + 3.0 * 0.044715 * square)
    )
    return hidden * upper, slope


def high_low(value):
    high = value.astype(BF)
    return high, (value - high.astype(F32)).astype(BF)


class RowSums:
    def __init__(self, clip_row, clips):
        self.place = lax.broadcasted_iota(jnp.int32, (8, clip_row.shape[1]), 0)
        self.member = ((self.place == clip_row) & (self.place < clips)).astype(F32).astype(BF)

    def by_clip(self, value):
        high, low = high_low(value)
        return dot_low(
            jnp.concatenate([self.member, self.member], axis=1),
            jnp.concatenate([high, low], axis=0),
        )

    def whole(self, value, row):
        total = jnp.sum(value.astype(F32), axis=0, keepdims=True)
        place = lax.broadcasted_iota(jnp.int32, (8, value.shape[1]), 0)
        return jnp.where(place == row, total, 0.0)


def middle_kernel(
    clips, steps_ref, clipc_ref, clipr_ref, x_ref, dy_ref, o_ref, mod_ref, bo_ref, bu_ref, bd_ref,
    wo, wu, wd, *refs,
):
    out_ref, h2_ref, dx_ref, da_ref, do_ref, sums_ref = refs[-6:]
    width = x_ref.shape[1]
    ffn = wu.shape[1]
    clip = clipc_ref[...]

    def frame_rows(index):
        return by_clip(clip, mod_ref[:, (index - 2) * width : (index - 1) * width], 0, clips)

    gate_one, scale_two, gate_two = frame_rows(2), 1.0 + frame_rows(4), frame_rows(5)
    upstream = dy_ref[...].astype(F32)
    d_ffn = (gate_two * upstream).astype(BF)
    attn_out = dot_low(o_ref[...], wo[...]) + bo_ref[...]
    middle = x_ref[...].astype(F32) + gate_one * attn_out
    normed, rstd = norm_parts(middle)
    second = (normed * scale_two + frame_rows(3)).astype(BF)
    h2_ref[...] = second
    sums = RowSums(clipr_ref[...], clips)
    ffn_out = jnp.zeros(x_ref.shape, F32)
    d_second = jnp.zeros(x_ref.shape, F32)
    step = 512
    up_sums = []
    for start in range(0, ffn, step):
        here = slice(start, start + step)
        activated, slope = gelu_parts(dot_low(second, wu[:, here]) + bu_ref[:, here])
        ffn_out += dot_low(activated.astype(BF), wd[here, :])
        d_hidden = (contract_last(d_ffn, wd[here, :]) * slope).astype(BF)
        d_second += contract_last(d_hidden, wu[:, here])
        up_sums.append(sums.whole(d_hidden, clips))
    ffn_out += bd_ref[...]
    out_ref[...] = (middle + gate_two * ffn_out).astype(BF)
    d_middle = upstream + norm_back(normed, rstd, d_second * scale_two)
    dx_ref[...] = d_middle
    d_attn = (gate_one * d_middle).astype(BF)
    da_ref[...] = d_attn
    d_o = contract_last(d_attn, wo[...]).astype(BF)
    for k in range(width // LANES):
        do_ref[k] = d_o[:, k * LANES : (k + 1) * LANES]
    up_sums = jnp.concatenate(up_sums, axis=1)
    place = lax.broadcasted_iota(jnp.int32, (8, width), 0)
    lane = lax.broadcasted_iota(jnp.int32, (8, width), 1)
    steps = jnp.zeros((8, width), F32)
    for c in range(clips):
        here = (place == clips + 1) & (lane == c)
        steps = jnp.where(here, steps_ref[0, c].astype(F32), steps)
    sums_ref[:, :width] = (
        sums.by_clip(d_middle * attn_out) + sums.whole(d_attn, clips) + steps
    )
    sums_ref[:, width : 2 * width] = sums.by_clip(d_second) + up_sums[:, :width]
    sums_ref[:, 2 * width : 3 * width] = sums.by_clip(d_second * normed) + up_sums[:, width:]
    sums_ref[:, 3 * width :] = sums.by_clip(upstream * ffn_out) + sums.whole(d_ffn, clips)


def middle_part(
    steps, clip_col, clip_row, frames, cotangent, attended, modulation, b_out, b_up, b_down,
    w_out, w_up, w_down, earlier,
):
    rows, width = frames.shape
    clips = modulation.shape[0]
    small = [
        clip_col, clip_row, frames, cotangent, attended, modulation, b_out, b_up, b_down
    ]
    out_shape = [
        shape_of((rows, width)),
        shape_of((rows, width)),
        shape_of((rows, width), F32),
        shape_of((rows, width)),
        shape_of((width // LANES, rows, LANES)),
        shape_of((8, 4 * width), F32),
    ]
    return pl.pallas_call(
        lambda *refs: middle_kernel(clips, *refs),
        grid=(1,),
        in_specs=[SCALARS, full((rows, 1)), full((1, rows))]
        + [full(v.shape) for v in small[2:]]
        + [KEPT] * 3
        + [ANYWHERE] * len(earlier),
        out_specs=[full(o.shape) for o in out_shape],
        out_shape=out_shape,
        compiler_params=params(),
        cost_estimate=cost(20 * rows * width * width, 3 * MIB),
    )(steps, *all_in_hbm(small), w_out, w_up, w_down, *all_in_hbm(earlier))


def last_kernel(clips, clipc_ref, clipr_ref, x_ref, mod_ref, dx_ref, d_ref, w_hbm, *refs):
    passed = (len(refs) - 5) // 2
    out_ref, sums_ref = refs[passed : passed + 2]
    d_all, w, sems = refs[-3:]
    width = x_ref.shape[1]
    parts = 3
    copies = [
        pltpu.make_async_copy(
            w_hbm.at[:, pl.ds(i * width, width)], w.at[:, pl.ds(i * width, width)], sems.at[i]
        )
        for i in range(parts)
    ]
    for copy in copies:
        copy.start()
    for k in range(d_ref.shape[0]):
        for i in range(3):
            at = i * width + k * LANES
            d_all[:, at : at + LANES] = d_ref[k, :, i * LANES : (i + 1) * LANES]
    normed, rstd = norm_parts(x_ref[...].astype(F32))
    scale = 1.0 + by_clip(clipc_ref[...], mod_ref[...], 0, clips)
    d_first = jnp.zeros(x_ref.shape, F32)
    for i in range(parts):
        copies[i].wait()
        here = slice(i * width, (i + 1) * width)
        d_first += contract_last(d_all[:, here], w[:, here])
    out_ref[...] = (dx_ref[...] + norm_back(normed, rstd, d_first * scale)).astype(BF)
    sums = RowSums(clipr_ref[...], clips)
    sums_ref[:, :width] = (
        sums.by_clip(d_first)
        + sums.whole(d_all[:, :width], clips)
        + sums.whole(d_all[:, width : 2 * width], clips + 1)
    )
    sums_ref[:, width:] = sums.by_clip(d_first * normed) + sums.whole(d_all[:, 2 * width :], clips)


def last_part(clip_col, clip_row, frames, modulation, d_middle, d_own, w_qkv, passed):
    rows, width = frames.shape
    clips = modulation.shape[0]
    return pl.pallas_call(
        lambda *refs: last_kernel(clips, *refs),
        grid=(1,),
        in_specs=[
            full((rows, 1)),
            full((1, rows)),
            full(frames.shape),
            pl.BlockSpec((clips, width), lambda *_: (0, 1)),
            full(d_middle.shape),
            full(d_own.shape),
        ]
        + [ANYWHERE] * (1 + len(passed)),
        out_specs=[full((rows, width)), full((8, 2 * width))] + [ANYWHERE] * len(passed),
        out_shape=[shape_of((rows, width)), shape_of((8, 2 * width), F32)]
        + [shape_of(v.shape, v.dtype) for v in passed],
        input_output_aliases={7 + i: 2 + i for i in range(len(passed))},
        scratch_shapes=[
            pltpu.VMEM((rows, 3 * width), BF),
            pltpu.VMEM(w_qkv.shape, BF),
            pltpu.SemaphoreType.DMA((3,)),
        ],
        compiler_params=params(),
        cost_estimate=cost(6 * rows * width * width, 2 * MIB),
    )(
        *all_in_hbm([clip_col, clip_row, frames, modulation, d_middle]),
        d_own,
        *all_in_hbm([w_qkv, *passed]),
    )


def half_rows(core, value, kept_ref, sent_refs, at, columns):
    half = value.shape[0] // 2
    low, high = value[:half], value[half:]
    here = slice(at, at + half)
    kept_ref[here, columns] = jnp.where(core == 0, low, high)
    sent = jnp.where(core == 0, high, low).astype(BF)
    wide = sent_refs[0].shape[1]
    for i, ref in enumerate(sent_refs):
        start, stop = max(columns.start, i * wide), min(columns.stop, (i + 1) * wide)
        if start < stop:
            ref[here, start - i * wide : stop - i * wide] = sent[
                :, start - columns.start : stop - columns.start
            ]


def weights_kernel(clips, count, who_ref, clip_ref, gate_ref, bu_ref, wu_hbm, wd_hbm, *refs):
    kept_ref, sent_ref, (up_sum, down_sum, wu, wd, sems) = refs[-9], refs[-8:-5], refs[-5:]
    ha_ref, hb_ref, d_ref, mine_ref, theirs_ref = refs[:5]
    blocks = refs[5 : 5 + count]
    seconds, upstreams = blocks[: len(blocks) // 2], blocks[len(blocks) // 2 :]
    me, core = who_ref[0], who_ref[1]
    rows, width = seconds[0].shape
    part = up_sum.shape[1]
    columns = d_ref.shape[1]
    half = ha_ref.shape[0]
    own = pl.ds(pl.multiple_of((me // 2) * part, part), part)
    copies = [
        pltpu.make_async_copy(wu_hbm.at[:, own], wu, sems.at[0]),
        pltpu.make_async_copy(wd_hbm.at[own, :], wd, sems.at[1]),
    ]
    for copy in copies:
        copy.start()
    shard = part // 2

    step = 2 * LANES
    for start in range(0, width, step):
        here = slice(start, start + step)
        value = dot_rows(ha_ref[:, here], d_ref[:half, :])
        value += dot_rows(hb_ref[:, here], d_ref[half:, :])
        for inner in range(0, step, LANES):
            half_rows(
                core, value[inner : inner + LANES], kept_ref, sent_ref, (start + inner) // 2,
                slice(0, columns),
            )

    left = jnp.concatenate([mine_ref[:, :width], theirs_ref[:, :width]], axis=0)
    right = jnp.concatenate([mine_ref[:, width:], theirs_ref[:, width:]], axis=0)
    at = columns + 2 * part
    for start in range(0, width, step):
        value = dot_rows(left[:, start : start + step], right)
        for inner in range(0, step, LANES):
            half_rows(
                core, value[inner : inner + LANES], kept_ref, sent_ref, (start + inner) // 2,
                slice(at, at + width // 2),
            )

    for copy in copies:
        copy.wait()
    up_weights, down_weights = wu[...], wd[...]
    for pair in range(len(seconds) // 2):
        here = slice(2 * pair * rows, 2 * (pair + 1) * rows)
        second = jnp.concatenate([r[...] for r in seconds[2 * pair : 2 * pair + 2]], axis=0)
        upstream = jnp.concatenate([r[...] for r in upstreams[2 * pair : 2 * pair + 2]], axis=0)
        gate = by_clip(clip_ref[here, :], gate_ref[...], 0, clips)
        d_ffn = (gate * upstream.astype(F32)).astype(BF)
        activated, slope = gelu_parts(dot_low(second, up_weights) + bu_ref[:, own])
        d_hidden = (contract_last(d_ffn, down_weights) * slope).astype(BF)
        up, down = dot_rows(second, d_hidden), dot_rows(activated.astype(BF), d_ffn)
        if pair == 0:
            up_sum[...] = up
            down_sum[...] = down
        else:
            up_sum[...] += up
            down_sum[...] += down
    for y in range(2):
        mine = slice(y * shard, (y + 1) * shard)
        at = columns + 2 * y * shard
        for k in range(width // LANES):
            half_rows(
                core, up_sum[k * LANES : (k + 1) * LANES, mine], kept_ref, sent_ref,
                k * LANES // 2, slice(at, at + shard),
            )
        for c in range(width // shard):
            half_rows(
                core, down_sum[mine, c * shard : (c + 1) * shard], kept_ref, sent_ref,
                c * shard // 2, slice(at + shard, at + 2 * shard),
            )


def weights_part(who, clip_col, modulation, b_up, w_up, w_down, h1_a, h1_b, d_qkv, outs, seconds, upstreams):
    width, ffn = w_up.shape
    count = 2 * len(seconds)
    part = 2 * ffn // count
    clips = modulation.shape[0]
    shape = (width // 2, d_qkv.shape[1] + 2 * part + width // 2)
    rows = d_qkv.shape[0]
    arrays = [h1_a, h1_b, d_qkv, *outs, *seconds, *upstreams]
    return pl.pallas_call(
        lambda *refs: weights_kernel(clips, count, *refs),
        grid=(1,),
        in_specs=[
            SCALARS,
            pl.BlockSpec((rows // 2, 1), lambda *_: (0, 0)),
            pl.BlockSpec((clips, width), lambda *_: (0, 3)),
            full(b_up.shape),
            ANYWHERE,
            ANYWHERE,
        ]
        + [full(v.shape) for v in arrays],
        out_specs=[full(shape)] + [full((shape[0], shape[1] // 3))] * 3,
        out_shape=[shape_of(shape, F32)] + [shape_of((shape[0], shape[1] // 3))] * 3,
        scratch_shapes=[
            pltpu.VMEM((width, part), F32),
            pltpu.VMEM((part, width), F32),
            pltpu.VMEM((width, part), BF),
            pltpu.VMEM((part, width), BF),
            pltpu.SemaphoreType.DMA((2,)),
        ],
        compiler_params=params(36),
        cost_estimate=cost(7 * rows * width * part, 10 * MIB),
    )(who, *all_in_hbm([clip_col, modulation, b_up, w_up, w_down, *arrays]))


def table_kernel(first, clips, place_ref, *refs):
    parts, refs = refs[:4], refs[4:]
    if first:
        silu_ref, w_ref = refs[:2]
        dw_ref, db_ref, out_ref, total, sums = refs[-5:]
    else:
        silu_ref, w_ref, cond_ref, pick_ref, earlier_ref, _, _ = refs[:7]
        dw_ref, db_ref, out_ref, total, sums = refs[7:]
    i = pl.program_id(0)

    @pl.when(i == 0)
    def _():
        total[...] = jnp.zeros_like(total) if first else earlier_ref[...]

    for j, part in enumerate(parts):
        value = part[...]
        valid = lax.broadcasted_iota(jnp.int32, value.shape, 0) < clips
        sums[pl.ds(pl.multiple_of((place_ref[0] ^ j) * 8, 8), 8), :] = jnp.where(valid, value, 0.0)
    high, low = high_low(sums[...])
    total[...] += contract_last(w_ref[...], jnp.concatenate([high, low], axis=0))
    silu = silu_ref[...]
    dw_ref[...] = dot_rows(
        jnp.concatenate([silu, silu], axis=0), jnp.concatenate([high, low], axis=0)
    )
    db_ref[...] = jnp.sum(sums[...], axis=0, keepdims=True)

    @pl.when(i == pl.num_programs(0) - 1)
    def _():
        if first:
            out_ref[...] = total[...]
        else:
            rows = high.shape[0]
            d_silu = total[:, :rows] + total[:, rows:]
            cond = cond_ref[...]
            gate = 1.0 / (1.0 + jnp.exp(-cond))
            d_cond = d_silu.T * (gate * (1.0 + cond * (1.0 - gate)))
            d_high, d_low = high_low(d_cond)
            lowest = (d_cond - d_high.astype(F32) - d_low.astype(F32)).astype(BF)
            pick = pick_ref[...].astype(BF)
            out_ref[...] = dot_rows(pick, d_high) + dot_rows(pick, d_low) + dot_rows(pick, lowest)


def table_part(place, sums, silu, w_mod, column, clips, rest=None, earlier=()):
    columns = sums[0].shape[1]
    width = w_mod.shape[0]
    all_columns = 6 * width
    rows, own = silu.shape
    tile = 2048
    skip = column // tile
    first = rest is None
    shapes = [
        shape_of((own, all_columns), F32),
        shape_of((1, all_columns), F32),
        shape_of((width, 2 * rows), F32),
    ]
    in_specs = [SCALARS] + [pl.BlockSpec((8, tile), lambda i: (0, i))] * 4 + [
        pl.BlockSpec((rows, own), lambda i: (0, 0)),
        pl.BlockSpec((width, tile), lambda i: (0, skip + i)),
    ]
    args = [place, *all_in_hbm([*sums, silu]), in_hbm(w_mod)]
    aliases = {}
    if first:
        in_specs += [ANYWHERE] * len(earlier)
        args += all_in_hbm(earlier)
    else:
        condition, pick, earlier, d_w, d_b = rest
        in_specs += [
            pl.BlockSpec((rows, width), lambda i: (0, 0)),
            pl.BlockSpec(pick.shape, lambda i: (0, 0)),
            pl.BlockSpec((width, 2 * rows), lambda i: (0, 0)),
            ANYWHERE,
            ANYWHERE,
        ]
        args += all_in_hbm([condition, pick, earlier, d_w, d_b])
        aliases = {10: 0, 11: 1}
        shapes[2] = shape_of((pick.shape[1], width), F32)
    return pl.pallas_call(
        lambda *refs: table_kernel(first, clips, *refs),
        grid=(columns // tile,),
        in_specs=in_specs,
        out_specs=[
            pl.BlockSpec((own, tile), lambda i: (0, skip + i)),
            pl.BlockSpec((1, tile), lambda i: (0, skip + i)),
            pl.BlockSpec(shapes[2].shape, lambda i: (0, 0)),
        ],
        out_shape=shapes,
        scratch_shapes=[
            pltpu.VMEM((width, 2 * rows), F32),
            pltpu.VMEM((rows, tile), F32),
        ],
        input_output_aliases=aliases,
        compiler_params=params(),
        cost_estimate=cost(rows * width, width),
    )(*args)


def in_order(bit, mine, other):
    return jnp.stack([jnp.where(bit == 0, mine, other), jnp.where(bit == 0, other, mine)])


def batch_parts(sums):
    return [sums] + [swapped_with(sums, "batch", k) for k in range(1, 4)]


def share_kernel(columns, part, who_ref, kept_ref, *refs):
    others = refs[:3]
    own_ref, x_ref, y_ref, both_ref, out_ref = refs[-5:]
    far, odd = who_ref[2] // 2 == 1, who_ref[0] % 2 == 1
    rows = own_ref.shape[1]
    first, second = slice(columns, columns + part), slice(columns + part, columns + 2 * part)
    for k in range(own_ref.shape[0]):
        here = slice(2 * k * rows, 2 * (k + 1) * rows)
        other = jnp.concatenate([ref[here, :] for ref in others], axis=1)
        value = kept_ref[here, :] + other.astype(F32)
        low, high = value[:rows], value[rows:]
        near, away = jnp.where(far, high, low), jnp.where(far, low, high)
        own_ref[k, :, :columns] = near[:, :columns]
        own_ref[k, :, columns:] = jnp.where(odd, near[:, second], near[:, first])
        y_ref[k] = jnp.where(odd, near[:, first], near[:, second]).astype(BF)
        x_ref[k, :, :columns] = away[:, :columns].astype(BF)
        x_ref[k, :, columns:] = jnp.where(odd, away[:, second], away[:, first]).astype(BF)
        both_ref[k] = jnp.where(odd, away[:, first], away[:, second]).astype(BF)
        out_ref[k] = jnp.concatenate(
            [low[:, columns + 2 * part :], high[:, columns + 2 * part :]], axis=1
        ).astype(BF)


def share(who, kept, others, count, columns, part):
    rows = kept.shape[0] // count // 2
    width = 2 * (kept.shape[1] - columns - 2 * part)
    shapes = [
        shape_of((count, rows, columns + part), F32),
        shape_of((count, rows, columns + part)),
        shape_of((count, rows, part)),
        shape_of((count, rows, part)),
        shape_of((count, rows, width)),
    ]
    return pl.pallas_call(
        lambda *refs: share_kernel(columns, part, *refs),
        grid=(1,),
        in_specs=[SCALARS, full(kept.shape)] + [full(v.shape) for v in others],
        out_specs=[full(v.shape) for v in shapes],
        out_shape=shapes,
        compiler_params=params(),
        cost_estimate=cost(0, 8 * MIB),
    )(who, in_hbm(kept), *others)


def gather_sums_kernel(columns, own_ref, x_ref, y_ref, both_ref, out_ref, *refs):
    sent_ref, down_ref = refs[-2:]
    count, rows, _ = own_ref.shape
    shard = y_ref.shape[2] // 2
    ready = columns + shard
    for k in range(count):
        from_x = x_ref[k].astype(F32)
        sent_ref[k, :, :columns] = (own_ref[k, :, :columns] + from_x[:, :columns]).astype(BF)
        value = (own_ref[k, :, columns:] + from_x[:, columns:]) + (
            y_ref[k].astype(F32) + both_ref[k].astype(F32)
        )
        sent_ref[k, :, columns:ready] = value[:, :shard].astype(BF)
        group, at = k % 2, k // 2 * shard
        down_ref[group * rows : (group + 1) * rows, at : at + shard] = value[:, shard:].astype(BF)
        sent_ref[k, :, ready:] = out_ref[k]


def gather_sums(own, from_x, from_y, from_both, out_parts, columns, passed):
    count, rows, _ = own.shape
    width = out_parts.shape[2]
    args = [own, from_x, from_y, from_both, out_parts]
    shapes = [
        shape_of((count, rows, columns + from_y.shape[2] // 2 + width)),
        shape_of((2 * rows, width)),
    ]
    return pl.pallas_call(
        lambda *refs: gather_sums_kernel(columns, *refs),
        grid=(1,),
        in_specs=[full(v.shape) for v in args] + [ANYWHERE] * len(passed),
        out_specs=[ANYWHERE] * len(passed) + [full(v.shape) for v in shapes],
        out_shape=[shape_of(v.shape, v.dtype) for v in passed] + shapes,
        input_output_aliases={5 + i: i for i in range(len(passed))},
        compiler_params=params(),
        cost_estimate=cost(0, 4 * MIB),
    )(in_hbm(own), from_x, from_y, from_both, *all_in_hbm([out_parts, *passed]))


def rows_kernel(columns, rows_ref, *refs):
    out_ref = refs[-1]
    count, rows, wide = rows_ref.shape
    width = out_ref.shape[1]
    shard = wide - width - columns
    total = jnp.zeros((rows, width), F32)
    for k in range(count):
        for i in range(columns // LANES):
            out_ref[i * rows : (i + 1) * rows, k * LANES : (k + 1) * LANES] = rows_ref[
                k, :, i * LANES : (i + 1) * LANES
            ]
        piece = columns // LANES + k * shard // width
        at = k * shard % width
        out_ref[piece * rows : (piece + 1) * rows, at : at + shard] = rows_ref[
            k, :, columns : columns + shard
        ]
        total += rows_ref[k, :, columns + shard :].astype(F32)
    piece = columns // LANES + count * shard // width
    out_ref[piece * rows :, :] = total.astype(BF)


def gather_rows(rows_mine, width, columns, passed, earlier):
    count, rows, wide = rows_mine.shape
    shard = wide - width - columns
    shape = ((columns // LANES + count * shard // width + 1) * rows, width)
    return pl.pallas_call(
        lambda *refs: rows_kernel(columns, *refs),
        grid=(1,),
        in_specs=[full(rows_mine.shape), ANYWHERE, ANYWHERE],
        out_specs=[ANYWHERE, full(shape)],
        out_shape=[shape_of(passed.shape, passed.dtype), shape_of(shape)],
        input_output_aliases={1: 0},
        compiler_params=params(),
        cost_estimate=cost(0, 2 * MIB),
    )(rows_mine, *all_in_hbm([passed, earlier]))


def assemble_kernel(ffn, who_ref, *refs):
    qkv_ref, out_ref, up_ref, down_ref = refs[-4:]
    width = out_ref.shape[1]
    rows = qkv_ref.shape[0] // 4
    for j, (ref, own_down) in enumerate(zip(refs[:4], refs[4:8])):
        owner = who_ref[2] ^ j
        core, far = owner % 2, owner // 2
        at = pl.multiple_of(core * 2 * rows + far * rows, rows)
        piece = 0
        for target, count in ((qkv_ref, 3), (up_ref, ffn // width)):
            for i in range(count):
                here = slice(piece * rows, (piece + 1) * rows)
                target[pl.ds(at, rows), i * width : (i + 1) * width] = ref[here, :].astype(F32)
                piece += 1
        for g in range(2):
            here = slice(g * rows, (g + 1) * rows)
            there = pl.multiple_of(core * 4 * rows + g * 2 * rows + far * rows, rows)
            down_ref[pl.ds(there, rows), :] = own_down[here, :].astype(F32)
        part = width // 2
        column = pl.multiple_of(far * part, part)
        for g in range(2):
            there = pl.multiple_of(core * 2 * rows + g * rows, rows)
            out_ref[pl.ds(there, rows), pl.ds(column, part)] = ref[
                piece * rows : (piece + 1) * rows, g * part : (g + 1) * part
            ].astype(F32)


def assemble(who, parts, own_rows, ffn):
    width = parts[0].shape[1]
    shapes = [
        shape_of((own_rows, 3 * width), F32),
        shape_of((own_rows, width), F32),
        shape_of((own_rows, ffn), F32),
        shape_of((2 * own_rows, width), F32),
    ]
    return pl.pallas_call(
        lambda *refs: assemble_kernel(ffn, *refs),
        grid=(1,),
        in_specs=[SCALARS] + [full(v.shape) for v in parts],
        out_specs=[full(o.shape) for o in shapes],
        out_shape=shapes,
        compiler_params=params(),
        cost_estimate=cost(0, 6 * MIB),
    )(who, *parts)


def heads_body(
    frames, step_table, clip_lengths, clip_steps, w_mod, b_mod, w_qkv, b_qkv, w_out, b_out,
    w_up, b_up, w_down, b_down, cotangent,
):
    own_rows, width = frames.shape
    ffn = w_up.shape[1]
    count = lax.axis_size("blk")
    me = lax.axis_index("blk")
    place = lax.axis_index("batch")
    core, far = place % 2, place // 2
    who = jnp.stack([me, core, place])
    clips = clip_lengths.shape[1]
    rows = own_rows * count

    head_size = width // HEADS
    half = head_size // 2
    lane = jnp.arange(LANES, dtype=jnp.int32)
    freqs = 10000.0 ** (-2.0 * (lane % half).astype(F32) / head_size)
    rows_of_table = jnp.arange(step_table.shape[0], dtype=jnp.int32)
    (
        modulation, silu_own, clip_col, clip_row, cosine, sine, marks, kept_qkv,
    ) = prepare(
        me[None], clip_lengths, clip_steps, step_table, freqs[None, :], w_mod, b_mod[None, :],
        [w_qkv], own_rows, count,
    )
    modulation_two = modulate(silu_own, w_mod, b_mod[None, :])
    evens, odds = gathered_blocks(frames, count, (modulation_two[0, 0] * 0.0).astype(BF))

    shared = (b_qkv[None, :], cosine, sine)
    first = (me[None], clip_col, modulation)
    h1_a, kv_a, q_a, q_own, later = project(0, evens, *first, kept_qkv, *shared, cotangent)
    upstreams = even_blocks(later, count)
    h1_b, kv_b, q_b = project(1, odds, *first, w_qkv, *shared)
    attended, kept_out, kept_up, kept_down = attend(
        q_own, kv_a, kv_b, marks, [w_out, w_up, w_down]
    )
    result, second, d_middle, d_attn, d_o, sums_two = middle_part(
        clip_steps, clip_col, clip_row, frames, cotangent, attended, modulation_two,
        b_out[None, :], b_up[None, :], b_down[None, :], kept_out, kept_up, kept_down,
        upstreams,
    )
    d_o = lax.all_to_all(d_o, "blk", 0, 0, tiled=True)
    seconds = even_blocks(second, count)
    probs, d_attn = heads_probs(
        me[None], q_a, q_b, kv_a, kv_b, clip_col, clip_row, count, d_middle, d_attn
    )
    sums_two = sums_two + swapped_with(sums_two, "blk", 1)
    sums_two = sums_two + swapped_with(sums_two, "blk", 2)

    wide = width // 2
    da_low, da_high = d_attn[:, :wide], d_attn[:, wide:]
    out_sent = jnp.concatenate([attended, jnp.where(far == 0, da_high, da_low)], axis=1)
    out_kept = jnp.concatenate([attended, jnp.where(far == 0, da_low, da_high)], axis=1)
    out_sent = swapped_with(out_sent, "batch", 2)

    d_qkv, d_qkv_sent, sums_two = attend_back(
        me[None], probs, q_a, q_b, kv_a, kv_b, d_o, cosine, sine, sums_two, seconds[:3]
    )
    d_own = lax.all_to_all(d_qkv_sent, "blk", 0, 0, tiled=True)
    kept, *sent = weights_part(
        who, clip_col, modulation_two, b_up[None, :], w_up, w_down, h1_a, h1_b, d_qkv,
        [out_kept, out_sent], seconds, upstreams,
    )
    own_sums, for_x, for_y, for_both, out_parts = share(
        who, kept, [swapped_with(v, "batch", 1) for v in sent], count, 3 * LANES, 2 * ffn // count
    )

    d_inputs, sums_one, own_sums, sums_two = last_part(
        clip_col, clip_row, frames, modulation, d_middle, d_own, w_qkv,
        [own_sums, sums_two],
    )
    sums_one = sums_one + swapped_with(sums_one, "blk", 2)
    sums_two = sums_two + swapped_with(sums_two, "blk", 4)

    pairs = [
        (b * count + k, (b ^ 2) * count + (k ^ 1)) for b in range(4) for k in range(count)
    ]
    sums_one, sums_two, sent, down_rows = gather_sums(
        own_sums,
        swapped_with(for_x, "batch", 2),
        swapped_with(for_y, "blk", 1),
        lax.ppermute(for_both, ("batch", "blk"), pairs),
        out_parts,
        3 * LANES,
        [sums_one, sums_two],
    )
    rows_mine = lax.all_to_all(sent, "blk", 0, 0, tiled=True)
    sums_one = sums_one + swapped_with(sums_one, "blk", 1)
    sums_two = batch_parts(sums_two)
    steps_all = jnp.stack([v[clips + 1, :clips] for v in sums_two]) * (1.0 / count)
    steps_all = steps_all[place ^ jnp.arange(4, dtype=jnp.int32)].astype(jnp.int32)
    pick_all = (steps_all[:, :, None] == rows_of_table[None, None, :]).astype(F32)
    pick_all = jnp.pad(pick_all, ((0, 0), (0, 8 - clips), (0, 0))).reshape(32, -1)
    condition_all = exact_dot(pick_all, step_table)
    silu_all = jax.nn.silu(condition_all).astype(BF)
    silu_cols = lax.dynamic_slice_in_dim(silu_all, me * own_rows, own_rows, 1)
    d_w_mod, d_b_mod, d_silu = table_part(
        place[None], sums_two, silu_cols, w_mod, 2 * width, clips
    )
    sums_one, mine = gather_rows(rows_mine, width, 3 * LANES, sums_one, d_silu)
    sums_one = batch_parts(sums_one + swapped_with(sums_one, "blk", 4))
    d_w_mod, d_b_mod, d_table = table_part(
        place[None], sums_one, silu_cols, w_mod, 0, clips,
        (condition_all, pick_all, d_silu, d_w_mod, d_b_mod),
    )

    def batch_total(parts):
        return (parts[0] + parts[1]) + (parts[2] + parts[3])

    bias_two = batch_total([v[clips] for v in sums_two])
    bias_one = batch_total([v[clips : clips + 2] for v in sums_one])
    d_b_qkv = jnp.concatenate(
        [bias_one[0, :width], bias_one[1, :width], bias_one[0, width:]], axis=0
    )
    d_b_out, d_b_up, d_b_down = jnp.split(bias_two, [width, width + ffn])

    def everyone(value):
        other = swapped_with(value, "batch", 2)
        return [value, swapped_with(value, "batch", 1), other, swapped_with(other, "batch", 1)]

    d_w_qkv, d_w_out, d_w_up, d_w_down = assemble(
        who, everyone(mine) + everyone(down_rows), own_rows, ffn
    )

    return (
        result,
        d_inputs,
        d_table,
        d_w_mod,
        d_b_mod[0],
        d_w_qkv,
        d_b_qkv,
        d_w_out,
        d_b_out,
        d_w_up,
        d_b_up,
        d_w_down,
        d_b_down,
    )


def solution(mesh):
    blk = mesh.shape["blk"]
    heads_fit = HEADS == 2 * blk and mesh.shape["batch"] == 4
    chosen = heads_body if heads_fit else ring_body
    placed = (
        P(("batch", "blk"), None),
        P(),
        P("batch", None),
        P("batch", None),
        P(),
        P(),
        P(),
        P(),
        P(),
        P(),
        P(),
        P(),
        P(),
        P(),
        P(("batch", "blk"), None),
    )
    return jax.shard_map(
        chosen,
        mesh=mesh,
        in_specs=placed,
        out_specs=(
            P(("batch", "blk"), None),
            P(("batch", "blk"), None),
            P(),
            P("blk", None),
            P(),
            P("blk", None),
            P(),
            P("blk", None),
            P(),
            P("blk", None),
            P(),
            P("blk", None),
            P(),
        ),
        check_vma=False,
    )
```
